128 devices in a mesh: dp: 32 (over z_lo, x, y), tensor: 4 (over z_hi, core).
Axes of the slice: x: 4, y: 4, z: 4 (z_hi: 2, z_lo: 2; z = z_hi * 2 + z_lo), core: 2. Of those that a mesh axis runs over, the one named last changes fastest.
Arguments:
- images: bfloat16 [12608, 768], P('dp'), may hold values from -6 to 6
- routes: int32 [12608, 2], P('dp'), may hold values from 0 to 31, all different within a row; in each aligned block of 394 rows (0 to 393, 394 to 787, ...) at most 37 rows name the same one
- cotangent: bfloat16 [12608, 768], P('dp'), may hold values from -6 to 6
- qkv_weight: bfloat16 [2, 768, 3, 768], P(None, None, None, 'tensor'), may hold values from -0.21875 to 0.21875
- out_weight: bfloat16 [2, 768, 768], P(None, 'tensor'), may hold values from -1.5 to 1.5
- qv_bias: float32 [2, 2, 768], P(None, None, 'tensor'), may hold values from -1.5 to 1.5
- out_bias: float32 [2, 768], replicated, may hold values from -1.5 to 1.5
- ln_gain: float32 [4, 768], replicated, may hold values from 0.5 to 1.5
- ln_bias: float32 [4, 768], replicated, may hold values from -1.5 to 1.5
- dense_in: bfloat16 [768, 3072], P(None, 'tensor'), may hold values from -0.21875 to 0.21875
- dense_out: bfloat16 [3072, 768], P('tensor'), may hold values from -0.109375 to 0.109375
- router: bfloat16 [768, 32], replicated, may hold values from -0.15625 to 0.15625
- expert_in: bfloat16 [32, 768, 3072], P('dp', None, 'tensor'), may hold values from -0.21875 to 0.21875
- expert_out: bfloat16 [32, 3072, 768], P('dp', 'tensor'), may hold values from -0.109375 to 0.109375
Outputs:
- output: bfloat16 [12608, 768], P('dp')
- input_grad: float32 [12608, 768], P('dp')
- qkv_weight_grad: float32 [2, 768, 3, 768], P(None, None, None, 'tensor')
- out_weight_grad: float32 [2, 768, 768], P(None, 'tensor')
- qv_bias_grad: float32 [2, 2, 768], P(None, None, 'tensor')
- out_bias_grad: float32 [2, 768], replicated
- ln_gain_grad: float32 [4, 768], replicated
- ln_bias_grad: float32 [4, 768], replicated
- dense_in_grad: float32 [768, 3072], P(None, 'tensor')
- dense_out_grad: float32 [3072, 768], P('tensor')
- router_grad: float32 [768, 32], replicated
- expert_in_grad: float32 [32, 768, 3072], P('dp', None, 'tensor')
- expert_out_grad: float32 [32, 3072, 768], P('dp', 'tensor')
The draws below stay inside these ranges and needn't reach their ends.
Inputs may be any that keep to these rules, and one draw needn't show every extreme that they name: `routes`: each token names two different experts. Among the 394 tokens of one index of dp no expert is named by more than 37 tokens, a bound that some expert reaches in some index's tokens.
All inputs are finite; a program needn't handle non-finite values.
Results may differ from the reference program's by a relative error of at most 0.038.
Values may be sent and summed in bfloat16 or wider, within the bound.
A program may use at most 128 MiB of HBM per device.

```python
import math
import jax
import jax.numpy as jnp
import numpy as np
from jax import lax

D = 768
HEADS = 12
HEAD = 64
FF = 3072
SEQ = 197
TOK_DEV = 394
TOKENS = 12608
EXPERTS = 32
CAP = 37
N_DP = 32


def steps_of(own_key, dims, split, low, largest):
    def one(position, blocks):
        steps = jax.random.uniform(jax.random.fold_in(jax.random.fold_in(own_key, 6), position), (blocks,), jnp.float32, low / len(split), largest / len(split))
        return jnp.repeat(jnp.exp(steps), dims[position] // blocks).reshape((-1,) + (1,) * (len(dims) - position - 1))

    level = one(*split[0])
    for cut in split[1:]:
        level = level * one(*cut)
    return level


def assign_block(own_key, own, number, rows, count, top, limit, lean):
    sequence = jax.random.permutation(own_key, count)
    packed, ordinary = portions_of(count, rows * top, limit, lean, True), portions_of(count, rows * top, limit, lean, False)
    places = jnp.arange(count)

    def named(tallies, rotation):
        used = int((tallies > 0).sum())
        fixed = max(1, used // 4)
        passed = fixed + (places - fixed + rotation * (used - fixed)) % max(1, count - fixed)
        return jnp.zeros((count,), jnp.int32).at[sequence[jnp.where(places < fixed, places, passed)]].set(jnp.asarray(tallies, jnp.int32))

    tallies = jnp.where(number % 4 == 0, named(packed, number // 4), named(ordinary, number - number // 4 - 1))
    mixed = jax.random.permutation(jax.random.fold_in(own, 3), count)
    giver, sink = mixed[0:count // 2 * 2:2], mixed[1:count // 2 * 2:2]
    room = jnp.minimum(tallies[giver] - 1, limit - tallies[sink]) // 2
    room = jnp.where((giver == sequence[0]) | (sink == sequence[0]) | (tallies[sink] == 0), 0, jnp.maximum(room, 0))
    passed = jax.random.randint(jax.random.fold_in(own, 4), (count // 2,), 0, 1 << 20) % (room + 1)
    tallies = tallies.at[giver].add(-passed).at[sink].add(passed)
    members = jnp.searchsorted(jnp.cumsum(tallies), jnp.arange(rows * top), side="right").astype(jnp.int32)
    table = members.reshape(top, rows).T
    table = table[jax.random.permutation(jax.random.fold_in(own, 1), rows)]
    rotation = jax.random.randint(jax.random.fold_in(own, 2), (rows, 1), 0, top)
    return jnp.take_along_axis(table, (jnp.arange(top)[None, :] + rotation) % top, axis=1)


def portions_of(number_of, total, bound, slope, full):
    portions = [(1 << 20) // math.isqrt(rank ** slope) + 1 for rank in range(1, number_of + 1)]
    largest = bound if full else min(bound, max(-(-total // number_of), total * portions[0] // sum(portions)))
    least = 1 if total - largest >= number_of - 1 else 0
    given, spare = [largest] + [least] * (number_of - 1), total - largest - least * (number_of - 1)
    while spare > 0:
        movable = [i for i in range(1, number_of) if given[i] < largest] or [i for i in range(1, number_of) if given[i] < bound]
        pool, budget = sum([portions[i] for i in movable]), spare
        for i in movable:
            extra = min(bound - given[i], max(1, budget * portions[i] // pool), spare)
            given[i] = given[i] + extra
            spare = spare - extra
    return np.array(given)


def gaussian(rng, extent, scale, bound, shards=(), held_as=jnp.bfloat16):
    drawn = scale * jax.random.normal(rng, extent, jnp.float32)
    if shards:
        drawn = drawn * steps_of(rng, extent, shards, -0.22, 0.18)
    return jnp.clip(drawn, -bound, bound).astype(held_as)


def setup_inputs(seed: int = 0) -> dict:
    splits = jax.random.split(jax.random.key(seed), 15)
    images = gaussian(splits[0], (TOKENS, D), 1.0, 6.0, ((0, 32),))
    routes_keys = jax.random.split(jax.random.fold_in(splits[1], 1), TOKENS // TOK_DEV)
    routes_turns = jax.random.permutation(jax.random.fold_in(splits[1], 3), TOKENS // TOK_DEV)
    routes = jax.vmap(lambda own, number: assign_block(jax.random.fold_in(splits[1], 2), own, number, TOK_DEV, EXPERTS, 2, CAP, 1))(routes_keys, routes_turns).reshape((TOKENS, 2))
    cotangent = gaussian(splits[2], (TOKENS, D), 1.0, 6.0, ((0, 32),))
    qkv_weight = gaussian(splits[3], (2, D, 3, D), D ** -0.5, 0.21875, ((3, 4),))
    out_weight = gaussian(splits[4], (2, D, D), (D * 4 // SEQ) ** -0.5, 1.5, ((1, 4),))
    qv_bias = gaussian(splits[5], (2, 2, D), 0.3, 1.5, ((2, 4),), jnp.float32)
    out_bias = gaussian(splits[6], (2, D), 0.3, 1.5, (), jnp.float32)
    ln_gain = jnp.clip(1.0 + 0.1 * jax.random.normal(splits[7], (4, D), jnp.float32), 0.5, 1.5)
    ln_bias = gaussian(splits[8], (4, D), 0.3, 1.5, (), jnp.float32)
    dense_in = gaussian(splits[9], (D, FF), D ** -0.5, 0.21875, ((1, 4),))
    dense_out = gaussian(splits[10], (FF, D), FF ** -0.5, 0.109375, ((0, 4),))
    router = gaussian(splits[11], (D, EXPERTS), (2 * D) ** -0.5, 0.15625)
    expert_in = gaussian(splits[12], (EXPERTS, D, FF), D ** -0.5, 0.21875, ((0, 32), (2, 4)))
    expert_out = gaussian(splits[13], (EXPERTS, FF, D), FF ** -0.5, 0.109375, ((0, 32), (1, 4)))
    return dict(images=images, routes=routes, cotangent=cotangent, qkv_weight=qkv_weight, out_weight=out_weight, qv_bias=qv_bias, out_bias=out_bias, ln_gain=ln_gain, ln_bias=ln_bias, dense_in=dense_in, dense_out=dense_out, router=router, expert_in=expert_in, expert_out=expert_out)


highest = lax.Precision.HIGHEST
epsilon = 1e-06

@jax.custom_vjp
def low(v):
    return lax.optimization_barrier(v.astype(jnp.bfloat16)).astype(jnp.float32)

@jax.custom_vjp
def low_back(v):
    return v

def low_keep(v):
    return (low(v), None)

def low_pass(kept, grad):
    return (grad,)

def back_keep(v):
    return (v, None)

def back_low(kept, grad):
    return (low(grad),)
low.defvjp(low_keep, low_pass)
low_back.defvjp(back_keep, back_low)

def layer_norm(inputs, gain_row, shift_row):
    average = lax.optimization_barrier(jnp.mean(inputs, axis=-1, keepdims=True))
    centered = inputs - average
    variance = lax.optimization_barrier(jnp.mean(centered * centered, axis=-1, keepdims=True))
    return centered * lax.rsqrt(variance + epsilon) * gain_row + shift_row

def attention(inputs, layer_index, qkv_w, out_w, qv_b, out_b, gains, shifts):
    normed = low(layer_norm(inputs, gains[2 * layer_index], shifts[2 * layer_index]))
    projected = jnp.einsum('td,dcf->tcf', normed, qkv_w[layer_index], precision=highest)
    queries = low(low_back(projected[:, 0] + qv_b[layer_index, 0]))
    key_rows = low(low_back(projected[:, 1]))
    value_rows = low(low_back(projected[:, 2] + qv_b[layer_index, 1]))
    image_count = inputs.shape[0] // SEQ
    head_shape = (image_count, SEQ, HEADS, HEAD)
    queries = queries.reshape(head_shape)
    key_rows = key_rows.reshape(head_shape)
    value_rows = value_rows.reshape(head_shape)
    scores = low_back(jnp.einsum('bqhd,bkhd->bhqk', queries, key_rows, precision=highest) * HEAD ** (-0.5))
    probs_low = low(jax.nn.softmax(scores, axis=-1))
    context = jnp.einsum('bhqk,bkhd->bqhd', probs_low, value_rows, precision=highest)
    context = low(low_back(context.reshape(inputs.shape[0], D)))
    projection = low_back(jnp.dot(context, out_w[layer_index], precision=highest))
    return inputs + projection + out_b[layer_index]

def dense_block(inputs, d_in, d_out, gains, shifts):
    normed = low(layer_norm(inputs, gains[1], shifts[1]))
    pre_act = low_back(jnp.dot(normed, d_in, precision=highest))
    activated = low(jax.nn.gelu(pre_act, approximate=False))
    return inputs + low_back(jnp.dot(activated, d_out, precision=highest))

def slot_rows(routes):
    one_hot = (routes[:, :, None] == jnp.arange(EXPERTS, dtype=jnp.int32)).astype(jnp.int32)
    grouped = one_hot.reshape(N_DP, TOK_DEV * 2, EXPERTS)
    running = jnp.cumsum(grouped, axis=1)
    ranking = lax.optimization_barrier(jnp.sum((running - 1) * grouped, axis=-1)).reshape(TOKENS, 2)
    block_of = (jnp.arange(TOKENS, dtype=jnp.int32) // TOK_DEV)[:, None]
    return (block_of * CAP + ranking).astype(jnp.int32)

def expert_block(inputs, routes, rout, e_in, e_out, gains, shifts):
    normed = low(layer_norm(inputs, gains[3], shifts[3]))
    logits = low_back(jnp.dot(normed, rout, precision=highest))
    chosen = jnp.take_along_axis(logits, routes, axis=1)
    gate_values = jax.nn.softmax(chosen, axis=1)
    row_index = slot_rows(routes)
    slot_buffer = jnp.zeros((EXPERTS, N_DP * CAP, D), jnp.float32)
    spread = jnp.broadcast_to(normed[:, None, :], (TOKENS, 2, D))
    slot_buffer = slot_buffer.at[routes, row_index].add(spread)
    pre_act = low_back(jnp.einsum('erd,edf->erf', slot_buffer, e_in, precision=highest))
    activated = low(jax.nn.gelu(pre_act, approximate=False))
    expert_result = low_back(jnp.einsum('erf,efd->erd', activated, e_out, precision=highest))
    picked = expert_result[routes, row_index]
    return inputs + lax.optimization_barrier(jnp.sum(gate_values[:, :, None] * picked, axis=1))

def reference(images, routes, cotangent, qkv_weight, out_weight, qv_bias, out_bias, ln_gain, ln_bias, dense_in, dense_out, router, expert_in, expert_out):

    def forward(image_rows, qkv_w, out_w, qv_b, out_b, gains, shifts, d_in, d_out, rout, e_in, e_out):
        hidden = attention(image_rows, 0, qkv_w, out_w, qv_b, out_b, gains, shifts)
        hidden = dense_block(hidden, d_in, d_out, gains, shifts)
        hidden = attention(hidden, 1, qkv_w, out_w, qv_b, out_b, gains, shifts)
        return expert_block(hidden, routes, rout, e_in, e_out, gains, shifts)
    primals = (images.astype(jnp.float32), qkv_weight.astype(jnp.float32), out_weight.astype(jnp.float32), qv_bias.astype(jnp.float32), out_bias.astype(jnp.float32), ln_gain.astype(jnp.float32), ln_bias.astype(jnp.float32), dense_in.astype(jnp.float32), dense_out.astype(jnp.float32), router.astype(jnp.float32), expert_in.astype(jnp.float32), expert_out.astype(jnp.float32))
    result, pullback = jax.vjp(forward, *primals)
    grads = pullback(cotangent.astype(jnp.float32))
    return (result.astype(jnp.bfloat16), grads[0], grads[1], grads[2], grads[3], grads[4], grads[5], grads[6], grads[7], grads[8], grads[9], grads[10], grads[11])
```

```python
import functools

import jax
import jax.numpy as jnp
from jax import lax
from jax.experimental import pallas as pl
from jax.experimental.pallas import tpu as pltpu
from jax.sharding import PartitionSpec as P

HEAD = 64
SEQ = 197


epsilon = 1e-06
bfloat = jnp.bfloat16
single = jnp.float32


MESH = pl.DeviceIdType.MESH


def tensor_sum_kernel(count, rows, p_ref, o_ref, got_one, sum_one, got_two, sum_two, got_three, sems):
    t = lax.axis_index("tensor")
    core = lax.rem(t, 2)
    sibling = {"tensor": t + 1 - 2 * core}
    opposite = {"tensor": lax.rem(t + 2, 4)}
    barrier = pltpu.get_barrier_semaphore()
    for peer in (sibling, opposite):
        pl.semaphore_signal(barrier, inc=1, device_id=peer, device_id_type=MESH)
    pl.semaphore_wait(barrier, 2)

    def columns(which, j):
        return pl.ds(pl.multiple_of((which * count + j) * 128, 128), 128)

    def copy(source, target, step, j, peer):
        return pltpu.make_async_remote_copy(
            src_ref=source,
            dst_ref=target,
            send_sem=sems.at[0, step, j],
            recv_sem=sems.at[1, step, j],
            device_id=peer,
            device_id_type=MESH,
        )

    first = [copy(p_ref.at[:, columns(1 - core, j)], got_one.at[j], 0, j, sibling) for j in range(count)]
    second = [copy(sum_one.at[j], got_two.at[j], 1, j, opposite) for j in range(count)]
    third = [copy(sum_two.at[j], got_three.at[j], 2, j, sibling) for j in range(count)]
    for j in range(count):
        first[j].start()
    for j in range(count):
        first[j].wait_recv()
        own = p_ref[:, columns(core, j)].astype(single)
        sum_one[j] = (own + got_one[j].astype(single)).astype(bfloat)
        second[j].start()
    for j in range(count):
        second[j].wait_recv()
        whole = (sum_one[j].astype(single) + got_two[j].astype(single)).astype(bfloat)
        sum_two[j] = whole
        third[j].start()
        o_ref[:, columns(core, j)] = whole
    for j in range(count):
        third[j].wait_recv()
        o_ref[:, columns(1 - core, j)] = got_three[j]
    for j in range(count):
        first[j].wait_send()
        second[j].wait_send()
        third[j].wait_send()


def tensor_sum(partial, collective_id):
    rows, width = partial.shape
    count = width // 256
    block = pltpu.VMEM((count, rows, 128), bfloat)
    return pl.pallas_call(
        functools.partial(tensor_sum_kernel, count, rows),
        out_shape=jax.ShapeDtypeStruct((rows, width), bfloat),
        in_specs=[pl.BlockSpec(memory_space=pltpu.VMEM)],
        out_specs=pl.BlockSpec(memory_space=pltpu.VMEM),
        scratch_shapes=[block] * 5 + [pltpu.SemaphoreType.DMA((2, 3, count))],
        compiler_params=pltpu.CompilerParams(
            collective_id=collective_id, has_side_effects=True, vmem_limit_bytes=32 * 2**20
        ),
        name="tensor_sum",
    )(partial)


BIG = 3072
HALF = BIG // 2
PART = HALF // 4
PIECE = PART // 4
SMALL = 48


def add_rows(target, target_row, sources, rows):
    def body(i, carry):
        total = None
        for ref, row in sources:
            value = ref[pl.ds(pl.multiple_of(row + i * 16, 16), 16), :].astype(single)
            total = value if total is None else total + value
        target[pl.ds(pl.multiple_of(target_row + i * 16, 16), 16), :] = total.astype(bfloat)
        return carry

    lax.fori_loop(0, rows // 16, body, 0)


def grad_sum_kernel(*refs):
    ins, small_in = refs[:6], refs[6]
    outs, small_out = refs[7:13], refs[13]
    (given, result, near_a, near_b, left_a, right_a, left_b, right_b, pass_a, pass_b, sum_a, sum_b) = refs[14:26]
    (near_c, near_d, left_c, right_c, left_d, right_d, pass_c, pass_d, sum_c, sum_d) = refs[26:36]
    z_got, small_x, small_y, small_z, small_one, small_two = refs[36:42]
    local_sem, send_sem, recv_sem, small_send, small_recv = refs[42:47]

    dp = lax.axis_index("dp")
    plane, x, y = dp // 16, lax.rem(dp // 4, 4), lax.rem(dp, 4)

    def at(plane_to, x_to, y_to):
        return {"dp": plane_to * 16 + x_to * 4 + y_to}

    def along_x(step):
        return at(plane, lax.rem(x + step, 4), y)

    def along_y(step):
        return at(plane, x, lax.rem(y + step, 4))

    across = at(1 - plane, x, y)
    barrier = pltpu.get_barrier_semaphore()
    peers = [along_x(1), along_x(2), along_x(3), along_y(1), along_y(2), along_y(3), across]
    for peer in peers:
        pl.semaphore_signal(barrier, inc=1, device_id=peer, device_id_type=MESH)

    sizes = [ref.shape[0] for ref in ins]
    starts = [sum(sizes[:i]) for i in range(6)]
    loads = [
        pltpu.make_async_copy(ins[i], given.at[pl.ds(starts[i], sizes[i]), :], local_sem.at[i])
        for i in range(6)
    ]
    for load in loads:
        load.start()
    for load in loads:
        load.wait()
    pl.semaphore_wait(barrier, 7)

    used = []

    def send(source, target, peer):
        k = len(used)
        copy = pltpu.make_async_remote_copy(
            src_ref=source,
            dst_ref=target,
            send_sem=send_sem.at[k],
            recv_sem=recv_sem.at[k],
            device_id=peer,
            device_id_type=MESH,
        )
        used.append(copy)
        copy.start()
        return copy

    small_used = []

    def send_small(source, target, peer):
        k = len(small_used)
        copy = pltpu.make_async_remote_copy(
            src_ref=source,
            dst_ref=target,
            send_sem=small_send.at[k],
            recv_sem=small_recv.at[k],
            device_id=peer,
            device_id_type=MESH,
        )
        small_used.append(copy)
        copy.start()
        return copy

    def rows_of(ref, row, count):
        return ref.at[pl.ds(pl.multiple_of(row, 16), count), :]

    class Scatter:
        def __init__(self, source, base, size, place, along, near, left, right, onward, total):
            self.source, self.base, self.size, self.place = source, base, size, place
            self.along, self.near, self.left, self.right = along, near, left, right
            self.onward, self.total = onward, total

        def row(self, step):
            return self.base + lax.rem(self.place + step, 4) * self.size

        def start(self):
            half = self.size // 2
            s = self.source
            self.far_right = send(rows_of(s, self.row(2), half), rows_of(self.near, 0, half), self.along(1))
            self.far_left = send(rows_of(s, self.row(2) + half, half), rows_of(self.near, half, half), self.along(3))
            self.to_right = send(rows_of(s, self.row(1) + half, half), rows_of(self.left, half, half), self.along(1))
            self.to_left = send(rows_of(s, self.row(3), half), rows_of(self.right, 0, half), self.along(3))

        def middle(self):
            half = self.size // 2
            s = self.source
            self.far_right.wait_recv()
            add_rows(self.onward, 0, [(s, self.row(1)), (self.near, 0)], half)
            self.on_right = send(rows_of(self.onward, 0, half), rows_of(self.left, 0, half), self.along(1))
            self.far_left.wait_recv()
            add_rows(self.onward, half, [(s, self.row(3) + half), (self.near, half)], half)
            self.on_left = send(rows_of(self.onward, half, half), rows_of(self.right, half, half), self.along(3))

        def finish(self):
            for copy in (self.to_right, self.to_left, self.on_right, self.on_left):
                copy.wait_recv()
            add_rows(self.total, 0, [(self.source, self.row(0)), (self.left, 0), (self.right, 0)], self.size)

    class Gather:
        def __init__(self, base, size, place, along):
            self.base, self.size, self.place, self.along = base, size, place, along

        def row(self, step):
            return self.base + lax.rem(self.place + step, 4) * self.size

        def start(self):
            own, half = self.row(0), self.size // 2
            first, second = rows_of(result, own, half), rows_of(result, own + half, half)
            self.right_one = send(first, first, self.along(1))
            self.left_two = send(second, second, self.along(3))
            self.right_two = send(second, second, self.along(1))
            self.left_one = send(first, first, self.along(3))

        def middle(self):
            half = self.size // 2
            self.right_one.wait_recv()
            from_left = rows_of(result, self.row(3), half)
            self.on_right = send(from_left, from_left, self.along(1))
            self.left_two.wait_recv()
            from_right = rows_of(result, self.row(1) + half, half)
            self.on_left = send(from_right, from_right, self.along(3))

        def finish(self):
            for copy in (self.right_two, self.left_one, self.on_right, self.on_left):
                copy.wait_recv()

    def together(parts):
        for part in parts:
            part.start()
        for part in parts:
            part.middle()
        for part in parts:
            part.finish()

    def add_small(target, ref, count):
        def body(i, carry):
            at_rows = pl.ds(pl.multiple_of(i * 16, 16), 16)
            total = ref[0, at_rows, :].astype(single)
            for k in range(1, count):
                total = total + ref[k, at_rows, :].astype(single)
            target[at_rows, :] = total.astype(bfloat)
            return carry

        lax.fori_loop(0, SMALL // 16, body, 0)

    small_x[x] = small_in[...]
    first_small = [send_small(small_in, small_x.at[x], along_x(k)) for k in (1, 2, 3)]
    together(
        [
            Scatter(given, 0, PART, x, along_x, near_a, left_a, right_a, pass_a, sum_a),
            Scatter(given, HALF, PART, y, along_y, near_b, left_b, right_b, pass_b, sum_b),
        ]
    )
    for copy in first_small:
        copy.wait_recv()
    add_small(small_one, small_x, 4)
    small_y[y] = small_one[...]
    second_small = [send_small(small_one, small_y.at[y], along_y(k)) for k in (1, 2, 3)]
    together(
        [
            Scatter(sum_a, 0, PIECE, y, along_y, near_c, left_c, right_c, pass_c, sum_c),
            Scatter(sum_b, 0, PIECE, x, along_x, near_d, left_d, right_d, pass_d, sum_d),
        ]
    )
    for copy in second_small:
        copy.wait_recv()
    add_small(small_two, small_y, 4)
    small_z[plane] = small_two[...]
    pair_small = send_small(small_two, small_z.at[plane], across)
    pair_a = send(sum_c, rows_of(z_got, 0, PIECE), across)
    pair_b = send(sum_d, rows_of(z_got, PIECE, PIECE), across)
    row_a = x * PART + y * PIECE
    row_b = HALF + y * PART + x * PIECE
    pair_a.wait_recv()
    add_rows(result, row_a, [(sum_c, 0), (z_got, 0)], PIECE)
    pair_b.wait_recv()
    add_rows(result, row_b, [(sum_d, 0), (z_got, PIECE)], PIECE)
    together([Gather(x * PART, PIECE, y, along_y), Gather(HALF + y * PART, PIECE, x, along_x)])
    together([Gather(0, PART, x, along_x), Gather(HALF, PART, y, along_y)])
    stores = [
        pltpu.make_async_copy(result.at[pl.ds(starts[i], sizes[i]), :], outs[i], local_sem.at[i])
        for i in range(6)
    ]
    for store in stores:
        store.start()
    pair_small.wait_recv()
    add_small(small_out, small_z, 2)
    for copy in used:
        copy.wait_send()
    for copy in small_used:
        copy.wait_send()
    for store in stores:
        store.wait()


def grad_sum(arrays, small, collective_id):
    def rows(count):
        return pltpu.VMEM((count, 768), bfloat)

    scratch = [rows(BIG), rows(BIG)]
    scratch += [rows(PART)] * 10
    scratch += [rows(PIECE)] * 10
    scratch += [rows(2 * PIECE)]
    scratch += [pltpu.VMEM((4, SMALL, 768), bfloat)] * 2 + [pltpu.VMEM((2, SMALL, 768), bfloat)]
    scratch += [rows(SMALL)] * 2
    scratch += [
        pltpu.SemaphoreType.DMA((6,)),
        pltpu.SemaphoreType.DMA((50,)),
        pltpu.SemaphoreType.DMA((50,)),
        pltpu.SemaphoreType.DMA((7,)),
        pltpu.SemaphoreType.DMA((7,)),
    ]
    hbm = pl.BlockSpec(memory_space=pl.ANY)
    vmem = pl.BlockSpec(memory_space=pltpu.VMEM)
    return pl.pallas_call(
        grad_sum_kernel,
        out_shape=[jax.ShapeDtypeStruct(a.shape, bfloat) for a in arrays]
        + [jax.ShapeDtypeStruct(small.shape, bfloat)],
        in_specs=[hbm] * 6 + [vmem],
        out_specs=[hbm] * 6 + [vmem],
        scratch_shapes=scratch,
        compiler_params=pltpu.CompilerParams(
            collective_id=collective_id, has_side_effects=True, vmem_limit_bytes=40 * 2**20
        ),
        name="grad_sum",
    )(*arrays, small)


def norm_forward(inputs, gain_row, shift_row):
    average = jnp.mean(inputs, axis=-1, keepdims=True)
    centered = inputs - average
    variance = jnp.mean(centered * centered, axis=-1, keepdims=True)
    inverse = lax.rsqrt(variance + epsilon)
    normal = centered * inverse
    return (normal * gain_row + shift_row, normal, inverse)


def norm_backward(grad_out, normal, inverse, gain_row):
    scaled = grad_out * gain_row
    mean_one = jnp.mean(scaled, axis=-1, keepdims=True)
    mean_two = jnp.mean(scaled * normal, axis=-1, keepdims=True)
    grad_in = inverse * (scaled - mean_one - normal * mean_two)
    return (grad_in, jnp.sum(grad_out * normal, axis=0), jnp.sum(grad_out, axis=0))


def gelu_exact(inputs):
    return jax.nn.gelu(inputs, approximate=False)


def gelu_slope(inputs, grad_out):
    unused, pullback = jax.vjp(gelu_exact, inputs)
    return pullback(grad_out)[0]


def attend_forward(
    inputs, layer_index, qkv_weight, out_weight, qv_bias, out_bias, ln_gain, ln_bias
):
    normed, normal, inverse = norm_forward(
        inputs, ln_gain[2 * layer_index], ln_bias[2 * layer_index]
    )
    normed_low = normed.astype(bfloat)
    projected = jnp.einsum(
        "td,dcf->tcf", normed_low, qkv_weight[layer_index], preferred_element_type=single
    )
    tokens_here, local_width = (projected.shape[0], projected.shape[2])
    head_shape = (tokens_here // SEQ, SEQ, local_width // HEAD, HEAD)
    queries = (projected[:, 0] + qv_bias[layer_index, 0]).astype(bfloat).reshape(head_shape)
    key_rows = projected[:, 1].astype(bfloat).reshape(head_shape)
    value_rows = (projected[:, 2] + qv_bias[layer_index, 1]).astype(bfloat).reshape(head_shape)
    scores = jnp.einsum(
        "bqhd,bkhd->bhqk", queries, key_rows, preferred_element_type=single
    ) * HEAD ** (-0.5)
    largest = jnp.max(scores, axis=-1, keepdims=True)
    exponent = jnp.exp(scores - largest)
    totals = jnp.sum(exponent, axis=-1, keepdims=True)
    probs_low = (exponent / totals).astype(bfloat)
    log_total = largest + jnp.log(totals)
    context = jnp.einsum("bhqk,bkhd->bqhd", probs_low, value_rows, preferred_element_type=single)
    context = context.reshape(tokens_here, local_width).astype(bfloat)
    partial_out = jnp.dot(context, out_weight[layer_index], preferred_element_type=single)
    summed = tensor_sum(partial_out.astype(jnp.bfloat16), 1).astype(jnp.float32)
    stored = (normal, inverse, normed_low, queries, key_rows, value_rows, log_total, context)
    return (inputs + summed + out_bias[layer_index], stored)


def attend_backward(grad_out, layer_index, stored, qkv_weight, out_weight, ln_gain):
    normal, inverse, normed_low, queries, key_rows, value_rows, log_total, context = stored
    tokens_here, local_width = context.shape
    grad_low = grad_out.astype(bfloat)
    out_bias_part = jnp.sum(grad_out, axis=0)
    out_weight_part = jnp.einsum("tf,td->fd", context, grad_low, preferred_element_type=single)
    grad_context = jnp.einsum(
        "td,fd->tf", grad_low, out_weight[layer_index], preferred_element_type=single
    )
    grad_context = grad_context.astype(bfloat).reshape(queries.shape)
    scale_factor = HEAD ** (-0.5)
    scores = (
        jnp.einsum("bqhd,bkhd->bhqk", queries, key_rows, preferred_element_type=single)
        * scale_factor
    )
    probs_again = jnp.exp(scores - log_total)
    grad_values = jnp.einsum(
        "bhqk,bqhd->bkhd", probs_again.astype(bfloat), grad_context, preferred_element_type=single
    )
    grad_probs = jnp.einsum(
        "bqhd,bkhd->bhqk", grad_context, value_rows, preferred_element_type=single
    )
    row_total = jnp.sum(probs_again * grad_probs, axis=-1, keepdims=True)
    grad_scores = (probs_again * (grad_probs - row_total)).astype(bfloat)
    grad_queries = (
        jnp.einsum("bhqk,bkhd->bqhd", grad_scores, key_rows, preferred_element_type=single)
        * scale_factor
    )
    grad_keys = (
        jnp.einsum("bhqk,bqhd->bkhd", grad_scores, queries, preferred_element_type=single)
        * scale_factor
    )
    stacked = jnp.stack(
        [
            grad_queries.reshape(tokens_here, local_width),
            grad_keys.reshape(tokens_here, local_width),
            grad_values.reshape(tokens_here, local_width),
        ],
        axis=1,
    ).astype(bfloat)
    bias_part = jnp.stack(
        [
            jnp.sum(stacked[:, 0].astype(single), axis=0),
            jnp.sum(stacked[:, 2].astype(single), axis=0),
        ]
    )
    qkv_part = jnp.einsum("td,tcf->dcf", normed_low, stacked, preferred_element_type=single)
    normed_part = jnp.einsum(
        "tcf,dcf->td", stacked, qkv_weight[layer_index], preferred_element_type=single
    )
    grad_normed = tensor_sum(normed_part.astype(jnp.bfloat16), 1).astype(jnp.float32)
    grad_in, gain_part, shift_part = norm_backward(
        grad_normed, normal, inverse, ln_gain[2 * layer_index]
    )
    return (
        grad_out + grad_in,
        (qkv_part, out_weight_part, bias_part, out_bias_part, gain_part, shift_part),
    )


def dense_forward(inputs, dense_in, dense_out, ln_gain, ln_bias):
    normed, normal, inverse = norm_forward(inputs, ln_gain[1], ln_bias[1])
    normed_low = normed.astype(bfloat)
    pre_act = jnp.dot(normed_low, dense_in, preferred_element_type=single)
    activated = gelu_exact(pre_act).astype(bfloat)
    partial_out = jnp.dot(activated, dense_out, preferred_element_type=single)
    summed = tensor_sum(partial_out.astype(jnp.bfloat16), 1).astype(jnp.float32)
    return (inputs + summed, (normal, inverse, normed_low, pre_act, activated))


def dense_backward(grad_out, stored, dense_in, dense_out, ln_gain):
    normal, inverse, normed_low, pre_act, activated = stored
    grad_low = grad_out.astype(bfloat)
    out_part = jnp.einsum("tf,td->fd", activated, grad_low, preferred_element_type=single)
    grad_act = jnp.einsum("td,fd->tf", grad_low, dense_out, preferred_element_type=single)
    grad_pre = gelu_slope(pre_act, grad_act).astype(bfloat)
    in_part = jnp.einsum("td,tf->df", normed_low, grad_pre, preferred_element_type=single)
    normed_part = jnp.einsum("tf,df->td", grad_pre, dense_in, preferred_element_type=single)
    grad_normed = tensor_sum(normed_part.astype(jnp.bfloat16), 1).astype(jnp.float32)
    grad_in, gain_part, shift_part = norm_backward(grad_normed, normal, inverse, ln_gain[1])
    return (grad_out + grad_in, (in_part, out_part, gain_part, shift_part))


def moe_forward(inputs, routes, router, expert_in, expert_out, ln_gain, ln_bias):
    normed, normal, inverse = norm_forward(inputs, ln_gain[3], ln_bias[3])
    normed_low = normed.astype(bfloat)
    logits = jnp.dot(normed_low, router, preferred_element_type=single)
    chosen = jnp.take_along_axis(logits, routes, axis=1)
    gate_values = jax.nn.softmax(chosen, axis=1)
    tokens_here, feature_width = normed_low.shape
    expert_count = router.shape[1]
    capacity = max(2, (3 * tokens_here + expert_count - 1) // expert_count)
    one_hot = (routes[:, :, None] == jnp.arange(expert_count, dtype=jnp.int32)).astype(jnp.int32)
    running = jnp.cumsum(one_hot.reshape(tokens_here * 2, expert_count), axis=0).reshape(
        tokens_here, 2, expert_count
    )
    slot_index = routes * capacity + jnp.sum((running - 1) * one_hot, axis=-1)
    slot_ids = jnp.arange(expert_count * capacity, dtype=jnp.int32)
    dispatch_pair = (slot_ids[None, :, None] == slot_index.T[:, None, :]).astype(bfloat)
    gathered = jnp.dot(
        jnp.sum(dispatch_pair, axis=0), normed_low, preferred_element_type=single
    ).astype(bfloat)
    outgoing = gathered.reshape(expert_count, capacity, feature_width)
    arrived_rows = lax.all_to_all(outgoing, "dp", split_axis=0, concat_axis=0, tiled=True)
    sources = arrived_rows.shape[0]
    items = arrived_rows.shape[1]
    rows_flat = arrived_rows.reshape(sources * items, feature_width)
    pre_rows = jnp.dot(rows_flat, expert_in[0], preferred_element_type=single)
    act_rows = gelu_exact(pre_rows).astype(bfloat)
    partial_out = jnp.dot(act_rows, expert_out[0], preferred_element_type=single)
    back_rows = lax.all_to_all(
        partial_out.reshape(sources, items, feature_width).astype(jnp.bfloat16),
        "dp",
        split_axis=0,
        concat_axis=0,
        tiled=True,
    ).astype(jnp.float32)
    hidden_width = pre_rows.shape[1]
    pre_act = pre_rows.reshape(sources, items, hidden_width)
    activated = act_rows.reshape(sources, items, hidden_width)
    picked = jnp.take(back_rows.reshape(expert_count * capacity, feature_width), slot_index, axis=0)
    mixed_part = jnp.sum(gate_values[:, :, None] * picked, axis=1)
    mixed = tensor_sum(mixed_part.astype(jnp.bfloat16), 1).astype(jnp.float32)
    stored = (
        normal,
        inverse,
        normed_low,
        gate_values,
        slot_index,
        dispatch_pair,
        arrived_rows,
        pre_act,
        activated,
        picked,
    )
    return (inputs + mixed, stored)


def moe_backward(grad_out, routes, stored, router, expert_in, expert_out, ln_gain):
    (
        normal,
        inverse,
        normed_low,
        gate_values,
        slot_index,
        dispatch_pair,
        arrived,
        pre_act,
        activated,
        picked,
    ) = stored
    expert_count, capacity, feature_width = arrived.shape
    scaled = (gate_values[:, :, None] * grad_out[:, None, :]).astype(bfloat)
    outgoing = jnp.einsum(
        "kst,tkd->sd", dispatch_pair, scaled, preferred_element_type=single
    ).astype(bfloat)
    gate_part = jnp.sum(picked * grad_out[:, None, :], axis=-1)
    arrived_grad = lax.all_to_all(
        outgoing.reshape(expert_count, capacity, feature_width),
        "dp",
        split_axis=0,
        concat_axis=0,
        tiled=True,
    )
    row_count = expert_count * capacity
    rows_grad = arrived_grad.reshape(row_count, feature_width)
    flat_rows = arrived.reshape(row_count, feature_width)
    flat_pre = pre_act.reshape(row_count, pre_act.shape[2])
    flat_act = activated.reshape(row_count, activated.shape[2])
    expert_out_part = jnp.einsum("sf,sd->fd", flat_act, rows_grad, preferred_element_type=single)
    grad_act = jnp.einsum("sd,fd->sf", rows_grad, expert_out[0], preferred_element_type=single)
    grad_pre = gelu_slope(flat_pre, grad_act).astype(bfloat)
    expert_in_part = jnp.einsum("sd,sf->df", flat_rows, grad_pre, preferred_element_type=single)
    rows_back = jnp.einsum("sf,df->sd", grad_pre, expert_in[0], preferred_element_type=single)
    returned = lax.all_to_all(
        rows_back.reshape(expert_count, capacity, feature_width).astype(jnp.bfloat16),
        "dp",
        split_axis=0,
        concat_axis=0,
        tiled=True,
    ).astype(jnp.float32)
    normed_part = jnp.sum(
        jnp.take(returned.reshape(row_count, feature_width), slot_index, axis=0), axis=1
    )
    grad_experts, grad_gates = (
        tensor_sum(normed_part.astype(jnp.bfloat16), 1).astype(jnp.float32),
        lax.psum(gate_part.astype(jnp.bfloat16), "tensor").astype(jnp.float32),
    )
    grad_chosen = gate_values * (
        grad_gates - jnp.sum(gate_values * grad_gates, axis=1, keepdims=True)
    )
    one_hot = (routes[:, :, None] == jnp.arange(router.shape[1], dtype=jnp.int32)).astype(single)
    grad_logits = jnp.sum(one_hot * grad_chosen[:, :, None], axis=1).astype(bfloat)
    router_part = jnp.einsum("td,te->de", normed_low, grad_logits, preferred_element_type=single)
    grad_normed = grad_experts + jnp.einsum(
        "te,de->td", grad_logits, router, preferred_element_type=single
    )
    grad_in, gain_part, shift_part = norm_backward(grad_normed, normal, inverse, ln_gain[3])
    return (
        grad_out + grad_in,
        (router_part, expert_in_part[None], expert_out_part[None], gain_part, shift_part),
    )


def per_device(
    images,
    routes,
    cotangent,
    qkv_weight,
    out_weight,
    qv_bias,
    out_bias,
    ln_gain,
    ln_bias,
    dense_in,
    dense_out,
    router,
    expert_in,
    expert_out,
):
    start_rows = images.astype(single)
    section_one, stored_one = attend_forward(
        start_rows, 0, qkv_weight, out_weight, qv_bias, out_bias, ln_gain, ln_bias
    )
    section_two, stored_dense = dense_forward(section_one, dense_in, dense_out, ln_gain, ln_bias)
    section_three, stored_two = attend_forward(
        section_two, 1, qkv_weight, out_weight, qv_bias, out_bias, ln_gain, ln_bias
    )
    section_four, stored_moe = moe_forward(
        section_three, routes, router, expert_in, expert_out, ln_gain, ln_bias
    )
    output = section_four.astype(bfloat)
    grad_four = cotangent.astype(single)
    grad_three, moe_parts = moe_backward(
        grad_four, routes, stored_moe, router, expert_in, expert_out, ln_gain
    )
    router_grad, expert_in_grad, expert_out_grad, gain_three, shift_three = moe_parts
    grad_two, upper_parts = attend_backward(
        grad_three, 1, stored_two, qkv_weight, out_weight, ln_gain
    )
    qkv_upper, outw_upper, bias_upper, outb_upper, gain_two, shift_two = upper_parts
    grad_one, dense_parts = dense_backward(grad_two, stored_dense, dense_in, dense_out, ln_gain)
    dense_in_grad, dense_out_grad, gain_one, shift_one = dense_parts
    input_grad, lower_parts = attend_backward(
        grad_one, 0, stored_one, qkv_weight, out_weight, ln_gain
    )
    qkv_lower, outw_lower, bias_lower, outb_lower, gain_zero, shift_zero = lower_parts
    local_width = qkv_lower.shape[2]
    arrays = [
        jnp.transpose(qkv_lower, (1, 2, 0)).reshape(3 * local_width, -1),
        jnp.transpose(qkv_upper, (1, 2, 0)).reshape(3 * local_width, -1),
        outw_lower,
        outw_upper,
        dense_in_grad,
        dense_out_grad,
    ]
    small = jnp.concatenate(
        [
            router_grad.T,
            jnp.stack([gain_zero, gain_one, gain_two, gain_three]),
            jnp.stack([shift_zero, shift_one, shift_two, shift_three]),
            jnp.stack([outb_lower, outb_upper]),
            jnp.stack([bias_lower, bias_upper]).reshape(1, -1),
            jnp.zeros((5, router_grad.shape[0]), single),
        ]
    )
    summed = grad_sum([a.astype(bfloat) for a in arrays], small.astype(bfloat), 2)
    big = [a.astype(single) for a in summed]
    small = big[6]
    qkv_weight_grad = jnp.transpose(
        jnp.stack([big[0], big[1]]).reshape(2, 3, local_width, -1), (0, 3, 1, 2)
    )
    out_weight_grad = jnp.stack([big[2], big[3]])
    dense_in_grad, dense_out_grad = big[4], big[5]
    router_grad = small[:32].T
    ln_gain_grad, ln_bias_grad, out_bias_grad = small[32:36], small[36:40], small[40:42]
    qv_bias_grad = small[42].reshape(2, 2, local_width)
    return (
        output,
        input_grad,
        qkv_weight_grad,
        out_weight_grad,
        qv_bias_grad,
        out_bias_grad,
        ln_gain_grad,
        ln_bias_grad,
        dense_in_grad,
        dense_out_grad,
        router_grad,
        expert_in_grad,
        expert_out_grad,
    )


def solution(mesh):
    in_specs = (
        P("dp", None),
        P("dp", None),
        P("dp", None),
        P(None, None, None, "tensor"),
        P(None, "tensor", None),
        P(None, None, "tensor"),
        P(),
        P(),
        P(),
        P(None, "tensor"),
        P("tensor", None),
        P(),
        P("dp", None, "tensor"),
        P("dp", "tensor", None),
    )
    out_specs = (
        P("dp", None),
        P("dp", None),
        P(None, None, None, "tensor"),
        P(None, "tensor", None),
        P(None, None, "tensor"),
        P(),
        P(),
        P(),
        P(None, "tensor"),
        P("tensor", None),
        P(),
        P("dp", None, "tensor"),
        P("dp", "tensor", None),
    )
    return jax.shard_map(
        per_device, mesh=mesh, in_specs=in_specs, out_specs=out_specs, check_vma=False
    )
```

```python
import functools

import jax
import jax.numpy as jnp
from jax import lax
from jax.experimental import pallas as pl
from jax.experimental.pallas import tpu as pltpu
from jax.sharding import PartitionSpec as P

HEAD = 64
SEQ = 197


epsilon = 1e-06
bfloat = jnp.bfloat16
single = jnp.float32


MESH = pl.DeviceIdType.MESH


def tensor_sum_kernel(count, rows, p_ref, o_ref, got_one, sum_one, got_two, sum_two, got_three, sems):
    t = lax.axis_index("tensor")
    core = lax.rem(t, 2)
    sibling = {"tensor": t + 1 - 2 * core}
    opposite = {"tensor": lax.rem(t + 2, 4)}
    barrier = pltpu.get_barrier_semaphore()
    for peer in (sibling, opposite):
        pl.semaphore_signal(barrier, inc=1, device_id=peer, device_id_type=MESH)
    pl.semaphore_wait(barrier, 2)

    def columns(which, j):
        return pl.ds(pl.multiple_of((which * count + j) * 128, 128), 128)

    def copy(source, target, step, j, peer):
        return pltpu.make_async_remote_copy(
            src_ref=source,
            dst_ref=target,
            send_sem=sems.at[0, step, j],
            recv_sem=sems.at[1, step, j],
            device_id=peer,
            device_id_type=MESH,
        )

    first = [copy(p_ref.at[:, columns(1 - core, j)], got_one.at[j], 0, j, sibling) for j in range(count)]
    second = [copy(sum_one.at[j], got_two.at[j], 1, j, opposite) for j in range(count)]
    third = [copy(sum_two.at[j], got_three.at[j], 2, j, sibling) for j in range(count)]
    for j in range(count):
        first[j].start()
    for j in range(count):
        first[j].wait_recv()
        own = p_ref[:, columns(core, j)].astype(single)
        sum_one[j] = (own + got_one[j].astype(single)).astype(bfloat)
        second[j].start()
    for j in range(count):
        second[j].wait_recv()
        whole = (sum_one[j].astype(single) + got_two[j].astype(single)).astype(bfloat)
        sum_two[j] = whole
        third[j].start()
        o_ref[:, columns(core, j)] = whole
    for j in range(count):
        third[j].wait_recv()
        o_ref[:, columns(1 - core, j)] = got_three[j]
    for j in range(count):
        first[j].wait_send()
        second[j].wait_send()
        third[j].wait_send()


def tensor_sum(partial, collective_id):
    rows, width = partial.shape
    count = width // 256
    block = pltpu.VMEM((count, rows, 128), bfloat)
    return pl.pallas_call(
        functools.partial(tensor_sum_kernel, count, rows),
        out_shape=jax.ShapeDtypeStruct((rows, width), bfloat),
        in_specs=[pl.BlockSpec(memory_space=pltpu.VMEM)],
        out_specs=pl.BlockSpec(memory_space=pltpu.VMEM),
        scratch_shapes=[block] * 5 + [pltpu.SemaphoreType.DMA((2, 3, count))],
        compiler_params=pltpu.CompilerParams(
            collective_id=collective_id, has_side_effects=True, vmem_limit_bytes=32 * 2**20
        ),
        name="tensor_sum",
    )(partial)


BIG = 3072
HALF = BIG // 2
PART = HALF // 4
PIECE = PART // 4
SMALL = 48


def add_rows(target, target_row, sources, rows):
    def body(i, carry):
        total = None
        for ref, row in sources:
            value = ref[pl.ds(pl.multiple_of(row + i * 16, 16), 16), :].astype(single)
            total = value if total is None else total + value
        target[pl.ds(pl.multiple_of(target_row + i * 16, 16), 16), :] = total.astype(bfloat)
        return carry

    lax.fori_loop(0, rows // 16, body, 0)


def grad_sum_kernel(*refs):
    ins, small_in = refs[:6], refs[6]
    outs, small_out = refs[7:13], refs[13]
    (given, result, near_a, near_b, left_a, right_a, left_b, right_b, pass_a, pass_b, sum_a, sum_b) = refs[14:26]
    (near_c, near_d, left_c, right_c, left_d, right_d, pass_c, pass_d, sum_c, sum_d) = refs[26:36]
    z_got, small_x, small_y, small_z, small_one, small_two = refs[36:42]
    local_sem, send_sem, recv_sem, small_send, small_recv = refs[42:47]

    dp = lax.axis_index("dp")
    plane, x, y = dp // 16, lax.rem(dp // 4, 4), lax.rem(dp, 4)

    def at(plane_to, x_to, y_to):
        return {"dp": plane_to * 16 + x_to * 4 + y_to}

    def along_x(step):
        return at(plane, lax.rem(x + step, 4), y)

    def along_y(step):
        return at(plane, x, lax.rem(y + step, 4))

    across = at(1 - plane, x, y)
    barrier = pltpu.get_barrier_semaphore()
    peers = [along_x(1), along_x(2), along_x(3), along_y(1), along_y(2), along_y(3), across]
    for peer in peers:
        pl.semaphore_signal(barrier, inc=1, device_id=peer, device_id_type=MESH)

    sizes = [ref.shape[0] for ref in ins]
    starts = [sum(sizes[:i]) for i in range(6)]
    loads = [
        pltpu.make_async_copy(ins[i], given.at[pl.ds(starts[i], sizes[i]), :], local_sem.at[i])
        for i in range(6)
    ]
    for load in loads:
        load.start()
    for load in loads:
        load.wait()
    pl.semaphore_wait(barrier, 7)

    used = []

    def send(source, target, peer):
        k = len(used)
        copy = pltpu.make_async_remote_copy(
            src_ref=source,
            dst_ref=target,
            send_sem=send_sem.at[k],
            recv_sem=recv_sem.at[k],
            device_id=peer,
            device_id_type=MESH,
        )
        used.append(copy)
        copy.start()
        return copy

    small_used = []

    def send_small(source, target, peer):
        k = len(small_used)
        copy = pltpu.make_async_remote_copy(
            src_ref=source,
            dst_ref=target,
            send_sem=small_send.at[k],
            recv_sem=small_recv.at[k],
            device_id=peer,
            device_id_type=MESH,
        )
        small_used.append(copy)
        copy.start()
        return copy

    def rows_of(ref, row, count):
        return ref.at[pl.ds(pl.multiple_of(row, 16), count), :]

    class Scatter:
        def __init__(self, source, base, size, place, along, near, left, right, onward, total):
            self.source, self.base, self.size, self.place = source, base, size, place
            self.along, self.near, self.left, self.right = along, near, left, right
            self.onward, self.total = onward, total

        def row(self, step):
            return self.base + lax.rem(self.place + step, 4) * self.size

        def start(self):
            half = self.size // 2
            s = self.source
            self.far_right = send(rows_of(s, self.row(2), half), rows_of(self.near, 0, half), self.along(1))
            self.far_left = send(rows_of(s, self.row(2) + half, half), rows_of(self.near, half, half), self.along(3))
            self.to_right = send(rows_of(s, self.row(1) + half, half), rows_of(self.left, half, half), self.along(1))
            self.to_left = send(rows_of(s, self.row(3), half), rows_of(self.right, 0, half), self.along(3))

        def middle(self):
            half = self.size // 2
            s = self.source
            self.far_right.wait_recv()
            add_rows(self.onward, 0, [(s, self.row(1)), (self.near, 0)], half)
            self.on_right = send(rows_of(self.onward, 0, half), rows_of(self.left, 0, half), self.along(1))
            self.far_left.wait_recv()
            add_rows(self.onward, half, [(s, self.row(3) + half), (self.near, half)], half)
            self.on_left = send(rows_of(self.onward, half, half), rows_of(self.right, half, half), self.along(3))

        def finish(self):
            for copy in (self.to_right, self.to_left, self.on_right, self.on_left):
                copy.wait_recv()
            add_rows(self.total, 0, [(self.source, self.row(0)), (self.left, 0), (self.right, 0)], self.size)

    class Gather:
        def __init__(self, base, size, place, along):
            self.base, self.size, self.place, self.along = base, size, place, along

        def row(self, step):
            return self.base + lax.rem(self.place + step, 4) * self.size

        def start(self):
            own, half = self.row(0), self.size // 2
            first, second = rows_of(result, own, half), rows_of(result, own + half, half)
            self.right_one = send(first, first, self.along(1))
            self.left_two = send(second, second, self.along(3))
            self.right_two = send(second, second, self.along(1))
            self.left_one = send(first, first, self.along(3))

        def middle(self):
            half = self.size // 2
            self.right_one.wait_recv()
            from_left = rows_of(result, self.row(3), half)
            self.on_right = send(from_left, from_left, self.along(1))
            self.left_two.wait_recv()
            from_right = rows_of(result, self.row(1) + half, half)
            self.on_left = send(from_right, from_right, self.along(3))

        def finish(self):
            for copy in (self.right_two, self.left_one, self.on_right, self.on_left):
                copy.wait_recv()

    def together(parts):
        for part in parts:
            part.start()
        for part in parts:
            part.middle()
        for part in parts:
            part.finish()

    def add_small(target, ref, count):
        def body(i, carry):
            at_rows = pl.ds(pl.multiple_of(i * 16, 16), 16)
            total = ref[0, at_rows, :].astype(single)
            for k in range(1, count):
                total = total + ref[k, at_rows, :].astype(single)
            target[at_rows, :] = total.astype(bfloat)
            return carry

        lax.fori_loop(0, SMALL // 16, body, 0)

    small_x[x] = small_in[...]
    first_small = [send_small(small_in, small_x.at[x], along_x(k)) for k in (1, 2, 3)]
    together(
        [
            Scatter(given, 0, PART, x, along_x, near_a, left_a, right_a, pass_a, sum_a),
            Scatter(given, HALF, PART, y, along_y, near_b, left_b, right_b, pass_b, sum_b),
        ]
    )
    for copy in first_small:
        copy.wait_recv()
    add_small(small_one, small_x, 4)
    small_y[y] = small_one[...]
    second_small = [send_small(small_one, small_y.at[y], along_y(k)) for k in (1, 2, 3)]
    together(
        [
            Scatter(sum_a, 0, PIECE, y, along_y, near_c, left_c, right_c, pass_c, sum_c),
            Scatter(sum_b, 0, PIECE, x, along_x, near_d, left_d, right_d, pass_d, sum_d),
        ]
    )
    for copy in second_small:
        copy.wait_recv()
    add_small(small_two, small_y, 4)
    small_z[plane] = small_two[...]
    pair_small = send_small(small_two, small_z.at[plane], across)
    pair_a = send(sum_c, rows_of(z_got, 0, PIECE), across)
    pair_b = send(sum_d, rows_of(z_got, PIECE, PIECE), across)
    row_a = x * PART + y * PIECE
    row_b = HALF + y * PART + x * PIECE
    pair_a.wait_recv()
    add_rows(result, row_a, [(sum_c, 0), (z_got, 0)], PIECE)
    pair_b.wait_recv()
    add_rows(result, row_b, [(sum_d, 0), (z_got, PIECE)], PIECE)
    together([Gather(x * PART, PIECE, y, along_y), Gather(HALF + y * PART, PIECE, x, along_x)])
    together([Gather(0, PART, x, along_x), Gather(HALF, PART, y, along_y)])
    stores = [
        pltpu.make_async_copy(result.at[pl.ds(starts[i], sizes[i]), :], outs[i], local_sem.at[i])
        for i in range(6)
    ]
    for store in stores:
        store.start()
    pair_small.wait_recv()
    add_small(small_out, small_z, 2)
    for copy in used:
        copy.wait_send()
    for copy in small_used:
        copy.wait_send()
    for store in stores:
        store.wait()


def grad_sum(arrays, small, collective_id):
    def rows(count):
        return pltpu.VMEM((count, 768), bfloat)

    scratch = [rows(BIG), rows(BIG)]
    scratch += [rows(PART)] * 10
    scratch += [rows(PIECE)] * 10
    scratch += [rows(2 * PIECE)]
    scratch += [pltpu.VMEM((4, SMALL, 768), bfloat)] * 2 + [pltpu.VMEM((2, SMALL, 768), bfloat)]
    scratch += [rows(SMALL)] * 2
    scratch += [
        pltpu.SemaphoreType.DMA((6,)),
        pltpu.SemaphoreType.DMA((50,)),
        pltpu.SemaphoreType.DMA((50,)),
        pltpu.SemaphoreType.DMA((7,)),
        pltpu.SemaphoreType.DMA((7,)),
    ]
    hbm = pl.BlockSpec(memory_space=pl.ANY)
    vmem = pl.BlockSpec(memory_space=pltpu.VMEM)
    return pl.pallas_call(
        grad_sum_kernel,
        out_shape=[jax.ShapeDtypeStruct(a.shape, bfloat) for a in arrays]
        + [jax.ShapeDtypeStruct(small.shape, bfloat)],
        in_specs=[hbm] * 6 + [vmem],
        out_specs=[hbm] * 6 + [vmem],
        scratch_shapes=scratch,
        compiler_params=pltpu.CompilerParams(
            collective_id=collective_id, has_side_effects=True, vmem_limit_bytes=40 * 2**20
        ),
        name="grad_sum",
    )(*arrays, small)


def norm_forward(inputs, gain_row, shift_row):
    average = jnp.mean(inputs, axis=-1, keepdims=True)
    centered = inputs - average
    variance = jnp.mean(centered * centered, axis=-1, keepdims=True)
    inverse = lax.rsqrt(variance + epsilon)
    normal = centered * inverse
    return (normal * gain_row + shift_row, normal, inverse)


def norm_backward(grad_out, normal, inverse, gain_row):
    scaled = grad_out * gain_row
    mean_one = jnp.mean(scaled, axis=-1, keepdims=True)
    mean_two = jnp.mean(scaled * normal, axis=-1, keepdims=True)
    grad_in = inverse * (scaled - mean_one - normal * mean_two)
    return (grad_in, jnp.sum(grad_out * normal, axis=0), jnp.sum(grad_out, axis=0))


def gelu_exact(inputs):
    return jax.nn.gelu(inputs, approximate=False)


def gelu_slope(inputs, grad_out):
    unused, pullback = jax.vjp(gelu_exact, inputs)
    return pullback(grad_out)[0]


def attend_forward(
    inputs, layer_index, qkv_weight, out_weight, qv_bias, out_bias, ln_gain, ln_bias
):
    normed, normal, inverse = norm_forward(
        inputs, ln_gain[2 * layer_index], ln_bias[2 * layer_index]
    )
    normed_low = normed.astype(bfloat)
    projected = jnp.einsum(
        "td,dcf->tcf", normed_low, qkv_weight[layer_index], preferred_element_type=single
    )
    tokens_here, local_width = (projected.shape[0], projected.shape[2])
    head_shape = (tokens_here // SEQ, SEQ, local_width // HEAD, HEAD)
    queries = (projected[:, 0] + qv_bias[layer_index, 0]).astype(bfloat).reshape(head_shape)
    key_rows = projected[:, 1].astype(bfloat).reshape(head_shape)
    value_rows = (projected[:, 2] + qv_bias[layer_index, 1]).astype(bfloat).reshape(head_shape)
    scores = jnp.einsum(
        "bqhd,bkhd->bhqk", queries, key_rows, preferred_element_type=single
    ) * HEAD ** (-0.5)
    largest = jnp.max(scores, axis=-1, keepdims=True)
    exponent = jnp.exp(scores - largest)
    totals = jnp.sum(exponent, axis=-1, keepdims=True)
    probs_low = (exponent / totals).astype(bfloat)
    log_total = largest + jnp.log(totals)
    context = jnp.einsum("bhqk,bkhd->bqhd", probs_low, value_rows, preferred_element_type=single)
    context = context.reshape(tokens_here, local_width).astype(bfloat)
    partial_out = jnp.dot(context, out_weight[layer_index], preferred_element_type=single)
    summed = tensor_sum(partial_out.astype(jnp.bfloat16), 1).astype(jnp.float32)
    stored = (normal, inverse, normed_low, queries, key_rows, value_rows, log_total, context)
    return (inputs + summed + out_bias[layer_index], stored)


def attend_backward(grad_out, layer_index, stored, qkv_weight, out_weight, ln_gain):
    normal, inverse, normed_low, queries, key_rows, value_rows, log_total, context = stored
    tokens_here, local_width = context.shape
    grad_low = grad_out.astype(bfloat)
    out_bias_part = jnp.sum(grad_out, axis=0)
    out_weight_part = jnp.einsum("tf,td->fd", context, grad_low, preferred_element_type=single)
    grad_context = jnp.einsum(
        "td,fd->tf", grad_low, out_weight[layer_index], preferred_element_type=single
    )
    grad_context = grad_context.astype(bfloat).reshape(queries.shape)
    scale_factor = HEAD ** (-0.5)
    scores = (
        jnp.einsum("bqhd,bkhd->bhqk", queries, key_rows, preferred_element_type=single)
        * scale_factor
    )
    probs_again = jnp.exp(scores - log_total)
    grad_values = jnp.einsum(
        "bhqk,bqhd->bkhd", probs_again.astype(bfloat), grad_context, preferred_element_type=single
    )
    grad_probs = jnp.einsum(
        "bqhd,bkhd->bhqk", grad_context, value_rows, preferred_element_type=single
    )
    row_total = jnp.sum(probs_again * grad_probs, axis=-1, keepdims=True)
    grad_scores = (probs_again * (grad_probs - row_total)).astype(bfloat)
    grad_queries = (
        jnp.einsum("bhqk,bkhd->bqhd", grad_scores, key_rows, preferred_element_type=single)
        * scale_factor
    )
    grad_keys = (
        jnp.einsum("bhqk,bqhd->bkhd", grad_scores, queries, preferred_element_type=single)
        * scale_factor
    )
    stacked = jnp.stack(
        [
            grad_queries.reshape(tokens_here, local_width),
            grad_keys.reshape(tokens_here, local_width),
            grad_values.reshape(tokens_here, local_width),
        ],
        axis=1,
    ).astype(bfloat)
    bias_part = jnp.stack(
        [
            jnp.sum(stacked[:, 0].astype(single), axis=0),
            jnp.sum(stacked[:, 2].astype(single), axis=0),
        ]
    )
    qkv_part = jnp.einsum("td,tcf->dcf", normed_low, stacked, preferred_element_type=single)
    normed_part = jnp.einsum(
        "tcf,dcf->td", stacked, qkv_weight[layer_index], preferred_element_type=single
    )
    grad_normed = tensor_sum(normed_part.astype(jnp.bfloat16), 1).astype(jnp.float32)
    grad_in, gain_part, shift_part = norm_backward(
        grad_normed, normal, inverse, ln_gain[2 * layer_index]
    )
    return (
        grad_out + grad_in,
        (qkv_part, out_weight_part, bias_part, out_bias_part, gain_part, shift_part),
    )


def dense_forward(inputs, dense_in, dense_out, ln_gain, ln_bias):
    normed, normal, inverse = norm_forward(inputs, ln_gain[1], ln_bias[1])
    normed_low = normed.astype(bfloat)
    pre_act = jnp.dot(normed_low, dense_in, preferred_element_type=single)
    activated = gelu_exact(pre_act).astype(bfloat)
    partial_out = jnp.dot(activated, dense_out, preferred_element_type=single)
    summed = tensor_sum(partial_out.astype(jnp.bfloat16), 1).astype(jnp.float32)
    return (inputs + summed, (normal, inverse, normed_low, pre_act, activated))


def dense_backward(grad_out, stored, dense_in, dense_out, ln_gain):
    normal, inverse, normed_low, pre_act, activated = stored
    grad_low = grad_out.astype(bfloat)
    out_part = jnp.einsum("tf,td->fd", activated, grad_low, preferred_element_type=single)
    grad_act = jnp.einsum("td,fd->tf", grad_low, dense_out, preferred_element_type=single)
    grad_pre = gelu_slope(pre_act, grad_act).astype(bfloat)
    in_part = jnp.einsum("td,tf->df", normed_low, grad_pre, preferred_element_type=single)
    normed_part = jnp.einsum("tf,df->td", grad_pre, dense_in, preferred_element_type=single)
    grad_normed = tensor_sum(normed_part.astype(jnp.bfloat16), 1).astype(jnp.float32)
    grad_in, gain_part, shift_part = norm_backward(grad_normed, normal, inverse, ln_gain[1])
    return (grad_out + grad_in, (in_part, out_part, gain_part, shift_part))


EXPERTS = 32
STRIDE = 40
SLOTS = EXPERTS * STRIDE


def dot_rows(a, b):
    return lax.dot_general(a, b, (((1,), (0,)), ((), ())), preferred_element_type=single)


def dot_last(a, b):
    return lax.dot_general(a, b, (((1,), (1,)), ((), ())), preferred_element_type=single)


def dot_first(a, b):
    return lax.dot_general(a, b, (((0,), (0,)), ((), ())), preferred_element_type=single)


def moe_route_kernel(
    rows_ref, cotangent_ref, routes_ref, routes_row_ref, router_ref, gain_ref, shift_ref,
    out_ref, low_ref, normal_ref, inverse_ref, gates_ref, slots_ref,
):
    tokens, width = rows_ref.shape
    half = width // 2
    normed, normal, inverse = norm_forward(rows_ref[...], gain_ref[...], shift_ref[...])
    low = normed.astype(bfloat)
    low_ref[...] = low
    normal_ref[...] = normal
    inverse_ref[...] = inverse
    logits = dot_last(low, router_ref[...])
    experts = lax.broadcasted_iota(jnp.int32, (tokens, EXPERTS), 1)
    picks = [routes_ref[:, k : k + 1] == experts for k in range(2)]
    chosen = [jnp.sum(jnp.where(pick, logits, 0.0), axis=1, keepdims=True) for pick in picks]
    largest = jnp.maximum(chosen[0], chosen[1])
    powers = [jnp.exp(c - largest) for c in chosen]
    total = powers[0] + powers[1]
    gates = [power / total for power in powers]
    gates_ref[:, 0:1] = gates[0]
    gates_ref[:, 1:2] = gates[1]

    before = lax.broadcasted_iota(jnp.int32, (tokens, tokens), 0)
    after = lax.broadcasted_iota(jnp.int32, (tokens, tokens), 1)
    either = [jnp.where(pick, 1.0, 0.0) for pick in picks]
    lower = jnp.where(after < before, 1.0, 0.0).astype(bfloat)
    running = dot_rows(lower, (either[0] + either[1]).astype(bfloat))
    for k in range(2):
        rank = jnp.sum(running * either[k], axis=1, keepdims=True).astype(jnp.int32)
        slots_ref[:, k : k + 1] = routes_ref[:, k : k + 1] * STRIDE + rank

    experts_row = lax.broadcasted_iota(jnp.int32, (EXPERTS, tokens), 0)
    either_row = [
        jnp.where(routes_row_ref[k : k + 1, :] == experts_row, 1.0, 0.0) for k in range(2)
    ]
    upper = jnp.where(before < after, 1.0, 0.0).astype(bfloat)
    running_row = dot_rows((either_row[0] + either_row[1]).astype(bfloat), upper)
    slots_row = []
    for k in range(2):
        rank = jnp.sum(running_row * either_row[k], axis=0, keepdims=True).astype(jnp.int32)
        slots_row.append(routes_row_ref[k : k + 1, :] * STRIDE + rank)

    cotangent = cotangent_ref[...].astype(single)
    scaled = [(gate * cotangent).astype(bfloat) for gate in gates]
    block = SLOTS // 8
    for i in range(8):
        ids = lax.broadcasted_iota(jnp.int32, (block, tokens), 0) + i * block
        hits = [jnp.where(ids == slots_row[k], 1.0, 0.0) for k in range(2)]
        moved = dot_rows((hits[0] + hits[1]).astype(bfloat), low).astype(bfloat)
        moved_grad = (
            dot_rows(hits[0].astype(bfloat), scaled[0]) + dot_rows(hits[1].astype(bfloat), scaled[1])
        ).astype(bfloat)
        at = slice(i * block, (i + 1) * block)
        for h in range(2):
            out_ref[h, at, :half] = moved[:, h * half : (h + 1) * half]
            out_ref[h, at, half:] = moved_grad[:, h * half : (h + 1) * half]


VMEM_SPEC = pl.BlockSpec(memory_space=pltpu.VMEM)


def moe_route(rows, cotangent, routes, router, gain_row, shift_row):
    tokens, width = rows.shape
    shapes = [
        jax.ShapeDtypeStruct((2, SLOTS, width), bfloat),
        jax.ShapeDtypeStruct((tokens, width), bfloat),
        jax.ShapeDtypeStruct((tokens, width), single),
        jax.ShapeDtypeStruct((tokens, 1), single),
        jax.ShapeDtypeStruct((tokens, 2), single),
        jax.ShapeDtypeStruct((tokens, 2), jnp.int32),
    ]
    return pl.pallas_call(
        moe_route_kernel,
        out_shape=shapes,
        in_specs=[VMEM_SPEC] * 7,
        out_specs=[VMEM_SPEC] * 6,
        compiler_params=pltpu.CompilerParams(vmem_limit_bytes=48 * 2**20),
        name="moe_route",
    )(rows, cotangent, routes, routes.T, router.T, gain_row[None], shift_row[None])


def dp_peer(k):
    dp = lax.axis_index("dp")
    plane = lax.rem(dp // 16 + k // 16, 2)
    x = lax.rem(lax.rem(dp // 4, 4) + lax.rem(k // 4, 4), 4)
    y = lax.rem(lax.rem(dp, 4) + lax.rem(k, 4), 4)
    return plane * 16 + x * 4 + y


def dp_source(k):
    dp = lax.axis_index("dp")
    plane = lax.rem(dp // 16 + k // 16, 2)
    x = lax.rem(lax.rem(dp // 4, 4) + 4 - lax.rem(k // 4, 4), 4)
    y = lax.rem(lax.rem(dp, 4) + 4 - lax.rem(k, 4), 4)
    return plane * 16 + x * 4 + y


def order_of(i):
    return lax.rem(i * 11, EXPERTS)


def meet_all(sibling):
    barrier = pltpu.get_barrier_semaphore()

    def greet(k, carry):
        pl.semaphore_signal(barrier, inc=1, device_id={"dp": dp_peer(k)}, device_id_type=MESH)
        return carry

    lax.fori_loop(1, EXPERTS, greet, 0)
    pl.semaphore_signal(barrier, inc=1, device_id=sibling, device_id_type=MESH)
    pl.semaphore_wait(barrier, EXPERTS)


def moe_send_kernel(in_ref, out_ref, local_sem, send_sem, recv_sem, pass_sem, land_sem):
    t = lax.axis_index("tensor")
    dp = lax.axis_index("dp")
    core = lax.rem(t, 2)
    sibling = {"tensor": t + 1 - 2 * core}
    own = pltpu.make_async_copy(in_ref.at[core, dp], out_ref.at[core, dp], local_sem)
    own.start()
    meet_all(sibling)

    def across(k):
        peer = dp_peer(k)
        return pltpu.make_async_remote_copy(
            src_ref=in_ref.at[core, peer],
            dst_ref=out_ref.at[core, dp],
            send_sem=send_sem.at[k],
            recv_sem=recv_sem.at[k],
            device_id={"dp": peer},
            device_id_type=MESH,
        )

    def beside(k):
        block = out_ref.at[core, dp_source(k)]
        return pltpu.make_async_remote_copy(
            src_ref=block,
            dst_ref=block,
            send_sem=pass_sem.at[k],
            recv_sem=land_sem.at[k],
            device_id=sibling,
            device_id_type=MESH,
        )

    def start(i, carry):
        across(order_of(i)).start()
        return carry

    def forward(i, carry):
        k = order_of(i)
        across(k).wait_recv()
        beside(k).start()
        return carry

    def land(k, carry):
        beside(k).wait_recv()
        return carry

    def drain(k, carry):
        across(k).wait_send()
        return carry

    def drain_pass(k, carry):
        beside(k).wait_send()
        return carry

    lax.fori_loop(1, EXPERTS, start, 0)
    own.wait()
    beside(0).start()
    lax.fori_loop(1, EXPERTS, forward, 0)
    lax.fori_loop(0, EXPERTS, land, 0)
    lax.fori_loop(1, EXPERTS, drain, 0)
    lax.fori_loop(0, EXPERTS, drain_pass, 0)


def moe_send(rows, collective_id):
    every = pltpu.SemaphoreType.DMA((EXPERTS,))
    hbm = pl.BlockSpec(memory_space=pl.ANY)
    return pl.pallas_call(
        moe_send_kernel,
        out_shape=jax.ShapeDtypeStruct(rows.shape, bfloat),
        in_specs=[hbm],
        out_specs=hbm,
        scratch_shapes=[pltpu.SemaphoreType.DMA, every, every, every, every],
        compiler_params=pltpu.CompilerParams(collective_id=collective_id, has_side_effects=True),
        name="moe_send",
    )(rows)


def expert_kernel(in_ref, ein_ref, eout_ref, out_ref, ein_grad_ref, eout_grad_ref, act_ref, grad_ref):
    half = in_ref.shape[2] // 2
    width = 2 * half
    block = SLOTS // 4

    def both(at, first):
        parts = [in_ref[h, at, first : first + half] for h in range(2)]
        return jnp.concatenate(parts, axis=1)

    def forward(i, carry):
        at = pl.ds(pl.multiple_of(i * block, 16), block)
        rows = both(at, 0)
        rows_grad = both(at, half)
        pre = dot_rows(rows, ein_ref[0])
        grad_act = dot_last(rows_grad, eout_ref[0])
        tail = 0.5 * (1.0 + lax.erf(pre * (0.5**0.5)))
        act = (pre * tail).astype(bfloat)
        slope = tail + pre * (jnp.exp(-0.5 * pre * pre) * 0.3989422804014327)
        grad_pre = (grad_act * slope).astype(bfloat)
        act_ref[at, :] = act
        grad_ref[at, :] = grad_pre
        out = dot_rows(act, eout_ref[0]).astype(bfloat)
        back = dot_last(grad_pre, ein_ref[0]).astype(bfloat)
        for h in range(2):
            out_ref[h, at, :half] = out[:, h * half : (h + 1) * half]
            out_ref[h, at, half:] = back[:, h * half : (h + 1) * half]
        return carry

    lax.fori_loop(0, SLOTS // block, forward, 0)
    for h in range(2):
        eout_grad_ref[0, :, h * half : (h + 1) * half] = dot_first(act_ref[...], in_ref[h, :, half:])
        ein_grad_ref[0, h * half : (h + 1) * half, :] = dot_first(in_ref[h, :, :half], grad_ref[...])


def expert_ffn(rows, expert_in, expert_out):
    width = rows.shape[2]
    weight = jax.ShapeDtypeStruct(expert_in.shape, single)
    return pl.pallas_call(
        expert_kernel,
        out_shape=[jax.ShapeDtypeStruct(rows.shape, bfloat), weight, weight],
        in_specs=[VMEM_SPEC] * 3,
        out_specs=[VMEM_SPEC] * 3,
        scratch_shapes=[pltpu.VMEM((SLOTS, width), bfloat)] * 2,
        compiler_params=pltpu.CompilerParams(vmem_limit_bytes=56 * 2**20),
        name="expert_ffn",
    )(rows, expert_in, expert_out)


def moe_return_kernel(in_ref, out_ref, got_ref, sum_ref, local_sem, send_sem, recv_sem, pass_sem, land_sem):
    t = lax.axis_index("tensor")
    dp = lax.axis_index("dp")
    core = lax.rem(t, 2)
    sibling = {"tensor": t + 1 - 2 * core}
    meet_all(sibling)

    def beside(k):
        peer = dp_peer(k)
        return pltpu.make_async_remote_copy(
            src_ref=in_ref.at[1 - core, peer],
            dst_ref=got_ref.at[peer],
            send_sem=pass_sem.at[k],
            recv_sem=land_sem.at[k],
            device_id=sibling,
            device_id_type=MESH,
        )

    def across(k):
        peer = dp_peer(k)
        return pltpu.make_async_remote_copy(
            src_ref=sum_ref.at[peer],
            dst_ref=out_ref.at[dp],
            send_sem=send_sem.at[k],
            recv_sem=recv_sem.at[k],
            device_id={"dp": peer},
            device_id_type=MESH,
        )

    def start(i, carry):
        beside(order_of(i)).start()
        return carry

    def combine(i, carry):
        k = order_of(i)
        peer = dp_peer(k)
        beside(k).wait_recv()
        total = in_ref[core, peer].astype(single) + got_ref[peer].astype(single)
        sum_ref[peer] = total.astype(bfloat)
        return k

    def onward(i, carry):
        k = combine(i, carry)
        across(k).start()
        return carry

    def arrive(k, carry):
        across(k).wait_recv()
        return carry

    def drain(k, carry):
        across(k).wait_send()
        return carry

    def drain_pass(k, carry):
        beside(k).wait_send()
        return carry

    lax.fori_loop(1, EXPERTS + 1, start, 0)
    lax.fori_loop(1, EXPERTS, onward, 0)
    combine(EXPERTS, 0)
    own = pltpu.make_async_copy(sum_ref.at[dp], out_ref.at[dp], local_sem)
    own.start()
    lax.fori_loop(1, EXPERTS, arrive, 0)
    lax.fori_loop(1, EXPERTS, drain, 0)
    lax.fori_loop(0, EXPERTS, drain_pass, 0)
    own.wait()


def moe_return(rows, collective_id):
    every = pltpu.SemaphoreType.DMA((EXPERTS,))
    block = pltpu.VMEM(rows.shape[1:], bfloat)
    return pl.pallas_call(
        moe_return_kernel,
        out_shape=jax.ShapeDtypeStruct(rows.shape[1:], bfloat),
        in_specs=[VMEM_SPEC],
        out_specs=pl.BlockSpec(memory_space=pl.ANY),
        scratch_shapes=[block, block, pltpu.SemaphoreType.DMA, every, every, every, every],
        compiler_params=pltpu.CompilerParams(
            collective_id=collective_id, has_side_effects=True, vmem_limit_bytes=32 * 2**20
        ),
        name="moe_return",
    )(rows)


def combine_kernel(back_ref, slots_ref, gates_ref, cotangent_ref, out_ref):
    tokens = slots_ref.shape[0]
    half = back_ref.shape[1] // 2
    core = lax.rem(lax.axis_index("tensor"), 2)
    own = cotangent_ref[:, pl.ds(pl.multiple_of(core * half, 128), half)].astype(single)
    ids = lax.broadcasted_iota(jnp.int32, (tokens, SLOTS), 1)
    hits = [jnp.where(ids == slots_ref[:, k : k + 1], 1.0, 0.0) for k in range(2)]
    picked = [dot_rows(hit.astype(bfloat), back_ref[:, :half]) for hit in hits]
    mixed = gates_ref[:, 0:1] * picked[0] + gates_ref[:, 1:2] * picked[1]
    gate = [jnp.sum(p * own, axis=1, keepdims=True) for p in picked]
    normed = dot_rows((hits[0] + hits[1]).astype(bfloat), back_ref[:, half:])
    for j in range(half // 128):
        out_ref[j] = mixed[:, j * 128 : (j + 1) * 128].astype(bfloat)
        out_ref[half // 128 + j] = normed[:, j * 128 : (j + 1) * 128].astype(bfloat)
    lane = lax.broadcasted_iota(jnp.int32, (tokens, 128), 1)
    spread = jnp.where(lane == 0, gate[0], jnp.where(lane == 1, gate[1], 0.0))
    out_ref[2 * (half // 128)] = spread.astype(bfloat)


def combine(back, slots, gates, cotangent):
    tokens = slots.shape[0]
    return pl.pallas_call(
        combine_kernel,
        out_shape=jax.ShapeDtypeStruct((7, tokens, 128), bfloat),
        in_specs=[VMEM_SPEC] * 4,
        out_specs=VMEM_SPEC,
        compiler_params=pltpu.CompilerParams(vmem_limit_bytes=48 * 2**20),
        name="combine",
    )(back, slots, gates, cotangent)


def combine_sum_kernel(p_ref, mixed_ref, normed_ref, gates_ref, got_two, sum_two, got_three, sems):
    t = lax.axis_index("tensor")
    core = lax.rem(t, 2)
    sibling = {"tensor": t + 1 - 2 * core}
    opposite = {"tensor": lax.rem(t + 2, 4)}
    barrier = pltpu.get_barrier_semaphore()
    for peer in (sibling, opposite):
        pl.semaphore_signal(barrier, inc=1, device_id=peer, device_id_type=MESH)
    pl.semaphore_wait(barrier, 2)

    def copy(source, target, step, j, peer):
        return pltpu.make_async_remote_copy(
            src_ref=source,
            dst_ref=target,
            send_sem=sems.at[0, step, j],
            recv_sem=sems.at[1, step, j],
            device_id=peer,
            device_id_type=MESH,
        )

    count = p_ref.shape[0]
    order = [6, 0, 1, 2, 3, 4, 5]
    second = [copy(p_ref.at[j], got_two.at[j], 0, j, opposite) for j in range(count)]
    third = [copy(sum_two.at[j], got_three.at[j], 1, j, sibling) for j in range(count)]
    for j in order:
        second[j].start()

    def place(j, which):
        ref = mixed_ref if j < 3 else normed_ref
        return ref, pl.ds(pl.multiple_of((which * 3 + j % 3) * 128, 128), 128)

    for j in order:
        second[j].wait_recv()
        whole = (p_ref[j].astype(single) + got_two[j].astype(single)).astype(bfloat)
        sum_two[j] = whole
        third[j].start()
        if j < 6:
            ref, at = place(j, core)
            ref[:, at] = whole
    for j in order:
        third[j].wait_recv()
        if j < 6:
            ref, at = place(j, 1 - core)
            ref[:, at] = got_three[j]
        else:
            gates_ref[...] = sum_two[j].astype(single) + got_three[j].astype(single)
    for j in range(count):
        second[j].wait_send()
        third[j].wait_send()


def combine_sum(parts, collective_id):
    count, tokens, lanes = parts.shape
    block = pltpu.VMEM(parts.shape, bfloat)
    whole = jax.ShapeDtypeStruct((tokens, 768), bfloat)
    return pl.pallas_call(
        combine_sum_kernel,
        out_shape=[whole, whole, jax.ShapeDtypeStruct((tokens, lanes), single)],
        in_specs=[VMEM_SPEC],
        out_specs=[VMEM_SPEC] * 3,
        scratch_shapes=[block] * 3 + [pltpu.SemaphoreType.DMA((2, 2, count))],
        compiler_params=pltpu.CompilerParams(
            collective_id=collective_id, has_side_effects=True, vmem_limit_bytes=32 * 2**20
        ),
        name="combine_sum",
    )(parts)


def moe_block(inputs, cotangent, routes, router, expert_in, expert_out, ln_gain, ln_bias):
    tokens_here, feature_width = inputs.shape
    sent, normed_low, normal, inverse, gate_values, slots = moe_route(
        inputs, cotangent, routes, router, ln_gain[3], ln_bias[3]
    )
    arrived = moe_send(sent.reshape(2, EXPERTS, STRIDE, feature_width), 3)
    answers, expert_in_grad, expert_out_grad = expert_ffn(
        arrived.reshape(2, SLOTS, feature_width), expert_in, expert_out
    )
    returned = moe_return(answers.reshape(2, EXPERTS, STRIDE, feature_width), 4)
    parts = combine(returned.reshape(SLOTS, feature_width), slots, gate_values, cotangent)
    mixed, grad_experts, gate_sums = combine_sum(parts, 5)
    output = (inputs + mixed.astype(single)).astype(bfloat)
    grad_out = cotangent.astype(single)
    grad_gates = gate_sums[:, :2]
    grad_chosen = gate_values * (
        grad_gates - jnp.sum(gate_values * grad_gates, axis=1, keepdims=True)
    )
    one_hot = (routes[:, :, None] == jnp.arange(router.shape[1], dtype=jnp.int32)).astype(single)
    grad_logits = jnp.sum(one_hot * grad_chosen[:, :, None], axis=1).astype(bfloat)
    router_part = jnp.einsum("td,te->de", normed_low, grad_logits, preferred_element_type=single)
    grad_normed = grad_experts.astype(single) + jnp.einsum(
        "te,de->td", grad_logits, router, preferred_element_type=single
    )
    grad_in, gain_part, shift_part = norm_backward(grad_normed, normal, inverse, ln_gain[3])
    return (
        output,
        grad_out + grad_in,
        (router_part, expert_in_grad, expert_out_grad, gain_part, shift_part),
    )


def per_device(
    images,
    routes,
    cotangent,
    qkv_weight,
    out_weight,
    qv_bias,
    out_bias,
    ln_gain,
    ln_bias,
    dense_in,
    dense_out,
    router,
    expert_in,
    expert_out,
):
    start_rows = images.astype(single)
    section_one, stored_one = attend_forward(
        start_rows, 0, qkv_weight, out_weight, qv_bias, out_bias, ln_gain, ln_bias
    )
    section_two, stored_dense = dense_forward(section_one, dense_in, dense_out, ln_gain, ln_bias)
    section_three, stored_two = attend_forward(
        section_two, 1, qkv_weight, out_weight, qv_bias, out_bias, ln_gain, ln_bias
    )
    output, grad_three, moe_parts = moe_block(
        section_three, cotangent, routes, router, expert_in, expert_out, ln_gain, ln_bias
    )
    router_grad, expert_in_grad, expert_out_grad, gain_three, shift_three = moe_parts
    grad_two, upper_parts = attend_backward(
        grad_three, 1, stored_two, qkv_weight, out_weight, ln_gain
    )
    qkv_upper, outw_upper, bias_upper, outb_upper, gain_two, shift_two = upper_parts
    grad_one, dense_parts = dense_backward(grad_two, stored_dense, dense_in, dense_out, ln_gain)
    dense_in_grad, dense_out_grad, gain_one, shift_one = dense_parts
    input_grad, lower_parts = attend_backward(
        grad_one, 0, stored_one, qkv_weight, out_weight, ln_gain
    )
    qkv_lower, outw_lower, bias_lower, outb_lower, gain_zero, shift_zero = lower_parts
    local_width = qkv_lower.shape[2]
    arrays = [
        jnp.transpose(qkv_lower, (1, 2, 0)).reshape(3 * local_width, -1),
        jnp.transpose(qkv_upper, (1, 2, 0)).reshape(3 * local_width, -1),
        outw_lower,
        outw_upper,
        dense_in_grad,
        dense_out_grad,
    ]
    small = jnp.concatenate(
        [
            router_grad.T,
            jnp.stack([gain_zero, gain_one, gain_two, gain_three]),
            jnp.stack([shift_zero, shift_one, shift_two, shift_three]),
            jnp.stack([outb_lower, outb_upper]),
            jnp.stack([bias_lower, bias_upper]).reshape(1, -1),
            jnp.zeros((5, router_grad.shape[0]), single),
        ]
    )
    summed = grad_sum([a.astype(bfloat) for a in arrays], small.astype(bfloat), 2)
    big = [a.astype(single) for a in summed]
    small = big[6]
    qkv_weight_grad = jnp.transpose(
        jnp.stack([big[0], big[1]]).reshape(2, 3, local_width, -1), (0, 3, 1, 2)
    )
    out_weight_grad = jnp.stack([big[2], big[3]])
    dense_in_grad, dense_out_grad = big[4], big[5]
    router_grad = small[:32].T
    ln_gain_grad, ln_bias_grad, out_bias_grad = small[32:36], small[36:40], small[40:42]
    qv_bias_grad = small[42].reshape(2, 2, local_width)
    return (
        output,
        input_grad,
        qkv_weight_grad,
        out_weight_grad,
        qv_bias_grad,
        out_bias_grad,
        ln_gain_grad,
        ln_bias_grad,
        dense_in_grad,
        dense_out_grad,
        router_grad,
        expert_in_grad,
        expert_out_grad,
    )


def solution(mesh):
    in_specs = (
        P("dp", None),
        P("dp", None),
        P("dp", None),
        P(None, None, None, "tensor"),
        P(None, "tensor", None),
        P(None, None, "tensor"),
        P(),
        P(),
        P(),
        P(None, "tensor"),
        P("tensor", None),
        P(),
        P("dp", None, "tensor"),
        P("dp", "tensor", None),
    )
    out_specs = (
        P("dp", None),
        P("dp", None),
        P(None, None, None, "tensor"),
        P(None, "tensor", None),
        P(None, None, "tensor"),
        P(),
        P(),
        P(),
        P(None, "tensor"),
        P("tensor", None),
        P(),
        P("dp", None, "tensor"),
        P("dp", "tensor", None),
    )
    return jax.shard_map(
        per_device, mesh=mesh, in_specs=in_specs, out_specs=out_specs, check_vma=False
    )
```

```python
import functools

import jax
import jax.numpy as jnp
from jax import lax
from jax.experimental import pallas as pl
from jax.experimental.pallas import tpu as pltpu
from jax.sharding import PartitionSpec as P

HEAD = 64
SEQ = 197


epsilon = 1e-06
bfloat = jnp.bfloat16
single = jnp.float32


MESH = pl.DeviceIdType.MESH


def tensor_sum_kernel(count, rows, p_ref, o_ref, got_one, sum_one, got_two, sum_two, got_three, sems):
    t = lax.axis_index("tensor")
    core = lax.rem(t, 2)
    sibling = {"tensor": t + 1 - 2 * core}
    opposite = {"tensor": lax.rem(t + 2, 4)}
    barrier = pltpu.get_barrier_semaphore()
    for peer in (sibling, opposite):
        pl.semaphore_signal(barrier, inc=1, device_id=peer, device_id_type=MESH)
    pl.semaphore_wait(barrier, 2)

    def columns(which, j):
        return pl.ds(pl.multiple_of((which * count + j) * 128, 128), 128)

    def copy(source, target, step, j, peer):
        return pltpu.make_async_remote_copy(
            src_ref=source,
            dst_ref=target,
            send_sem=sems.at[0, step, j],
            recv_sem=sems.at[1, step, j],
            device_id=peer,
            device_id_type=MESH,
        )

    first = [copy(p_ref.at[:, columns(1 - core, j)], got_one.at[j], 0, j, sibling) for j in range(count)]
    second = [copy(sum_one.at[j], got_two.at[j], 1, j, opposite) for j in range(count)]
    third = [copy(sum_two.at[j], got_three.at[j], 2, j, sibling) for j in range(count)]
    for j in range(count):
        first[j].start()
    for j in range(count):
        first[j].wait_recv()
        own = p_ref[:, columns(core, j)].astype(single)
        sum_one[j] = (own + got_one[j].astype(single)).astype(bfloat)
        second[j].start()
    for j in range(count):
        second[j].wait_recv()
        whole = (sum_one[j].astype(single) + got_two[j].astype(single)).astype(bfloat)
        sum_two[j] = whole
        third[j].start()
        o_ref[:, columns(core, j)] = whole
    for j in range(count):
        third[j].wait_recv()
        o_ref[:, columns(1 - core, j)] = got_three[j]
    for j in range(count):
        first[j].wait_send()
        second[j].wait_send()
        third[j].wait_send()


def tensor_sum(partial, collective_id):
    rows, width = partial.shape
    count = width // 256
    block = pltpu.VMEM((count, rows, 128), bfloat)
    return pl.pallas_call(
        functools.partial(tensor_sum_kernel, count, rows),
        out_shape=jax.ShapeDtypeStruct((rows, width), bfloat),
        in_specs=[pl.BlockSpec(memory_space=pltpu.VMEM)],
        out_specs=pl.BlockSpec(memory_space=pltpu.VMEM),
        scratch_shapes=[block] * 5 + [pltpu.SemaphoreType.DMA((2, 3, count))],
        compiler_params=pltpu.CompilerParams(
            collective_id=collective_id, has_side_effects=True, vmem_limit_bytes=32 * 2**20
        ),
        name="tensor_sum",
    )(partial)


BIG = 3072
HALF = BIG // 2
PART = HALF // 4
PIECE = PART // 4
SMALL = 48


def add_rows(target, target_row, sources, rows):
    def body(i, carry):
        total = None
        for ref, row in sources:
            value = ref[pl.ds(pl.multiple_of(row + i * 16, 16), 16), :].astype(single)
            total = value if total is None else total + value
        target[pl.ds(pl.multiple_of(target_row + i * 16, 16), 16), :] = total.astype(bfloat)
        return carry

    lax.fori_loop(0, rows // 16, body, 0)


def grad_sum_kernel(*refs):
    ins, small_in = refs[:6], refs[6]
    outs, small_out = refs[7:13], refs[13]
    (given, result, near_a, near_b, left_a, right_a, left_b, right_b, pass_a, pass_b, sum_a, sum_b) = refs[14:26]
    (near_c, near_d, left_c, right_c, left_d, right_d, pass_c, pass_d, sum_c, sum_d) = refs[26:36]
    z_got, small_x, small_y, small_z, small_one, small_two = refs[36:42]
    local_sem, send_sem, recv_sem, small_send, small_recv = refs[42:47]

    dp = lax.axis_index("dp")
    plane, x, y = dp // 16, lax.rem(dp // 4, 4), lax.rem(dp, 4)

    def at(plane_to, x_to, y_to):
        return {"dp": plane_to * 16 + x_to * 4 + y_to}

    def along_x(step):
        return at(plane, lax.rem(x + step, 4), y)

    def along_y(step):
        return at(plane, x, lax.rem(y + step, 4))

    across = at(1 - plane, x, y)
    barrier = pltpu.get_barrier_semaphore()
    peers = [along_x(1), along_x(2), along_x(3), along_y(1), along_y(2), along_y(3), across]
    for peer in peers:
        pl.semaphore_signal(barrier, inc=1, device_id=peer, device_id_type=MESH)

    sizes = [ref.shape[0] for ref in ins]
    starts = [sum(sizes[:i]) for i in range(6)]
    loads = [
        pltpu.make_async_copy(ins[i], given.at[pl.ds(starts[i], sizes[i]), :], local_sem.at[i])
        for i in range(6)
    ]
    for load in loads:
        load.start()
    for load in loads:
        load.wait()
    pl.semaphore_wait(barrier, 7)

    used = []

    def send(source, target, peer):
        k = len(used)
        copy = pltpu.make_async_remote_copy(
            src_ref=source,
            dst_ref=target,
            send_sem=send_sem.at[k],
            recv_sem=recv_sem.at[k],
            device_id=peer,
            device_id_type=MESH,
        )
        used.append(copy)
        copy.start()
        return copy

    small_used = []

    def send_small(source, target, peer):
        k = len(small_used)
        copy = pltpu.make_async_remote_copy(
            src_ref=source,
            dst_ref=target,
            send_sem=small_send.at[k],
            recv_sem=small_recv.at[k],
            device_id=peer,
            device_id_type=MESH,
        )
        small_used.append(copy)
        copy.start()
        return copy

    def rows_of(ref, row, count):
        return ref.at[pl.ds(pl.multiple_of(row, 16), count), :]

    class Scatter:
        def __init__(self, source, base, size, place, along, near, left, right, onward, total):
            self.source, self.base, self.size, self.place = source, base, size, place
            self.along, self.near, self.left, self.right = along, near, left, right
            self.onward, self.total = onward, total

        def row(self, step):
            return self.base + lax.rem(self.place + step, 4) * self.size

        def start(self):
            half = self.size // 2
            s = self.source
            self.far_right = send(rows_of(s, self.row(2), half), rows_of(self.near, 0, half), self.along(1))
            self.far_left = send(rows_of(s, self.row(2) + half, half), rows_of(self.near, half, half), self.along(3))
            self.to_right = send(rows_of(s, self.row(1) + half, half), rows_of(self.left, half, half), self.along(1))
            self.to_left = send(rows_of(s, self.row(3), half), rows_of(self.right, 0, half), self.along(3))

        def middle(self):
            half = self.size // 2
            s = self.source
            self.far_right.wait_recv()
            add_rows(self.onward, 0, [(s, self.row(1)), (self.near, 0)], half)
            self.on_right = send(rows_of(self.onward, 0, half), rows_of(self.left, 0, half), self.along(1))
            self.far_left.wait_recv()
            add_rows(self.onward, half, [(s, self.row(3) + half), (self.near, half)], half)
            self.on_left = send(rows_of(self.onward, half, half), rows_of(self.right, half, half), self.along(3))

        def finish(self):
            for copy in (self.to_right, self.to_left, self.on_right, self.on_left):
                copy.wait_recv()
            add_rows(self.total, 0, [(self.source, self.row(0)), (self.left, 0), (self.right, 0)], self.size)

    class Gather:
        def __init__(self, base, size, place, along):
            self.base, self.size, self.place, self.along = base, size, place, along

        def row(self, step):
            return self.base + lax.rem(self.place + step, 4) * self.size

        def start(self):
            own, half = self.row(0), self.size // 2
            first, second = rows_of(result, own, half), rows_of(result, own + half, half)
            self.right_one = send(first, first, self.along(1))
            self.left_two = send(second, second, self.along(3))
            self.right_two = send(second, second, self.along(1))
            self.left_one = send(first, first, self.along(3))

        def middle(self):
            half = self.size // 2
            self.right_one.wait_recv()
            from_left = rows_of(result, self.row(3), half)
            self.on_right = send(from_left, from_left, self.along(1))
            self.left_two.wait_recv()
            from_right = rows_of(result, self.row(1) + half, half)
            self.on_left = send(from_right, from_right, self.along(3))

        def finish(self):
            for copy in (self.right_two, self.left_one, self.on_right, self.on_left):
                copy.wait_recv()

    def together(parts):
        for part in parts:
            part.start()
        for part in parts:
            part.middle()
        for part in parts:
            part.finish()

    def add_small(target, ref, count):
        def body(i, carry):
            at_rows = pl.ds(pl.multiple_of(i * 16, 16), 16)
            total = ref[0, at_rows, :].astype(single)
            for k in range(1, count):
                total = total + ref[k, at_rows, :].astype(single)
            target[at_rows, :] = total.astype(bfloat)
            return carry

        lax.fori_loop(0, SMALL // 16, body, 0)

    small_x[x] = small_in[...]
    first_small = [send_small(small_in, small_x.at[x], along_x(k)) for k in (1, 2, 3)]
    together(
        [
            Scatter(given, 0, PART, x, along_x, near_a, left_a, right_a, pass_a, sum_a),
            Scatter(given, HALF, PART, y, along_y, near_b, left_b, right_b, pass_b, sum_b),
        ]
    )
    for copy in first_small:
        copy.wait_recv()
    add_small(small_one, small_x, 4)
    small_y[y] = small_one[...]
    second_small = [send_small(small_one, small_y.at[y], along_y(k)) for k in (1, 2, 3)]
    together(
        [
            Scatter(sum_a, 0, PIECE, y, along_y, near_c, left_c, right_c, pass_c, sum_c),
            Scatter(sum_b, 0, PIECE, x, along_x, near_d, left_d, right_d, pass_d, sum_d),
        ]
    )
    for copy in second_small:
        copy.wait_recv()
    add_small(small_two, small_y, 4)
    small_z[plane] = small_two[...]
    pair_small = send_small(small_two, small_z.at[plane], across)
    pair_a = send(sum_c, rows_of(z_got, 0, PIECE), across)
    pair_b = send(sum_d, rows_of(z_got, PIECE, PIECE), across)
    row_a = x * PART + y * PIECE
    row_b = HALF + y * PART + x * PIECE
    pair_a.wait_recv()
    add_rows(result, row_a, [(sum_c, 0), (z_got, 0)], PIECE)
    pair_b.wait_recv()
    add_rows(result, row_b, [(sum_d, 0), (z_got, PIECE)], PIECE)
    together([Gather(x * PART, PIECE, y, along_y), Gather(HALF + y * PART, PIECE, x, along_x)])
    together([Gather(0, PART, x, along_x), Gather(HALF, PART, y, along_y)])
    stores = [
        pltpu.make_async_copy(result.at[pl.ds(starts[i], sizes[i]), :], outs[i], local_sem.at[i])
        for i in range(6)
    ]
    for store in stores:
        store.start()
    pair_small.wait_recv()
    add_small(small_out, small_z, 2)
    for copy in used:
        copy.wait_send()
    for copy in small_used:
        copy.wait_send()
    for store in stores:
        store.wait()


def grad_sum(arrays, small, collective_id):
    def rows(count):
        return pltpu.VMEM((count, 768), bfloat)

    scratch = [rows(BIG), rows(BIG)]
    scratch += [rows(PART)] * 10
    scratch += [rows(PIECE)] * 10
    scratch += [rows(2 * PIECE)]
    scratch += [pltpu.VMEM((4, SMALL, 768), bfloat)] * 2 + [pltpu.VMEM((2, SMALL, 768), bfloat)]
    scratch += [rows(SMALL)] * 2
    scratch += [
        pltpu.SemaphoreType.DMA((6,)),
        pltpu.SemaphoreType.DMA((50,)),
        pltpu.SemaphoreType.DMA((50,)),
        pltpu.SemaphoreType.DMA((7,)),
        pltpu.SemaphoreType.DMA((7,)),
    ]
    hbm = pl.BlockSpec(memory_space=pl.ANY)
    vmem = pl.BlockSpec(memory_space=pltpu.VMEM)
    return pl.pallas_call(
        grad_sum_kernel,
        out_shape=[jax.ShapeDtypeStruct(a.shape, bfloat) for a in arrays]
        + [jax.ShapeDtypeStruct(small.shape, bfloat)],
        in_specs=[hbm] * 6 + [vmem],
        out_specs=[hbm] * 6 + [vmem],
        scratch_shapes=scratch,
        compiler_params=pltpu.CompilerParams(
            collective_id=collective_id, has_side_effects=True, vmem_limit_bytes=40 * 2**20
        ),
        name="grad_sum",
    )(*arrays, small)


EXPERTS = 32
STRIDE = 40
SLOTS = EXPERTS * STRIDE


def dot_rows(a, b):
    return lax.dot_general(a, b, (((1,), (0,)), ((), ())), preferred_element_type=single)


def dot_last(a, b):
    return lax.dot_general(a, b, (((1,), (1,)), ((), ())), preferred_element_type=single)


def dot_first(a, b):
    return lax.dot_general(a, b, (((0,), (0,)), ((), ())), preferred_element_type=single)


def moe_route_kernel(
    rows_ref, sum_ref, out_bias_ref, cotangent_ref, routes_ref, routes_row_ref, router_ref,
    gain_ref, shift_ref, new_ref, out_ref, gates_ref, slots_ref,
):
    tokens, width = rows_ref.shape
    half = width // 2
    rows = rows_ref[...] + sum_ref[...].astype(single) + out_bias_ref[1:2, :]
    new_ref[...] = rows
    normal, unused = normal_of(rows)
    low = (normal * gain_ref[3:4, :] + shift_ref[3:4, :]).astype(bfloat)
    logits = dot_last(low, router_ref[...])
    experts = lax.broadcasted_iota(jnp.int32, (tokens, EXPERTS), 1)
    picks = [routes_ref[:, k : k + 1] == experts for k in range(2)]
    chosen = [jnp.sum(jnp.where(pick, logits, 0.0), axis=1, keepdims=True) for pick in picks]
    largest = jnp.maximum(chosen[0], chosen[1])
    powers = [jnp.exp(c - largest) for c in chosen]
    total = powers[0] + powers[1]
    gates = [power / total for power in powers]
    gates_ref[:, 0:1] = gates[0]
    gates_ref[:, 1:2] = gates[1]

    before = lax.broadcasted_iota(jnp.int32, (tokens, tokens), 0)
    after = lax.broadcasted_iota(jnp.int32, (tokens, tokens), 1)
    either = [jnp.where(pick, 1.0, 0.0) for pick in picks]
    lower = jnp.where(after < before, 1.0, 0.0).astype(bfloat)
    running = dot_rows(lower, (either[0] + either[1]).astype(bfloat))
    for k in range(2):
        rank = jnp.sum(running * either[k], axis=1, keepdims=True).astype(jnp.int32)
        slots_ref[:, k : k + 1] = routes_ref[:, k : k + 1] * STRIDE + rank

    experts_row = lax.broadcasted_iota(jnp.int32, (EXPERTS, tokens), 0)
    either_row = [
        jnp.where(routes_row_ref[k : k + 1, :] == experts_row, 1.0, 0.0) for k in range(2)
    ]
    upper = jnp.where(before < after, 1.0, 0.0).astype(bfloat)
    running_row = dot_rows((either_row[0] + either_row[1]).astype(bfloat), upper)
    slots_row = []
    for k in range(2):
        rank = jnp.sum(running_row * either_row[k], axis=0, keepdims=True).astype(jnp.int32)
        slots_row.append(routes_row_ref[k : k + 1, :] * STRIDE + rank)

    cotangent = cotangent_ref[...].astype(single)
    scaled = [(gate * cotangent).astype(bfloat) for gate in gates]
    block = SLOTS // 8
    for i in range(8):
        ids = lax.broadcasted_iota(jnp.int32, (block, tokens), 0) + i * block
        hits = [jnp.where(ids == slots_row[k], 1.0, 0.0) for k in range(2)]
        moved = dot_rows((hits[0] + hits[1]).astype(bfloat), low).astype(bfloat)
        moved_grad = (
            dot_rows(hits[0].astype(bfloat), scaled[0]) + dot_rows(hits[1].astype(bfloat), scaled[1])
        ).astype(bfloat)
        at = slice(i * block, (i + 1) * block)
        for h in range(2):
            out_ref[h, at, :half] = moved[:, h * half : (h + 1) * half]
            out_ref[h, at, half:] = moved_grad[:, h * half : (h + 1) * half]


VMEM_SPEC = pl.BlockSpec(memory_space=pltpu.VMEM)


def moe_route(rows, total, out_bias, cotangent, routes, router, ln_gain, ln_bias):
    tokens, width = rows.shape
    outs = [
        ((tokens, width), single),
        ((2, SLOTS, width), bfloat),
        ((tokens, 2), single),
        ((tokens, 2), jnp.int32),
    ]
    args = (rows, total, out_bias, cotangent, routes, routes.T, router.T, ln_gain, ln_bias)
    return local_call(moe_route_kernel, "moe_route", args, outs, limit=40)


def dp_peer(k):
    dp = lax.axis_index("dp")
    plane = lax.rem(dp // 16 + k // 16, 2)
    x = lax.rem(lax.rem(dp // 4, 4) + lax.rem(k // 4, 4), 4)
    y = lax.rem(lax.rem(dp, 4) + lax.rem(k, 4), 4)
    return plane * 16 + x * 4 + y


def dp_source(k):
    dp = lax.axis_index("dp")
    plane = lax.rem(dp // 16 + k // 16, 2)
    x = lax.rem(lax.rem(dp // 4, 4) + 4 - lax.rem(k // 4, 4), 4)
    y = lax.rem(lax.rem(dp, 4) + 4 - lax.rem(k, 4), 4)
    return plane * 16 + x * 4 + y


def order_of(i):
    return lax.rem(i * 11, EXPERTS)


def meet_all(sibling):
    barrier = pltpu.get_barrier_semaphore()

    def greet(k, carry):
        pl.semaphore_signal(barrier, inc=1, device_id={"dp": dp_peer(k)}, device_id_type=MESH)
        return carry

    lax.fori_loop(1, EXPERTS, greet, 0)
    pl.semaphore_signal(barrier, inc=1, device_id=sibling, device_id_type=MESH)
    pl.semaphore_wait(barrier, EXPERTS)


def moe_send_kernel(in_ref, out_ref, local_sem, send_sem, recv_sem, pass_sem, land_sem):
    t = lax.axis_index("tensor")
    dp = lax.axis_index("dp")
    core = lax.rem(t, 2)
    sibling = {"tensor": t + 1 - 2 * core}
    own = pltpu.make_async_copy(in_ref.at[core, dp], out_ref.at[core, dp], local_sem)
    own.start()
    meet_all(sibling)

    def across(k):
        peer = dp_peer(k)
        return pltpu.make_async_remote_copy(
            src_ref=in_ref.at[core, peer],
            dst_ref=out_ref.at[core, dp],
            send_sem=send_sem.at[k],
            recv_sem=recv_sem.at[k],
            device_id={"dp": peer},
            device_id_type=MESH,
        )

    def beside(k):
        block = out_ref.at[core, dp_source(k)]
        return pltpu.make_async_remote_copy(
            src_ref=block,
            dst_ref=block,
            send_sem=pass_sem.at[k],
            recv_sem=land_sem.at[k],
            device_id=sibling,
            device_id_type=MESH,
        )

    def start(i, carry):
        across(order_of(i)).start()
        return carry

    def forward(i, carry):
        k = order_of(i)
        across(k).wait_recv()
        beside(k).start()
        return carry

    def land(k, carry):
        beside(k).wait_recv()
        return carry

    def drain(k, carry):
        across(k).wait_send()
        return carry

    def drain_pass(k, carry):
        beside(k).wait_send()
        return carry

    lax.fori_loop(1, EXPERTS, start, 0)
    own.wait()
    beside(0).start()
    lax.fori_loop(1, EXPERTS, forward, 0)
    lax.fori_loop(0, EXPERTS, land, 0)
    lax.fori_loop(1, EXPERTS, drain, 0)
    lax.fori_loop(0, EXPERTS, drain_pass, 0)


def moe_send(rows, collective_id):
    every = pltpu.SemaphoreType.DMA((EXPERTS,))
    hbm = pl.BlockSpec(memory_space=pl.ANY)
    return pl.pallas_call(
        moe_send_kernel,
        out_shape=jax.ShapeDtypeStruct(rows.shape, bfloat),
        in_specs=[hbm],
        out_specs=hbm,
        scratch_shapes=[pltpu.SemaphoreType.DMA, every, every, every, every],
        compiler_params=pltpu.CompilerParams(collective_id=collective_id, has_side_effects=True),
        name="moe_send",
    )(rows)


def expert_kernel(in_ref, ein_ref, eout_ref, out_ref, ein_grad_ref, eout_grad_ref, act_ref, grad_ref):
    half = in_ref.shape[2] // 2
    width = 2 * half
    block = SLOTS // 4

    def both(at, first):
        parts = [in_ref[h, at, first : first + half] for h in range(2)]
        return jnp.concatenate(parts, axis=1)

    def forward(i, carry):
        at = pl.ds(pl.multiple_of(i * block, 16), block)
        rows = both(at, 0)
        rows_grad = both(at, half)
        pre = dot_rows(rows, ein_ref[0])
        grad_act = dot_last(rows_grad, eout_ref[0])
        tail = 0.5 * (1.0 + lax.erf(pre * (0.5**0.5)))
        act = (pre * tail).astype(bfloat)
        slope = tail + pre * (jnp.exp(-0.5 * pre * pre) * 0.3989422804014327)
        grad_pre = (grad_act * slope).astype(bfloat)
        act_ref[at, :] = act
        grad_ref[at, :] = grad_pre
        out = dot_rows(act, eout_ref[0]).astype(bfloat)
        back = dot_last(grad_pre, ein_ref[0]).astype(bfloat)
        for h in range(2):
            out_ref[h, at, :half] = out[:, h * half : (h + 1) * half]
            out_ref[h, at, half:] = back[:, h * half : (h + 1) * half]
        return carry

    lax.fori_loop(0, SLOTS // block, forward, 0)
    for h in range(2):
        eout_grad_ref[0, :, h * half : (h + 1) * half] = dot_first(act_ref[...], in_ref[h, :, half:])
        ein_grad_ref[0, h * half : (h + 1) * half, :] = dot_first(in_ref[h, :, :half], grad_ref[...])


def expert_ffn(rows, expert_in, expert_out):
    width = rows.shape[2]
    weight = jax.ShapeDtypeStruct(expert_in.shape, single)
    return pl.pallas_call(
        expert_kernel,
        out_shape=[jax.ShapeDtypeStruct(rows.shape, bfloat), weight, weight],
        in_specs=[VMEM_SPEC] * 3,
        out_specs=[VMEM_SPEC] * 3,
        scratch_shapes=[pltpu.VMEM((SLOTS, width), bfloat)] * 2,
        compiler_params=pltpu.CompilerParams(vmem_limit_bytes=56 * 2**20),
        name="expert_ffn",
    )(rows, expert_in, expert_out)


def moe_return_kernel(in_ref, out_ref, got_ref, sum_ref, local_sem, send_sem, recv_sem, pass_sem, land_sem):
    t = lax.axis_index("tensor")
    dp = lax.axis_index("dp")
    core = lax.rem(t, 2)
    sibling = {"tensor": t + 1 - 2 * core}
    meet_all(sibling)

    def beside(k):
        peer = dp_peer(k)
        return pltpu.make_async_remote_copy(
            src_ref=in_ref.at[1 - core, peer],
            dst_ref=got_ref.at[peer],
            send_sem=pass_sem.at[k],
            recv_sem=land_sem.at[k],
            device_id=sibling,
            device_id_type=MESH,
        )

    def across(k):
        peer = dp_peer(k)
        return pltpu.make_async_remote_copy(
            src_ref=sum_ref.at[peer],
            dst_ref=out_ref.at[dp],
            send_sem=send_sem.at[k],
            recv_sem=recv_sem.at[k],
            device_id={"dp": peer},
            device_id_type=MESH,
        )

    def start(i, carry):
        beside(order_of(i)).start()
        return carry

    def combine(i, carry):
        k = order_of(i)
        peer = dp_peer(k)
        beside(k).wait_recv()
        total = in_ref[core, peer].astype(single) + got_ref[peer].astype(single)
        sum_ref[peer] = total.astype(bfloat)
        return k

    def onward(i, carry):
        k = combine(i, carry)
        across(k).start()
        return carry

    def arrive(k, carry):
        across(k).wait_recv()
        return carry

    def drain(k, carry):
        across(k).wait_send()
        return carry

    def drain_pass(k, carry):
        beside(k).wait_send()
        return carry

    lax.fori_loop(1, EXPERTS + 1, start, 0)
    lax.fori_loop(1, EXPERTS, onward, 0)
    combine(EXPERTS, 0)
    own = pltpu.make_async_copy(sum_ref.at[dp], out_ref.at[dp], local_sem)
    own.start()
    lax.fori_loop(1, EXPERTS, arrive, 0)
    lax.fori_loop(1, EXPERTS, drain, 0)
    lax.fori_loop(0, EXPERTS, drain_pass, 0)
    own.wait()


def moe_return(rows, collective_id):
    every = pltpu.SemaphoreType.DMA((EXPERTS,))
    block = pltpu.VMEM(rows.shape[1:], bfloat)
    return pl.pallas_call(
        moe_return_kernel,
        out_shape=jax.ShapeDtypeStruct(rows.shape[1:], bfloat),
        in_specs=[VMEM_SPEC],
        out_specs=pl.BlockSpec(memory_space=pl.ANY),
        scratch_shapes=[block, block, pltpu.SemaphoreType.DMA, every, every, every, every],
        compiler_params=pltpu.CompilerParams(
            collective_id=collective_id, has_side_effects=True, vmem_limit_bytes=32 * 2**20
        ),
        name="moe_return",
    )(rows)


def combine_kernel(back_ref, slots_ref, gates_ref, cotangent_ref, out_ref):
    tokens = slots_ref.shape[0]
    half = back_ref.shape[1] // 2
    core = lax.rem(lax.axis_index("tensor"), 2)
    own = cotangent_ref[:, pl.ds(pl.multiple_of(core * half, 128), half)].astype(single)
    ids = lax.broadcasted_iota(jnp.int32, (tokens, SLOTS), 1)
    hits = [jnp.where(ids == slots_ref[:, k : k + 1], 1.0, 0.0) for k in range(2)]
    picked = [dot_rows(hit.astype(bfloat), back_ref[:, :half]) for hit in hits]
    mixed = gates_ref[:, 0:1] * picked[0] + gates_ref[:, 1:2] * picked[1]
    gate = [jnp.sum(p * own, axis=1, keepdims=True) for p in picked]
    normed = dot_rows((hits[0] + hits[1]).astype(bfloat), back_ref[:, half:])
    for j in range(half // 128):
        out_ref[j] = mixed[:, j * 128 : (j + 1) * 128].astype(bfloat)
        out_ref[half // 128 + j] = normed[:, j * 128 : (j + 1) * 128].astype(bfloat)
    lane = lax.broadcasted_iota(jnp.int32, (tokens, 128), 1)
    spread = jnp.where(lane == 0, gate[0], jnp.where(lane == 1, gate[1], 0.0))
    out_ref[2 * (half // 128)] = spread.astype(bfloat)


def combine(back, slots, gates, cotangent):
    tokens = slots.shape[0]
    return pl.pallas_call(
        combine_kernel,
        out_shape=jax.ShapeDtypeStruct((7, tokens, 128), bfloat),
        in_specs=[VMEM_SPEC] * 4,
        out_specs=VMEM_SPEC,
        compiler_params=pltpu.CompilerParams(vmem_limit_bytes=48 * 2**20),
        name="combine",
    )(back, slots, gates, cotangent)


def combine_sum_kernel(p_ref, mixed_ref, normed_ref, gates_ref, got_two, sum_two, got_three, sems):
    t = lax.axis_index("tensor")
    core = lax.rem(t, 2)
    sibling = {"tensor": t + 1 - 2 * core}
    opposite = {"tensor": lax.rem(t + 2, 4)}
    barrier = pltpu.get_barrier_semaphore()
    for peer in (sibling, opposite):
        pl.semaphore_signal(barrier, inc=1, device_id=peer, device_id_type=MESH)
    pl.semaphore_wait(barrier, 2)

    def copy(source, target, step, j, peer):
        return pltpu.make_async_remote_copy(
            src_ref=source,
            dst_ref=target,
            send_sem=sems.at[0, step, j],
            recv_sem=sems.at[1, step, j],
            device_id=peer,
            device_id_type=MESH,
        )

    count = p_ref.shape[0]
    order = [6, 0, 1, 2, 3, 4, 5]
    second = [copy(p_ref.at[j], got_two.at[j], 0, j, opposite) for j in range(count)]
    third = [copy(sum_two.at[j], got_three.at[j], 1, j, sibling) for j in range(count)]
    for j in order:
        second[j].start()

    def place(j, which):
        ref = mixed_ref if j < 3 else normed_ref
        return ref, pl.ds(pl.multiple_of((which * 3 + j % 3) * 128, 128), 128)

    for j in order:
        second[j].wait_recv()
        whole = (p_ref[j].astype(single) + got_two[j].astype(single)).astype(bfloat)
        sum_two[j] = whole
        third[j].start()
        if j < 6:
            ref, at = place(j, core)
            ref[:, at] = whole
    for j in order:
        third[j].wait_recv()
        if j < 6:
            ref, at = place(j, 1 - core)
            ref[:, at] = got_three[j]
        else:
            gates_ref[...] = sum_two[j].astype(single) + got_three[j].astype(single)
    for j in range(count):
        second[j].wait_send()
        third[j].wait_send()


def combine_sum(parts, collective_id):
    count, tokens, lanes = parts.shape
    block = pltpu.VMEM(parts.shape, bfloat)
    whole = jax.ShapeDtypeStruct((tokens, 768), bfloat)
    return pl.pallas_call(
        combine_sum_kernel,
        out_shape=[whole, whole, jax.ShapeDtypeStruct((tokens, lanes), single)],
        in_specs=[VMEM_SPEC],
        out_specs=[VMEM_SPEC] * 3,
        scratch_shapes=[block] * 3 + [pltpu.SemaphoreType.DMA((2, 2, count))],
        compiler_params=pltpu.CompilerParams(
            collective_id=collective_id, has_side_effects=True, vmem_limit_bytes=32 * 2**20
        ),
        name="combine_sum",
    )(parts)


def normal_of(rows):
    average = jnp.mean(rows, axis=-1, keepdims=True)
    centered = rows - average
    variance = jnp.mean(centered * centered, axis=-1, keepdims=True)
    inverse = lax.rsqrt(variance + epsilon)
    return centered * inverse, inverse


def norm_back(grad_normed, rows, gain_row):
    normal, inverse = normal_of(rows)
    scaled = grad_normed * gain_row
    mean_one = jnp.mean(scaled, axis=-1, keepdims=True)
    mean_two = jnp.mean(scaled * normal, axis=-1, keepdims=True)
    grad_in = inverse * (scaled - mean_one - normal * mean_two)
    gain_part = jnp.sum(grad_normed * normal, axis=0, keepdims=True)
    return grad_in, gain_part, jnp.sum(grad_normed, axis=0, keepdims=True)


def attend_forward_body(rows, layer, qkv_ref, out_ref, qv_bias_ref, gain_ref, shift_ref, refs):
    partial_ref, low_ref, q_ref, k_ref, v_ref, log_ref, context_ref = refs
    width = qkv_ref.shape[1] // 3
    norm = 2 * layer
    normal, unused = normal_of(rows)
    low = (normal * gain_ref[norm : norm + 1, :] + shift_ref[norm : norm + 1, :]).astype(bfloat)
    low_ref[...] = low
    bias = qv_bias_ref[layer]
    q = (dot_last(low, qkv_ref[layer, :width, :]) + bias[0:1, :]).astype(bfloat)
    k = dot_last(low, qkv_ref[layer, width : 2 * width, :]).astype(bfloat)
    v = (dot_last(low, qkv_ref[layer, 2 * width :, :]) + bias[1:2, :]).astype(bfloat)
    q_ref[...] = q
    k_ref[...] = k
    v_ref[...] = v
    same = same_image(rows.shape[0])
    contexts = []
    for h in range(width // HEAD):
        at = slice(h * HEAD, (h + 1) * HEAD)
        scores = jnp.where(same, dot_last(q[:, at], k[:, at]) * HEAD ** (-0.5), -1e30)
        largest = jnp.max(scores, axis=-1, keepdims=True)
        exponent = jnp.exp(scores - largest)
        totals = jnp.sum(exponent, axis=-1, keepdims=True)
        log_ref[:, h : h + 1] = largest + jnp.log(totals)
        contexts.append(dot_rows((exponent / totals).astype(bfloat), v[:, at]))
    context = jnp.concatenate(contexts, axis=1).astype(bfloat)
    context_ref[...] = context
    partial_ref[...] = dot_rows(context, out_ref[layer]).astype(bfloat)


def same_image(tokens):
    first = lax.broadcasted_iota(jnp.int32, (tokens, tokens), 0) // SEQ
    second = lax.broadcasted_iota(jnp.int32, (tokens, tokens), 1) // SEQ
    return first == second


def attend_backward_body(grad_out, layer, saved, qkv_ref, out_ref, refs):
    low_ref, q_ref, k_ref, v_ref, log_ref, context_ref = saved
    partial_ref, qkv_grad_ref, out_grad_ref, bias_grad_ref = refs
    width = qkv_ref.shape[1] // 3
    grad_low = grad_out.astype(bfloat)
    out_grad_ref[...] = dot_first(context_ref[...], grad_low).astype(bfloat)
    grad_context = dot_last(grad_low, out_ref[layer]).astype(bfloat)
    q, k, v = q_ref[...], k_ref[...], v_ref[...]
    same = same_image(q.shape[0])
    grads = [[], [], []]
    for h in range(width // HEAD):
        at = slice(h * HEAD, (h + 1) * HEAD)
        scores = jnp.where(same, dot_last(q[:, at], k[:, at]) * HEAD ** (-0.5), -1e30)
        probs = jnp.exp(scores - log_ref[:, h : h + 1])
        grad_probs = dot_last(grad_context[:, at], v[:, at])
        row_total = jnp.sum(probs * grad_probs, axis=-1, keepdims=True)
        grad_scores = (probs * (grad_probs - row_total)).astype(bfloat)
        grads[0].append(dot_rows(grad_scores, k[:, at]) * HEAD ** (-0.5))
        grads[1].append(dot_first(grad_scores, q[:, at]) * HEAD ** (-0.5))
        grads[2].append(dot_first(probs.astype(bfloat), grad_context[:, at]))
    low = low_ref[...]
    total = None
    for part in range(3):
        grad = jnp.concatenate(grads[part], axis=1).astype(bfloat)
        at = slice(part * width, (part + 1) * width)
        qkv_grad_ref[at, :] = dot_first(grad, low).astype(bfloat)
        term = dot_rows(grad, qkv_ref[layer, at, :])
        total = term if total is None else total + term
        if part != 1:
            row = part // 2
            bias_grad_ref[row : row + 1, :] = jnp.sum(grad.astype(single), axis=0, keepdims=True)
    partial_ref[...] = total.astype(bfloat)


def first_attend_kernel(images_ref, qkv_ref, out_ref, qv_bias_ref, gain_ref, shift_ref, *refs):
    attend_forward_body(
        images_ref[...].astype(single), 0, qkv_ref, out_ref, qv_bias_ref, gain_ref, shift_ref, refs
    )


def second_attend_kernel(
    rows_ref, sum_ref, qkv_ref, out_ref, qv_bias_ref, gain_ref, shift_ref, new_ref, *refs
):
    rows = rows_ref[...] + sum_ref[...].astype(single)
    new_ref[...] = rows
    attend_forward_body(rows, 1, qkv_ref, out_ref, qv_bias_ref, gain_ref, shift_ref, refs)


def dense_forward_kernel(
    images_ref, sum_ref, out_bias_ref, gain_ref, shift_ref, in_ref, out_ref,
    new_ref, partial_ref, low_ref, slope_ref, act_ref,
):
    rows = images_ref[...].astype(single) + sum_ref[...].astype(single) + out_bias_ref[0:1, :]
    new_ref[...] = rows
    normal, unused = normal_of(rows)
    low = (normal * gain_ref[1:2, :] + shift_ref[1:2, :]).astype(bfloat)
    low_ref[...] = low
    pre = dot_rows(low, in_ref[...])
    tail = 0.5 * (1.0 + lax.erf(pre * (0.5**0.5)))
    slope_ref[...] = tail + pre * (jnp.exp(-0.5 * pre * pre) * 0.3989422804014327)
    act = (pre * tail).astype(bfloat)
    act_ref[...] = act
    partial_ref[...] = dot_rows(act, out_ref[...]).astype(bfloat)


def dense_backward_kernel(
    grad_ref, sum_ref, above_ref, gain_ref, low_ref, slope_ref, act_ref, in_ref, out_ref,
    new_ref, partial_ref, in_grad_ref, out_grad_ref, norm_ref,
):
    grad_in, gain_part, shift_part = norm_back(
        sum_ref[...].astype(single), above_ref[...], gain_ref[2:3, :]
    )
    norm_ref[0:1, :] = gain_part
    norm_ref[1:2, :] = shift_part
    grad_out = grad_ref[...] + grad_in
    new_ref[...] = grad_out
    grad_low = grad_out.astype(bfloat)
    grad_pre = (dot_last(grad_low, out_ref[...]) * slope_ref[...]).astype(bfloat)
    partial_ref[...] = dot_last(grad_pre, in_ref[...]).astype(bfloat)
    out_grad_ref[...] = dot_first(act_ref[...], grad_low).astype(bfloat)
    in_grad_ref[...] = dot_first(low_ref[...], grad_pre).astype(bfloat)


def first_attend_backward_kernel(
    grad_ref, sum_ref, rows_ref, gain_ref, low_ref, q_ref, k_ref, v_ref, log_ref, context_ref,
    qkv_ref, out_ref, new_ref, norm_ref, *refs,
):
    grad_in, gain_part, shift_part = norm_back(
        sum_ref[...].astype(single), rows_ref[...], gain_ref[1:2, :]
    )
    grad_out = grad_ref[...] + grad_in
    new_ref[...] = grad_out
    norm_ref[0:1, :] = gain_part
    norm_ref[1:2, :] = shift_part
    norm_ref[2:3, :] = jnp.sum(grad_out, axis=0, keepdims=True)
    saved = (low_ref, q_ref, k_ref, v_ref, log_ref, context_ref)
    attend_backward_body(grad_out, 0, saved, qkv_ref, out_ref, refs)


def second_attend_backward_kernel(
    rows_ref, cotangent_ref, mixed_ref, experts_ref, gate_sums_ref, gates_ref, routes_ref,
    router_ref, gain_ref, shift_ref, low_ref, q_ref, k_ref, v_ref, log_ref, context_ref,
    qkv_ref, out_ref, output_ref, new_ref, norm_ref, router_grad_ref, *refs,
):
    rows = rows_ref[...]
    output_ref[...] = (rows + mixed_ref[...].astype(single)).astype(bfloat)
    normal, unused = normal_of(rows)
    moe_low = (normal * gain_ref[3:4, :] + shift_ref[3:4, :]).astype(bfloat)
    gates = [gates_ref[:, k : k + 1] for k in range(2)]
    sums = [gate_sums_ref[:, k : k + 1] for k in range(2)]
    mean = gates[0] * sums[0] + gates[1] * sums[1]
    experts = lax.broadcasted_iota(jnp.int32, (rows.shape[0], EXPERTS), 1)
    grad_logits = 0.0
    for k in range(2):
        pick = routes_ref[:, k : k + 1] == experts
        grad_logits = grad_logits + jnp.where(pick, gates[k] * (sums[k] - mean), 0.0)
    grad_logits = grad_logits.astype(bfloat)
    router_grad_ref[...] = dot_first(grad_logits, moe_low)
    grad_normed = experts_ref[...].astype(single) + dot_rows(grad_logits, router_ref[...])
    grad_in, gain_part, shift_part = norm_back(grad_normed, rows, gain_ref[3:4, :])
    grad_out = cotangent_ref[...].astype(single) + grad_in
    new_ref[...] = grad_out
    norm_ref[0:1, :] = gain_part
    norm_ref[1:2, :] = shift_part
    norm_ref[2:3, :] = jnp.sum(grad_out, axis=0, keepdims=True)
    saved = (low_ref, q_ref, k_ref, v_ref, log_ref, context_ref)
    attend_backward_body(grad_out, 1, saved, qkv_ref, out_ref, refs)


def local_call(kernel, name, args, outs, limit=28):
    return pl.pallas_call(
        kernel,
        out_shape=[jax.ShapeDtypeStruct(shape, kind) for shape, kind in outs],
        in_specs=[VMEM_SPEC] * len(args),
        out_specs=[VMEM_SPEC] * len(outs),
        compiler_params=pltpu.CompilerParams(vmem_limit_bytes=limit * 2**20),
        name=name,
    )(*args)


def final_kernel(grad_ref, sum_ref, rows_ref, gain_ref, new_ref, norm_ref):
    grad_in, gain_part, shift_part = norm_back(
        sum_ref[...].astype(single), rows_ref[...].astype(single), gain_ref[0:1, :]
    )
    new_ref[...] = grad_ref[...] + grad_in
    norm_ref[0:1, :] = gain_part
    norm_ref[1:2, :] = shift_part


def per_device(
    images,
    routes,
    cotangent,
    qkv_weight,
    out_weight,
    qv_bias,
    out_bias,
    ln_gain,
    ln_bias,
    dense_in,
    dense_out,
    router,
    expert_in,
    expert_out,
):
    tokens, width = images.shape
    part = out_weight.shape[1]
    qkv = jnp.transpose(qkv_weight, (0, 2, 3, 1)).reshape(2, 3 * part, width)
    full, full_low = ((tokens, width), single), ((tokens, width), bfloat)
    head_rows = ((tokens, part), bfloat)
    attend_outs = [full_low, full_low, head_rows, head_rows, head_rows]
    attend_outs += [((tokens, part // HEAD), single), head_rows]
    partial, *saved_one = local_call(
        first_attend_kernel, "first_attend",
        (images, qkv, out_weight, qv_bias, ln_gain, ln_bias), attend_outs,
    )
    total = tensor_sum(partial, 1)
    section_one, partial, dense_low, slope, act = local_call(
        dense_forward_kernel, "dense_forward",
        (images, total, out_bias, ln_gain, ln_bias, dense_in, dense_out),
        [full, full_low, full_low, full, full_low],
    )
    total = tensor_sum(partial, 1)
    section_two, partial, *saved_two = local_call(
        second_attend_kernel, "second_attend",
        (section_one, total, qkv, out_weight, qv_bias, ln_gain, ln_bias),
        [full] + attend_outs,
    )
    total = tensor_sum(partial, 1)
    section_three, sent, gates, slots = moe_route(
        section_two, total, out_bias, cotangent, routes, router, ln_gain, ln_bias
    )
    arrived = moe_send(sent.reshape(2, EXPERTS, STRIDE, width), 3)
    answers, expert_in_grad, expert_out_grad = expert_ffn(
        arrived.reshape(2, SLOTS, width), expert_in, expert_out
    )
    returned = moe_return(answers.reshape(2, EXPERTS, STRIDE, width), 4)
    parts = combine(returned.reshape(SLOTS, width), slots, gates, cotangent)
    mixed, grad_experts, gate_sums = combine_sum(parts, 5)
    grad_outs = [full_low, ((3 * part, width), bfloat), ((part, width), bfloat), ((2, part), single)]
    output, grad, norm_three, router_grad, partial, qkv_upper, outw_upper, bias_upper = local_call(
        second_attend_backward_kernel, "second_attend_backward",
        (section_three, cotangent, mixed, grad_experts, gate_sums, gates, routes, router.T,
         ln_gain, ln_bias, *saved_two, qkv, out_weight),
        [full_low, full, ((3, width), single), ((EXPERTS, width), single)] + grad_outs,
        36,
    )
    total = tensor_sum(partial, 1)
    square = ((dense_in.shape[0], dense_in.shape[1]), bfloat)
    grad, partial, dense_in_grad, dense_out_grad, norm_two = local_call(
        dense_backward_kernel, "dense_backward",
        (grad, total, section_two, ln_gain, dense_low, slope, act, dense_in, dense_out),
        [full, full_low, square, square, ((2, width), single)],
    )
    total = tensor_sum(partial, 1)
    grad, norm_one, partial, qkv_lower, outw_lower, bias_lower = local_call(
        first_attend_backward_kernel, "first_attend_backward",
        (grad, total, section_one, ln_gain, *saved_one, qkv, out_weight),
        [full, ((3, width), single)] + grad_outs, 36,
    )
    total = tensor_sum(partial, 1)
    input_grad, norm_zero = local_call(
        final_kernel, "final", (grad, total, images, ln_gain), [full, ((2, width), single)]
    )
    arrays = [qkv_lower, qkv_upper, outw_lower, outw_upper, dense_in_grad, dense_out_grad]
    small = jnp.concatenate(
        [
            router_grad,
            norm_zero[0:1], norm_one[0:1], norm_two[0:1], norm_three[0:1],
            norm_zero[1:2], norm_one[1:2], norm_two[1:2], norm_three[1:2],
            norm_one[2:3], norm_three[2:3],
            jnp.stack([bias_lower, bias_upper]).reshape(1, -1),
            jnp.zeros((5, width), single),
        ]
    )
    summed = grad_sum(arrays, small.astype(bfloat), 2)
    big = [a.astype(single) for a in summed]
    small = big[6]
    qkv_weight_grad = jnp.transpose(
        jnp.stack([big[0], big[1]]).reshape(2, 3, part, width), (0, 3, 1, 2)
    )
    out_weight_grad = jnp.stack([big[2], big[3]])
    dense_in_grad, dense_out_grad = big[4], big[5]
    router_grad = small[:32].T
    ln_gain_grad, ln_bias_grad, out_bias_grad = small[32:36], small[36:40], small[40:42]
    qv_bias_grad = small[42].reshape(2, 2, part)
    return (
        output,
        input_grad,
        qkv_weight_grad,
        out_weight_grad,
        qv_bias_grad,
        out_bias_grad,
        ln_gain_grad,
        ln_bias_grad,
        dense_in_grad,
        dense_out_grad,
        router_grad,
        expert_in_grad,
        expert_out_grad,
    )


def solution(mesh):
    in_specs = (
        P("dp", None),
        P("dp", None),
        P("dp", None),
        P(None, None, None, "tensor"),
        P(None, "tensor", None),
        P(None, None, "tensor"),
        P(),
        P(),
        P(),
        P(None, "tensor"),
        P("tensor", None),
        P(),
        P("dp", None, "tensor"),
        P("dp", "tensor", None),
    )
    out_specs = (
        P("dp", None),
        P("dp", None),
        P(None, None, None, "tensor"),
        P(None, "tensor", None),
        P(None, None, "tensor"),
        P(),
        P(),
        P(),
        P(None, "tensor"),
        P("tensor", None),
        P(),
        P("dp", None, "tensor"),
        P("dp", "tensor", None),
    )
    return jax.shard_map(
        per_device, mesh=mesh, in_specs=in_specs, out_specs=out_specs, check_vma=False
    )
```

```python
import functools

import jax
import jax.numpy as jnp
from jax import lax
from jax.experimental import pallas as pl
from jax.experimental.pallas import tpu as pltpu
from jax.sharding import PartitionSpec as P

HEAD = 64
SEQ = 197


epsilon = 1e-06
bfloat = jnp.bfloat16
single = jnp.float32


MESH = pl.DeviceIdType.MESH


BIG = 3072
SMALL = 48
EXPERTS = 32
STRIDE = 40
SLOTS = EXPERTS * STRIDE


def dot_rows(a, b):
    return lax.dot_general(a, b, (((1,), (0,)), ((), ())), preferred_element_type=single)


def dot_last(a, b):
    return lax.dot_general(a, b, (((1,), (1,)), ((), ())), preferred_element_type=single)


def dot_first(a, b):
    return lax.dot_general(a, b, (((0,), (0,)), ((), ())), preferred_element_type=single)


VMEM_SPEC = pl.BlockSpec(memory_space=pltpu.VMEM)


def dp_peer(k):
    dp = lax.axis_index("dp")
    plane = lax.rem(dp // 16 + k // 16, 2)
    x = lax.rem(lax.rem(dp // 4, 4) + lax.rem(k // 4, 4), 4)
    y = lax.rem(lax.rem(dp, 4) + lax.rem(k, 4), 4)
    return plane * 16 + x * 4 + y


def dp_source(k):
    dp = lax.axis_index("dp")
    plane = lax.rem(dp // 16 + k // 16, 2)
    x = lax.rem(lax.rem(dp // 4, 4) + 4 - lax.rem(k // 4, 4), 4)
    y = lax.rem(lax.rem(dp, 4) + 4 - lax.rem(k, 4), 4)
    return plane * 16 + x * 4 + y


def order_of(i):
    return lax.rem(i * 11, EXPERTS)


def meet_all(sibling):
    barrier = pltpu.get_barrier_semaphore()

    def greet(k, carry):
        pl.semaphore_signal(barrier, inc=1, device_id={"dp": dp_peer(k)}, device_id_type=MESH)
        return carry

    lax.fori_loop(1, EXPERTS, greet, 0)
    pl.semaphore_signal(barrier, inc=1, device_id=sibling, device_id_type=MESH)
    pl.semaphore_wait(barrier, EXPERTS)


def moe_send_kernel(in_ref, out_ref, local_sem, send_sem, recv_sem, pass_sem, land_sem):
    t = lax.axis_index("tensor")
    dp = lax.axis_index("dp")
    core = lax.rem(t, 2)
    sibling = {"tensor": t + 1 - 2 * core}
    own = pltpu.make_async_copy(in_ref.at[core, dp], out_ref.at[core, dp], local_sem)
    own.start()
    meet_all(sibling)

    def across(k):
        peer = dp_peer(k)
        return pltpu.make_async_remote_copy(
            src_ref=in_ref.at[core, peer],
            dst_ref=out_ref.at[core, dp],
            send_sem=send_sem.at[k],
            recv_sem=recv_sem.at[k],
            device_id={"dp": peer},
            device_id_type=MESH,
        )

    def beside(k):
        block = out_ref.at[core, dp_source(k)]
        return pltpu.make_async_remote_copy(
            src_ref=block,
            dst_ref=block,
            send_sem=pass_sem.at[k],
            recv_sem=land_sem.at[k],
            device_id=sibling,
            device_id_type=MESH,
        )

    def start(i, carry):
        across(order_of(i)).start()
        return carry

    def forward(i, carry):
        k = order_of(i)
        across(k).wait_recv()
        beside(k).start()
        return carry

    def land(k, carry):
        beside(k).wait_recv()
        return carry

    def drain(k, carry):
        across(k).wait_send()
        return carry

    def drain_pass(k, carry):
        beside(k).wait_send()
        return carry

    lax.fori_loop(1, EXPERTS, start, 0)
    own.wait()
    beside(0).start()
    lax.fori_loop(1, EXPERTS, forward, 0)
    lax.fori_loop(0, EXPERTS, land, 0)
    lax.fori_loop(1, EXPERTS, drain, 0)
    lax.fori_loop(0, EXPERTS, drain_pass, 0)


def moe_send(rows, collective_id):
    every = pltpu.SemaphoreType.DMA((EXPERTS,))
    hbm = pl.BlockSpec(memory_space=pl.ANY)
    return pl.pallas_call(
        moe_send_kernel,
        out_shape=jax.ShapeDtypeStruct(rows.shape, bfloat),
        in_specs=[hbm],
        out_specs=hbm,
        scratch_shapes=[pltpu.SemaphoreType.DMA, every, every, every, every],
        compiler_params=pltpu.CompilerParams(
            collective_id=collective_id, has_side_effects=True, vmem_limit_bytes=58 * 2**20
        ),
        name="moe_send",
    )(rows)


def expert_kernel(in_ref, ein_ref, eout_ref, out_ref, ein_grad_ref, eout_grad_ref, act_ref, grad_ref):
    half = in_ref.shape[2] // 2
    width = 2 * half
    block = SLOTS // 4

    def both(at, first):
        parts = [in_ref[h, at, first : first + half] for h in range(2)]
        return jnp.concatenate(parts, axis=1)

    def forward(i, carry):
        at = pl.ds(pl.multiple_of(i * block, 16), block)
        rows = both(at, 0)
        rows_grad = both(at, half)
        pre = dot_rows(rows, ein_ref[0])
        grad_act = dot_last(rows_grad, eout_ref[0])
        tail = 0.5 * (1.0 + lax.erf(pre * (0.5**0.5)))
        act = (pre * tail).astype(bfloat)
        slope = tail + pre * (jnp.exp(-0.5 * pre * pre) * 0.3989422804014327)
        grad_pre = (grad_act * slope).astype(bfloat)
        act_ref[at, :] = act
        grad_ref[at, :] = grad_pre
        out = dot_rows(act, eout_ref[0]).astype(bfloat)
        back = dot_last(grad_pre, ein_ref[0]).astype(bfloat)
        for h in range(2):
            out_ref[h, at, :half] = out[:, h * half : (h + 1) * half]
            out_ref[h, at, half:] = back[:, h * half : (h + 1) * half]
        return carry

    lax.fori_loop(0, SLOTS // block, forward, 0)
    for h in range(2):
        eout_grad_ref[0, :, h * half : (h + 1) * half] = dot_first(act_ref[...], in_ref[h, :, half:])
        ein_grad_ref[0, h * half : (h + 1) * half, :] = dot_first(in_ref[h, :, :half], grad_ref[...])


def expert_ffn(rows, expert_in, expert_out):
    width = rows.shape[2]
    weight = jax.ShapeDtypeStruct(expert_in.shape, single)
    return pl.pallas_call(
        expert_kernel,
        out_shape=[jax.ShapeDtypeStruct(rows.shape, bfloat), weight, weight],
        in_specs=[VMEM_SPEC] * 3,
        out_specs=[VMEM_SPEC] * 3,
        scratch_shapes=[pltpu.VMEM((SLOTS, width), bfloat)] * 2,
        compiler_params=pltpu.CompilerParams(vmem_limit_bytes=58 * 2**20),
        name="expert_ffn",
    )(rows, expert_in, expert_out)


def moe_return_kernel(in_ref, out_ref, got_ref, sum_ref, local_sem, send_sem, recv_sem, pass_sem, land_sem):
    t = lax.axis_index("tensor")
    dp = lax.axis_index("dp")
    core = lax.rem(t, 2)
    sibling = {"tensor": t + 1 - 2 * core}
    meet_all(sibling)

    def beside(k):
        peer = dp_peer(k)
        return pltpu.make_async_remote_copy(
            src_ref=in_ref.at[1 - core, peer],
            dst_ref=got_ref.at[peer],
            send_sem=pass_sem.at[k],
            recv_sem=land_sem.at[k],
            device_id=sibling,
            device_id_type=MESH,
        )

    def across(k):
        peer = dp_peer(k)
        return pltpu.make_async_remote_copy(
            src_ref=sum_ref.at[peer],
            dst_ref=out_ref.at[dp],
            send_sem=send_sem.at[k],
            recv_sem=recv_sem.at[k],
            device_id={"dp": peer},
            device_id_type=MESH,
        )

    def start(i, carry):
        beside(order_of(i)).start()
        return carry

    def combine(i, carry):
        k = order_of(i)
        peer = dp_peer(k)
        beside(k).wait_recv()
        total = in_ref[core, peer].astype(single) + got_ref[peer].astype(single)
        sum_ref[peer] = total.astype(bfloat)
        return k

    def onward(i, carry):
        k = combine(i, carry)
        across(k).start()
        return carry

    def arrive(k, carry):
        across(k).wait_recv()
        return carry

    def drain(k, carry):
        across(k).wait_send()
        return carry

    def drain_pass(k, carry):
        beside(k).wait_send()
        return carry

    lax.fori_loop(1, EXPERTS + 1, start, 0)
    lax.fori_loop(1, EXPERTS, onward, 0)
    combine(EXPERTS, 0)
    own = pltpu.make_async_copy(sum_ref.at[dp], out_ref.at[dp], local_sem)
    own.start()
    lax.fori_loop(1, EXPERTS, arrive, 0)
    lax.fori_loop(1, EXPERTS, drain, 0)
    lax.fori_loop(0, EXPERTS, drain_pass, 0)
    own.wait()


def moe_return(rows, collective_id):
    every = pltpu.SemaphoreType.DMA((EXPERTS,))
    block = pltpu.VMEM(rows.shape[1:], bfloat)
    return pl.pallas_call(
        moe_return_kernel,
        out_shape=jax.ShapeDtypeStruct(rows.shape[1:], bfloat),
        in_specs=[VMEM_SPEC],
        out_specs=pl.BlockSpec(memory_space=pl.ANY),
        scratch_shapes=[block, block, pltpu.SemaphoreType.DMA, every, every, every, every],
        compiler_params=pltpu.CompilerParams(
            collective_id=collective_id, has_side_effects=True, vmem_limit_bytes=58 * 2**20
        ),
        name="moe_return",
    )(rows)


def combine_kernel(back_ref, slots_ref, gates_ref, cotangent_ref, out_ref):
    tokens = slots_ref.shape[0]
    half = back_ref.shape[1] // 2
    core = lax.rem(lax.axis_index("tensor"), 2)
    own = cotangent_ref[:, pl.ds(pl.multiple_of(core * half, 128), half)].astype(single)
    ids = lax.broadcasted_iota(jnp.int32, (tokens, SLOTS), 1)
    hits = [jnp.where(ids == slots_ref[:, k : k + 1], 1.0, 0.0) for k in range(2)]
    picked = [dot_rows(hit.astype(bfloat), back_ref[:, :half]) for hit in hits]
    mixed = gates_ref[:, 0:1] * picked[0] + gates_ref[:, 1:2] * picked[1]
    gate = [jnp.sum(p * own, axis=1, keepdims=True) for p in picked]
    normed = dot_rows((hits[0] + hits[1]).astype(bfloat), back_ref[:, half:])
    for j in range(half // 128):
        out_ref[j] = mixed[:, j * 128 : (j + 1) * 128].astype(bfloat)
        out_ref[half // 128 + j] = normed[:, j * 128 : (j + 1) * 128].astype(bfloat)
    lane = lax.broadcasted_iota(jnp.int32, (tokens, 128), 1)
    spread = jnp.where(lane == 0, gate[0], jnp.where(lane == 1, gate[1], 0.0))
    out_ref[2 * (half // 128)] = spread.astype(bfloat)


def combine(back, slots, gates, cotangent):
    tokens = slots.shape[0]
    return pl.pallas_call(
        combine_kernel,
        out_shape=jax.ShapeDtypeStruct((7, tokens, 128), bfloat),
        in_specs=[VMEM_SPEC] * 4,
        out_specs=VMEM_SPEC,
        compiler_params=pltpu.CompilerParams(vmem_limit_bytes=58 * 2**20),
        name="combine",
    )(back, slots, gates, cotangent)


def combine_sum_kernel(p_ref, mixed_ref, normed_ref, gates_ref, got_two, sum_two, got_three, sems):
    t = lax.axis_index("tensor")
    core = lax.rem(t, 2)
    sibling = {"tensor": t + 1 - 2 * core}
    opposite = {"tensor": lax.rem(t + 2, 4)}
    barrier = pltpu.get_barrier_semaphore()
    for peer in (sibling, opposite):
        pl.semaphore_signal(barrier, inc=1, device_id=peer, device_id_type=MESH)
    pl.semaphore_wait(barrier, 2)

    def copy(source, target, step, j, peer):
        return pltpu.make_async_remote_copy(
            src_ref=source,
            dst_ref=target,
            send_sem=sems.at[0, step, j],
            recv_sem=sems.at[1, step, j],
            device_id=peer,
            device_id_type=MESH,
        )

    count = p_ref.shape[0]
    order = [6, 0, 1, 2, 3, 4, 5]
    second = [copy(p_ref.at[j], got_two.at[j], 0, j, opposite) for j in range(count)]
    third = [copy(sum_two.at[j], got_three.at[j], 1, j, sibling) for j in range(count)]
    for j in order:
        second[j].start()

    def place(j, which):
        ref = mixed_ref if j < 3 else normed_ref
        return ref, pl.ds(pl.multiple_of((which * 3 + j % 3) * 128, 128), 128)

    for j in order:
        second[j].wait_recv()
        whole = (p_ref[j].astype(single) + got_two[j].astype(single)).astype(bfloat)
        sum_two[j] = whole
        third[j].start()
        if j < 6:
            ref, at = place(j, core)
            ref[:, at] = whole
    for j in order:
        third[j].wait_recv()
        if j < 6:
            ref, at = place(j, 1 - core)
            ref[:, at] = got_three[j]
        else:
            gates_ref[...] = sum_two[j].astype(single) + got_three[j].astype(single)
    for j in range(count):
        second[j].wait_send()
        third[j].wait_send()


def combine_sum(parts, collective_id):
    count, tokens, lanes = parts.shape
    block = pltpu.VMEM(parts.shape, bfloat)
    whole = jax.ShapeDtypeStruct((tokens, 768), bfloat)
    return pl.pallas_call(
        combine_sum_kernel,
        out_shape=[whole, whole, jax.ShapeDtypeStruct((tokens, lanes), single)],
        in_specs=[VMEM_SPEC],
        out_specs=[VMEM_SPEC] * 3,
        scratch_shapes=[block] * 3 + [pltpu.SemaphoreType.DMA((2, 2, count))],
        compiler_params=pltpu.CompilerParams(
            collective_id=collective_id, has_side_effects=True, vmem_limit_bytes=58 * 2**20
        ),
        name="combine_sum",
    )(parts)


def normal_of(rows):
    average = jnp.mean(rows, axis=-1, keepdims=True)
    centered = rows - average
    variance = jnp.mean(centered * centered, axis=-1, keepdims=True)
    inverse = lax.rsqrt(variance + epsilon)
    return centered * inverse, inverse


def norm_back(grad_normed, rows, gain_row):
    normal, inverse = normal_of(rows)
    scaled = grad_normed * gain_row
    mean_one = jnp.mean(scaled, axis=-1, keepdims=True)
    mean_two = jnp.mean(scaled * normal, axis=-1, keepdims=True)
    grad_in = inverse * (scaled - mean_one - normal * mean_two)
    gain_part = jnp.sum(grad_normed * normal, axis=0, keepdims=True)
    return grad_in, gain_part, jnp.sum(grad_normed, axis=0, keepdims=True)


def same_image(tokens):
    first = lax.broadcasted_iota(jnp.int32, (tokens, tokens), 0) // SEQ
    second = lax.broadcasted_iota(jnp.int32, (tokens, tokens), 1) // SEQ
    return first == second


class Refs:
    def __init__(self, names, refs):
        for name, ref in zip(names, refs):
            setattr(self, name, ref)


def big_call(kernel, name, ins, outs, scratch, collective_id=None, limit=58):
    names = list(ins) + list(outs) + list(scratch)
    hbm = pl.BlockSpec(memory_space=pl.ANY)

    def body(*refs):
        kernel(Refs(names, refs))

    found = pl.pallas_call(
        body,
        out_shape=[jax.ShapeDtypeStruct(shape, kind) for shape, kind, unused in outs.values()],
        in_specs=[hbm if place == "hbm" else VMEM_SPEC for unused, place in ins.values()],
        out_specs=[hbm if place == "hbm" else VMEM_SPEC for _, _, place in outs.values()],
        scratch_shapes=list(scratch.values()),
        compiler_params=pltpu.CompilerParams(
            collective_id=collective_id, has_side_effects=True, vmem_limit_bytes=limit * 2**20
        ),
        name=name,
    )(*[array for array, unused in ins.values()])
    return Refs(list(outs), found)


def tensor_place():
    t = lax.axis_index("tensor")
    core = lax.rem(t, 2)
    return core, {"tensor": t + 1 - 2 * core}, {"tensor": lax.rem(t + 2, 4)}


def remote(source, target, sends, recvs, index, peer):
    return pltpu.make_async_remote_copy(
        src_ref=source,
        dst_ref=target,
        send_sem=sends.at[index],
        recv_sem=recvs.at[index],
        device_id=peer,
        device_id_type=MESH,
    )


LANES = 128
THIRDS = 3


def sum_scratch(tokens, count):
    block = pltpu.VMEM((count, THIRDS, tokens, LANES), bfloat)
    names = ["give", "got_one", "sum_one", "got_two", "sum_two", "got_three"]
    found = {"t_" + name: block for name in names}
    found["t_own"] = pltpu.VMEM((tokens, THIRDS * LANES), single)
    found["t_sends"] = pltpu.SemaphoreType.DMA((count * 9,))
    found["t_recvs"] = pltpu.SemaphoreType.DMA((count * 9,))
    return found


class TensorSum:
    def __init__(self, r, number, total_ref):
        core, sibling, opposite = tensor_place()
        self.core, self.r, self.n, self.total = core, r, number, total_ref

        def copies(source, target, step, peer):
            return [
                remote(source.at[number, j], target.at[number, j], r.t_sends, r.t_recvs, number * 9 + step * 3 + j, peer)
                for j in range(THIRDS)
            ]

        self.first = copies(r.t_give, r.t_got_one, 0, sibling)
        self.second = copies(r.t_sum_one, r.t_got_two, 1, opposite)
        self.third = copies(r.t_sum_two, r.t_got_three, 2, sibling)

    def columns(self, which, j=0, count=1):
        return pl.ds(pl.multiple_of((which * THIRDS + j) * LANES, LANES), count * LANES)

    def start(self, partial):
        r, n = self.r, self.n
        other = partial(self.columns(1 - self.core, 0, THIRDS)).astype(bfloat)
        for j in range(THIRDS):
            r.t_give[n, j] = other[:, j * LANES : (j + 1) * LANES]
            self.first[j].start()
        r.t_own[...] = partial(self.columns(self.core, 0, THIRDS))
        for j in range(THIRDS):
            self.first[j].wait_recv()
            own = r.t_own[:, j * LANES : (j + 1) * LANES]
            r.t_sum_one[n, j] = (own + r.t_got_one[n, j].astype(single)).astype(bfloat)
            self.second[j].start()

    def finish(self):
        r, n = self.r, self.n
        for j in range(THIRDS):
            self.second[j].wait_recv()
            whole = (r.t_sum_one[n, j].astype(single) + r.t_got_two[n, j].astype(single)).astype(bfloat)
            r.t_sum_two[n, j] = whole
            self.third[j].start()
            self.total[:, self.columns(self.core, j)] = whole
        for j in range(THIRDS):
            self.third[j].wait_recv()
            self.total[:, self.columns(1 - self.core, j)] = r.t_got_three[n, j]

    def drain(self):
        for copy in self.first + self.second + self.third:
            copy.wait_send()


class Moves:
    def __init__(self, sems):
        self.sems, self.count = sems, 0

    def start(self, source, target):
        copy = pltpu.make_async_copy(source, target, self.sems.at[self.count])
        self.count += 1
        copy.start()
        return copy


def greet(peers):
    barrier = pltpu.get_barrier_semaphore()
    for peer in peers:
        pl.semaphore_signal(barrier, inc=1, device_id=peer, device_id_type=MESH)


def attend(r, rows, layer):
    width = r.out.shape[1]
    norm = 2 * layer
    normal, unused = normal_of(rows)
    low = (normal * r.gain[norm : norm + 1, :] + r.shift[norm : norm + 1, :]).astype(bfloat)
    r.low[layer] = low
    bias = r.qv_bias[layer]
    q = (dot_last(low, r.qkv[layer, :width, :]) + bias[0:1, :]).astype(bfloat)
    k = dot_last(low, r.qkv[layer, width : 2 * width, :]).astype(bfloat)
    v = (dot_last(low, r.qkv[layer, 2 * width :, :]) + bias[1:2, :]).astype(bfloat)
    r.qkvc[layer, 0], r.qkvc[layer, 1], r.qkvc[layer, 2] = q, k, v
    same = same_image(rows.shape[0])
    contexts = []
    for h in range(width // HEAD):
        at = slice(h * HEAD, (h + 1) * HEAD)
        scores = jnp.where(same, dot_last(q[:, at], k[:, at]) * HEAD ** (-0.5), -1e30)
        largest = jnp.max(scores, axis=-1, keepdims=True)
        exponent = jnp.exp(scores - largest)
        totals = jnp.sum(exponent, axis=-1, keepdims=True)
        r.log[layer, :, h : h + 1] = largest + jnp.log(totals)
        contexts.append(dot_rows((exponent / totals).astype(bfloat), v[:, at]))
    r.qkvc[layer, 3] = jnp.concatenate(contexts, axis=1).astype(bfloat)


def forward_kernel(r):
    core, sibling, opposite = tensor_place()
    greet([sibling, opposite])
    moves = Moves(r.moves)
    loads = [moves.start(r.dense_in_h, r.dense_in), moves.start(r.dense_out_h, r.dense_out)]
    loads += [moves.start(r.cotangent_h, r.cotangent)]
    stores = []
    sums = [TensorSum(r, n, r.total) for n in range(3)]

    def save(source, target):
        stores.append(moves.start(source, target))

    def out_part(layer):
        return lambda at: dot_rows(r.qkvc[layer, 3], r.out[layer, :, at])

    attend(r, r.images[...].astype(single), 0)
    pl.semaphore_wait(pltpu.get_barrier_semaphore(), 2)
    sums[0].start(out_part(0))
    sums[0].finish()

    rows = r.images[...].astype(single) + r.total[...].astype(single) + r.out_bias[0:1, :]
    r.section[0] = rows
    save(r.section.at[0], r.section_one)
    normal, unused = normal_of(rows)
    low = (normal * r.gain[1:2, :] + r.shift[1:2, :]).astype(bfloat)
    r.dense_low[...] = low
    save(r.dense_low, r.dense_low_h)
    for load in loads:
        load.wait()
    pre = dot_rows(low, r.dense_in[...])
    tail = 0.5 * (1.0 + lax.erf(pre * (0.5**0.5)))
    r.slope[...] = tail + pre * (jnp.exp(-0.5 * pre * pre) * 0.3989422804014327)
    save(r.slope, r.slope_h)
    r.act[...] = (pre * tail).astype(bfloat)
    save(r.act, r.act_h)
    sums[1].start(lambda at: dot_rows(r.act[...], r.dense_out[:, at]))
    sums[1].finish()

    rows = r.section[0] + r.total[...].astype(single)
    r.section[1] = rows
    save(r.section.at[1], r.section_two)
    attend(r, rows, 1)
    save(r.low, r.low_h)
    save(r.qkvc, r.qkvc_h)
    save(r.log, r.log_h)
    sums[2].start(out_part(1))
    sums[2].finish()

    rows = r.section[1] + r.total[...].astype(single) + r.out_bias[1:2, :]
    r.section[2] = rows
    save(r.section.at[2], r.section_three)
    moe_route_body(r, rows, save)
    for one in sums:
        one.drain()
    for store in stores:
        store.wait()


def moe_route_body(r, rows, save):
    tokens, width = rows.shape
    half = width // 2
    normal, unused = normal_of(rows)
    r.moe_low[...] = (normal * r.gain[3:4, :] + r.shift[3:4, :]).astype(bfloat)
    logits = dot_last(r.moe_low[...], r.router[...])
    experts = lax.broadcasted_iota(jnp.int32, (tokens, EXPERTS), 1)
    picks = [r.routes[:, k : k + 1] == experts for k in range(2)]
    chosen = [jnp.sum(jnp.where(pick, logits, 0.0), axis=1, keepdims=True) for pick in picks]
    largest = jnp.maximum(chosen[0], chosen[1])
    powers = [jnp.exp(c - largest) for c in chosen]
    total = powers[0] + powers[1]
    gates = [power / total for power in powers]
    r.gates[:, 0:1] = gates[0]
    r.gates[:, 1:2] = gates[1]
    cotangent = r.cotangent[...].astype(single)
    for k in range(2):
        r.scaled[k] = (gates[k] * cotangent).astype(bfloat)

    before = lax.broadcasted_iota(jnp.int32, (tokens, tokens), 0)
    after = lax.broadcasted_iota(jnp.int32, (tokens, tokens), 1)
    either = [jnp.where(pick, 1.0, 0.0) for pick in picks]
    lower = jnp.where(after < before, 1.0, 0.0).astype(bfloat)
    running = dot_rows(lower, (either[0] + either[1]).astype(bfloat))
    for k in range(2):
        rank = jnp.sum(running * either[k], axis=1, keepdims=True).astype(jnp.int32)
        r.slots[:, k : k + 1] = r.routes[:, k : k + 1] * STRIDE + rank

    experts_row = lax.broadcasted_iota(jnp.int32, (EXPERTS, tokens), 0)
    either_row = [jnp.where(r.routes_row[k : k + 1, :] == experts_row, 1.0, 0.0) for k in range(2)]
    upper = jnp.where(before < after, 1.0, 0.0).astype(bfloat)
    running_row = dot_rows((either_row[0] + either_row[1]).astype(bfloat), upper)
    slots_row = []
    for k in range(2):
        rank = jnp.sum(running_row * either_row[k], axis=0, keepdims=True).astype(jnp.int32)
        slots_row.append(r.routes_row[k : k + 1, :] * STRIDE + rank)

    block = SLOTS // 4
    for i in range(4):
        ids = lax.broadcasted_iota(jnp.int32, (block, tokens), 0) + i * block
        hits = [jnp.where(ids == slots_row[k], 1.0, 0.0) for k in range(2)]
        moved = dot_rows((hits[0] + hits[1]).astype(bfloat), r.moe_low[...]).astype(bfloat)
        moved_grad = (
            dot_rows(hits[0].astype(bfloat), r.scaled[0]) + dot_rows(hits[1].astype(bfloat), r.scaled[1])
        ).astype(bfloat)
        at = slice(i * block, (i + 1) * block)
        for h in range(2):
            r.routed[h, at, :half] = moved[:, h * half : (h + 1) * half]
            r.routed[h, at, half:] = moved_grad[:, h * half : (h + 1) * half]
            save(r.routed.at[h, pl.ds(i * block, block), :], r.sent.at[h, pl.ds(i * block, block), :])


def attend_back(r, layer, grad_out, base):
    width = r.out.shape[1]
    grad_low = grad_out.astype(bfloat)
    q, k, v = r.qkvc[layer, 0], r.qkvc[layer, 1], r.qkvc[layer, 2]
    put_grad(r, base + 3 * width, dot_first(r.qkvc[layer, 3], grad_low))
    grad_context = dot_last(grad_low, r.out[layer]).astype(bfloat)
    same = same_image(q.shape[0])
    grads = [[], [], []]
    for h in range(width // HEAD):
        at = slice(h * HEAD, (h + 1) * HEAD)
        scores = jnp.where(same, dot_last(q[:, at], k[:, at]) * HEAD ** (-0.5), -1e30)
        probs = jnp.exp(scores - r.log[layer, :, h : h + 1])
        grad_probs = dot_last(grad_context[:, at], v[:, at])
        row_total = jnp.sum(probs * grad_probs, axis=-1, keepdims=True)
        grad_scores = (probs * (grad_probs - row_total)).astype(bfloat)
        grads[0].append(dot_rows(grad_scores, k[:, at]) * HEAD ** (-0.5))
        grads[1].append(dot_first(grad_scores, q[:, at]) * HEAD ** (-0.5))
        grads[2].append(dot_first(probs.astype(bfloat), grad_context[:, at]))
    low = r.low[layer]
    for part in range(3):
        grad = jnp.concatenate(grads[part], axis=1).astype(bfloat)
        r.grad_qkv[part] = grad
        put_grad(r, base + part * width, dot_first(grad, low))
        if part != 1:
            row = 42 + 2 * layer + part // 2
            r.small_wide[row : row + 1, :width] = jnp.sum(grad.astype(single), axis=0, keepdims=True)


def attend_back_part(r, layer):
    width = r.out.shape[1]

    def partial(at):
        total = None
        for part in range(3):
            term = dot_rows(r.grad_qkv[part], r.qkv[layer, part * width : (part + 1) * width, at])
            total = term if total is None else total + term
        return total

    return partial


def put_grad(r, row, value):
    low = value.astype(bfloat)
    half = low.shape[1] // 2
    for h in range(2):
        r.given[h, row : row + low.shape[0], :] = low[:, h * half : (h + 1) * half]


def add_blocks(target, row, sources, rows):
    def body(i, carry):
        total = None
        for ref, start in sources:
            value = ref[pl.ds(pl.multiple_of(start + i * 16, 16), 16), :].astype(single)
            total = value if total is None else total + value
        target[pl.ds(pl.multiple_of(row + i * 16, 16), 16), :] = total.astype(bfloat)
        return carry

    lax.fori_loop(0, rows // 16, body, 0)


GROUP_COPIES = 38


def group_scratch(tag, rows, width):
    part, piece = rows // 4, rows // 16
    found = {}
    for name in ("near", "left", "right", "onward", "sum"):
        found[f"{tag}_{name}"] = pltpu.VMEM((2, part, width), bfloat)
    found[f"{tag}_got"] = pltpu.VMEM((2, 3, piece, width), bfloat)
    found[f"{tag}_piece"] = pltpu.VMEM((2, piece, width), bfloat)
    found[f"{tag}_pair"] = pltpu.VMEM((2, piece, width), bfloat)
    found[f"{tag}_sends"] = pltpu.SemaphoreType.DMA((GROUP_COPIES,))
    found[f"{tag}_recvs"] = pltpu.SemaphoreType.DMA((GROUP_COPIES,))
    return found


class Grid:
    def __init__(self):
        dp = lax.axis_index("dp")
        self.plane, self.x, self.y = dp // 16, lax.rem(dp // 4, 4), lax.rem(dp, 4)
        self.across = self.at(1 - self.plane, self.x, self.y)

    def at(self, plane, x, y):
        return {"dp": plane * 16 + x * 4 + y}

    def along_x(self, step):
        return self.at(self.plane, lax.rem(self.x + step, 4), self.y)

    def along_y(self, step):
        return self.at(self.plane, self.x, lax.rem(self.y + step, 4))


class GroupSum:
    def __init__(self, r, tag, base, rows, grid):
        self.r, self.base, self.part, self.piece, self.grid = r, base, rows // 4, rows // 16, grid
        names = ("near", "left", "right", "onward", "sum", "got", "piece", "pair", "sends", "recvs")
        for name in names:
            setattr(self, "b_" + name, getattr(r, f"{tag}_{name}"))
        self.used = []
        self.place = [grid.x, grid.y]
        self.along = [grid.along_x, grid.along_y]

    def send(self, source, target, peer):
        copy = remote(source, target, self.b_sends, self.b_recvs, len(self.used), peer)
        self.used.append(copy)
        copy.start()
        return copy

    def rows(self, ref, row, count):
        return ref.at[pl.ds(pl.multiple_of(row, 16), count), :]

    def row(self, h, step):
        return self.base + lax.rem(self.place[h] + step, 4) * self.part

    def both(self, ref):
        return [ref.at[h] for h in range(2)]

    def step_one(self):
        half = self.part // 2
        self.copies = []
        for h in range(2):
            s, near, left, right = (
                ref.at[h] for ref in (self.r.given, self.b_near, self.b_left, self.b_right)
            )
            fwd, back = self.along[h](1), self.along[h](3)
            self.copies.append([
                self.send(self.rows(s, self.row(h, 2), half), self.rows(near, 0, half), fwd),
                self.send(self.rows(s, self.row(h, 2) + half, half), self.rows(near, half, half), back),
                self.send(self.rows(s, self.row(h, 1) + half, half), self.rows(left, half, half), fwd),
                self.send(self.rows(s, self.row(h, 3), half), self.rows(right, 0, half), back),
            ])

    def step_two(self):
        half = self.part // 2
        for h in range(2):
            s, near, onward, left, right = (
                ref.at[h]
                for ref in (self.r.given, self.b_near, self.b_onward, self.b_left, self.b_right)
            )
            self.copies[h][0].wait_recv()
            add_blocks(onward, 0, [(s, self.row(h, 1)), (near, 0)], half)
            self.copies[h].append(
                self.send(self.rows(onward, 0, half), self.rows(left, 0, half), self.along[h](1))
            )
            self.copies[h][1].wait_recv()
            add_blocks(onward, half, [(s, self.row(h, 3) + half), (near, half)], half)
            self.copies[h].append(
                self.send(self.rows(onward, half, half), self.rows(right, half, half), self.along[h](3))
            )

    def step_three(self):
        self.pieces = []
        for h in range(2):
            for copy in self.copies[h][2:]:
                copy.wait_recv()
            s, left, right, total = (
                ref.at[h] for ref in (self.r.given, self.b_left, self.b_right, self.b_sum)
            )
            add_blocks(total, 0, [(s, self.row(h, 0)), (left, 0), (right, 0)], self.part)
            other = 1 - h
            for k in (2, 1, 3):
                row = lax.rem(self.place[other] + k, 4) * self.piece
                self.pieces.append(
                    self.send(self.rows(total, row, self.piece), self.b_got.at[h, k - 1], self.along[other](k))
                )

    def step_four(self):
        self.pairs = []
        for h in range(2):
            for copy in self.pieces[3 * h : 3 * h + 3]:
                copy.wait_recv()
            row = self.place[1 - h] * self.piece
            sources = [(self.b_sum.at[h], row)] + [(self.b_got.at[h, k], 0) for k in range(3)]
            add_blocks(self.b_piece.at[h], 0, sources, self.piece)
            self.pairs.append(self.send(self.b_piece.at[h], self.b_pair.at[h], self.grid.across))

    def own(self, h):
        return self.row(h, 0) + self.place[1 - h] * self.piece

    def step_five(self):
        self.spread = []
        for h in range(2):
            self.pairs[h].wait_recv()
            result = self.r.result.at[h]
            add_blocks(result, self.own(h), [(self.b_piece.at[h], 0), (self.b_pair.at[h], 0)], self.piece)
            mine = self.rows(result, self.own(h), self.piece)
            for k in (2, 1, 3):
                self.spread.append(self.send(mine, mine, self.along[1 - h](k)))

    def step_six(self):
        half = self.part // 2
        self.copies = []
        for h in range(2):
            for copy in self.spread[3 * h : 3 * h + 3]:
                copy.wait_recv()
            result = self.r.result.at[h]
            first = self.rows(result, self.row(h, 0), half)
            second = self.rows(result, self.row(h, 0) + half, half)
            fwd, back = self.along[h](1), self.along[h](3)
            self.copies.append([
                self.send(first, first, fwd),
                self.send(second, second, back),
                self.send(second, second, fwd),
                self.send(first, first, back),
            ])

    def step_seven(self):
        half = self.part // 2
        for h in range(2):
            result = self.r.result.at[h]
            self.copies[h][0].wait_recv()
            from_left = self.rows(result, self.row(h, 3), half)
            self.copies[h].append(self.send(from_left, from_left, self.along[h](1)))
            self.copies[h][1].wait_recv()
            from_right = self.rows(result, self.row(h, 1) + half, half)
            self.copies[h].append(self.send(from_right, from_right, self.along[h](3)))

    def step_eight(self):
        for h in range(2):
            for copy in self.copies[h][2:]:
                copy.wait_recv()

    def drain(self):
        for copy in self.used:
            copy.wait_send()


class SmallSum:
    def __init__(self, r, grid):
        self.r, self.grid, self.used = r, grid, []

    def send(self, source, target, peer):
        copy = remote(source, target, self.r.s_sends, self.r.s_recvs, len(self.used), peer)
        self.used.append(copy)
        copy.start()

    def add(self, target, ref, count):
        def body(i, carry):
            at_rows = pl.ds(pl.multiple_of(i * 16, 16), 16)
            total = ref[0, at_rows, :].astype(single)
            for k in range(1, count):
                total = total + ref[k, at_rows, :].astype(single)
            target[at_rows, :] = total.astype(bfloat)
            return carry

        lax.fori_loop(0, SMALL // 16, body, 0)

    def step_one(self):
        r, grid = self.r, self.grid
        r.small_in[...] = r.small_wide[...].astype(bfloat)
        r.small_x[grid.x] = r.small_in[...]
        for k in (2, 1, 3):
            self.send(r.small_in, r.small_x.at[grid.x], grid.along_x(k))

    def step_two(self):
        r, grid = self.r, self.grid
        for copy in self.used[:3]:
            copy.wait_recv()
        self.add(r.small_one, r.small_x, 4)
        r.small_y[grid.y] = r.small_one[...]
        for k in (2, 1, 3):
            self.send(r.small_one, r.small_y.at[grid.y], grid.along_y(k))

    def step_three(self):
        r, grid = self.r, self.grid
        for copy in self.used[3:6]:
            copy.wait_recv()
        self.add(r.small_two, r.small_y, 4)
        r.small_z[grid.plane] = r.small_two[...]
        self.send(r.small_two, r.small_z.at[grid.plane], grid.across)

    def step_four(self):
        self.used[6].wait_recv()
        self.add(self.r.small_out, self.r.small_z, 2)

    def drain(self):
        for copy in self.used:
            copy.wait_send()


def backward_kernel(r):
    core, sibling, opposite = tensor_place()
    grid = Grid()
    peers = [sibling, opposite, grid.across]
    peers += [grid.along_x(k) for k in (1, 2, 3)] + [grid.along_y(k) for k in (1, 2, 3)]
    greet(peers)
    moves = Moves(r.moves)

    def fetch(*names):
        return [moves.start(getattr(r, name + "_h"), getattr(r, name)) for name in names]

    def ready(copies):
        for copy in copies:
            copy.wait()

    loads_one = fetch("section_three", "qkvc", "log", "out", "low", "qkv")
    loads_two = fetch("section_two", "slope", "act", "dense_low", "dense_in", "dense_out")
    loads_three = fetch("section_one", "images")
    stores = []
    sums = [TensorSum(r, n, r.total) for n in range(3)]
    width = r.out.shape[1]
    upper = GroupSum(r, "u", 0, 768, grid)
    dense = GroupSum(r, "d", 768, 1536, grid)
    lower = GroupSum(r, "l", 2304, 768, grid)
    small = SmallSum(r, grid)

    def deliver(array, row):
        rows = array.shape[0]
        half = array.shape[1] // 2
        for h in range(2):
            stores.append(
                moves.start(r.result.at[h, pl.ds(row, rows), :], array.at[:, pl.ds(h * half, half)])
            )

    r.small_wide[...] = jnp.zeros_like(r.small_wide)
    gates = [r.gates[:, k : k + 1] for k in range(2)]
    pulls = [r.gate_sums[:, k : k + 1] for k in range(2)]
    mean = gates[0] * pulls[0] + gates[1] * pulls[1]
    experts = lax.broadcasted_iota(jnp.int32, (r.gates.shape[0], EXPERTS), 1)
    grad_logits = 0.0
    for k in range(2):
        pick = r.routes[:, k : k + 1] == experts
        grad_logits = grad_logits + jnp.where(pick, gates[k] * (pulls[k] - mean), 0.0)
    grad_logits = grad_logits.astype(bfloat)
    ready(loads_one)
    rows = r.section_three[...]
    r.output[...] = (rows + r.mixed[...].astype(single)).astype(bfloat)
    normal, unused = normal_of(rows)
    moe_low = (normal * r.gain[3:4, :] + r.shift[3:4, :]).astype(bfloat)
    r.small_wide[0:EXPERTS, :] = dot_first(grad_logits, moe_low)
    grad_normed = r.grad_experts[...].astype(single) + dot_rows(grad_logits, r.router[...])
    grad_in, gain_part, shift_part = norm_back(grad_normed, rows, r.gain[3:4, :])
    grad = r.cotangent[...].astype(single) + grad_in
    r.grad[...] = grad
    r.small_wide[35:36, :] = gain_part
    r.small_wide[39:40, :] = shift_part
    r.small_wide[41:42, :] = jnp.sum(grad, axis=0, keepdims=True)
    attend_back(r, 1, grad, 0)
    pl.semaphore_wait(pltpu.get_barrier_semaphore(), 9)
    sums[0].start(attend_back_part(r, 1))
    upper.step_one()
    sums[0].finish()

    ready(loads_two)
    grad_in, gain_part, shift_part = norm_back(
        r.total[...].astype(single), r.section_two[...], r.gain[2:3, :]
    )
    r.small_wide[34:35, :] = gain_part
    r.small_wide[38:39, :] = shift_part
    grad = r.grad[...] + grad_in
    r.grad[...] = grad
    upper.step_two()
    grad_low = grad.astype(bfloat)
    r.grad_pre[...] = (dot_last(grad_low, r.dense_out[...]) * r.slope[...]).astype(bfloat)
    sums[1].start(lambda at: dot_last(r.grad_pre[...], r.dense_in[at, :]))
    put_grad(r, 768, dot_first(r.dense_low[...], r.grad_pre[...]))
    put_grad(r, 1536, dot_first(r.act[...], grad_low))
    upper.step_three()
    dense.step_one()
    sums[1].finish()

    ready(loads_three)
    grad_in, gain_part, shift_part = norm_back(
        r.total[...].astype(single), r.section_one[...], r.gain[1:2, :]
    )
    r.small_wide[33:34, :] = gain_part
    r.small_wide[37:38, :] = shift_part
    grad = r.grad[...] + grad_in
    r.grad[...] = grad
    r.small_wide[40:41, :] = jnp.sum(grad, axis=0, keepdims=True)
    upper.step_four()
    dense.step_two()
    attend_back(r, 0, grad, 2304)
    sums[2].start(attend_back_part(r, 0))
    lower.step_one()
    upper.step_five()
    dense.step_three()
    sums[2].finish()

    grad_in, gain_part, shift_part = norm_back(
        r.total[...].astype(single), r.images[...].astype(single), r.gain[0:1, :]
    )
    r.small_wide[32:33, :] = gain_part
    r.small_wide[36:37, :] = shift_part
    r.input_grad[...] = r.grad[...] + grad_in
    small.step_one()
    lower.step_two()
    upper.step_six()
    dense.step_four()
    small.step_two()
    lower.step_three()
    dense.step_five()
    upper.step_seven()
    small.step_three()
    lower.step_four()
    dense.step_six()
    lower.step_five()
    small.step_four()
    upper.step_eight()
    deliver(r.qkv_upper, 0)
    deliver(r.out_upper, 3 * width)
    dense.step_seven()
    lower.step_six()
    lower.step_seven()
    dense.step_eight()
    deliver(r.dense_in_grad, 768)
    deliver(r.dense_out_grad, 1536)
    lower.step_eight()
    deliver(r.qkv_lower, 2304)
    deliver(r.out_lower, 2304 + 3 * width)
    for one in sums + [upper, dense, lower, small]:
        one.drain()
    ready(stores)


def per_device(
    images,
    routes,
    cotangent,
    qkv_weight,
    out_weight,
    qv_bias,
    out_bias,
    ln_gain,
    ln_bias,
    dense_in,
    dense_out,
    router,
    expert_in,
    expert_out,
):
    tokens, width = images.shape
    part = out_weight.shape[1]
    hidden = dense_in.shape[1]
    qkv = jnp.transpose(qkv_weight, (0, 2, 3, 1)).reshape(2, 3 * part, width)
    full, low = (tokens, width), bfloat
    kept = {
        "section_one": (full, single),
        "section_two": (full, single),
        "section_three": (full, single),
        "dense_low": (full, low),
        "slope": ((tokens, hidden), single),
        "act": ((tokens, hidden), low),
        "low": ((2, tokens, width), low),
        "qkvc": ((2, 4, tokens, part), low),
        "log": ((2, tokens, part // HEAD), single),
    }
    weights = {
        "dense_in": (dense_in.shape, low),
        "dense_out": (dense_out.shape, low),
    }

    def vmem(names, table):
        return {name: pltpu.VMEM(*table[name]) for name in names}

    sections = ("section_one", "section_two", "section_three")
    outs = {name + ("" if name in sections else "_h"): kept[name] + ("hbm",) for name in kept}
    outs["sent"] = ((2, SLOTS, width), low, "hbm")
    outs["gates"] = ((tokens, 2), single, "vmem")
    outs["slots"] = ((tokens, 2), jnp.int32, "vmem")
    scratch = sum_scratch(tokens, 3)
    scratch.update(vmem([name for name in kept if name not in sections], kept))
    scratch.update(vmem(list(weights), weights))
    scratch.update(
        section=pltpu.VMEM((3, tokens, width), single),
        cotangent=pltpu.VMEM(full, low),
        moe_low=pltpu.VMEM(full, low),
        scaled=pltpu.VMEM((2, tokens, width), low),
        routed=pltpu.VMEM((2, SLOTS, width), low),
        total=pltpu.VMEM(full, low),
        moves=pltpu.SemaphoreType.DMA((24,)),
    )
    done = big_call(
        forward_kernel,
        "forward",
        {
            "images": (images, "vmem"),
            "qkv": (qkv, "vmem"),
            "out": (out_weight, "vmem"),
            "qv_bias": (qv_bias, "vmem"),
            "out_bias": (out_bias, "vmem"),
            "gain": (ln_gain, "vmem"),
            "shift": (ln_bias, "vmem"),
            "dense_in_h": (dense_in, "hbm"),
            "dense_out_h": (dense_out, "hbm"),
            "cotangent_h": (cotangent, "hbm"),
            "routes": (routes, "vmem"),
            "routes_row": (routes.T, "vmem"),
            "router": (router.T, "vmem"),
        },
        outs,
        scratch,
        1,
    )
    arrived = moe_send(done.sent.reshape(2, EXPERTS, STRIDE, width), 3)
    answers, expert_in_grad, expert_out_grad = expert_ffn(
        arrived.reshape(2, SLOTS, width), expert_in, expert_out
    )
    returned = moe_return(answers.reshape(2, EXPERTS, STRIDE, width), 4)
    parts = combine(returned.reshape(SLOTS, width), done.slots, done.gates, cotangent)
    mixed, grad_experts, gate_sums = combine_sum(parts, 5)

    outs = {
        "output": (full, low, "vmem"),
        "input_grad": (full, single, "vmem"),
        "qkv_upper": ((3 * part, width), low, "hbm"),
        "out_upper": ((part, width), low, "hbm"),
        "dense_in_grad": (dense_in.shape, low, "hbm"),
        "dense_out_grad": (dense_out.shape, low, "hbm"),
        "qkv_lower": ((3 * part, width), low, "hbm"),
        "out_lower": ((part, width), low, "hbm"),
        "small_out": ((SMALL, width), low, "vmem"),
    }
    scratch = sum_scratch(tokens, 3)
    scratch.update(vmem(list(kept), kept))
    scratch.update(vmem(list(weights), weights))
    for tag, rows in (("u", 768), ("d", 1536), ("l", 768)):
        scratch.update(group_scratch(tag, rows, width // 2))
    block = pltpu.VMEM((SMALL, width), low)
    scratch.update(
        images=pltpu.VMEM(full, low),
        qkv=pltpu.VMEM(qkv.shape, low),
        out=pltpu.VMEM(out_weight.shape, low),
        total=pltpu.VMEM(full, low),
        grad=pltpu.VMEM(full, single),
        grad_pre=pltpu.VMEM((tokens, hidden), low),
        grad_qkv=pltpu.VMEM((3, tokens, part), low),
        given=pltpu.VMEM((2, BIG, width // 2), low),
        result=pltpu.VMEM((2, BIG, width // 2), low),
        small_wide=pltpu.VMEM((SMALL, width), single),
        small_in=block,
        small_one=block,
        small_two=block,
        small_x=pltpu.VMEM((4, SMALL, width), low),
        small_y=pltpu.VMEM((4, SMALL, width), low),
        small_z=pltpu.VMEM((2, SMALL, width), low),
        s_sends=pltpu.SemaphoreType.DMA((7,)),
        s_recvs=pltpu.SemaphoreType.DMA((7,)),
        moves=pltpu.SemaphoreType.DMA((32,)),
    )
    ins = {
        "mixed": (mixed, "vmem"),
        "grad_experts": (grad_experts, "vmem"),
        "gate_sums": (gate_sums, "vmem"),
        "gates": (done.gates, "vmem"),
        "routes": (routes, "vmem"),
        "router": (router.T, "vmem"),
        "cotangent": (cotangent, "vmem"),
        "gain": (ln_gain, "vmem"),
        "shift": (ln_bias, "vmem"),
        "images_h": (images, "hbm"),
        "qkv_h": (qkv, "hbm"),
        "out_h": (out_weight, "hbm"),
        "dense_in_h": (dense_in, "hbm"),
        "dense_out_h": (dense_out, "hbm"),
    }
    for name in kept:
        ins[name + "_h"] = (getattr(done, name if name in sections else name + "_h"), "hbm")
    last = big_call(backward_kernel, "backward", ins, outs, scratch, 2)
    small = last.small_out.astype(single)
    qkv_weight_grad = jnp.stack([last.qkv_lower, last.qkv_upper]).astype(single)
    qkv_weight_grad = jnp.transpose(
        qkv_weight_grad.reshape(2, 3, part, width), (0, 3, 1, 2)
    )
    out_weight_grad = jnp.stack([last.out_lower, last.out_upper]).astype(single)
    dense_in_grad = last.dense_in_grad.astype(single)
    dense_out_grad = last.dense_out_grad.astype(single)
    router_grad = small[:32].T
    ln_gain_grad, ln_bias_grad, out_bias_grad = small[32:36], small[36:40], small[40:42]
    qv_bias_grad = small[42:46, :part].reshape(2, 2, part)
    output, input_grad = last.output, last.input_grad
    return (
        output,
        input_grad,
        qkv_weight_grad,
        out_weight_grad,
        qv_bias_grad,
        out_bias_grad,
        ln_gain_grad,
        ln_bias_grad,
        dense_in_grad,
        dense_out_grad,
        router_grad,
        expert_in_grad,
        expert_out_grad,
    )


def solution(mesh):
    in_specs = (
        P("dp", None),
        P("dp", None),
        P("dp", None),
        P(None, None, None, "tensor"),
        P(None, "tensor", None),
        P(None, None, "tensor"),
        P(),
        P(),
        P(),
        P(None, "tensor"),
        P("tensor", None),
        P(),
        P("dp", None, "tensor"),
        P("dp", "tensor", None),
    )
    out_specs = (
        P("dp", None),
        P("dp", None),
        P(None, None, None, "tensor"),
        P(None, "tensor", None),
        P(None, None, "tensor"),
        P(),
        P(),
        P(),
        P(None, "tensor"),
        P("tensor", None),
        P(),
        P("dp", None, "tensor"),
        P("dp", "tensor", None),
    )
    return jax.shard_map(
        per_device, mesh=mesh, in_specs=in_specs, out_specs=out_specs, check_vma=False
    )
```

```python
import functools

import jax
import jax.numpy as jnp
from jax import lax
from jax.experimental import pallas as pl
from jax.experimental.pallas import tpu as pltpu
from jax.sharding import PartitionSpec as P

HEAD = 64
SEQ = 197


epsilon = 1e-06
bfloat = jnp.bfloat16
single = jnp.float32


MESH = pl.DeviceIdType.MESH


BIG = 3072
SMALL = 48
EXPERTS = 32
STRIDE = 40
SLOTS = EXPERTS * STRIDE


def dot_rows(a, b):
    return lax.dot_general(a, b, (((1,), (0,)), ((), ())), preferred_element_type=single)


def dot_last(a, b):
    return lax.dot_general(a, b, (((1,), (1,)), ((), ())), preferred_element_type=single)


def dot_first(a, b):
    return lax.dot_general(a, b, (((0,), (0,)), ((), ())), preferred_element_type=single)


VMEM_SPEC = pl.BlockSpec(memory_space=pltpu.VMEM)


def dp_peer(k):
    dp = lax.axis_index("dp")
    plane = lax.rem(dp // 16 + k // 16, 2)
    x = lax.rem(lax.rem(dp // 4, 4) + lax.rem(k // 4, 4), 4)
    y = lax.rem(lax.rem(dp, 4) + lax.rem(k, 4), 4)
    return plane * 16 + x * 4 + y


def normal_of(rows):
    average = jnp.mean(rows, axis=-1, keepdims=True)
    centered = rows - average
    variance = jnp.mean(centered * centered, axis=-1, keepdims=True)
    inverse = lax.rsqrt(variance + epsilon)
    return centered * inverse, inverse


def norm_back(grad_normed, rows, gain_row):
    normal, inverse = normal_of(rows)
    scaled = grad_normed * gain_row
    mean_one = jnp.mean(scaled, axis=-1, keepdims=True)
    mean_two = jnp.mean(scaled * normal, axis=-1, keepdims=True)
    grad_in = inverse * (scaled - mean_one - normal * mean_two)
    gain_part = jnp.sum(grad_normed * normal, axis=0, keepdims=True)
    return grad_in, gain_part, jnp.sum(grad_normed, axis=0, keepdims=True)


def same_image(tokens):
    first = lax.broadcasted_iota(jnp.int32, (tokens, tokens), 0) // SEQ
    second = lax.broadcasted_iota(jnp.int32, (tokens, tokens), 1) // SEQ
    return first == second


class Refs:
    def __init__(self, names, refs):
        for name, ref in zip(names, refs):
            setattr(self, name, ref)


def big_call(kernel, name, ins, outs, scratch, collective_id=None, limit=58):
    names = list(ins) + list(outs) + list(scratch)
    hbm = pl.BlockSpec(memory_space=pl.ANY)

    def body(*refs):
        kernel(Refs(names, refs))

    found = pl.pallas_call(
        body,
        out_shape=[jax.ShapeDtypeStruct(shape, kind) for shape, kind, unused in outs.values()],
        in_specs=[hbm if place == "hbm" else VMEM_SPEC for unused, place in ins.values()],
        out_specs=[hbm if place == "hbm" else VMEM_SPEC for _, _, place in outs.values()],
        scratch_shapes=list(scratch.values()),
        compiler_params=pltpu.CompilerParams(
            collective_id=collective_id, has_side_effects=True, vmem_limit_bytes=limit * 2**20
        ),
        name=name,
    )(*[array for array, unused in ins.values()])
    return Refs(list(outs), found)


def tensor_place():
    t = lax.axis_index("tensor")
    core = lax.rem(t, 2)
    return core, {"tensor": t + 1 - 2 * core}, {"tensor": lax.rem(t + 2, 4)}


def remote(source, target, sends, recvs, index, peer):
    return pltpu.make_async_remote_copy(
        src_ref=source,
        dst_ref=target,
        send_sem=sends.at[index],
        recv_sem=recvs.at[index],
        device_id=peer,
        device_id_type=MESH,
    )


LANES = 128
THIRDS = 3


def sum_scratch(tokens, count):
    block = pltpu.VMEM((count, THIRDS, tokens, LANES), bfloat)
    names = ["give", "got_one", "sum_one", "got_two", "sum_two", "got_three"]
    found = {"t_" + name: block for name in names}
    found["t_own"] = pltpu.VMEM((tokens, THIRDS * LANES), single)
    found["t_sends"] = pltpu.SemaphoreType.DMA((count * 9,))
    found["t_recvs"] = pltpu.SemaphoreType.DMA((count * 9,))
    return found


class TensorSum:
    def __init__(self, r, number, total_ref):
        core, sibling, opposite = tensor_place()
        self.core, self.r, self.n, self.total = core, r, number, total_ref

        def copies(source, target, step, peer):
            return [
                remote(source.at[number, j], target.at[number, j], r.t_sends, r.t_recvs, number * 9 + step * 3 + j, peer)
                for j in range(THIRDS)
            ]

        self.first = copies(r.t_give, r.t_got_one, 0, sibling)
        self.second = copies(r.t_sum_one, r.t_got_two, 1, opposite)
        self.third = copies(r.t_sum_two, r.t_got_three, 2, sibling)

    def columns(self, which, j=0, count=1):
        return pl.ds(pl.multiple_of((which * THIRDS + j) * LANES, LANES), count * LANES)

    def start(self, partial):
        r, n = self.r, self.n
        other = partial(self.columns(1 - self.core, 0, THIRDS)).astype(bfloat)
        for j in range(THIRDS):
            r.t_give[n, j] = other[:, j * LANES : (j + 1) * LANES]
            self.first[j].start()
        r.t_own[...] = partial(self.columns(self.core, 0, THIRDS))
        for j in range(THIRDS):
            self.first[j].wait_recv()
            own = r.t_own[:, j * LANES : (j + 1) * LANES]
            r.t_sum_one[n, j] = (own + r.t_got_one[n, j].astype(single)).astype(bfloat)
            self.second[j].start()

    def finish(self):
        r, n = self.r, self.n
        for j in range(THIRDS):
            self.second[j].wait_recv()
            whole = (r.t_sum_one[n, j].astype(single) + r.t_got_two[n, j].astype(single)).astype(bfloat)
            r.t_sum_two[n, j] = whole
            self.third[j].start()
            self.total[:, self.columns(self.core, j)] = whole
        for j in range(THIRDS):
            self.third[j].wait_recv()
            self.total[:, self.columns(1 - self.core, j)] = r.t_got_three[n, j]

    def drain(self):
        for copy in self.first + self.second + self.third:
            copy.wait_send()


class Moves:
    def __init__(self, sems):
        self.sems, self.count = sems, 0

    def start(self, source, target):
        copy = pltpu.make_async_copy(source, target, self.sems.at[self.count])
        self.count += 1
        copy.start()
        return copy


def greet(peers):
    barrier = pltpu.get_barrier_semaphore()
    for peer in peers:
        pl.semaphore_signal(barrier, inc=1, device_id=peer, device_id_type=MESH)


def attend(r, rows, layer):
    width = r.out.shape[1]
    norm = 2 * layer
    normal, unused = normal_of(rows)
    low = (normal * r.gain[norm : norm + 1, :] + r.shift[norm : norm + 1, :]).astype(bfloat)
    r.low[layer] = low
    bias = r.qv_bias[layer]
    q = (dot_last(low, r.qkv[layer, :width, :]) + bias[0:1, :]).astype(bfloat)
    k = dot_last(low, r.qkv[layer, width : 2 * width, :]).astype(bfloat)
    v = (dot_last(low, r.qkv[layer, 2 * width :, :]) + bias[1:2, :]).astype(bfloat)
    r.qkvc[layer, 0], r.qkvc[layer, 1], r.qkvc[layer, 2] = q, k, v
    same = same_image(rows.shape[0])
    contexts = []
    for h in range(width // HEAD):
        at = slice(h * HEAD, (h + 1) * HEAD)
        scores = jnp.where(same, dot_last(q[:, at], k[:, at]) * HEAD ** (-0.5), -1e30)
        largest = jnp.max(scores, axis=-1, keepdims=True)
        exponent = jnp.exp(scores - largest)
        totals = jnp.sum(exponent, axis=-1, keepdims=True)
        r.log[layer, :, h : h + 1] = largest + jnp.log(totals)
        contexts.append(dot_rows((exponent / totals).astype(bfloat), v[:, at]))
    r.qkvc[layer, 3] = jnp.concatenate(contexts, axis=1).astype(bfloat)


def forward_kernel(r):
    core, sibling, opposite = tensor_place()
    greet([sibling, opposite])
    moves = Moves(r.moves)
    loads = [moves.start(r.dense_in_h, r.dense_in), moves.start(r.dense_out_h, r.dense_out)]
    loads += [moves.start(r.cotangent_h, r.cotangent)]
    stores = []
    sums = [TensorSum(r, n, r.total) for n in range(3)]

    def save(source, target):
        stores.append(moves.start(source, target))

    def out_part(layer):
        return lambda at: dot_rows(r.qkvc[layer, 3], r.out[layer, :, at])

    attend(r, r.images[...].astype(single), 0)
    pl.semaphore_wait(pltpu.get_barrier_semaphore(), 2)
    sums[0].start(out_part(0))
    sums[0].finish()

    rows = r.images[...].astype(single) + r.total[...].astype(single) + r.out_bias[0:1, :]
    r.section[0] = rows
    save(r.section.at[0], r.section_one)
    normal, unused = normal_of(rows)
    low = (normal * r.gain[1:2, :] + r.shift[1:2, :]).astype(bfloat)
    r.dense_low[...] = low
    save(r.dense_low, r.dense_low_h)
    for load in loads:
        load.wait()
    pre = dot_rows(low, r.dense_in[...])
    tail = 0.5 * (1.0 + lax.erf(pre * (0.5**0.5)))
    r.slope[...] = tail + pre * (jnp.exp(-0.5 * pre * pre) * 0.3989422804014327)
    save(r.slope, r.slope_h)
    r.act[...] = (pre * tail).astype(bfloat)
    save(r.act, r.act_h)
    sums[1].start(lambda at: dot_rows(r.act[...], r.dense_out[:, at]))
    sums[1].finish()

    rows = r.section[0] + r.total[...].astype(single)
    r.section[1] = rows
    save(r.section.at[1], r.section_two)
    attend(r, rows, 1)
    save(r.low, r.low_h)
    save(r.qkvc, r.qkvc_h)
    save(r.log, r.log_h)
    sums[2].start(out_part(1))
    sums[2].finish()

    rows = r.section[1] + r.total[...].astype(single) + r.out_bias[1:2, :]
    r.section[2] = rows
    save(r.section.at[2], r.section_three)
    moe_route_body(r, rows, save)
    for one in sums:
        one.drain()
    for store in stores:
        store.wait()


def moe_route_body(r, rows, save):
    tokens, width = rows.shape
    half = width // 2
    normal, unused = normal_of(rows)
    r.moe_low[...] = (normal * r.gain[3:4, :] + r.shift[3:4, :]).astype(bfloat)
    logits = dot_last(r.moe_low[...], r.router[...])
    experts = lax.broadcasted_iota(jnp.int32, (tokens, EXPERTS), 1)
    picks = [r.routes[:, k : k + 1] == experts for k in range(2)]
    chosen = [jnp.sum(jnp.where(pick, logits, 0.0), axis=1, keepdims=True) for pick in picks]
    largest = jnp.maximum(chosen[0], chosen[1])
    powers = [jnp.exp(c - largest) for c in chosen]
    total = powers[0] + powers[1]
    gates = [power / total for power in powers]
    r.gates[:, 0:1] = gates[0]
    r.gates[:, 1:2] = gates[1]
    cotangent = r.cotangent[...].astype(single)
    for k in range(2):
        r.scaled[k] = (gates[k] * cotangent).astype(bfloat)

    before = lax.broadcasted_iota(jnp.int32, (tokens, tokens), 0)
    after = lax.broadcasted_iota(jnp.int32, (tokens, tokens), 1)
    either = [jnp.where(pick, 1.0, 0.0) for pick in picks]
    lower = jnp.where(after < before, 1.0, 0.0).astype(bfloat)
    running = dot_rows(lower, (either[0] + either[1]).astype(bfloat))
    for k in range(2):
        rank = jnp.sum(running * either[k], axis=1, keepdims=True).astype(jnp.int32)
        r.slots[:, k : k + 1] = r.routes[:, k : k + 1] * STRIDE + rank

    experts_row = lax.broadcasted_iota(jnp.int32, (EXPERTS, tokens), 0)
    either_row = [jnp.where(r.routes_row[k : k + 1, :] == experts_row, 1.0, 0.0) for k in range(2)]
    upper = jnp.where(before < after, 1.0, 0.0).astype(bfloat)
    running_row = dot_rows((either_row[0] + either_row[1]).astype(bfloat), upper)
    slots_row = []
    for k in range(2):
        rank = jnp.sum(running_row * either_row[k], axis=0, keepdims=True).astype(jnp.int32)
        slots_row.append(r.routes_row[k : k + 1, :] * STRIDE + rank)

    block = SLOTS // 4
    for i in range(4):
        ids = lax.broadcasted_iota(jnp.int32, (block, tokens), 0) + i * block
        hits = [jnp.where(ids == slots_row[k], 1.0, 0.0) for k in range(2)]
        moved = dot_rows((hits[0] + hits[1]).astype(bfloat), r.moe_low[...]).astype(bfloat)
        moved_grad = (
            dot_rows(hits[0].astype(bfloat), r.scaled[0]) + dot_rows(hits[1].astype(bfloat), r.scaled[1])
        ).astype(bfloat)
        at = slice(i * block, (i + 1) * block)
        for h in range(2):
            r.routed[h, at, :half] = moved[:, h * half : (h + 1) * half]
            r.routed[h, at, half:] = moved_grad[:, h * half : (h + 1) * half]
            save(r.routed.at[h, pl.ds(i * block, block), :], r.sent.at[h, pl.ds(i * block, block), :])


def attend_back(r, layer, grad_out, base):
    width = r.out.shape[1]
    grad_low = grad_out.astype(bfloat)
    q, k, v = r.qkvc[layer, 0], r.qkvc[layer, 1], r.qkvc[layer, 2]
    put_grad(r, base + 3 * width, dot_first(r.qkvc[layer, 3], grad_low))
    grad_context = dot_last(grad_low, r.out[layer]).astype(bfloat)
    same = same_image(q.shape[0])
    grads = [[], [], []]
    for h in range(width // HEAD):
        at = slice(h * HEAD, (h + 1) * HEAD)
        scores = jnp.where(same, dot_last(q[:, at], k[:, at]) * HEAD ** (-0.5), -1e30)
        probs = jnp.exp(scores - r.log[layer, :, h : h + 1])
        grad_probs = dot_last(grad_context[:, at], v[:, at])
        row_total = jnp.sum(probs * grad_probs, axis=-1, keepdims=True)
        grad_scores = (probs * (grad_probs - row_total)).astype(bfloat)
        grads[0].append(dot_rows(grad_scores, k[:, at]) * HEAD ** (-0.5))
        grads[1].append(dot_first(grad_scores, q[:, at]) * HEAD ** (-0.5))
        grads[2].append(dot_first(probs.astype(bfloat), grad_context[:, at]))
    low = r.low[layer]
    for part in range(3):
        grad = jnp.concatenate(grads[part], axis=1).astype(bfloat)
        r.grad_qkv[part] = grad
        put_grad(r, base + part * width, dot_first(grad, low))
        if part != 1:
            row = 42 + 2 * layer + part // 2
            r.small_wide[row : row + 1, :width] = jnp.sum(grad.astype(single), axis=0, keepdims=True)


def attend_back_part(r, layer):
    width = r.out.shape[1]

    def partial(at):
        total = None
        for part in range(3):
            term = dot_rows(r.grad_qkv[part], r.qkv[layer, part * width : (part + 1) * width, at])
            total = term if total is None else total + term
        return total

    return partial


def put_grad(r, row, value):
    low = value.astype(bfloat)
    half = low.shape[1] // 2
    for h in range(2):
        r.given[h, row : row + low.shape[0], :] = low[:, h * half : (h + 1) * half]


def add_blocks(target, row, sources, rows):
    def body(i, carry):
        total = None
        for ref, start in sources:
            value = ref[pl.ds(pl.multiple_of(start + i * 16, 16), 16), :].astype(single)
            total = value if total is None else total + value
        target[pl.ds(pl.multiple_of(row + i * 16, 16), 16), :] = total.astype(bfloat)
        return carry

    lax.fori_loop(0, rows // 16, body, 0)


GROUP_COPIES = 38


def group_scratch(tag, rows, width):
    part, piece = rows // 4, rows // 16
    found = {}
    for name in ("near", "left", "right", "onward", "sum"):
        found[f"{tag}_{name}"] = pltpu.VMEM((2, part, width), bfloat)
    found[f"{tag}_got"] = pltpu.VMEM((2, 3, piece, width), bfloat)
    found[f"{tag}_piece"] = pltpu.VMEM((2, piece, width), bfloat)
    found[f"{tag}_pair"] = pltpu.VMEM((2, piece, width), bfloat)
    found[f"{tag}_sends"] = pltpu.SemaphoreType.DMA((GROUP_COPIES,))
    found[f"{tag}_recvs"] = pltpu.SemaphoreType.DMA((GROUP_COPIES,))
    return found


class Grid:
    def __init__(self):
        dp = lax.axis_index("dp")
        self.plane, self.x, self.y = dp // 16, lax.rem(dp // 4, 4), lax.rem(dp, 4)
        self.across = self.at(1 - self.plane, self.x, self.y)

    def at(self, plane, x, y):
        return {"dp": plane * 16 + x * 4 + y}

    def along_x(self, step):
        return self.at(self.plane, lax.rem(self.x + step, 4), self.y)

    def along_y(self, step):
        return self.at(self.plane, self.x, lax.rem(self.y + step, 4))


class GroupSum:
    def __init__(self, r, tag, base, rows, grid):
        self.r, self.base, self.part, self.piece, self.grid = r, base, rows // 4, rows // 16, grid
        names = ("near", "left", "right", "onward", "sum", "got", "piece", "pair", "sends", "recvs")
        for name in names:
            setattr(self, "b_" + name, getattr(r, f"{tag}_{name}"))
        self.used = []
        self.place = [grid.x, grid.y]
        self.along = [grid.along_x, grid.along_y]

    def send(self, source, target, peer):
        copy = remote(source, target, self.b_sends, self.b_recvs, len(self.used), peer)
        self.used.append(copy)
        copy.start()
        return copy

    def rows(self, ref, row, count):
        return ref.at[pl.ds(pl.multiple_of(row, 16), count), :]

    def row(self, h, step):
        return self.base + lax.rem(self.place[h] + step, 4) * self.part

    def both(self, ref):
        return [ref.at[h] for h in range(2)]

    def step_one(self):
        half = self.part // 2
        self.copies = []
        for h in range(2):
            s, near, left, right = (
                ref.at[h] for ref in (self.r.given, self.b_near, self.b_left, self.b_right)
            )
            fwd, back = self.along[h](1), self.along[h](3)
            self.copies.append([
                self.send(self.rows(s, self.row(h, 2), half), self.rows(near, 0, half), fwd),
                self.send(self.rows(s, self.row(h, 2) + half, half), self.rows(near, half, half), back),
                self.send(self.rows(s, self.row(h, 1) + half, half), self.rows(left, half, half), fwd),
                self.send(self.rows(s, self.row(h, 3), half), self.rows(right, 0, half), back),
            ])

    def step_two(self):
        half = self.part // 2
        for h in range(2):
            s, near, onward, left, right = (
                ref.at[h]
                for ref in (self.r.given, self.b_near, self.b_onward, self.b_left, self.b_right)
            )
            self.copies[h][0].wait_recv()
            add_blocks(onward, 0, [(s, self.row(h, 1)), (near, 0)], half)
            self.copies[h].append(
                self.send(self.rows(onward, 0, half), self.rows(left, 0, half), self.along[h](1))
            )
            self.copies[h][1].wait_recv()
            add_blocks(onward, half, [(s, self.row(h, 3) + half), (near, half)], half)
            self.copies[h].append(
                self.send(self.rows(onward, half, half), self.rows(right, half, half), self.along[h](3))
            )

    def step_three(self):
        self.pieces = []
        for h in range(2):
            for copy in self.copies[h][2:]:
                copy.wait_recv()
            s, left, right, total = (
                ref.at[h] for ref in (self.r.given, self.b_left, self.b_right, self.b_sum)
            )
            add_blocks(total, 0, [(s, self.row(h, 0)), (left, 0), (right, 0)], self.part)
            other = 1 - h
            for k in (2, 1, 3):
                row = lax.rem(self.place[other] + k, 4) * self.piece
                self.pieces.append(
                    self.send(self.rows(total, row, self.piece), self.b_got.at[h, k - 1], self.along[other](k))
                )

    def step_four(self):
        self.pairs = []
        for h in range(2):
            for copy in self.pieces[3 * h : 3 * h + 3]:
                copy.wait_recv()
            row = self.place[1 - h] * self.piece
            sources = [(self.b_sum.at[h], row)] + [(self.b_got.at[h, k], 0) for k in range(3)]
            add_blocks(self.b_piece.at[h], 0, sources, self.piece)
            self.pairs.append(self.send(self.b_piece.at[h], self.b_pair.at[h], self.grid.across))

    def own(self, h):
        return self.row(h, 0) + self.place[1 - h] * self.piece

    def step_five(self):
        self.spread = []
        for h in range(2):
            self.pairs[h].wait_recv()
            result = self.r.result.at[h]
            add_blocks(result, self.own(h), [(self.b_piece.at[h], 0), (self.b_pair.at[h], 0)], self.piece)
            mine = self.rows(result, self.own(h), self.piece)
            for k in (2, 1, 3):
                self.spread.append(self.send(mine, mine, self.along[1 - h](k)))

    def step_six(self):
        half = self.part // 2
        self.copies = []
        for h in range(2):
            for copy in self.spread[3 * h : 3 * h + 3]:
                copy.wait_recv()
            result = self.r.result.at[h]
            first = self.rows(result, self.row(h, 0), half)
            second = self.rows(result, self.row(h, 0) + half, half)
            fwd, back = self.along[h](1), self.along[h](3)
            self.copies.append([
                self.send(first, first, fwd),
                self.send(second, second, back),
                self.send(second, second, fwd),
                self.send(first, first, back),
            ])

    def step_seven(self):
        half = self.part // 2
        for h in range(2):
            result = self.r.result.at[h]
            self.copies[h][0].wait_recv()
            from_left = self.rows(result, self.row(h, 3), half)
            self.copies[h].append(self.send(from_left, from_left, self.along[h](1)))
            self.copies[h][1].wait_recv()
            from_right = self.rows(result, self.row(h, 1) + half, half)
            self.copies[h].append(self.send(from_right, from_right, self.along[h](3)))

    def step_eight(self):
        for h in range(2):
            for copy in self.copies[h][2:]:
                copy.wait_recv()

    def drain(self):
        for copy in self.used:
            copy.wait_send()


class SmallSum:
    def __init__(self, r, grid):
        self.r, self.grid, self.used = r, grid, []

    def send(self, source, target, peer):
        copy = remote(source, target, self.r.s_sends, self.r.s_recvs, len(self.used), peer)
        self.used.append(copy)
        copy.start()

    def add(self, target, ref, count):
        def body(i, carry):
            at_rows = pl.ds(pl.multiple_of(i * 16, 16), 16)
            total = ref[0, at_rows, :].astype(single)
            for k in range(1, count):
                total = total + ref[k, at_rows, :].astype(single)
            target[at_rows, :] = total.astype(bfloat)
            return carry

        lax.fori_loop(0, SMALL // 16, body, 0)

    def step_one(self):
        r, grid = self.r, self.grid
        r.small_in[...] = r.small_wide[...].astype(bfloat)
        r.small_x[grid.x] = r.small_in[...]
        for k in (2, 1, 3):
            self.send(r.small_in, r.small_x.at[grid.x], grid.along_x(k))

    def step_two(self):
        r, grid = self.r, self.grid
        for copy in self.used[:3]:
            copy.wait_recv()
        self.add(r.small_one, r.small_x, 4)
        r.small_y[grid.y] = r.small_one[...]
        for k in (2, 1, 3):
            self.send(r.small_one, r.small_y.at[grid.y], grid.along_y(k))

    def step_three(self):
        r, grid = self.r, self.grid
        for copy in self.used[3:6]:
            copy.wait_recv()
        self.add(r.small_two, r.small_y, 4)
        r.small_z[grid.plane] = r.small_two[...]
        self.send(r.small_two, r.small_z.at[grid.plane], grid.across)

    def step_four(self):
        self.used[6].wait_recv()
        self.add(self.r.small_out, self.r.small_z, 2)

    def drain(self):
        for copy in self.used:
            copy.wait_send()


def backward_kernel(r):
    core, sibling, opposite = tensor_place()
    grid = Grid()
    peers = [sibling, opposite, grid.across]
    peers += [grid.along_x(k) for k in (1, 2, 3)] + [grid.along_y(k) for k in (1, 2, 3)]
    greet(peers)
    moves = Moves(r.moves)

    def fetch(*names):
        return [moves.start(getattr(r, name + "_h"), getattr(r, name)) for name in names]

    def ready(copies):
        for copy in copies:
            copy.wait()

    loads_one = fetch("section_three", "qkvc", "log", "out", "low", "qkv")
    loads_two = fetch("section_two", "slope", "act", "dense_low", "dense_in", "dense_out")
    loads_three = fetch("section_one", "images")
    stores = []
    sums = [TensorSum(r, n, r.total) for n in range(3)]
    width = r.out.shape[1]
    upper = GroupSum(r, "u", 0, 768, grid)
    dense = GroupSum(r, "d", 768, 1536, grid)
    lower = GroupSum(r, "l", 2304, 768, grid)
    small = SmallSum(r, grid)
    mixed = MixedSum(r)

    def deliver(array, row, rows, target):
        half = array.shape[1] // 2
        for h in range(2):
            source = r.result.at[h, pl.ds(row, rows), :]
            stores.append(
                moves.start(source, array.at[pl.ds(target, rows), pl.ds(h * half, half)])
            )

    r.small_wide[...] = jnp.zeros_like(r.small_wide)
    gates = [r.gates[:, k : k + 1] for k in range(2)]
    pulls = [r.gate_sums[:, k : k + 1] for k in range(2)]
    mean = gates[0] * pulls[0] + gates[1] * pulls[1]
    experts = lax.broadcasted_iota(jnp.int32, (r.gates.shape[0], EXPERTS), 1)
    grad_logits = 0.0
    for k in range(2):
        pick = r.routes[:, k : k + 1] == experts
        grad_logits = grad_logits + jnp.where(pick, gates[k] * (pulls[k] - mean), 0.0)
    grad_logits = grad_logits.astype(bfloat)
    ready(loads_one)
    rows = r.section_three[...]
    normal, unused = normal_of(rows)
    moe_low = (normal * r.gain[3:4, :] + r.shift[3:4, :]).astype(bfloat)
    r.small_wide[0:EXPERTS, :] = dot_first(grad_logits, moe_low)
    grad_normed = r.grad_experts[...].astype(single) + dot_rows(grad_logits, r.router[...])
    grad_in, gain_part, shift_part = norm_back(grad_normed, rows, r.gain[3:4, :])
    grad = r.cotangent[...].astype(single) + grad_in
    r.grad[...] = grad
    r.small_wide[35:36, :] = gain_part
    r.small_wide[39:40, :] = shift_part
    r.small_wide[41:42, :] = jnp.sum(grad, axis=0, keepdims=True)
    attend_back(r, 1, grad, 0)
    pl.semaphore_wait(pltpu.get_barrier_semaphore(), 9)
    sums[0].start(attend_back_part(r, 1))
    upper.step_one()
    sums[0].finish()

    ready(loads_two)
    grad_in, gain_part, shift_part = norm_back(
        r.total[...].astype(single), r.section_two[...], r.gain[2:3, :]
    )
    r.small_wide[34:35, :] = gain_part
    r.small_wide[38:39, :] = shift_part
    grad = r.grad[...] + grad_in
    r.grad[...] = grad
    upper.step_two()
    grad_low = grad.astype(bfloat)
    r.grad_pre[...] = (dot_last(grad_low, r.dense_out[...]) * r.slope[...]).astype(bfloat)
    sums[1].start(lambda at: dot_last(r.grad_pre[...], r.dense_in[at, :]))
    put_grad(r, 768, dot_first(r.dense_low[...], r.grad_pre[...]))
    put_grad(r, 1536, dot_first(r.act[...], grad_low))
    upper.step_three()
    dense.step_one()
    sums[1].finish()

    ready(loads_three)
    grad_in, gain_part, shift_part = norm_back(
        r.total[...].astype(single), r.section_one[...], r.gain[1:2, :]
    )
    r.small_wide[33:34, :] = gain_part
    r.small_wide[37:38, :] = shift_part
    grad = r.grad[...] + grad_in
    r.grad[...] = grad
    r.small_wide[40:41, :] = jnp.sum(grad, axis=0, keepdims=True)
    upper.step_four()
    dense.step_two()
    attend_back(r, 0, grad, 2304)
    sums[2].start(attend_back_part(r, 0))
    lower.step_one()
    upper.step_five()
    dense.step_three()
    sums[2].finish()
    mixed.step_one()

    grad_in, gain_part, shift_part = norm_back(
        r.total[...].astype(single), r.images[...].astype(single), r.gain[0:1, :]
    )
    r.small_wide[32:33, :] = gain_part
    r.small_wide[36:37, :] = shift_part
    r.input_grad[...] = r.grad[...] + grad_in
    small.step_one()
    lower.step_two()
    upper.step_six()
    dense.step_four()
    small.step_two()
    lower.step_three()
    dense.step_five()
    upper.step_seven()
    mixed.step_two()
    small.step_three()
    lower.step_four()
    dense.step_six()
    lower.step_five()
    small.step_four()
    upper.step_eight()
    deliver(r.qkv_grad, 0, 3 * width, 3 * width)
    deliver(r.out_grad, 3 * width, width, width)
    mixed.step_three()
    dense.step_seven()
    lower.step_six()
    lower.step_seven()
    dense.step_eight()
    deliver(r.dense_in_grad, 768, 768, 0)
    deliver(r.dense_out_grad, 1536, 768, 0)
    lower.step_eight()
    deliver(r.qkv_grad, 2304, 3 * width, 0)
    deliver(r.out_grad, 2304 + 3 * width, width, 0)
    for one in sums + [upper, dense, lower, small, mixed]:
        one.drain()
    ready(stores)


def moe_kernel(r):
    core, sibling, opposite = tensor_place()
    dp = lax.axis_index("dp")
    grid = Grid()
    half = r.arrived.shape[3] // 2
    tokens = r.slots.shape[0]
    block = 4 * STRIDE
    barrier = pltpu.get_barrier_semaphore()

    def greet_one(k, carry):
        pl.semaphore_signal(barrier, inc=1, device_id={"dp": dp_peer(k)}, device_id_type=MESH)
        return carry

    lax.fori_loop(1, EXPERTS, greet_one, 0)
    greet([sibling, opposite])
    moves = Moves(r.moves)
    load_in = moves.start(r.expert_in_h.at[0], r.expert_in)
    load_out = moves.start(r.expert_out_h.at[0], r.expert_out)
    own_block = moves.start(r.sent.at[core, dp], r.arrived.at[core, dp])
    pl.semaphore_wait(barrier, EXPERTS + 1)

    def dispatch(peer, here):
        return pltpu.make_async_remote_copy(
            src_ref=r.sent.at[core, peer],
            dst_ref=r.arrived.at[core, here],
            send_sem=r.send_sems.at[peer],
            recv_sem=r.recv_sems.at[here],
            device_id={"dp": peer},
            device_id_type=MESH,
        )

    def share(source):
        block_ref = r.arrived.at[core, source]
        return remote(block_ref, block_ref, r.pass_sems, r.land_sems, source, sibling)

    def swap(source):
        return remote(r.give.at[source], r.got.at[source], r.give_sems, r.got_sems, source, sibling)

    def answer(peer, here):
        return pltpu.make_async_remote_copy(
            src_ref=r.answer.at[peer],
            dst_ref=r.returned.at[here],
            send_sem=r.back_sems.at[peer],
            recv_sem=r.home_sems.at[here],
            device_id={"dp": peer},
            device_id_type=MESH,
        )

    def offsets(p):
        return lax.rem(p, 2), lax.rem(p // 2 + lax.rem(p, 2), 4)

    def send_block(p, carry):
        dz, dx = offsets(p)
        base = lax.rem(grid.plane + dz, 2) * 16 + lax.rem(grid.x + dx, 4) * 4
        for dy in range(4):
            peer = base + lax.rem(grid.y + dy, 4)

            @pl.when(peer != dp)
            def start():
                dispatch(peer, dp).start()

        return carry

    def base_of(p):
        dz, dx = offsets(p)
        return lax.rem(grid.plane + dz, 2) * 16 + lax.rem(grid.x + 4 - dx, 4) * 4

    def receive(p):
        base = base_of(p)
        for dy in range(4):
            source = base + lax.rem(grid.y + 4 - dy, 4)

            @pl.when(source != dp)
            def wait():
                dispatch(source, source).wait_recv()

            @pl.when(source == dp)
            def wait_own():
                own_block.wait()

            share(source).start()

    def compute(p):
        base = base_of(p)
        for y in range(4):
            share(base + y).wait_recv()
            at = slice(y * STRIDE, (y + 1) * STRIDE)
            for h in range(2):
                rows = r.arrived[h, base + y].astype(single)
                r.wide_x[at, h * half : (h + 1) * half] = rows[:, :half]
                r.wide_g[at, h * half : (h + 1) * half] = rows[:, half:]
        at = pl.ds(pl.multiple_of(p * block, 16), block)
        rows = r.wide_x[...].astype(bfloat)
        rows_grad = r.wide_g[...].astype(bfloat)
        r.rows[at, :] = rows
        r.rows_grad[at, :] = rows_grad
        pre = dot_rows(rows, r.expert_in[...])
        grad_act = dot_last(rows_grad, r.expert_out[...])
        tail = 0.5 * (1.0 + lax.erf(pre * (0.5**0.5)))
        act = (pre * tail).astype(bfloat)
        slope = tail + pre * (jnp.exp(-0.5 * pre * pre) * 0.3989422804014327)
        grad_pre = (grad_act * slope).astype(bfloat)
        r.act[at, :] = act
        r.grad_pre[at, :] = grad_pre
        r.wide_x[...] = dot_rows(act, r.expert_out[...])
        r.wide_g[...] = dot_last(grad_pre, r.expert_in[...])
        for y in range(4):
            at = slice(y * STRIDE, (y + 1) * STRIDE)
            for which, target in ((1 - core, r.give), (core, r.kept)):
                columns = pl.ds(pl.multiple_of(which * half, LANES), half)
                target[base + y, :, :half] = r.wide_x[at, columns].astype(bfloat)
                target[base + y, :, half:] = r.wide_g[at, columns].astype(bfloat)
            swap(base + y).start()

    def respond(p):
        base = base_of(p)
        for y in range(4):
            source = base + y
            swap(source).wait_recv()
            total = r.kept[source].astype(single) + r.got[source].astype(single)
            r.answer[source] = total.astype(bfloat)

            @pl.when(source != dp)
            def start():
                answer(source, dp).start()

            @pl.when(source == dp)
            def keep():
                r.returned[dp] = total.astype(bfloat)

    def step(i, carry):
        pl.when(i < 8)(lambda: receive(i))
        pl.when((i >= 1) & (i < 9))(lambda: compute(i - 1))
        pl.when(i >= 2)(lambda: respond(i - 2))
        return carry

    lax.fori_loop(0, 8, send_block, 0)
    load_in.wait()
    load_out.wait()
    lax.fori_loop(0, 10, step, 0)
    r.weight_grad[0] = dot_first(r.act[...], r.rows_grad[...])
    store_out = moves.start(r.weight_grad.at[0], r.expert_out_grad.at[0])
    r.weight_grad[1] = dot_first(r.rows[...], r.grad_pre[...])
    store_in = moves.start(r.weight_grad.at[1], r.expert_in_grad.at[0])

    ids = lax.broadcasted_iota(jnp.int32, (tokens, SLOTS), 1)
    for k in range(2):
        r.hits[k] = jnp.where(ids == r.slots[:, k : k + 1], 1.0, 0.0).astype(bfloat)

    def come_home(i, carry):
        p, dy = i // 4, lax.rem(i, 4)
        dz, dx = offsets(p)
        source = lax.rem(grid.plane + dz, 2) * 16 + lax.rem(grid.x + dx, 4) * 4 + lax.rem(grid.y + dy, 4)

        @pl.when(source != dp)
        def wait():
            answer(source, source).wait_recv()

        at = pl.ds(pl.multiple_of(source * STRIDE, 8), STRIDE)
        r.wide_home[at, :] = r.returned[source].astype(single)
        return carry

    lax.fori_loop(0, EXPERTS, come_home, 0)
    back = r.wide_home[:, half:].astype(bfloat)
    r.home[...] = r.wide_home[:, :half].astype(bfloat)
    own = r.cotangent[:, pl.ds(pl.multiple_of(core * half, LANES), half)].astype(single)

    second = [remote(r.part.at[j], r.part_got.at[j], r.z_sends, r.z_recvs, j, opposite) for j in range(4)]
    third = [remote(r.part_sum.at[j], r.part_end.at[j], r.z_sends, r.z_recvs, 4 + j, sibling) for j in range(4)]
    normed = dot_rows(r.hits[0], back) + dot_rows(r.hits[1], back)
    for j in range(3):
        r.part[j] = normed[:, j * LANES : (j + 1) * LANES].astype(bfloat)
        second[j].start()
    picked = [dot_rows(r.hits[k], r.home[...]) for k in range(2)]
    gate = [jnp.sum(p * own, axis=1, keepdims=True) for p in picked]
    lane = lax.broadcasted_iota(jnp.int32, (tokens, LANES), 1)
    spread = jnp.where(lane == 0, gate[0], jnp.where(lane == 1, gate[1], 0.0))
    r.part[3] = spread.astype(bfloat)
    second[3].start()
    mixed = r.gates[:, 0:1] * picked[0] + r.gates[:, 1:2] * picked[1]
    for j in range(3):
        r.mixed[j] = mixed[:, j * LANES : (j + 1) * LANES].astype(bfloat)

    def columns(which, j):
        return pl.ds(pl.multiple_of((which * THIRDS + j) * LANES, LANES), LANES)

    for j in range(4):
        second[j].wait_recv()
        whole = (r.part[j].astype(single) + r.part_got[j].astype(single)).astype(bfloat)
        r.part_sum[j] = whole
        third[j].start()
        if j < 3:
            r.grad_experts[:, columns(core, j)] = whole
    for j in range(4):
        third[j].wait_recv()
        if j < 3:
            r.grad_experts[:, columns(1 - core, j)] = r.part_end[j]
        else:
            r.gate_sums[...] = r.part_sum[j].astype(single) + r.part_end[j].astype(single)
    for copy in second + third:
        copy.wait_send()

    def drain(k, carry):
        share(k).wait_send()
        swap(k).wait_send()

        @pl.when(k != dp)
        def wait():
            dispatch(k, dp).wait_send()
            answer(k, dp).wait_send()

        return carry

    lax.fori_loop(0, EXPERTS, drain, 0)
    store_out.wait()
    store_in.wait()


def moe_whole(sent, slots, gates, cotangent, expert_in, expert_out, collective_id):
    tokens, width = cotangent.shape
    half = width // 2
    slab = pltpu.VMEM((EXPERTS, STRIDE, width), bfloat)
    rows = pltpu.VMEM((SLOTS, width), bfloat)
    parts = pltpu.VMEM((4, tokens, LANES), bfloat)
    block = pltpu.VMEM((4 * STRIDE, width), single)
    every = pltpu.SemaphoreType.DMA((EXPERTS,))
    scratch = {name: slab for name in ("give", "kept", "got", "answer", "returned")}
    scratch.update({name: rows for name in ("rows", "rows_grad", "act", "grad_pre")})
    scratch.update({name: parts for name in ("part", "part_got", "part_sum", "part_end")})
    names = ("send", "recv", "pass", "land", "give", "got", "back", "home")
    scratch.update({name + "_sems": every for name in names})
    scratch.update(
        arrived=pltpu.VMEM((2, EXPERTS, STRIDE, width), bfloat),
        expert_in=pltpu.VMEM(expert_in.shape[1:], bfloat),
        expert_out=pltpu.VMEM(expert_out.shape[1:], bfloat),
        weight_grad=pltpu.VMEM((2,) + expert_in.shape[1:], single),
        wide_x=block,
        wide_g=block,
        wide_home=pltpu.VMEM((SLOTS, width), single),
        home=pltpu.VMEM((SLOTS, half), bfloat),
        hits=pltpu.VMEM((2, tokens, SLOTS), bfloat),
        z_sends=pltpu.SemaphoreType.DMA((8,)),
        z_recvs=pltpu.SemaphoreType.DMA((8,)),
        moves=pltpu.SemaphoreType.DMA((8,)),
    )
    return big_call(
        moe_kernel,
        "moe",
        {
            "sent": (sent.reshape(2, EXPERTS, STRIDE, width), "hbm"),
            "slots": (slots, "vmem"),
            "gates": (gates, "vmem"),
            "cotangent": (cotangent, "vmem"),
            "expert_in_h": (expert_in, "hbm"),
            "expert_out_h": (expert_out, "hbm"),
        },
        {
            "expert_in_grad": (expert_in.shape, single, "hbm"),
            "expert_out_grad": (expert_out.shape, single, "hbm"),
            "mixed": ((3, tokens, LANES), bfloat, "vmem"),
            "grad_experts": ((tokens, width), bfloat, "vmem"),
            "gate_sums": ((tokens, LANES), single, "vmem"),
        },
        scratch,
        collective_id,
    )


class MixedSum:
    def __init__(self, r):
        core, sibling, opposite = tensor_place()
        self.r, self.core = r, core
        self.second = [
            remote(r.mixed.at[j], r.m_got.at[j], r.m_sends, r.m_recvs, j, opposite) for j in range(3)
        ]
        self.third = [
            remote(r.m_sum.at[j], r.m_end.at[j], r.m_sends, r.m_recvs, 3 + j, sibling) for j in range(3)
        ]

    def step_one(self):
        for copy in self.second:
            copy.start()

    def step_two(self):
        r = self.r
        for j in range(3):
            self.second[j].wait_recv()
            whole = r.mixed[j].astype(single) + r.m_got[j].astype(single)
            r.m_sum[j] = whole.astype(bfloat)
            self.third[j].start()
            self.put(self.core, j, r.m_sum[j])

    def put(self, which, j, value):
        at = pl.ds(pl.multiple_of((which * THIRDS + j) * LANES, LANES), LANES)
        rows = self.r.section_three[:, at] + value.astype(single)
        self.r.output[:, at] = rows.astype(bfloat)

    def step_three(self):
        for j in range(3):
            self.third[j].wait_recv()
            self.put(1 - self.core, j, self.r.m_end[j])

    def drain(self):
        for copy in self.second + self.third:
            copy.wait_send()


def finish_kernel(r):
    moves = Moves(r.moves)
    names = ("qkv", "out", "dense_in", "dense_out")
    loads = [moves.start(getattr(r, name + "_h"), getattr(r, name + "_low")) for name in names]
    small = r.small[...].astype(single)
    part = r.qv_bias.shape[2]
    r.router[...] = small[:EXPERTS]
    r.gain[...] = small[32:36]
    r.shift[...] = small[36:40]
    r.out_bias[...] = small[40:42]
    r.qv_bias[0] = small[42:44, :part]
    r.qv_bias[1] = small[44:46, :part]
    stores = []
    for name, load in zip(names, loads):
        load.wait()
        low, wide = getattr(r, name + "_low"), getattr(r, name + "_wide")
        rows = low.shape[0]
        piece = 192

        def cast(i, carry):
            at = pl.ds(pl.multiple_of(i * piece, 16), piece)
            wide[at, :] = low[at, :].astype(single)
            return carry

        lax.fori_loop(0, rows // piece, cast, 0)
        stores.append(moves.start(wide, getattr(r, name + "_f")))
    for store in stores:
        store.wait()


def finish(last, part, width):
    arrays = {"qkv": last.qkv_grad, "out": last.out_grad}
    arrays.update({"dense_in": last.dense_in_grad, "dense_out": last.dense_out_grad})
    ins = {name + "_h": (array, "hbm") for name, array in arrays.items()}
    ins["small"] = (last.small_out, "vmem")
    outs = {name + "_f": (array.shape, single, "hbm") for name, array in arrays.items()}
    outs.update(
        router=((EXPERTS, width), single, "vmem"),
        gain=((4, width), single, "vmem"),
        shift=((4, width), single, "vmem"),
        out_bias=((2, width), single, "vmem"),
        qv_bias=((2, 2, part), single, "vmem"),
    )
    scratch = {name + "_low": pltpu.VMEM(array.shape, bfloat) for name, array in arrays.items()}
    scratch.update({name + "_wide": pltpu.VMEM(a.shape, single) for name, a in arrays.items()})
    scratch["moves"] = pltpu.SemaphoreType.DMA((8,))
    return big_call(finish_kernel, "finish", ins, outs, scratch)


def per_device(
    images,
    routes,
    cotangent,
    qkv_weight,
    out_weight,
    qv_bias,
    out_bias,
    ln_gain,
    ln_bias,
    dense_in,
    dense_out,
    router,
    expert_in,
    expert_out,
):
    tokens, width = images.shape
    part = out_weight.shape[1]
    hidden = dense_in.shape[1]
    qkv = jnp.transpose(qkv_weight, (0, 2, 3, 1)).reshape(2, 3 * part, width)
    full, low = (tokens, width), bfloat
    kept = {
        "section_one": (full, single),
        "section_two": (full, single),
        "section_three": (full, single),
        "dense_low": (full, low),
        "slope": ((tokens, hidden), single),
        "act": ((tokens, hidden), low),
        "low": ((2, tokens, width), low),
        "qkvc": ((2, 4, tokens, part), low),
        "log": ((2, tokens, part // HEAD), single),
    }
    weights = {
        "dense_in": (dense_in.shape, low),
        "dense_out": (dense_out.shape, low),
    }

    def vmem(names, table):
        return {name: pltpu.VMEM(*table[name]) for name in names}

    sections = ("section_one", "section_two", "section_three")
    outs = {name + ("" if name in sections else "_h"): kept[name] + ("hbm",) for name in kept}
    outs["sent"] = ((2, SLOTS, width), low, "hbm")
    outs["gates"] = ((tokens, 2), single, "vmem")
    outs["slots"] = ((tokens, 2), jnp.int32, "vmem")
    scratch = sum_scratch(tokens, 3)
    scratch.update(vmem([name for name in kept if name not in sections], kept))
    scratch.update(vmem(list(weights), weights))
    scratch.update(
        section=pltpu.VMEM((3, tokens, width), single),
        cotangent=pltpu.VMEM(full, low),
        moe_low=pltpu.VMEM(full, low),
        scaled=pltpu.VMEM((2, tokens, width), low),
        routed=pltpu.VMEM((2, SLOTS, width), low),
        total=pltpu.VMEM(full, low),
        moves=pltpu.SemaphoreType.DMA((24,)),
    )
    done = big_call(
        forward_kernel,
        "forward",
        {
            "images": (images, "vmem"),
            "qkv": (qkv, "vmem"),
            "out": (out_weight, "vmem"),
            "qv_bias": (qv_bias, "vmem"),
            "out_bias": (out_bias, "vmem"),
            "gain": (ln_gain, "vmem"),
            "shift": (ln_bias, "vmem"),
            "dense_in_h": (dense_in, "hbm"),
            "dense_out_h": (dense_out, "hbm"),
            "cotangent_h": (cotangent, "hbm"),
            "routes": (routes, "vmem"),
            "routes_row": (routes.T, "vmem"),
            "router": (router.T, "vmem"),
        },
        outs,
        scratch,
        1,
    )
    moe = moe_whole(done.sent, done.slots, done.gates, cotangent, expert_in, expert_out, 3)
    expert_in_grad, expert_out_grad = moe.expert_in_grad, moe.expert_out_grad

    outs = {
        "output": (full, low, "vmem"),
        "input_grad": (full, single, "vmem"),
        "qkv_grad": ((6 * part, width), low, "hbm"),
        "out_grad": ((2 * part, width), low, "hbm"),
        "dense_in_grad": (dense_in.shape, low, "hbm"),
        "dense_out_grad": (dense_out.shape, low, "hbm"),
        "small_out": ((SMALL, width), low, "vmem"),
    }
    scratch = sum_scratch(tokens, 3)
    scratch.update(vmem(list(kept), kept))
    scratch.update(vmem(list(weights), weights))
    for tag, rows in (("u", 768), ("d", 1536), ("l", 768)):
        scratch.update(group_scratch(tag, rows, width // 2))
    block = pltpu.VMEM((SMALL, width), low)
    scratch.update(
        images=pltpu.VMEM(full, low),
        qkv=pltpu.VMEM(qkv.shape, low),
        out=pltpu.VMEM(out_weight.shape, low),
        total=pltpu.VMEM(full, low),
        grad=pltpu.VMEM(full, single),
        grad_pre=pltpu.VMEM((tokens, hidden), low),
        grad_qkv=pltpu.VMEM((3, tokens, part), low),
        given=pltpu.VMEM((2, BIG, width // 2), low),
        result=pltpu.VMEM((2, BIG, width // 2), low),
        small_wide=pltpu.VMEM((SMALL, width), single),
        small_in=block,
        small_one=block,
        small_two=block,
        small_x=pltpu.VMEM((4, SMALL, width), low),
        small_y=pltpu.VMEM((4, SMALL, width), low),
        small_z=pltpu.VMEM((2, SMALL, width), low),
        m_got=pltpu.VMEM((3, tokens, LANES), low),
        m_sum=pltpu.VMEM((3, tokens, LANES), low),
        m_end=pltpu.VMEM((3, tokens, LANES), low),
        m_sends=pltpu.SemaphoreType.DMA((6,)),
        m_recvs=pltpu.SemaphoreType.DMA((6,)),
        s_sends=pltpu.SemaphoreType.DMA((7,)),
        s_recvs=pltpu.SemaphoreType.DMA((7,)),
        moves=pltpu.SemaphoreType.DMA((32,)),
    )
    ins = {
        "mixed": (moe.mixed, "vmem"),
        "grad_experts": (moe.grad_experts, "vmem"),
        "gate_sums": (moe.gate_sums, "vmem"),
        "gates": (done.gates, "vmem"),
        "routes": (routes, "vmem"),
        "router": (router.T, "vmem"),
        "cotangent": (cotangent, "vmem"),
        "gain": (ln_gain, "vmem"),
        "shift": (ln_bias, "vmem"),
        "images_h": (images, "hbm"),
        "qkv_h": (qkv, "hbm"),
        "out_h": (out_weight, "hbm"),
        "dense_in_h": (dense_in, "hbm"),
        "dense_out_h": (dense_out, "hbm"),
    }
    for name in kept:
        ins[name + "_h"] = (getattr(done, name if name in sections else name + "_h"), "hbm")
    last = big_call(backward_kernel, "backward", ins, outs, scratch, 2)
    end = finish(last, part, width)
    qkv_weight_grad = jnp.transpose(end.qkv_f.reshape(2, 3, part, width), (0, 3, 1, 2))
    out_weight_grad = end.out_f.reshape(2, part, width)
    dense_in_grad, dense_out_grad = end.dense_in_f, end.dense_out_f
    router_grad = end.router.T
    ln_gain_grad, ln_bias_grad, out_bias_grad = end.gain, end.shift, end.out_bias
    qv_bias_grad = end.qv_bias
    output, input_grad = last.output, last.input_grad
    return (
        output,
        input_grad,
        qkv_weight_grad,
        out_weight_grad,
        qv_bias_grad,
        out_bias_grad,
        ln_gain_grad,
        ln_bias_grad,
        dense_in_grad,
        dense_out_grad,
        router_grad,
        expert_in_grad,
        expert_out_grad,
    )


def solution(mesh):
    in_specs = (
        P("dp", None),
        P("dp", None),
        P("dp", None),
        P(None, None, None, "tensor"),
        P(None, "tensor", None),
        P(None, None, "tensor"),
        P(),
        P(),
        P(),
        P(None, "tensor"),
        P("tensor", None),
        P(),
        P("dp", None, "tensor"),
        P("dp", "tensor", None),
    )
    out_specs = (
        P("dp", None),
        P("dp", None),
        P(None, None, None, "tensor"),
        P(None, "tensor", None),
        P(None, None, "tensor"),
        P(),
        P(),
        P(),
        P(None, "tensor"),
        P("tensor", None),
        P(),
        P("dp", None, "tensor"),
        P("dp", "tensor", None),
    )
    return jax.shard_map(
        per_device, mesh=mesh, in_specs=in_specs, out_specs=out_specs, check_vma=False
    )
```

```python
import functools

import jax
import jax.numpy as jnp
from jax import lax
from jax.experimental import pallas as pl
from jax.experimental.pallas import tpu as pltpu
from jax.sharding import PartitionSpec as P

HEAD = 64
SEQ = 197


epsilon = 1e-06
bfloat = jnp.bfloat16
single = jnp.float32


MESH = pl.DeviceIdType.MESH


BIG = 3072
SMALL = 48
EXPERTS = 32
STRIDE = 40
SLOTS = EXPERTS * STRIDE


def dot_rows(a, b):
    return lax.dot_general(a, b, (((1,), (0,)), ((), ())), preferred_element_type=single)


def dot_last(a, b):
    return lax.dot_general(a, b, (((1,), (1,)), ((), ())), preferred_element_type=single)


def dot_first(a, b):
    return lax.dot_general(a, b, (((0,), (0,)), ((), ())), preferred_element_type=single)


VMEM_SPEC = pl.BlockSpec(memory_space=pltpu.VMEM)


def dp_peer(k):
    dp = lax.axis_index("dp")
    plane = lax.rem(dp // 16 + k // 16, 2)
    x = lax.rem(lax.rem(dp // 4, 4) + lax.rem(k // 4, 4), 4)
    y = lax.rem(lax.rem(dp, 4) + lax.rem(k, 4), 4)
    return plane * 16 + x * 4 + y


def normal_of(rows):
    average = jnp.mean(rows, axis=-1, keepdims=True)
    centered = rows - average
    variance = jnp.mean(centered * centered, axis=-1, keepdims=True)
    inverse = lax.rsqrt(variance + epsilon)
    return centered * inverse, inverse


def norm_back(grad_normed, rows, gain_row):
    normal, inverse = normal_of(rows)
    scaled = grad_normed * gain_row
    mean_one = jnp.mean(scaled, axis=-1, keepdims=True)
    mean_two = jnp.mean(scaled * normal, axis=-1, keepdims=True)
    grad_in = inverse * (scaled - mean_one - normal * mean_two)
    gain_part = jnp.sum(grad_normed * normal, axis=0, keepdims=True)
    return grad_in, gain_part, jnp.sum(grad_normed, axis=0, keepdims=True)


def same_image(tokens):
    first = lax.broadcasted_iota(jnp.int32, (tokens, tokens), 0) // SEQ
    second = lax.broadcasted_iota(jnp.int32, (tokens, tokens), 1) // SEQ
    return first == second


class Refs:
    def __init__(self, names, refs):
        for name, ref in zip(names, refs):
            setattr(self, name, ref)


def big_call(kernel, name, ins, outs, scratch, collective_id=None, limit=58):
    names = list(ins) + list(outs) + list(scratch)
    hbm = pl.BlockSpec(memory_space=pl.ANY)

    def body(*refs):
        kernel(Refs(names, refs))

    found = pl.pallas_call(
        body,
        out_shape=[jax.ShapeDtypeStruct(shape, kind) for shape, kind, unused in outs.values()],
        in_specs=[hbm if place == "hbm" else VMEM_SPEC for unused, place in ins.values()],
        out_specs=[hbm if place == "hbm" else VMEM_SPEC for _, _, place in outs.values()],
        scratch_shapes=list(scratch.values()),
        compiler_params=pltpu.CompilerParams(
            collective_id=collective_id, has_side_effects=True, vmem_limit_bytes=limit * 2**20
        ),
        name=name,
    )(*[array for array, unused in ins.values()])
    return Refs(list(outs), found)


def tensor_place():
    t = lax.axis_index("tensor")
    core = lax.rem(t, 2)
    return core, {"tensor": t + 1 - 2 * core}, {"tensor": lax.rem(t + 2, 4)}


def remote(source, target, sends, recvs, index, peer):
    return pltpu.make_async_remote_copy(
        src_ref=source,
        dst_ref=target,
        send_sem=sends.at[index],
        recv_sem=recvs.at[index],
        device_id=peer,
        device_id_type=MESH,
    )


LANES = 128
THIRDS = 3


def sum_scratch(tokens, count):
    block = pltpu.VMEM((count, THIRDS, tokens, LANES), bfloat)
    names = ["give", "got_one", "sum_one", "got_two", "sum_two", "got_three"]
    found = {"t_" + name: block for name in names}
    found["t_own"] = pltpu.VMEM((tokens, THIRDS * LANES), single)
    found["t_sends"] = pltpu.SemaphoreType.DMA((count * 9,))
    found["t_recvs"] = pltpu.SemaphoreType.DMA((count * 9,))
    return found


class TensorSum:
    def __init__(self, r, number, total_ref):
        core, sibling, opposite = tensor_place()
        self.core, self.r, self.n, self.total = core, r, number, total_ref

        def copies(source, target, step, peer):
            return [
                remote(source.at[number, j], target.at[number, j], r.t_sends, r.t_recvs, number * 9 + step * 3 + j, peer)
                for j in range(THIRDS)
            ]

        self.first = copies(r.t_give, r.t_got_one, 0, sibling)
        self.second = copies(r.t_sum_one, r.t_got_two, 1, opposite)
        self.third = copies(r.t_sum_two, r.t_got_three, 2, sibling)

    def columns(self, which, j=0, count=1):
        return pl.ds(pl.multiple_of((which * THIRDS + j) * LANES, LANES), count * LANES)

    def start(self, partial):
        r, n = self.r, self.n
        other = partial(self.columns(1 - self.core, 0, THIRDS)).astype(bfloat)
        for j in range(THIRDS):
            r.t_give[n, j] = other[:, j * LANES : (j + 1) * LANES]
            self.first[j].start()
        r.t_own[...] = partial(self.columns(self.core, 0, THIRDS))
        for j in range(THIRDS):
            self.first[j].wait_recv()
            own = r.t_own[:, j * LANES : (j + 1) * LANES]
            r.t_sum_one[n, j] = (own + r.t_got_one[n, j].astype(single)).astype(bfloat)
            self.second[j].start()

    def finish(self):
        r, n = self.r, self.n
        for j in range(THIRDS):
            self.second[j].wait_recv()
            whole = (r.t_sum_one[n, j].astype(single) + r.t_got_two[n, j].astype(single)).astype(bfloat)
            r.t_sum_two[n, j] = whole
            self.third[j].start()
            self.total[:, self.columns(self.core, j)] = whole
        for j in range(THIRDS):
            self.third[j].wait_recv()
            self.total[:, self.columns(1 - self.core, j)] = r.t_got_three[n, j]

    def drain(self):
        for copy in self.first + self.second + self.third:
            copy.wait_send()


class Moves:
    def __init__(self, sems):
        self.sems, self.count = sems, 0

    def start(self, source, target):
        copy = pltpu.make_async_copy(source, target, self.sems.at[self.count])
        self.count += 1
        copy.start()
        return copy


def greet(peers):
    barrier = pltpu.get_barrier_semaphore()
    for peer in peers:
        pl.semaphore_signal(barrier, inc=1, device_id=peer, device_id_type=MESH)


def attend(r, rows, layer):
    width = r.out.shape[1]
    norm = 2 * layer
    normal, unused = normal_of(rows)
    low = (normal * r.gain[norm : norm + 1, :] + r.shift[norm : norm + 1, :]).astype(bfloat)
    r.low[layer] = low
    bias = r.qv_bias[layer]
    q = (dot_last(low, r.qkv[layer, :width, :]) + bias[0:1, :]).astype(bfloat)
    k = dot_last(low, r.qkv[layer, width : 2 * width, :]).astype(bfloat)
    v = (dot_last(low, r.qkv[layer, 2 * width :, :]) + bias[1:2, :]).astype(bfloat)
    r.qkvc[layer, 0], r.qkvc[layer, 1], r.qkvc[layer, 2] = q, k, v
    same = same_image(rows.shape[0])
    contexts = []
    for h in range(width // HEAD):
        at = slice(h * HEAD, (h + 1) * HEAD)
        scores = jnp.where(same, dot_last(q[:, at], k[:, at]) * HEAD ** (-0.5), -1e30)
        largest = jnp.max(scores, axis=-1, keepdims=True)
        exponent = jnp.exp(scores - largest)
        totals = jnp.sum(exponent, axis=-1, keepdims=True)
        r.log[layer, :, h : h + 1] = largest + jnp.log(totals)
        contexts.append(dot_rows((exponent / totals).astype(bfloat), v[:, at]))
    r.qkvc[layer, 3] = jnp.concatenate(contexts, axis=1).astype(bfloat)


def forward_kernel(r):
    core, sibling, opposite = tensor_place()
    greet([sibling, opposite])
    moves = Moves(r.moves)
    loads = [moves.start(r.dense_in_h, r.dense_in), moves.start(r.dense_out_h, r.dense_out)]
    loads += [moves.start(r.cotangent_h, r.cotangent)]
    stores = []
    sums = [TensorSum(r, n, r.total) for n in range(3)]

    def save(source, target):
        stores.append(moves.start(source, target))

    def out_part(layer):
        return lambda at: dot_rows(r.qkvc[layer, 3], r.out[layer, :, at])

    attend(r, r.images[...].astype(single), 0)
    pl.semaphore_wait(pltpu.get_barrier_semaphore(), 2)
    sums[0].start(out_part(0))
    sums[0].finish()

    rows = r.images[...].astype(single) + r.total[...].astype(single) + r.out_bias[0:1, :]
    r.section[0] = rows
    save(r.section.at[0], r.section_one)
    normal, unused = normal_of(rows)
    low = (normal * r.gain[1:2, :] + r.shift[1:2, :]).astype(bfloat)
    r.dense_low[...] = low
    save(r.dense_low, r.dense_low_h)
    for load in loads:
        load.wait()
    pre = dot_rows(low, r.dense_in[...])
    tail = 0.5 * (1.0 + lax.erf(pre * (0.5**0.5)))
    r.slope[...] = tail + pre * (jnp.exp(-0.5 * pre * pre) * 0.3989422804014327)
    save(r.slope, r.slope_h)
    r.act[...] = (pre * tail).astype(bfloat)
    save(r.act, r.act_h)
    sums[1].start(lambda at: dot_rows(r.act[...], r.dense_out[:, at]))
    sums[1].finish()

    rows = r.section[0] + r.total[...].astype(single)
    r.section[1] = rows
    save(r.section.at[1], r.section_two)
    attend(r, rows, 1)
    save(r.low, r.low_h)
    save(r.qkvc, r.qkvc_h)
    save(r.log, r.log_h)
    sums[2].start(out_part(1))
    sums[2].finish()

    rows = r.section[1] + r.total[...].astype(single) + r.out_bias[1:2, :]
    r.section[2] = rows
    save(r.section.at[2], r.section_three)
    moe_route_body(r, rows, save)
    for one in sums:
        one.drain()
    for store in stores:
        store.wait()


def moe_route_body(r, rows, save):
    tokens, width = rows.shape
    half = width // 2
    normal, unused = normal_of(rows)
    r.moe_low[...] = (normal * r.gain[3:4, :] + r.shift[3:4, :]).astype(bfloat)
    logits = dot_last(r.moe_low[...], r.router[...])
    experts = lax.broadcasted_iota(jnp.int32, (tokens, EXPERTS), 1)
    before = lax.broadcasted_iota(jnp.int32, (tokens, tokens), 0)
    after = lax.broadcasted_iota(jnp.int32, (tokens, tokens), 1)
    for k in range(2):
        spread = jnp.where(before == after, r.routes_row[k : k + 1, :].astype(single), 0.0)
        r.routes[:, k : k + 1] = jnp.sum(spread, axis=1, keepdims=True).astype(jnp.int32)
    picks = [r.routes[:, k : k + 1] == experts for k in range(2)]
    chosen = [jnp.sum(jnp.where(pick, logits, 0.0), axis=1, keepdims=True) for pick in picks]
    largest = jnp.maximum(chosen[0], chosen[1])
    powers = [jnp.exp(c - largest) for c in chosen]
    total = powers[0] + powers[1]
    gates = [power / total for power in powers]
    r.gates[:, 0:1] = gates[0]
    r.gates[:, 1:2] = gates[1]
    cotangent = r.cotangent[...].astype(single)
    for k in range(2):
        r.scaled[k] = (gates[k] * cotangent).astype(bfloat)

    either = [jnp.where(pick, 1.0, 0.0) for pick in picks]
    lower = jnp.where(after < before, 1.0, 0.0).astype(bfloat)
    running = dot_rows(lower, (either[0] + either[1]).astype(bfloat))
    for k in range(2):
        rank = jnp.sum(running * either[k], axis=1, keepdims=True).astype(jnp.int32)
        r.slots[:, k : k + 1] = r.routes[:, k : k + 1] * STRIDE + rank

    experts_row = lax.broadcasted_iota(jnp.int32, (EXPERTS, tokens), 0)
    either_row = [jnp.where(r.routes_row[k : k + 1, :] == experts_row, 1.0, 0.0) for k in range(2)]
    upper = jnp.where(before < after, 1.0, 0.0).astype(bfloat)
    running_row = dot_rows((either_row[0] + either_row[1]).astype(bfloat), upper)
    slots_row = []
    for k in range(2):
        rank = jnp.sum(running_row * either_row[k], axis=0, keepdims=True).astype(jnp.int32)
        slots_row.append(r.routes_row[k : k + 1, :] * STRIDE + rank)

    block = SLOTS // 4
    for i in range(4):
        ids = lax.broadcasted_iota(jnp.int32, (block, tokens), 0) + i * block
        hits = [jnp.where(ids == slots_row[k], 1.0, 0.0) for k in range(2)]
        moved = dot_rows((hits[0] + hits[1]).astype(bfloat), r.moe_low[...]).astype(bfloat)
        moved_grad = (
            dot_rows(hits[0].astype(bfloat), r.scaled[0]) + dot_rows(hits[1].astype(bfloat), r.scaled[1])
        ).astype(bfloat)
        at = slice(i * block, (i + 1) * block)
        for h in range(2):
            r.routed[h, at, :half] = moved[:, h * half : (h + 1) * half]
            r.routed[h, at, half:] = moved_grad[:, h * half : (h + 1) * half]
            save(r.routed.at[h, pl.ds(i * block, block), :], r.sent.at[h, pl.ds(i * block, block), :])


def attend_back(r, layer, grad_out):
    width = r.out.shape[1]
    grad_low = grad_out.astype(bfloat)
    r.grad_low[...] = grad_low
    q, k, v = r.qkvc[layer, 0], r.qkvc[layer, 1], r.qkvc[layer, 2]
    grad_context = dot_last(grad_low, r.out[layer]).astype(bfloat)
    same = same_image(q.shape[0])
    grads = [[], [], []]
    for h in range(width // HEAD):
        at = slice(h * HEAD, (h + 1) * HEAD)
        scores = jnp.where(same, dot_last(q[:, at], k[:, at]) * HEAD ** (-0.5), -1e30)
        probs = jnp.exp(scores - r.log[layer, :, h : h + 1])
        grad_probs = dot_last(grad_context[:, at], v[:, at])
        row_total = jnp.sum(probs * grad_probs, axis=-1, keepdims=True)
        grad_scores = (probs * (grad_probs - row_total)).astype(bfloat)
        grads[0].append(dot_rows(grad_scores, k[:, at]) * HEAD ** (-0.5))
        grads[1].append(dot_first(grad_scores, q[:, at]) * HEAD ** (-0.5))
        grads[2].append(dot_first(probs.astype(bfloat), grad_context[:, at]))
    for part in range(3):
        r.grad_qkv[part] = jnp.concatenate(grads[part], axis=1).astype(bfloat)


def attend_weights(r, layer, base):
    width = r.out.shape[1]
    put_grad(r, base + 3 * width, dot_first(r.qkvc[layer, 3], r.grad_low[...]))
    for part in range(3):
        grad = r.grad_qkv[part]
        put_grad(r, base + part * width, dot_first(grad, r.low[layer]))
        if part != 1:
            row = 42 + 2 * layer + part // 2
            r.small_wide[row : row + 1, :width] = jnp.sum(grad.astype(single), axis=0, keepdims=True)


def attend_back_part(r, layer):
    width = r.out.shape[1]

    def partial(at):
        total = None
        for part in range(3):
            term = dot_rows(r.grad_qkv[part], r.qkv[layer, part * width : (part + 1) * width, at])
            total = term if total is None else total + term
        return total

    return partial


def put_grad(r, row, value):
    low = value.astype(bfloat)
    half = low.shape[1] // 2
    for h in range(2):
        r.given[h, row : row + low.shape[0], :] = low[:, h * half : (h + 1) * half]


def add_blocks(target, row, sources, rows):
    def body(i, carry):
        total = None
        for ref, start in sources:
            value = ref[pl.ds(pl.multiple_of(start + i * 16, 16), 16), :].astype(single)
            total = value if total is None else total + value
        target[pl.ds(pl.multiple_of(row + i * 16, 16), 16), :] = total.astype(bfloat)
        return carry

    lax.fori_loop(0, rows // 16, body, 0)


GROUP_COPIES = 38


def group_scratch(tag, rows, width):
    part, piece = rows // 4, rows // 16
    found = {}
    for name in ("near", "left", "right", "onward", "sum"):
        found[f"{tag}_{name}"] = pltpu.VMEM((2, part, width), bfloat)
    found[f"{tag}_got"] = pltpu.VMEM((2, 3, piece, width), bfloat)
    found[f"{tag}_piece"] = pltpu.VMEM((2, piece, width), bfloat)
    found[f"{tag}_pair"] = pltpu.VMEM((2, piece, width), bfloat)
    found[f"{tag}_sends"] = pltpu.SemaphoreType.DMA((GROUP_COPIES,))
    found[f"{tag}_recvs"] = pltpu.SemaphoreType.DMA((GROUP_COPIES,))
    return found


class Grid:
    def __init__(self):
        dp = lax.axis_index("dp")
        self.plane, self.x, self.y = dp // 16, lax.rem(dp // 4, 4), lax.rem(dp, 4)
        self.across = self.at(1 - self.plane, self.x, self.y)

    def at(self, plane, x, y):
        return {"dp": plane * 16 + x * 4 + y}

    def along_x(self, step):
        return self.at(self.plane, lax.rem(self.x + step, 4), self.y)

    def along_y(self, step):
        return self.at(self.plane, self.x, lax.rem(self.y + step, 4))


class GroupSum:
    def __init__(self, r, tag, base, rows, grid):
        self.r, self.base, self.part, self.piece, self.grid = r, base, rows // 4, rows // 16, grid
        names = ("near", "left", "right", "onward", "sum", "got", "piece", "pair", "sends", "recvs")
        for name in names:
            setattr(self, "b_" + name, getattr(r, f"{tag}_{name}"))
        self.used = []
        self.place = [grid.x, grid.y]
        self.along = [grid.along_x, grid.along_y]

    def send(self, source, target, peer):
        copy = remote(source, target, self.b_sends, self.b_recvs, len(self.used), peer)
        self.used.append(copy)
        copy.start()
        return copy

    def rows(self, ref, row, count):
        return ref.at[pl.ds(pl.multiple_of(row, 16), count), :]

    def row(self, h, step):
        return self.base + lax.rem(self.place[h] + step, 4) * self.part

    def both(self, ref):
        return [ref.at[h] for h in range(2)]

    def step_one(self):
        half = self.part // 2
        self.copies = []
        for h in range(2):
            s, near, left, right = (
                ref.at[h] for ref in (self.r.given, self.b_near, self.b_left, self.b_right)
            )
            fwd, back = self.along[h](1), self.along[h](3)
            self.copies.append([
                self.send(self.rows(s, self.row(h, 2), half), self.rows(near, 0, half), fwd),
                self.send(self.rows(s, self.row(h, 2) + half, half), self.rows(near, half, half), back),
                self.send(self.rows(s, self.row(h, 1) + half, half), self.rows(left, half, half), fwd),
                self.send(self.rows(s, self.row(h, 3), half), self.rows(right, 0, half), back),
            ])

    def step_two(self):
        half = self.part // 2
        for h in range(2):
            s, near, onward, left, right = (
                ref.at[h]
                for ref in (self.r.given, self.b_near, self.b_onward, self.b_left, self.b_right)
            )
            self.copies[h][0].wait_recv()
            add_blocks(onward, 0, [(s, self.row(h, 1)), (near, 0)], half)
            self.copies[h].append(
                self.send(self.rows(onward, 0, half), self.rows(left, 0, half), self.along[h](1))
            )
            self.copies[h][1].wait_recv()
            add_blocks(onward, half, [(s, self.row(h, 3) + half), (near, half)], half)
            self.copies[h].append(
                self.send(self.rows(onward, half, half), self.rows(right, half, half), self.along[h](3))
            )

    def step_three(self):
        self.pieces = []
        for h in range(2):
            for copy in self.copies[h][2:]:
                copy.wait_recv()
            s, left, right, total = (
                ref.at[h] for ref in (self.r.given, self.b_left, self.b_right, self.b_sum)
            )
            add_blocks(total, 0, [(s, self.row(h, 0)), (left, 0), (right, 0)], self.part)
            other = 1 - h
            for k in (2, 1, 3):
                row = lax.rem(self.place[other] + k, 4) * self.piece
                self.pieces.append(
                    self.send(self.rows(total, row, self.piece), self.b_got.at[h, k - 1], self.along[other](k))
                )

    def step_four(self):
        self.pairs = []
        for h in range(2):
            for copy in self.pieces[3 * h : 3 * h + 3]:
                copy.wait_recv()
            row = self.place[1 - h] * self.piece
            sources = [(self.b_sum.at[h], row)] + [(self.b_got.at[h, k], 0) for k in range(3)]
            add_blocks(self.b_piece.at[h], 0, sources, self.piece)
            self.pairs.append(self.send(self.b_piece.at[h], self.b_pair.at[h], self.grid.across))

    def own(self, h):
        return self.row(h, 0) + self.place[1 - h] * self.piece

    def step_five(self):
        self.spread = []
        for h in range(2):
            self.pairs[h].wait_recv()
            result = self.r.result.at[h]
            add_blocks(result, self.own(h), [(self.b_piece.at[h], 0), (self.b_pair.at[h], 0)], self.piece)
            mine = self.rows(result, self.own(h), self.piece)
            for k in (2, 1, 3):
                self.spread.append(self.send(mine, mine, self.along[1 - h](k)))

    def step_six(self):
        half = self.part // 2
        self.copies = []
        for h in range(2):
            for copy in self.spread[3 * h : 3 * h + 3]:
                copy.wait_recv()
            result = self.r.result.at[h]
            first = self.rows(result, self.row(h, 0), half)
            second = self.rows(result, self.row(h, 0) + half, half)
            fwd, back = self.along[h](1), self.along[h](3)
            self.copies.append([
                self.send(first, first, fwd),
                self.send(second, second, back),
                self.send(second, second, fwd),
                self.send(first, first, back),
            ])

    def step_seven(self):
        half = self.part // 2
        for h in range(2):
            result = self.r.result.at[h]
            self.copies[h][0].wait_recv()
            from_left = self.rows(result, self.row(h, 3), half)
            self.copies[h].append(self.send(from_left, from_left, self.along[h](1)))
            self.copies[h][1].wait_recv()
            from_right = self.rows(result, self.row(h, 1) + half, half)
            self.copies[h].append(self.send(from_right, from_right, self.along[h](3)))

    def step_eight(self):
        for h in range(2):
            for copy in self.copies[h][2:]:
                copy.wait_recv()

    def drain(self):
        for copy in self.used:
            copy.wait_send()


class SmallSum:
    def __init__(self, r, grid):
        self.r, self.grid, self.used = r, grid, []

    def send(self, source, target, peer):
        copy = remote(source, target, self.r.s_sends, self.r.s_recvs, len(self.used), peer)
        self.used.append(copy)
        copy.start()

    def add(self, target, ref, count):
        def body(i, carry):
            at_rows = pl.ds(pl.multiple_of(i * 16, 16), 16)
            total = ref[0, at_rows, :].astype(single)
            for k in range(1, count):
                total = total + ref[k, at_rows, :].astype(single)
            target[at_rows, :] = total.astype(bfloat)
            return carry

        lax.fori_loop(0, SMALL // 16, body, 0)

    def step_one(self):
        r, grid = self.r, self.grid
        r.small_in[...] = r.small_wide[...].astype(bfloat)
        r.small_x[grid.x] = r.small_in[...]
        for k in (2, 1, 3):
            self.send(r.small_in, r.small_x.at[grid.x], grid.along_x(k))

    def step_two(self):
        r, grid = self.r, self.grid
        for copy in self.used[:3]:
            copy.wait_recv()
        self.add(r.small_one, r.small_x, 4)
        r.small_y[grid.y] = r.small_one[...]
        for k in (2, 1, 3):
            self.send(r.small_one, r.small_y.at[grid.y], grid.along_y(k))

    def step_three(self):
        r, grid = self.r, self.grid
        for copy in self.used[3:6]:
            copy.wait_recv()
        self.add(r.small_two, r.small_y, 4)
        r.small_z[grid.plane] = r.small_two[...]
        self.send(r.small_two, r.small_z.at[grid.plane], grid.across)

    def step_four(self):
        self.used[6].wait_recv()
        self.add(self.r.small_out, self.r.small_z, 2)

    def drain(self):
        for copy in self.used:
            copy.wait_send()


def backward_kernel(r):
    core, sibling, opposite = tensor_place()
    grid = Grid()
    peers = [sibling, opposite, grid.across]
    peers += [grid.along_x(k) for k in (1, 2, 3)] + [grid.along_y(k) for k in (1, 2, 3)]
    greet(peers)
    moves = Moves(r.moves)

    def fetch(*names):
        return [moves.start(getattr(r, name + "_h"), getattr(r, name)) for name in names]

    def ready(copies):
        for copy in copies:
            copy.wait()

    loads_zero = fetch("section_three")
    loads_one = fetch("out", "qkvc", "log", "qkv", "low")
    loads_two = fetch("section_two", "slope", "act", "dense_low", "dense_in", "dense_out")
    loads_three = fetch("section_one", "images")
    stores = []
    sums = [TensorSum(r, n, r.total) for n in range(3)]
    width = r.out.shape[1]
    upper = GroupSum(r, "u", 0, 768, grid)
    dense = GroupSum(r, "d", 768, 1536, grid)
    lower = GroupSum(r, "l", 2304, 768, grid)
    small = SmallSum(r, grid)
    mixed = MixedSum(r)

    def deliver(array, row, rows, target):
        half = array.shape[1] // 2
        for h in range(2):
            source = r.result.at[h, pl.ds(row, rows), :]
            stores.append(
                moves.start(source, array.at[pl.ds(target, rows), pl.ds(h * half, half)])
            )

    r.small_wide[...] = jnp.zeros_like(r.small_wide)
    gates = [r.gates[:, k : k + 1] for k in range(2)]
    pulls = [r.gate_sums[:, k : k + 1] for k in range(2)]
    mean = gates[0] * pulls[0] + gates[1] * pulls[1]
    experts = lax.broadcasted_iota(jnp.int32, (r.gates.shape[0], EXPERTS), 1)
    grad_logits = 0.0
    for k in range(2):
        pick = r.routes[:, k : k + 1] == experts
        grad_logits = grad_logits + jnp.where(pick, gates[k] * (pulls[k] - mean), 0.0)
    grad_logits = grad_logits.astype(bfloat)
    ready(loads_zero)
    pl.semaphore_wait(pltpu.get_barrier_semaphore(), 9)
    mixed.step_one()
    rows = r.section_three[...]
    normal, unused = normal_of(rows)
    moe_low = (normal * r.gain[3:4, :] + r.shift[3:4, :]).astype(bfloat)
    r.small_wide[0:EXPERTS, :] = dot_first(grad_logits, moe_low)
    grad_normed = r.grad_experts[...].astype(single) + dot_rows(grad_logits, r.router[...])
    grad_in, gain_part, shift_part = norm_back(grad_normed, rows, r.gain[3:4, :])
    grad = r.cotangent[...].astype(single) + grad_in
    r.grad[...] = grad
    r.small_wide[35:36, :] = gain_part
    r.small_wide[39:40, :] = shift_part
    r.small_wide[41:42, :] = jnp.sum(grad, axis=0, keepdims=True)
    ready(loads_one)
    attend_back(r, 1, grad)
    sums[0].start(attend_back_part(r, 1))
    attend_weights(r, 1, 0)
    upper.step_one()
    mixed.step_two()
    sums[0].finish()

    ready(loads_two)
    grad_in, gain_part, shift_part = norm_back(
        r.total[...].astype(single), r.section_two[...], r.gain[2:3, :]
    )
    r.small_wide[34:35, :] = gain_part
    r.small_wide[38:39, :] = shift_part
    grad = r.grad[...] + grad_in
    r.grad[...] = grad
    upper.step_two()
    grad_low = grad.astype(bfloat)
    r.grad_pre[...] = (dot_last(grad_low, r.dense_out[...]) * r.slope[...]).astype(bfloat)
    sums[1].start(lambda at: dot_last(r.grad_pre[...], r.dense_in[at, :]))
    put_grad(r, 768, dot_first(r.dense_low[...], r.grad_pre[...]))
    put_grad(r, 1536, dot_first(r.act[...], grad_low))
    upper.step_three()
    dense.step_one()
    upper.step_four()
    upper.step_five()
    sums[1].finish()

    ready(loads_three)
    grad_in, gain_part, shift_part = norm_back(
        r.total[...].astype(single), r.section_one[...], r.gain[1:2, :]
    )
    r.small_wide[33:34, :] = gain_part
    r.small_wide[37:38, :] = shift_part
    grad = r.grad[...] + grad_in
    r.grad[...] = grad
    r.small_wide[40:41, :] = jnp.sum(grad, axis=0, keepdims=True)
    dense.step_two()
    upper.step_six()
    attend_back(r, 0, grad)
    sums[2].start(attend_back_part(r, 0))
    attend_weights(r, 0, 2304)
    lower.step_one()
    dense.step_three()
    upper.step_seven()
    dense.step_four()
    lower.step_two()
    sums[2].finish()
    dense.step_five()

    grad_in, gain_part, shift_part = norm_back(
        r.total[...].astype(single), r.images[...].astype(single), r.gain[0:1, :]
    )
    r.small_wide[32:33, :] = gain_part
    r.small_wide[36:37, :] = shift_part
    r.input_grad[...] = r.grad[...] + grad_in
    small.step_one()
    lower.step_three()
    dense.step_six()
    small.step_two()
    lower.step_four()
    upper.step_eight()
    deliver(r.qkv_grad, 0, 3 * width, 3 * width)
    deliver(r.out_grad, 3 * width, width, width)
    lower.step_five()
    small.step_three()
    dense.step_seven()
    lower.step_six()
    small.step_four()
    mixed.step_three()
    lower.step_seven()
    dense.step_eight()
    deliver(r.dense_in_grad, 768, 768, 0)
    deliver(r.dense_out_grad, 1536, 768, 0)
    lower.step_eight()
    deliver(r.qkv_grad, 2304, 3 * width, 0)
    deliver(r.out_grad, 2304 + 3 * width, width, 0)
    for one in sums + [upper, dense, lower, small, mixed]:
        one.drain()
    ready(stores)


def moe_kernel(r):
    core, sibling, opposite = tensor_place()
    dp = lax.axis_index("dp")
    grid = Grid()
    half = r.arrived.shape[3] // 2
    tokens = r.slots.shape[0]
    block = 4 * STRIDE
    barrier = pltpu.get_barrier_semaphore()

    def greet_one(k, carry):
        pl.semaphore_signal(barrier, inc=1, device_id={"dp": dp_peer(k)}, device_id_type=MESH)
        return carry

    lax.fori_loop(1, EXPERTS, greet_one, 0)
    greet([sibling, opposite])
    moves = Moves(r.moves)
    load_in = moves.start(r.expert_in_h.at[0], r.expert_in)
    load_out = moves.start(r.expert_out_h.at[0], r.expert_out)
    own_block = moves.start(r.sent.at[core, dp], r.arrived.at[core, dp])
    pl.semaphore_wait(barrier, EXPERTS + 1)

    def dispatch(peer, here):
        return pltpu.make_async_remote_copy(
            src_ref=r.sent.at[core, peer],
            dst_ref=r.arrived.at[core, here],
            send_sem=r.send_sems.at[peer],
            recv_sem=r.recv_sems.at[here],
            device_id={"dp": peer},
            device_id_type=MESH,
        )

    def share(source):
        block_ref = r.arrived.at[core, source]
        return remote(block_ref, block_ref, r.pass_sems, r.land_sems, source, sibling)

    def swap(source):
        return remote(r.give.at[source], r.got.at[source], r.give_sems, r.got_sems, source, sibling)

    def answer(peer, here):
        return pltpu.make_async_remote_copy(
            src_ref=r.answer.at[peer],
            dst_ref=r.returned.at[here],
            send_sem=r.back_sems.at[peer],
            recv_sem=r.home_sems.at[here],
            device_id={"dp": peer},
            device_id_type=MESH,
        )

    def offsets(p):
        return lax.rem(p, 2), lax.rem(p // 2 + lax.rem(p, 2), 4)

    def send_block(p, carry):
        dz, dx = offsets(p)
        base = lax.rem(grid.plane + dz, 2) * 16 + lax.rem(grid.x + dx, 4) * 4
        for dy in range(4):
            peer = base + lax.rem(grid.y + dy, 4)

            @pl.when(peer != dp)
            def start():
                dispatch(peer, dp).start()

        return carry

    def base_of(p):
        dz, dx = offsets(p)
        return lax.rem(grid.plane + dz, 2) * 16 + lax.rem(grid.x + 4 - dx, 4) * 4

    def receive(p):
        base = base_of(p)
        for dy in range(4):
            source = base + lax.rem(grid.y + 4 - dy, 4)

            @pl.when(source != dp)
            def wait():
                dispatch(source, source).wait_recv()

            @pl.when(source == dp)
            def wait_own():
                own_block.wait()

            share(source).start()

    def compute(p):
        base = base_of(p)
        for y in range(4):
            share(base + y).wait_recv()
            at = slice(y * STRIDE, (y + 1) * STRIDE)
            for h in range(2):
                rows = r.arrived[h, base + y].astype(single)
                r.wide_x[at, h * half : (h + 1) * half] = rows[:, :half]
                r.wide_g[at, h * half : (h + 1) * half] = rows[:, half:]
        at = pl.ds(pl.multiple_of(p * block, 16), block)
        rows = r.wide_x[...].astype(bfloat)
        rows_grad = r.wide_g[...].astype(bfloat)
        r.rows[at, :] = rows
        r.rows_grad[at, :] = rows_grad
        pre = dot_rows(rows, r.expert_in[...])
        grad_act = dot_last(rows_grad, r.expert_out[...])
        tail = 0.5 * (1.0 + lax.erf(pre * (0.5**0.5)))
        act = (pre * tail).astype(bfloat)
        slope = tail + pre * (jnp.exp(-0.5 * pre * pre) * 0.3989422804014327)
        grad_pre = (grad_act * slope).astype(bfloat)
        r.act[at, :] = act
        r.grad_pre[at, :] = grad_pre
        r.wide_x[...] = dot_rows(act, r.expert_out[...])
        r.wide_g[...] = dot_last(grad_pre, r.expert_in[...])
        for y in range(4):
            at = slice(y * STRIDE, (y + 1) * STRIDE)
            for which, target in ((1 - core, r.give), (core, r.kept)):
                columns = pl.ds(pl.multiple_of(which * half, LANES), half)
                target[base + y, :, :half] = r.wide_x[at, columns].astype(bfloat)
                target[base + y, :, half:] = r.wide_g[at, columns].astype(bfloat)
            swap(base + y).start()

    def respond(p):
        base = base_of(p)
        for y in range(4):
            source = base + y
            swap(source).wait_recv()
            total = r.kept[source].astype(single) + r.got[source].astype(single)
            r.answer[source] = total.astype(bfloat)

            @pl.when(source != dp)
            def start():
                answer(source, dp).start()

            @pl.when(source == dp)
            def keep():
                r.returned[dp] = total.astype(bfloat)

    def step(i, carry):
        pl.when(i < 8)(lambda: receive(i))
        pl.when((i >= 1) & (i < 9))(lambda: compute(i - 1))
        pl.when(i >= 2)(lambda: respond(i - 2))
        return carry

    lax.fori_loop(0, 8, send_block, 0)
    load_in.wait()
    load_out.wait()
    lax.fori_loop(0, 10, step, 0)
    r.weight_grad[0] = dot_first(r.act[...], r.rows_grad[...])
    store_out = moves.start(r.weight_grad.at[0], r.expert_out_grad.at[0])
    r.weight_grad[1] = dot_first(r.rows[...], r.grad_pre[...])
    store_in = moves.start(r.weight_grad.at[1], r.expert_in_grad.at[0])

    ids = lax.broadcasted_iota(jnp.int32, (tokens, SLOTS), 1)
    for k in range(2):
        r.hits[k] = jnp.where(ids == r.slots[:, k : k + 1], 1.0, 0.0).astype(bfloat)

    def come_home(i, carry):
        p, dy = i // 4, lax.rem(i, 4)
        dz, dx = offsets(p)
        source = lax.rem(grid.plane + dz, 2) * 16 + lax.rem(grid.x + dx, 4) * 4 + lax.rem(grid.y + dy, 4)

        @pl.when(source != dp)
        def wait():
            answer(source, source).wait_recv()

        at = pl.ds(pl.multiple_of(source * STRIDE, 8), STRIDE)
        r.wide_home[at, :] = r.returned[source].astype(single)
        return carry

    lax.fori_loop(0, EXPERTS, come_home, 0)
    back = r.wide_home[:, half:].astype(bfloat)
    r.home[...] = r.wide_home[:, :half].astype(bfloat)
    own = r.cotangent[:, pl.ds(pl.multiple_of(core * half, LANES), half)].astype(single)

    second = [remote(r.part.at[j], r.part_got.at[j], r.z_sends, r.z_recvs, j, opposite) for j in range(4)]
    third = [remote(r.part_sum.at[j], r.part_end.at[j], r.z_sends, r.z_recvs, 4 + j, sibling) for j in range(4)]
    normed = dot_rows(r.hits[0], back) + dot_rows(r.hits[1], back)
    for j in range(3):
        r.part[j] = normed[:, j * LANES : (j + 1) * LANES].astype(bfloat)
        second[j].start()
    picked = [dot_rows(r.hits[k], r.home[...]) for k in range(2)]
    gate = [jnp.sum(p * own, axis=1, keepdims=True) for p in picked]
    lane = lax.broadcasted_iota(jnp.int32, (tokens, LANES), 1)
    spread = jnp.where(lane == 0, gate[0], jnp.where(lane == 1, gate[1], 0.0))
    r.part[3] = spread.astype(bfloat)
    second[3].start()
    mixed = r.gates[:, 0:1] * picked[0] + r.gates[:, 1:2] * picked[1]
    for j in range(3):
        r.mixed[j] = mixed[:, j * LANES : (j + 1) * LANES].astype(bfloat)

    def columns(which, j):
        return pl.ds(pl.multiple_of((which * THIRDS + j) * LANES, LANES), LANES)

    for j in range(4):
        second[j].wait_recv()
        whole = (r.part[j].astype(single) + r.part_got[j].astype(single)).astype(bfloat)
        r.part_sum[j] = whole
        third[j].start()
        if j < 3:
            r.grad_experts[:, columns(core, j)] = whole
    for j in range(4):
        third[j].wait_recv()
        if j < 3:
            r.grad_experts[:, columns(1 - core, j)] = r.part_end[j]
        else:
            r.gate_sums[...] = r.part_sum[j].astype(single) + r.part_end[j].astype(single)
    for copy in second + third:
        copy.wait_send()

    def drain(k, carry):
        share(k).wait_send()
        swap(k).wait_send()

        @pl.when(k != dp)
        def wait():
            dispatch(k, dp).wait_send()
            answer(k, dp).wait_send()

        return carry

    lax.fori_loop(0, EXPERTS, drain, 0)
    store_out.wait()
    store_in.wait()


def moe_whole(sent, slots, gates, cotangent, expert_in, expert_out, collective_id):
    tokens, width = cotangent.shape
    half = width // 2
    slab = pltpu.VMEM((EXPERTS, STRIDE, width), bfloat)
    rows = pltpu.VMEM((SLOTS, width), bfloat)
    parts = pltpu.VMEM((4, tokens, LANES), bfloat)
    block = pltpu.VMEM((4 * STRIDE, width), single)
    every = pltpu.SemaphoreType.DMA((EXPERTS,))
    scratch = {name: slab for name in ("give", "kept", "got", "answer", "returned")}
    scratch.update({name: rows for name in ("rows", "rows_grad", "act", "grad_pre")})
    scratch.update({name: parts for name in ("part", "part_got", "part_sum", "part_end")})
    names = ("send", "recv", "pass", "land", "give", "got", "back", "home")
    scratch.update({name + "_sems": every for name in names})
    scratch.update(
        arrived=pltpu.VMEM((2, EXPERTS, STRIDE, width), bfloat),
        expert_in=pltpu.VMEM(expert_in.shape[1:], bfloat),
        expert_out=pltpu.VMEM(expert_out.shape[1:], bfloat),
        weight_grad=pltpu.VMEM((2,) + expert_in.shape[1:], single),
        wide_x=block,
        wide_g=block,
        wide_home=pltpu.VMEM((SLOTS, width), single),
        home=pltpu.VMEM((SLOTS, half), bfloat),
        hits=pltpu.VMEM((2, tokens, SLOTS), bfloat),
        z_sends=pltpu.SemaphoreType.DMA((8,)),
        z_recvs=pltpu.SemaphoreType.DMA((8,)),
        moves=pltpu.SemaphoreType.DMA((8,)),
    )
    return big_call(
        moe_kernel,
        "moe",
        {
            "sent": (sent.reshape(2, EXPERTS, STRIDE, width), "hbm"),
            "slots": (slots, "vmem"),
            "gates": (gates, "vmem"),
            "cotangent": (cotangent, "vmem"),
            "expert_in_h": (expert_in, "hbm"),
            "expert_out_h": (expert_out, "hbm"),
        },
        {
            "expert_in_grad": (expert_in.shape, single, "hbm"),
            "expert_out_grad": (expert_out.shape, single, "hbm"),
            "mixed": ((3, tokens, LANES), bfloat, "vmem"),
            "grad_experts": ((tokens, width), bfloat, "vmem"),
            "gate_sums": ((tokens, LANES), single, "vmem"),
        },
        scratch,
        collective_id,
    )


class MixedSum:
    def __init__(self, r):
        core, sibling, opposite = tensor_place()
        self.r, self.core = r, core
        self.second = [
            remote(r.mixed.at[j], r.m_got.at[j], r.m_sends, r.m_recvs, j, opposite) for j in range(3)
        ]
        self.third = [
            remote(r.m_sum.at[j], r.m_end.at[j], r.m_sends, r.m_recvs, 3 + j, sibling) for j in range(3)
        ]

    def step_one(self):
        for copy in self.second:
            copy.start()

    def step_two(self):
        r = self.r
        for j in range(3):
            self.second[j].wait_recv()
            whole = r.mixed[j].astype(single) + r.m_got[j].astype(single)
            r.m_sum[j] = whole.astype(bfloat)
            self.third[j].start()
            self.put(self.core, j, r.m_sum[j])

    def put(self, which, j, value):
        at = pl.ds(pl.multiple_of((which * THIRDS + j) * LANES, LANES), LANES)
        rows = self.r.section_three[:, at] + value.astype(single)
        self.r.output[:, at] = rows.astype(bfloat)

    def step_three(self):
        for j in range(3):
            self.third[j].wait_recv()
            self.put(1 - self.core, j, self.r.m_end[j])

    def drain(self):
        for copy in self.second + self.third:
            copy.wait_send()


def finish_kernel(r):
    moves = Moves(r.moves)
    names = ("qkv", "out", "dense_in", "dense_out")
    loads = [moves.start(getattr(r, name + "_h"), getattr(r, name + "_low")) for name in names]
    stores = [
        moves.start(getattr(r, name + "_h"), getattr(r, name + "_f"))
        for name in ("expert_in", "expert_out", "input_grad", "output")
    ]
    small = r.small[...].astype(single)
    part = r.qv_bias.shape[2]
    r.router[...] = small[:EXPERTS]
    r.gain[...] = small[32:36]
    r.shift[...] = small[36:40]
    r.out_bias[...] = small[40:42]
    r.qv_bias[0] = small[42:44, :part]
    r.qv_bias[1] = small[44:46, :part]
    for name, load in zip(names, loads):
        load.wait()
        low, wide = getattr(r, name + "_low"), getattr(r, name + "_wide")
        rows = low.shape[0]
        piece = 192

        def cast(i, carry):
            at = pl.ds(pl.multiple_of(i * piece, 16), piece)
            wide[at, :] = low[at, :].astype(single)
            return carry

        lax.fori_loop(0, rows // piece, cast, 0)
        stores.append(moves.start(wide, getattr(r, name + "_f")))
    for store in stores:
        store.wait()


def finish(last, moe, part, width):
    arrays = {"qkv": last.qkv_grad, "out": last.out_grad}
    arrays.update({"dense_in": last.dense_in_grad, "dense_out": last.dense_out_grad})
    ins = {name + "_h": (array, "hbm") for name, array in arrays.items()}
    ins["small"] = (last.small_out, "vmem")
    outs = {name + "_f": (array.shape, single, "hbm") for name, array in arrays.items()}
    whole = {"expert_in": moe.expert_in_grad, "expert_out": moe.expert_out_grad}
    whole.update(input_grad=last.input_grad, output=last.output)
    for name, array in whole.items():
        ins[name + "_h"] = (array, "hbm")
        outs[name + "_f"] = (array.shape, array.dtype, "hbm")
    outs.update(
        router=((EXPERTS, width), single, "vmem"),
        gain=((4, width), single, "vmem"),
        shift=((4, width), single, "vmem"),
        out_bias=((2, width), single, "vmem"),
        qv_bias=((2, 2, part), single, "vmem"),
    )
    scratch = {name + "_low": pltpu.VMEM(array.shape, bfloat) for name, array in arrays.items()}
    scratch.update({name + "_wide": pltpu.VMEM(a.shape, single) for name, a in arrays.items()})
    scratch["moves"] = pltpu.SemaphoreType.DMA((12,))
    return big_call(finish_kernel, "finish", ins, outs, scratch)


def per_device(
    images,
    routes,
    cotangent,
    qkv_weight,
    out_weight,
    qv_bias,
    out_bias,
    ln_gain,
    ln_bias,
    dense_in,
    dense_out,
    router,
    expert_in,
    expert_out,
):
    tokens, width = images.shape
    part = out_weight.shape[1]
    hidden = dense_in.shape[1]
    qkv = jnp.transpose(qkv_weight, (0, 2, 3, 1)).reshape(2, 3 * part, width)
    full, low = (tokens, width), bfloat
    kept = {
        "section_one": (full, single),
        "section_two": (full, single),
        "section_three": (full, single),
        "dense_low": (full, low),
        "slope": ((tokens, hidden), single),
        "act": ((tokens, hidden), low),
        "low": ((2, tokens, width), low),
        "qkvc": ((2, 4, tokens, part), low),
        "log": ((2, tokens, part // HEAD), single),
    }
    weights = {
        "dense_in": (dense_in.shape, low),
        "dense_out": (dense_out.shape, low),
    }

    def vmem(names, table):
        return {name: pltpu.VMEM(*table[name]) for name in names}

    sections = ("section_one", "section_two", "section_three")
    outs = {name + ("" if name in sections else "_h"): kept[name] + ("hbm",) for name in kept}
    outs["sent"] = ((2, SLOTS, width), low, "hbm")
    outs["gates"] = ((tokens, 2), single, "vmem")
    outs["slots"] = ((tokens, 2), jnp.int32, "vmem")
    outs["routes"] = ((tokens, 2), jnp.int32, "vmem")
    scratch = sum_scratch(tokens, 3)
    scratch.update(vmem([name for name in kept if name not in sections], kept))
    scratch.update(vmem(list(weights), weights))
    scratch.update(
        section=pltpu.VMEM((3, tokens, width), single),
        cotangent=pltpu.VMEM(full, low),
        moe_low=pltpu.VMEM(full, low),
        scaled=pltpu.VMEM((2, tokens, width), low),
        routed=pltpu.VMEM((2, SLOTS, width), low),
        total=pltpu.VMEM(full, low),
        moves=pltpu.SemaphoreType.DMA((24,)),
    )
    done = big_call(
        forward_kernel,
        "forward",
        {
            "images": (images, "vmem"),
            "qkv": (qkv, "vmem"),
            "out": (out_weight, "vmem"),
            "qv_bias": (qv_bias, "vmem"),
            "out_bias": (out_bias, "vmem"),
            "gain": (ln_gain, "vmem"),
            "shift": (ln_bias, "vmem"),
            "dense_in_h": (dense_in, "hbm"),
            "dense_out_h": (dense_out, "hbm"),
            "cotangent_h": (cotangent, "hbm"),
            "routes_row": (routes.T, "vmem"),
            "router": (router.T, "vmem"),
        },
        outs,
        scratch,
        1,
    )
    moe = moe_whole(done.sent, done.slots, done.gates, cotangent, expert_in, expert_out, 3)

    outs = {
        "output": (full, low, "vmem"),
        "input_grad": (full, single, "vmem"),
        "qkv_grad": ((6 * part, width), low, "hbm"),
        "out_grad": ((2 * part, width), low, "hbm"),
        "dense_in_grad": (dense_in.shape, low, "hbm"),
        "dense_out_grad": (dense_out.shape, low, "hbm"),
        "small_out": ((SMALL, width), low, "vmem"),
    }
    scratch = sum_scratch(tokens, 3)
    scratch.update(vmem(list(kept), kept))
    scratch.update(vmem(list(weights), weights))
    for tag, rows in (("u", 768), ("d", 1536), ("l", 768)):
        scratch.update(group_scratch(tag, rows, width // 2))
    block = pltpu.VMEM((SMALL, width), low)
    scratch.update(
        images=pltpu.VMEM(full, low),
        qkv=pltpu.VMEM(qkv.shape, low),
        out=pltpu.VMEM(out_weight.shape, low),
        total=pltpu.VMEM(full, low),
        grad=pltpu.VMEM(full, single),
        grad_low=pltpu.VMEM(full, low),
        grad_pre=pltpu.VMEM((tokens, hidden), low),
        grad_qkv=pltpu.VMEM((3, tokens, part), low),
        given=pltpu.VMEM((2, BIG, width // 2), low),
        result=pltpu.VMEM((2, BIG, width // 2), low),
        small_wide=pltpu.VMEM((SMALL, width), single),
        small_in=block,
        small_one=block,
        small_two=block,
        small_x=pltpu.VMEM((4, SMALL, width), low),
        small_y=pltpu.VMEM((4, SMALL, width), low),
        small_z=pltpu.VMEM((2, SMALL, width), low),
        m_got=pltpu.VMEM((3, tokens, LANES), low),
        m_sum=pltpu.VMEM((3, tokens, LANES), low),
        m_end=pltpu.VMEM((3, tokens, LANES), low),
        m_sends=pltpu.SemaphoreType.DMA((6,)),
        m_recvs=pltpu.SemaphoreType.DMA((6,)),
        s_sends=pltpu.SemaphoreType.DMA((7,)),
        s_recvs=pltpu.SemaphoreType.DMA((7,)),
        moves=pltpu.SemaphoreType.DMA((32,)),
    )
    ins = {
        "mixed": (moe.mixed, "vmem"),
        "grad_experts": (moe.grad_experts, "vmem"),
        "gate_sums": (moe.gate_sums, "vmem"),
        "gates": (done.gates, "vmem"),
        "routes": (done.routes, "vmem"),
        "router": (router.T, "vmem"),
        "cotangent": (cotangent, "vmem"),
        "gain": (ln_gain, "vmem"),
        "shift": (ln_bias, "vmem"),
        "images_h": (images, "hbm"),
        "qkv_h": (qkv, "hbm"),
        "out_h": (out_weight, "hbm"),
        "dense_in_h": (dense_in, "hbm"),
        "dense_out_h": (dense_out, "hbm"),
    }
    for name in kept:
        ins[name + "_h"] = (getattr(done, name if name in sections else name + "_h"), "hbm")
    last = big_call(backward_kernel, "backward", ins, outs, scratch, 2)
    end = finish(last, moe, part, width)
    qkv_weight_grad = jnp.transpose(end.qkv_f.reshape(2, 3, part, width), (0, 3, 1, 2))
    out_weight_grad = end.out_f.reshape(2, part, width)
    dense_in_grad, dense_out_grad = end.dense_in_f, end.dense_out_f
    router_grad = end.router.T
    ln_gain_grad, ln_bias_grad, out_bias_grad = end.gain, end.shift, end.out_bias
    qv_bias_grad = end.qv_bias
    output, input_grad = end.output_f, end.input_grad_f
    expert_in_grad, expert_out_grad = end.expert_in_f, end.expert_out_f
    return (
        output,
        input_grad,
        qkv_weight_grad,
        out_weight_grad,
        qv_bias_grad,
        out_bias_grad,
        ln_gain_grad,
        ln_bias_grad,
        dense_in_grad,
        dense_out_grad,
        router_grad,
        expert_in_grad,
        expert_out_grad,
    )


def solution(mesh):
    in_specs = (
        P("dp", None),
        P("dp", None),
        P("dp", None),
        P(None, None, None, "tensor"),
        P(None, "tensor", None),
        P(None, None, "tensor"),
        P(),
        P(),
        P(),
        P(None, "tensor"),
        P("tensor", None),
        P(),
        P("dp", None, "tensor"),
        P("dp", "tensor", None),
    )
    out_specs = (
        P("dp", None),
        P("dp", None),
        P(None, None, None, "tensor"),
        P(None, "tensor", None),
        P(None, None, "tensor"),
        P(),
        P(),
        P(),
        P(None, "tensor"),
        P("tensor", None),
        P(),
        P("dp", None, "tensor"),
        P("dp", "tensor", None),
    )
    return jax.shard_map(
        per_device, mesh=mesh, in_specs=in_specs, out_specs=out_specs, check_vma=False
    )
```

```python
import functools

import jax
import jax.numpy as jnp
from jax import lax
from jax.experimental import pallas as pl
from jax.experimental.pallas import tpu as pltpu
from jax.sharding import PartitionSpec as P

HEAD = 64
SEQ = 197


epsilon = 1e-06
bfloat = jnp.bfloat16
single = jnp.float32


MESH = pl.DeviceIdType.MESH


BIG = 3072
SMALL = 48
EXPERTS = 32
STRIDE = 40
SLOTS = EXPERTS * STRIDE


def dot_rows(a, b):
    return lax.dot_general(a, b, (((1,), (0,)), ((), ())), preferred_element_type=single)


def dot_last(a, b):
    return lax.dot_general(a, b, (((1,), (1,)), ((), ())), preferred_element_type=single)


def dot_first(a, b):
    return lax.dot_general(a, b, (((0,), (0,)), ((), ())), preferred_element_type=single)


VMEM_SPEC = pl.BlockSpec(memory_space=pltpu.VMEM)


def dp_peer(k):
    dp = lax.axis_index("dp")
    plane = lax.rem(dp // 16 + k // 16, 2)
    x = lax.rem(lax.rem(dp // 4, 4) + lax.rem(k // 4, 4), 4)
    y = lax.rem(lax.rem(dp, 4) + lax.rem(k, 4), 4)
    return plane * 16 + x * 4 + y


def normal_of(rows):
    average = jnp.mean(rows, axis=-1, keepdims=True)
    centered = rows - average
    variance = jnp.mean(centered * centered, axis=-1, keepdims=True)
    inverse = lax.rsqrt(variance + epsilon)
    return centered * inverse, inverse


def norm_back(grad_normed, rows, gain_row):
    normal, inverse = normal_of(rows)
    scaled = grad_normed * gain_row
    mean_one = jnp.mean(scaled, axis=-1, keepdims=True)
    mean_two = jnp.mean(scaled * normal, axis=-1, keepdims=True)
    grad_in = inverse * (scaled - mean_one - normal * mean_two)
    gain_part = jnp.sum(grad_normed * normal, axis=0, keepdims=True)
    return grad_in, gain_part, jnp.sum(grad_normed, axis=0, keepdims=True)


def same_image(tokens):
    first = lax.broadcasted_iota(jnp.int32, (tokens, tokens), 0) // SEQ
    second = lax.broadcasted_iota(jnp.int32, (tokens, tokens), 1) // SEQ
    return first == second


class Refs:
    def __init__(self, names, refs):
        for name, ref in zip(names, refs):
            setattr(self, name, ref)


def big_call(kernel, name, ins, outs, scratch, collective_id=None, limit=58):
    names = list(ins) + list(outs) + list(scratch)
    hbm = pl.BlockSpec(memory_space=pl.ANY)

    def body(*refs):
        kernel(Refs(names, refs))

    found = pl.pallas_call(
        body,
        out_shape=[jax.ShapeDtypeStruct(shape, kind) for shape, kind, unused in outs.values()],
        in_specs=[hbm if place == "hbm" else VMEM_SPEC for unused, place in ins.values()],
        out_specs=[hbm if place == "hbm" else VMEM_SPEC for _, _, place in outs.values()],
        scratch_shapes=list(scratch.values()),
        compiler_params=pltpu.CompilerParams(
            collective_id=collective_id, has_side_effects=True, vmem_limit_bytes=limit * 2**20
        ),
        name=name,
    )(*[array for array, unused in ins.values()])
    return Refs(list(outs), found)


def tensor_place():
    t = lax.axis_index("tensor")
    core = lax.rem(t, 2)
    return core, {"tensor": t + 1 - 2 * core}, {"tensor": lax.rem(t + 2, 4)}


def remote(source, target, sends, recvs, index, peer):
    return pltpu.make_async_remote_copy(
        src_ref=source,
        dst_ref=target,
        send_sem=sends.at[index],
        recv_sem=recvs.at[index],
        device_id=peer,
        device_id_type=MESH,
    )


LANES = 128
THIRDS = 3


def sum_scratch(tokens, count):
    block = pltpu.VMEM((count, THIRDS, tokens, LANES), bfloat)
    names = ["give", "got_one", "sum_one", "got_two", "sum_two", "got_three"]
    found = {"t_" + name: block for name in names}
    found["t_own"] = pltpu.VMEM((tokens, THIRDS * LANES), single)
    found["t_sends"] = pltpu.SemaphoreType.DMA((count * 9,))
    found["t_recvs"] = pltpu.SemaphoreType.DMA((count * 9,))
    return found


class TensorSum:
    def __init__(self, r, number, total_ref):
        core, sibling, opposite = tensor_place()
        self.core, self.r, self.n, self.total = core, r, number, total_ref

        def copies(source, target, step, peer):
            return [
                remote(source.at[number, j], target.at[number, j], r.t_sends, r.t_recvs, number * 9 + step * 3 + j, peer)
                for j in range(THIRDS)
            ]

        self.first = copies(r.t_give, r.t_got_one, 0, sibling)
        self.second = copies(r.t_sum_one, r.t_got_two, 1, opposite)
        self.third = copies(r.t_sum_two, r.t_got_three, 2, sibling)

    def columns(self, which, j=0, count=1):
        return pl.ds(pl.multiple_of((which * THIRDS + j) * LANES, LANES), count * LANES)

    def start(self, partial):
        r, n = self.r, self.n
        other = partial(self.columns(1 - self.core, 0, THIRDS)).astype(bfloat)
        for j in range(THIRDS):
            r.t_give[n, j] = other[:, j * LANES : (j + 1) * LANES]
            self.first[j].start()
        r.t_own[...] = partial(self.columns(self.core, 0, THIRDS))
        for j in range(THIRDS):
            self.first[j].wait_recv()
            own = r.t_own[:, j * LANES : (j + 1) * LANES]
            r.t_sum_one[n, j] = (own + r.t_got_one[n, j].astype(single)).astype(bfloat)
            self.second[j].start()

    def finish(self):
        r, n = self.r, self.n
        for j in range(THIRDS):
            self.second[j].wait_recv()
            whole = (r.t_sum_one[n, j].astype(single) + r.t_got_two[n, j].astype(single)).astype(bfloat)
            r.t_sum_two[n, j] = whole
            self.third[j].start()
            self.total[:, self.columns(self.core, j)] = whole
        for j in range(THIRDS):
            self.third[j].wait_recv()
            self.total[:, self.columns(1 - self.core, j)] = r.t_got_three[n, j]

    def drain(self):
        for copy in self.first + self.second + self.third:
            copy.wait_send()


class Moves:
    def __init__(self, sems):
        self.sems, self.count = sems, 0

    def start(self, source, target):
        copy = pltpu.make_async_copy(source, target, self.sems.at[self.count])
        self.count += 1
        copy.start()
        return copy


def greet(peers):
    barrier = pltpu.get_barrier_semaphore()
    for peer in peers:
        pl.semaphore_signal(barrier, inc=1, device_id=peer, device_id_type=MESH)


def attend(r, rows, layer):
    width = r.out.shape[1]
    norm = 2 * layer
    normal, unused = normal_of(rows)
    low = (normal * r.gain[norm : norm + 1, :] + r.shift[norm : norm + 1, :]).astype(bfloat)
    r.low[layer] = low
    bias = r.qv_bias[layer]
    q = (dot_last(low, r.qkv[layer, :width, :]) + bias[0:1, :]).astype(bfloat)
    k = dot_last(low, r.qkv[layer, width : 2 * width, :]).astype(bfloat)
    v = (dot_last(low, r.qkv[layer, 2 * width :, :]) + bias[1:2, :]).astype(bfloat)
    r.qkvc[layer, 0], r.qkvc[layer, 1], r.qkvc[layer, 2] = q, k, v
    same = same_image(rows.shape[0])
    contexts = []
    for h in range(width // HEAD):
        at = slice(h * HEAD, (h + 1) * HEAD)
        scores = jnp.where(same, dot_last(q[:, at], k[:, at]) * HEAD ** (-0.5), -1e30)
        largest = jnp.max(scores, axis=-1, keepdims=True)
        exponent = jnp.exp(scores - largest)
        totals = jnp.sum(exponent, axis=-1, keepdims=True)
        r.log[layer, :, h : h + 1] = largest + jnp.log(totals)
        contexts.append(dot_rows((exponent / totals).astype(bfloat), v[:, at]))
    r.qkvc[layer, 3] = jnp.concatenate(contexts, axis=1).astype(bfloat)


def forward_kernel(r):
    core, sibling, opposite = tensor_place()
    greet([sibling, opposite])
    moves = Moves(r.moves)
    loads = [moves.start(r.dense_in_h, r.dense_in), moves.start(r.dense_out_h, r.dense_out)]
    loads += [moves.start(r.cotangent_h, r.cotangent)]
    stores = []
    sums = [TensorSum(r, n, r.total) for n in range(3)]

    def save(source, target):
        stores.append(moves.start(source, target))

    def out_part(layer):
        return lambda at: dot_rows(r.qkvc[layer, 3], r.out[layer, :, at])

    attend(r, r.images[...].astype(single), 0)
    pl.semaphore_wait(pltpu.get_barrier_semaphore(), 2)
    sums[0].start(out_part(0))
    sums[0].finish()

    rows = r.images[...].astype(single) + r.total[...].astype(single) + r.out_bias[0:1, :]
    r.section[0] = rows
    save(r.section.at[0], r.section_one)
    normal, unused = normal_of(rows)
    low = (normal * r.gain[1:2, :] + r.shift[1:2, :]).astype(bfloat)
    r.dense_low[...] = low
    save(r.dense_low, r.dense_low_h)
    for load in loads:
        load.wait()
    pre = dot_rows(low, r.dense_in[...])
    tail = 0.5 * (1.0 + lax.erf(pre * (0.5**0.5)))
    r.slope[...] = tail + pre * (jnp.exp(-0.5 * pre * pre) * 0.3989422804014327)
    save(r.slope, r.slope_h)
    r.act[...] = (pre * tail).astype(bfloat)
    save(r.act, r.act_h)
    sums[1].start(lambda at: dot_rows(r.act[...], r.dense_out[:, at]))
    sums[1].finish()

    rows = r.section[0] + r.total[...].astype(single)
    r.section[1] = rows
    save(r.section.at[1], r.section_two)
    attend(r, rows, 1)
    save(r.low, r.low_h)
    save(r.qkvc, r.qkvc_h)
    save(r.log, r.log_h)
    sums[2].start(out_part(1))
    sums[2].finish()

    rows = r.section[1] + r.total[...].astype(single) + r.out_bias[1:2, :]
    r.section[2] = rows
    save(r.section.at[2], r.section_three)
    moe_route_body(r, rows, save)
    for one in sums:
        one.drain()
    for store in stores:
        store.wait()


def moe_route_body(r, rows, save):
    tokens, width = rows.shape
    half = width // 2
    normal, unused = normal_of(rows)
    r.moe_low[...] = (normal * r.gain[3:4, :] + r.shift[3:4, :]).astype(bfloat)
    logits = dot_last(r.moe_low[...], r.router[...])
    experts = lax.broadcasted_iota(jnp.int32, (tokens, EXPERTS), 1)
    before = lax.broadcasted_iota(jnp.int32, (tokens, tokens), 0)
    after = lax.broadcasted_iota(jnp.int32, (tokens, tokens), 1)
    for k in range(2):
        spread = jnp.where(before == after, r.routes_row[k : k + 1, :].astype(single), 0.0)
        r.routes[:, k : k + 1] = jnp.sum(spread, axis=1, keepdims=True).astype(jnp.int32)
    picks = [r.routes[:, k : k + 1] == experts for k in range(2)]
    chosen = [jnp.sum(jnp.where(pick, logits, 0.0), axis=1, keepdims=True) for pick in picks]
    largest = jnp.maximum(chosen[0], chosen[1])
    powers = [jnp.exp(c - largest) for c in chosen]
    total = powers[0] + powers[1]
    gates = [power / total for power in powers]
    r.gates[:, 0:1] = gates[0]
    r.gates[:, 1:2] = gates[1]
    cotangent = r.cotangent[...].astype(single)
    for k in range(2):
        r.scaled[k] = (gates[k] * cotangent).astype(bfloat)

    either = [jnp.where(pick, 1.0, 0.0) for pick in picks]
    lower = jnp.where(after < before, 1.0, 0.0).astype(bfloat)
    running = dot_rows(lower, (either[0] + either[1]).astype(bfloat))
    for k in range(2):
        rank = jnp.sum(running * either[k], axis=1, keepdims=True).astype(jnp.int32)
        r.slots[:, k : k + 1] = r.routes[:, k : k + 1] * STRIDE + rank

    experts_row = lax.broadcasted_iota(jnp.int32, (EXPERTS, tokens), 0)
    either_row = [jnp.where(r.routes_row[k : k + 1, :] == experts_row, 1.0, 0.0) for k in range(2)]
    upper = jnp.where(before < after, 1.0, 0.0).astype(bfloat)
    running_row = dot_rows((either_row[0] + either_row[1]).astype(bfloat), upper)
    slots_row = []
    for k in range(2):
        rank = jnp.sum(running_row * either_row[k], axis=0, keepdims=True).astype(jnp.int32)
        slots_row.append(r.routes_row[k : k + 1, :] * STRIDE + rank)

    block = SLOTS // 4
    for i in range(4):
        ids = lax.broadcasted_iota(jnp.int32, (block, tokens), 0) + i * block
        hits = [jnp.where(ids == slots_row[k], 1.0, 0.0) for k in range(2)]
        moved = dot_rows((hits[0] + hits[1]).astype(bfloat), r.moe_low[...]).astype(bfloat)
        moved_grad = (
            dot_rows(hits[0].astype(bfloat), r.scaled[0]) + dot_rows(hits[1].astype(bfloat), r.scaled[1])
        ).astype(bfloat)
        at = slice(i * block, (i + 1) * block)
        for h in range(2):
            r.routed[h, at, :half] = moved[:, h * half : (h + 1) * half]
            r.routed[h, at, half:] = moved_grad[:, h * half : (h + 1) * half]
            save(r.routed.at[h, pl.ds(i * block, block), :], r.sent.at[h, pl.ds(i * block, block), :])


def attend_back(r, layer, grad_out):
    width = r.out.shape[1]
    grad_low = grad_out.astype(bfloat)
    r.grad_low[...] = grad_low
    q, k, v = r.qkvc[layer, 0], r.qkvc[layer, 1], r.qkvc[layer, 2]
    grad_context = dot_last(grad_low, r.out[layer]).astype(bfloat)
    same = same_image(q.shape[0])
    grads = [[], [], []]
    for h in range(width // HEAD):
        at = slice(h * HEAD, (h + 1) * HEAD)
        scores = jnp.where(same, dot_last(q[:, at], k[:, at]) * HEAD ** (-0.5), -1e30)
        probs = jnp.exp(scores - r.log[layer, :, h : h + 1])
        grad_probs = dot_last(grad_context[:, at], v[:, at])
        row_total = jnp.sum(probs * grad_probs, axis=-1, keepdims=True)
        grad_scores = (probs * (grad_probs - row_total)).astype(bfloat)
        grads[0].append(dot_rows(grad_scores, k[:, at]) * HEAD ** (-0.5))
        grads[1].append(dot_first(grad_scores, q[:, at]) * HEAD ** (-0.5))
        grads[2].append(dot_first(probs.astype(bfloat), grad_context[:, at]))
    for part in range(3):
        r.grad_qkv[part] = jnp.concatenate(grads[part], axis=1).astype(bfloat)


def attend_weights(r, layer, base):
    width = r.out.shape[1]
    put_grad(r, base + 3 * width, dot_first(r.qkvc[layer, 3], r.grad_low[...]))
    for part in range(3):
        grad = r.grad_qkv[part]
        put_grad(r, base + part * width, dot_first(grad, r.low[layer]))
        if part != 1:
            row = 42 + 2 * layer + part // 2
            r.small_wide[row : row + 1, :width] = jnp.sum(grad.astype(single), axis=0, keepdims=True)


def attend_back_part(r, layer):
    width = r.out.shape[1]

    def partial(at):
        total = None
        for part in range(3):
            term = dot_rows(r.grad_qkv[part], r.qkv[layer, part * width : (part + 1) * width, at])
            total = term if total is None else total + term
        return total

    return partial


def put_grad(r, row, value):
    low = value.astype(bfloat)
    half = low.shape[1] // 2
    for h in range(2):
        r.given[h, row : row + low.shape[0], :] = low[:, h * half : (h + 1) * half]


def add_blocks(target, row, sources, rows):
    def body(i, carry):
        total = None
        for ref, start in sources:
            value = ref[pl.ds(pl.multiple_of(start + i * 16, 16), 16), :].astype(single)
            total = value if total is None else total + value
        target[pl.ds(pl.multiple_of(row + i * 16, 16), 16), :] = total.astype(bfloat)
        return carry

    lax.fori_loop(0, rows // 16, body, 0)


GROUP_COPIES = 38


def group_scratch(tag, rows, width):
    part, piece = rows // 4, rows // 16
    found = {}
    for name in ("near", "left", "right", "onward", "sum"):
        found[f"{tag}_{name}"] = pltpu.VMEM((2, part, width), bfloat)
    found[f"{tag}_got"] = pltpu.VMEM((2, 3, piece, width), bfloat)
    found[f"{tag}_piece"] = pltpu.VMEM((2, piece, width), bfloat)
    found[f"{tag}_pair"] = pltpu.VMEM((2, piece, width), bfloat)
    found[f"{tag}_sends"] = pltpu.SemaphoreType.DMA((GROUP_COPIES,))
    found[f"{tag}_recvs"] = pltpu.SemaphoreType.DMA((GROUP_COPIES,))
    return found


class Grid:
    def __init__(self):
        dp = lax.axis_index("dp")
        self.plane, self.x, self.y = dp // 16, lax.rem(dp // 4, 4), lax.rem(dp, 4)
        self.across = self.at(1 - self.plane, self.x, self.y)

    def at(self, plane, x, y):
        return {"dp": plane * 16 + x * 4 + y}

    def along_x(self, step):
        return self.at(self.plane, lax.rem(self.x + step, 4), self.y)

    def along_y(self, step):
        return self.at(self.plane, self.x, lax.rem(self.y + step, 4))


class GroupSum:
    def __init__(self, r, tag, base, rows, grid):
        self.r, self.base, self.part, self.piece, self.grid = r, base, rows // 4, rows // 16, grid
        names = ("near", "left", "right", "onward", "sum", "got", "piece", "pair", "sends", "recvs")
        for name in names:
            setattr(self, "b_" + name, getattr(r, f"{tag}_{name}"))
        self.used = []
        self.place = [grid.x, grid.y]
        self.along = [grid.along_x, grid.along_y]

    def send(self, source, target, peer):
        copy = remote(source, target, self.b_sends, self.b_recvs, len(self.used), peer)
        self.used.append(copy)
        copy.start()
        return copy

    def rows(self, ref, row, count):
        return ref.at[pl.ds(pl.multiple_of(row, 16), count), :]

    def row(self, h, step):
        return self.base + lax.rem(self.place[h] + step, 4) * self.part

    def both(self, ref):
        return [ref.at[h] for h in range(2)]

    def step_one(self):
        half = self.part // 2
        self.copies = []
        for h in range(2):
            s, near, left, right = (
                ref.at[h] for ref in (self.r.given, self.b_near, self.b_left, self.b_right)
            )
            fwd, back = self.along[h](1), self.along[h](3)
            self.copies.append([
                self.send(self.rows(s, self.row(h, 2), half), self.rows(near, 0, half), fwd),
                self.send(self.rows(s, self.row(h, 2) + half, half), self.rows(near, half, half), back),
                self.send(self.rows(s, self.row(h, 1) + half, half), self.rows(left, half, half), fwd),
                self.send(self.rows(s, self.row(h, 3), half), self.rows(right, 0, half), back),
            ])

    def step_two(self):
        half = self.part // 2
        for h in range(2):
            s, near, onward, left, right = (
                ref.at[h]
                for ref in (self.r.given, self.b_near, self.b_onward, self.b_left, self.b_right)
            )
            self.copies[h][0].wait_recv()
            add_blocks(onward, 0, [(s, self.row(h, 1)), (near, 0)], half)
            self.copies[h].append(
                self.send(self.rows(onward, 0, half), self.rows(left, 0, half), self.along[h](1))
            )
            self.copies[h][1].wait_recv()
            add_blocks(onward, half, [(s, self.row(h, 3) + half), (near, half)], half)
            self.copies[h].append(
                self.send(self.rows(onward, half, half), self.rows(right, half, half), self.along[h](3))
            )

    def step_three(self):
        self.pieces = []
        for h in range(2):
            for copy in self.copies[h][2:]:
                copy.wait_recv()
            s, left, right, total = (
                ref.at[h] for ref in (self.r.given, self.b_left, self.b_right, self.b_sum)
            )
            add_blocks(total, 0, [(s, self.row(h, 0)), (left, 0), (right, 0)], self.part)
            other = 1 - h
            for k in (2, 1, 3):
                row = lax.rem(self.place[other] + k, 4) * self.piece
                self.pieces.append(
                    self.send(self.rows(total, row, self.piece), self.b_got.at[h, k - 1], self.along[other](k))
                )

    def step_four(self):
        self.pairs = []
        for h in range(2):
            for copy in self.pieces[3 * h : 3 * h + 3]:
                copy.wait_recv()
            row = self.place[1 - h] * self.piece
            sources = [(self.b_sum.at[h], row)] + [(self.b_got.at[h, k], 0) for k in range(3)]
            add_blocks(self.b_piece.at[h], 0, sources, self.piece)
            self.pairs.append(self.send(self.b_piece.at[h], self.b_pair.at[h], self.grid.across))

    def own(self, h):
        return self.row(h, 0) + self.place[1 - h] * self.piece

    def step_five(self):
        self.spread = []
        for h in range(2):
            self.pairs[h].wait_recv()
            result = self.r.result.at[h]
            add_blocks(result, self.own(h), [(self.b_piece.at[h], 0), (self.b_pair.at[h], 0)], self.piece)
            mine = self.rows(result, self.own(h), self.piece)
            for k in (2, 1, 3):
                self.spread.append(self.send(mine, mine, self.along[1 - h](k)))

    def step_six(self):
        half = self.part // 2
        self.copies = []
        for h in range(2):
            for copy in self.spread[3 * h : 3 * h + 3]:
                copy.wait_recv()
            result = self.r.result.at[h]
            first = self.rows(result, self.row(h, 0), half)
            second = self.rows(result, self.row(h, 0) + half, half)
            fwd, back = self.along[h](1), self.along[h](3)
            self.copies.append([
                self.send(first, first, fwd),
                self.send(second, second, back),
                self.send(second, second, fwd),
                self.send(first, first, back),
            ])

    def step_seven(self):
        half = self.part // 2
        for h in range(2):
            result = self.r.result.at[h]
            self.copies[h][0].wait_recv()
            from_left = self.rows(result, self.row(h, 3), half)
            self.copies[h].append(self.send(from_left, from_left, self.along[h](1)))
            self.copies[h][1].wait_recv()
            from_right = self.rows(result, self.row(h, 1) + half, half)
            self.copies[h].append(self.send(from_right, from_right, self.along[h](3)))

    def step_eight(self):
        for h in range(2):
            for copy in self.copies[h][2:]:
                copy.wait_recv()

    def drain(self):
        for copy in self.used:
            copy.wait_send()


class SmallSum:
    def __init__(self, r, tag, first, rows, grid):
        self.r, self.first, self.rows, self.grid, self.used = r, first, rows, grid, []
        for name in ("given", "one", "two", "x", "y", "z", "sends", "recvs"):
            setattr(self, name, getattr(r, f"{tag}_{name}"))

    def send(self, source, target, peer):
        copy = remote(source, target, self.sends, self.recvs, len(self.used), peer)
        self.used.append(copy)
        copy.start()

    def add(self, ref, count):
        total = ref[0].astype(single)
        for k in range(1, count):
            total = total + ref[k].astype(single)
        return total.astype(bfloat)

    def step_one(self):
        grid = self.grid
        self.given[...] = self.r.small_wide[self.first : self.first + self.rows, :].astype(bfloat)
        self.x[grid.x] = self.given[...]
        for k in (2, 1, 3):
            self.send(self.given, self.x.at[grid.x], grid.along_x(k))

    def step_two(self):
        grid = self.grid
        for copy in self.used[:3]:
            copy.wait_recv()
        self.one[...] = self.add(self.x, 4)
        self.y[grid.y] = self.one[...]
        for k in (2, 1, 3):
            self.send(self.one, self.y.at[grid.y], grid.along_y(k))

    def step_three(self):
        grid = self.grid
        for copy in self.used[3:6]:
            copy.wait_recv()
        self.two[...] = self.add(self.y, 4)
        self.z[grid.plane] = self.two[...]
        self.send(self.two, self.z.at[grid.plane], grid.across)

    def step_four(self):
        self.used[6].wait_recv()
        self.r.small_out[self.first : self.first + self.rows, :] = self.add(self.z, 2)

    def drain(self):
        for copy in self.used:
            copy.wait_send()


def small_scratch(tag, rows, width):
    block = pltpu.VMEM((rows, width), bfloat)
    found = {f"{tag}_{name}": block for name in ("given", "one", "two")}
    for name, count in (("x", 4), ("y", 4), ("z", 2)):
        found[f"{tag}_{name}"] = pltpu.VMEM((count, rows, width), bfloat)
    found[f"{tag}_sends"] = pltpu.SemaphoreType.DMA((7,))
    found[f"{tag}_recvs"] = pltpu.SemaphoreType.DMA((7,))
    return found


def backward_kernel(r):
    core, sibling, opposite = tensor_place()
    grid = Grid()
    peers = [sibling, opposite, grid.across]
    peers += [grid.along_x(k) for k in (1, 2, 3)] + [grid.along_y(k) for k in (1, 2, 3)]
    greet(peers)
    moves = Moves(r.moves)

    def fetch(*names):
        return [moves.start(getattr(r, name + "_h"), getattr(r, name)) for name in names]

    def ready(copies):
        for copy in copies:
            copy.wait()

    loads_zero = fetch("section_three")
    loads_one = fetch("out", "qkvc", "log", "qkv", "low")
    loads_two = fetch("section_two", "slope", "act", "dense_low", "dense_in", "dense_out")
    loads_three = fetch("section_one", "images")
    stores = []
    sums = [TensorSum(r, n, r.total) for n in range(3)]
    width = r.out.shape[1]
    upper = GroupSum(r, "u", 0, 768, grid)
    dense = GroupSum(r, "d", 768, 1536, grid)
    lower = GroupSum(r, "l", 2304, 768, grid)
    early = SmallSum(r, "early", 0, EXPERTS, grid)
    late = SmallSum(r, "late", EXPERTS, SMALL - EXPERTS, grid)
    mixed = MixedSum(r)

    def deliver(array, row, rows, target):
        half = array.shape[1] // 2
        for h in range(2):
            source = r.result.at[h, pl.ds(row, rows), :]
            stores.append(
                moves.start(source, array.at[pl.ds(target, rows), pl.ds(h * half, half)])
            )

    r.small_wide[...] = jnp.zeros_like(r.small_wide)
    gates = [r.gates[:, k : k + 1] for k in range(2)]
    pulls = [r.gate_sums[:, k : k + 1] for k in range(2)]
    mean = gates[0] * pulls[0] + gates[1] * pulls[1]
    experts = lax.broadcasted_iota(jnp.int32, (r.gates.shape[0], EXPERTS), 1)
    grad_logits = 0.0
    for k in range(2):
        pick = r.routes[:, k : k + 1] == experts
        grad_logits = grad_logits + jnp.where(pick, gates[k] * (pulls[k] - mean), 0.0)
    grad_logits = grad_logits.astype(bfloat)
    ready(loads_zero)
    pl.semaphore_wait(pltpu.get_barrier_semaphore(), 9)
    mixed.step_one()
    rows = r.section_three[...]
    normal, unused = normal_of(rows)
    moe_low = (normal * r.gain[3:4, :] + r.shift[3:4, :]).astype(bfloat)
    r.small_wide[0:EXPERTS, :] = dot_first(grad_logits, moe_low)
    grad_normed = r.grad_experts[...].astype(single) + dot_rows(grad_logits, r.router[...])
    grad_in, gain_part, shift_part = norm_back(grad_normed, rows, r.gain[3:4, :])
    grad = r.cotangent[...].astype(single) + grad_in
    r.grad[...] = grad
    r.small_wide[35:36, :] = gain_part
    r.small_wide[39:40, :] = shift_part
    r.small_wide[41:42, :] = jnp.sum(grad, axis=0, keepdims=True)
    ready(loads_one)
    attend_back(r, 1, grad)
    sums[0].start(attend_back_part(r, 1))
    attend_weights(r, 1, 0)
    upper.step_one()
    early.step_one()
    mixed.step_two()
    upper.step_two()
    early.step_two()
    upper.step_three()
    sums[0].finish()

    ready(loads_two)
    grad_in, gain_part, shift_part = norm_back(
        r.total[...].astype(single), r.section_two[...], r.gain[2:3, :]
    )
    r.small_wide[34:35, :] = gain_part
    r.small_wide[38:39, :] = shift_part
    grad = r.grad[...] + grad_in
    r.grad[...] = grad
    upper.step_four()
    early.step_three()
    grad_low = grad.astype(bfloat)
    r.grad_pre[...] = (dot_last(grad_low, r.dense_out[...]) * r.slope[...]).astype(bfloat)
    sums[1].start(lambda at: dot_last(r.grad_pre[...], r.dense_in[at, :]))
    put_grad(r, 768, dot_first(r.dense_low[...], r.grad_pre[...]))
    put_grad(r, 1536, dot_first(r.act[...], grad_low))
    dense.step_one()
    upper.step_five()
    mixed.step_three()
    early.step_four()
    dense.step_two()
    upper.step_six()
    sums[1].finish()

    ready(loads_three)
    grad_in, gain_part, shift_part = norm_back(
        r.total[...].astype(single), r.section_one[...], r.gain[1:2, :]
    )
    r.small_wide[33:34, :] = gain_part
    r.small_wide[37:38, :] = shift_part
    grad = r.grad[...] + grad_in
    r.grad[...] = grad
    r.small_wide[40:41, :] = jnp.sum(grad, axis=0, keepdims=True)
    upper.step_seven()
    attend_back(r, 0, grad)
    dense.step_three()
    sums[2].start(attend_back_part(r, 0))
    attend_weights(r, 0, 2304)
    lower.step_one()
    upper.step_eight()
    deliver(r.qkv_grad, 0, 3 * width, 3 * width)
    deliver(r.out_grad, 3 * width, width, width)
    dense.step_four()
    lower.step_two()
    dense.step_five()
    lower.step_three()
    sums[2].finish()

    grad_in, gain_part, shift_part = norm_back(
        r.total[...].astype(single), r.images[...].astype(single), r.gain[0:1, :]
    )
    r.small_wide[32:33, :] = gain_part
    r.small_wide[36:37, :] = shift_part
    r.input_grad[...] = r.grad[...] + grad_in
    late.step_one()
    dense.step_six()
    lower.step_four()
    late.step_two()
    lower.step_five()
    dense.step_seven()
    late.step_three()
    lower.step_six()
    late.step_four()
    lower.step_seven()
    dense.step_eight()
    deliver(r.dense_in_grad, 768, 768, 0)
    deliver(r.dense_out_grad, 1536, 768, 0)
    lower.step_eight()
    deliver(r.qkv_grad, 2304, 3 * width, 0)
    deliver(r.out_grad, 2304 + 3 * width, width, 0)
    for one in sums + [upper, dense, lower, early, late, mixed]:
        one.drain()
    ready(stores)


def moe_kernel(r):
    core, sibling, opposite = tensor_place()
    dp = lax.axis_index("dp")
    grid = Grid()
    half = r.arrived.shape[3] // 2
    tokens = r.slots.shape[0]
    block = 4 * STRIDE
    barrier = pltpu.get_barrier_semaphore()

    def greet_one(k, carry):
        pl.semaphore_signal(barrier, inc=1, device_id={"dp": dp_peer(k)}, device_id_type=MESH)
        return carry

    lax.fori_loop(1, EXPERTS, greet_one, 0)
    greet([sibling, opposite])
    moves = Moves(r.moves)
    load_in = moves.start(r.expert_in_h.at[0], r.expert_in)
    load_out = moves.start(r.expert_out_h.at[0], r.expert_out)
    own_block = moves.start(r.sent.at[core, dp], r.arrived.at[core, dp])
    pl.semaphore_wait(barrier, EXPERTS + 1)

    def dispatch(peer, here):
        return pltpu.make_async_remote_copy(
            src_ref=r.sent.at[core, peer],
            dst_ref=r.arrived.at[core, here],
            send_sem=r.send_sems.at[peer],
            recv_sem=r.recv_sems.at[here],
            device_id={"dp": peer},
            device_id_type=MESH,
        )

    def share(source):
        block_ref = r.arrived.at[core, source]
        return remote(block_ref, block_ref, r.pass_sems, r.land_sems, source, sibling)

    def swap(source):
        return remote(r.give.at[source], r.got.at[source], r.give_sems, r.got_sems, source, sibling)

    def answer(peer, here):
        return pltpu.make_async_remote_copy(
            src_ref=r.answer.at[peer],
            dst_ref=r.returned.at[here],
            send_sem=r.back_sems.at[peer],
            recv_sem=r.home_sems.at[here],
            device_id={"dp": peer},
            device_id_type=MESH,
        )

    def offsets(p):
        return lax.rem(p, 2), lax.rem(p // 2 + lax.rem(p, 2), 4)

    def send_block(p, carry):
        dz, dx = offsets(p)
        base = lax.rem(grid.plane + dz, 2) * 16 + lax.rem(grid.x + dx, 4) * 4
        for dy in range(4):
            peer = base + lax.rem(grid.y + dy, 4)

            @pl.when(peer != dp)
            def start():
                dispatch(peer, dp).start()

        return carry

    def base_of(p):
        dz, dx = offsets(p)
        return lax.rem(grid.plane + dz, 2) * 16 + lax.rem(grid.x + 4 - dx, 4) * 4

    def receive(p):
        base = base_of(p)
        for dy in range(4):
            source = base + lax.rem(grid.y + 4 - dy, 4)

            @pl.when(source != dp)
            def wait():
                dispatch(source, source).wait_recv()

            @pl.when(source == dp)
            def wait_own():
                own_block.wait()

            share(source).start()

    def compute(p):
        base = base_of(p)
        for y in range(4):
            share(base + y).wait_recv()
            at = slice(y * STRIDE, (y + 1) * STRIDE)
            for h in range(2):
                rows = r.arrived[h, base + y].astype(single)
                r.wide_x[at, h * half : (h + 1) * half] = rows[:, :half]
                r.wide_g[at, h * half : (h + 1) * half] = rows[:, half:]
        at = pl.ds(pl.multiple_of(p * block, 16), block)
        rows = r.wide_x[...].astype(bfloat)
        rows_grad = r.wide_g[...].astype(bfloat)
        r.rows[at, :] = rows
        r.rows_grad[at, :] = rows_grad
        pre = dot_rows(rows, r.expert_in[...])
        grad_act = dot_last(rows_grad, r.expert_out[...])
        tail = 0.5 * (1.0 + lax.erf(pre * (0.5**0.5)))
        act = (pre * tail).astype(bfloat)
        slope = tail + pre * (jnp.exp(-0.5 * pre * pre) * 0.3989422804014327)
        grad_pre = (grad_act * slope).astype(bfloat)
        r.act[at, :] = act
        r.grad_pre[at, :] = grad_pre
        r.wide_x[...] = dot_rows(act, r.expert_out[...])
        r.wide_g[...] = dot_last(grad_pre, r.expert_in[...])
        for y in range(4):
            at = slice(y * STRIDE, (y + 1) * STRIDE)
            for which, target in ((1 - core, r.give), (core, r.kept)):
                columns = pl.ds(pl.multiple_of(which * half, LANES), half)
                target[base + y, :, :half] = r.wide_x[at, columns].astype(bfloat)
                target[base + y, :, half:] = r.wide_g[at, columns].astype(bfloat)
            swap(base + y).start()

    def respond(p):
        base = base_of(p)
        for y in range(4):
            source = base + y
            swap(source).wait_recv()
            total = r.kept[source].astype(single) + r.got[source].astype(single)
            r.answer[source] = total.astype(bfloat)

            @pl.when(source != dp)
            def start():
                answer(source, dp).start()

            @pl.when(source == dp)
            def keep():
                r.returned[dp] = total.astype(bfloat)

    def step(i, carry):
        pl.when(i < 8)(lambda: receive(i))
        pl.when((i >= 1) & (i < 9))(lambda: compute(i - 1))
        pl.when(i >= 2)(lambda: respond(i - 2))
        return carry

    lax.fori_loop(0, 8, send_block, 0)
    load_in.wait()
    load_out.wait()
    lax.fori_loop(0, 10, step, 0)
    r.weight_grad[0] = dot_first(r.act[...], r.rows_grad[...])
    store_out = moves.start(r.weight_grad.at[0], r.expert_out_grad.at[0])
    r.weight_grad[1] = dot_first(r.rows[...], r.grad_pre[...])
    store_in = moves.start(r.weight_grad.at[1], r.expert_in_grad.at[0])

    ids = lax.broadcasted_iota(jnp.int32, (tokens, SLOTS), 1)
    for k in range(2):
        r.hits[k] = jnp.where(ids == r.slots[:, k : k + 1], 1.0, 0.0).astype(bfloat)

    def come_home(i, carry):
        p, dy = i // 4, lax.rem(i, 4)
        dz, dx = offsets(p)
        source = lax.rem(grid.plane + dz, 2) * 16 + lax.rem(grid.x + dx, 4) * 4 + lax.rem(grid.y + dy, 4)

        @pl.when(source != dp)
        def wait():
            answer(source, source).wait_recv()

        at = pl.ds(pl.multiple_of(source * STRIDE, 8), STRIDE)
        r.wide_home[at, :] = r.returned[source].astype(single)
        return carry

    lax.fori_loop(0, EXPERTS, come_home, 0)
    back = r.wide_home[:, half:].astype(bfloat)
    r.home[...] = r.wide_home[:, :half].astype(bfloat)
    own = r.cotangent[:, pl.ds(pl.multiple_of(core * half, LANES), half)].astype(single)

    second = [remote(r.part.at[j], r.part_got.at[j], r.z_sends, r.z_recvs, j, opposite) for j in range(3)]
    third = [remote(r.part_sum.at[j], r.part_end.at[j], r.z_sends, r.z_recvs, 4 + j, sibling) for j in range(3)]
    second.append(remote(r.gate_rows, r.gate_got, r.z_sends, r.z_recvs, 3, opposite))
    third.append(remote(r.gate_mid, r.gate_end, r.z_sends, r.z_recvs, 7, sibling))
    normed = dot_rows(r.hits[0], back) + dot_rows(r.hits[1], back)
    for j in range(3):
        r.part[j] = normed[:, j * LANES : (j + 1) * LANES].astype(bfloat)
        second[j].start()
    picked = [dot_rows(r.hits[k], r.home[...]) for k in range(2)]
    gate = [jnp.sum(p * own, axis=1, keepdims=True) for p in picked]
    level = lax.broadcasted_iota(jnp.int32, (tokens, tokens), 0)
    across = lax.broadcasted_iota(jnp.int32, (tokens, tokens), 1)
    r.gate_rows[...] = jnp.zeros_like(r.gate_rows)
    for k in range(2):
        spread = jnp.where(level == across, gate[k], 0.0)
        r.gate_rows[k : k + 1, :] = jnp.sum(spread, axis=0, keepdims=True)
    second[3].start()
    mixed = r.gates[:, 0:1] * picked[0] + r.gates[:, 1:2] * picked[1]
    for j in range(3):
        r.mixed[j] = mixed[:, j * LANES : (j + 1) * LANES].astype(bfloat)

    def columns(which, j):
        return pl.ds(pl.multiple_of((which * THIRDS + j) * LANES, LANES), LANES)

    for j in range(3):
        second[j].wait_recv()
        whole = (r.part[j].astype(single) + r.part_got[j].astype(single)).astype(bfloat)
        r.part_sum[j] = whole
        third[j].start()
        r.grad_experts[:, columns(core, j)] = whole
    second[3].wait_recv()
    r.gate_mid[...] = r.gate_rows[...] + r.gate_got[...]
    third[3].start()
    for j in range(3):
        third[j].wait_recv()
        r.grad_experts[:, columns(1 - core, j)] = r.part_end[j]
    third[3].wait_recv()
    for k in range(2):
        sums = r.gate_mid[k : k + 1, :] + r.gate_end[k : k + 1, :]
        spread = jnp.where(level == across, sums, 0.0)
        r.gate_sums[:, k : k + 1] = jnp.sum(spread, axis=1, keepdims=True)
    for copy in second + third:
        copy.wait_send()

    def drain(k, carry):
        share(k).wait_send()
        swap(k).wait_send()

        @pl.when(k != dp)
        def wait():
            dispatch(k, dp).wait_send()
            answer(k, dp).wait_send()

        return carry

    lax.fori_loop(0, EXPERTS, drain, 0)
    store_out.wait()
    store_in.wait()


def moe_whole(sent, slots, gates, cotangent, expert_in, expert_out, collective_id):
    tokens, width = cotangent.shape
    half = width // 2
    slab = pltpu.VMEM((EXPERTS, STRIDE, width), bfloat)
    rows = pltpu.VMEM((SLOTS, width), bfloat)
    parts = pltpu.VMEM((3, tokens, LANES), bfloat)
    gate = pltpu.VMEM((8, tokens), single)
    block = pltpu.VMEM((4 * STRIDE, width), single)
    every = pltpu.SemaphoreType.DMA((EXPERTS,))
    scratch = {name: slab for name in ("give", "kept", "got", "answer", "returned")}
    scratch.update({name: rows for name in ("rows", "rows_grad", "act", "grad_pre")})
    scratch.update({name: parts for name in ("part", "part_got", "part_sum", "part_end")})
    scratch.update({"gate_" + name: gate for name in ("rows", "got", "mid", "end")})
    names = ("send", "recv", "pass", "land", "give", "got", "back", "home")
    scratch.update({name + "_sems": every for name in names})
    scratch.update(
        arrived=pltpu.VMEM((2, EXPERTS, STRIDE, width), bfloat),
        expert_in=pltpu.VMEM(expert_in.shape[1:], bfloat),
        expert_out=pltpu.VMEM(expert_out.shape[1:], bfloat),
        weight_grad=pltpu.VMEM((2,) + expert_in.shape[1:], single),
        wide_x=block,
        wide_g=block,
        wide_home=pltpu.VMEM((SLOTS, width), single),
        home=pltpu.VMEM((SLOTS, half), bfloat),
        hits=pltpu.VMEM((2, tokens, SLOTS), bfloat),
        z_sends=pltpu.SemaphoreType.DMA((8,)),
        z_recvs=pltpu.SemaphoreType.DMA((8,)),
        moves=pltpu.SemaphoreType.DMA((8,)),
    )
    return big_call(
        moe_kernel,
        "moe",
        {
            "sent": (sent.reshape(2, EXPERTS, STRIDE, width), "hbm"),
            "slots": (slots, "vmem"),
            "gates": (gates, "vmem"),
            "cotangent": (cotangent, "vmem"),
            "expert_in_h": (expert_in, "hbm"),
            "expert_out_h": (expert_out, "hbm"),
        },
        {
            "expert_in_grad": (expert_in.shape, single, "hbm"),
            "expert_out_grad": (expert_out.shape, single, "hbm"),
            "mixed": ((3, tokens, LANES), bfloat, "vmem"),
            "grad_experts": ((tokens, width), bfloat, "vmem"),
            "gate_sums": ((tokens, 2), single, "vmem"),
        },
        scratch,
        collective_id,
    )


class MixedSum:
    def __init__(self, r):
        core, sibling, opposite = tensor_place()
        self.r, self.core = r, core
        self.second = [
            remote(r.mixed.at[j], r.m_got.at[j], r.m_sends, r.m_recvs, j, opposite) for j in range(3)
        ]
        self.third = [
            remote(r.m_sum.at[j], r.m_end.at[j], r.m_sends, r.m_recvs, 3 + j, sibling) for j in range(3)
        ]

    def step_one(self):
        for copy in self.second:
            copy.start()

    def step_two(self):
        r = self.r
        for j in range(3):
            self.second[j].wait_recv()
            whole = r.mixed[j].astype(single) + r.m_got[j].astype(single)
            r.m_sum[j] = whole.astype(bfloat)
            self.third[j].start()
            self.put(self.core, j, r.m_sum[j])

    def put(self, which, j, value):
        at = pl.ds(pl.multiple_of((which * THIRDS + j) * LANES, LANES), LANES)
        rows = self.r.section_three[:, at] + value.astype(single)
        self.r.output[:, at] = rows.astype(bfloat)

    def step_three(self):
        for j in range(3):
            self.third[j].wait_recv()
            self.put(1 - self.core, j, self.r.m_end[j])

    def drain(self):
        for copy in self.second + self.third:
            copy.wait_send()


def finish_kernel(r):
    moves = Moves(r.moves)
    names = ("qkv", "out", "dense_in", "dense_out")
    loads = [moves.start(getattr(r, name + "_h"), getattr(r, name + "_low")) for name in names]
    whole = ("expert_in", "expert_out", "input_grad", "output")
    passing = [moves.start(getattr(r, name + "_h"), getattr(r, name + "_pass")) for name in whole]
    stores = []
    small = r.small[...].astype(single)
    part = r.qv_bias.shape[2]
    r.router[...] = small[:EXPERTS]
    r.gain[...] = small[32:36]
    r.shift[...] = small[36:40]
    r.out_bias[...] = small[40:42]
    r.qv_bias[0] = small[42:44, :part]
    r.qv_bias[1] = small[44:46, :part]
    for name, load in zip(names, loads):
        load.wait()
        low, wide = getattr(r, name + "_low"), getattr(r, name + "_wide")
        rows = low.shape[0]
        piece = 192

        def cast(i, carry):
            at = pl.ds(pl.multiple_of(i * piece, 16), piece)
            wide[at, :] = low[at, :].astype(single)
            return carry

        lax.fori_loop(0, rows // piece, cast, 0)
        stores.append(moves.start(wide, getattr(r, name + "_f")))
    for name, load in zip(whole, passing):
        load.wait()
        stores.append(moves.start(getattr(r, name + "_pass"), getattr(r, name + "_f")))
    for store in stores:
        store.wait()


def finish(last, moe, part, width):
    arrays = {"qkv": last.qkv_grad, "out": last.out_grad}
    arrays.update({"dense_in": last.dense_in_grad, "dense_out": last.dense_out_grad})
    ins = {name + "_h": (array, "hbm") for name, array in arrays.items()}
    ins["small"] = (last.small_out, "vmem")
    outs = {name + "_f": (array.shape, single, "hbm") for name, array in arrays.items()}
    whole = {"expert_in": moe.expert_in_grad, "expert_out": moe.expert_out_grad}
    whole.update(input_grad=last.input_grad, output=last.output)
    for name, array in whole.items():
        ins[name + "_h"] = (array, "hbm")
        outs[name + "_f"] = (array.shape, array.dtype, "hbm")
    outs.update(
        router=((EXPERTS, width), single, "vmem"),
        gain=((4, width), single, "vmem"),
        shift=((4, width), single, "vmem"),
        out_bias=((2, width), single, "vmem"),
        qv_bias=((2, 2, part), single, "vmem"),
    )
    scratch = {name + "_low": pltpu.VMEM(array.shape, bfloat) for name, array in arrays.items()}
    scratch.update({name + "_wide": pltpu.VMEM(a.shape, single) for name, a in arrays.items()})
    scratch.update({name + "_pass": pltpu.VMEM(a.shape, a.dtype) for name, a in whole.items()})
    scratch["moves"] = pltpu.SemaphoreType.DMA((16,))
    return big_call(finish_kernel, "finish", ins, outs, scratch)


def per_device(
    images,
    routes,
    cotangent,
    qkv_weight,
    out_weight,
    qv_bias,
    out_bias,
    ln_gain,
    ln_bias,
    dense_in,
    dense_out,
    router,
    expert_in,
    expert_out,
):
    tokens, width = images.shape
    part = out_weight.shape[1]
    hidden = dense_in.shape[1]
    qkv = jnp.transpose(qkv_weight, (0, 2, 3, 1)).reshape(2, 3 * part, width)
    full, low = (tokens, width), bfloat
    kept = {
        "section_one": (full, single),
        "section_two": (full, single),
        "section_three": (full, single),
        "dense_low": (full, low),
        "slope": ((tokens, hidden), single),
        "act": ((tokens, hidden), low),
        "low": ((2, tokens, width), low),
        "qkvc": ((2, 4, tokens, part), low),
        "log": ((2, tokens, part // HEAD), single),
    }
    weights = {
        "dense_in": (dense_in.shape, low),
        "dense_out": (dense_out.shape, low),
    }

    def vmem(names, table):
        return {name: pltpu.VMEM(*table[name]) for name in names}

    sections = ("section_one", "section_two", "section_three")
    outs = {name + ("" if name in sections else "_h"): kept[name] + ("hbm",) for name in kept}
    outs["sent"] = ((2, SLOTS, width), low, "hbm")
    outs["gates"] = ((tokens, 2), single, "vmem")
    outs["slots"] = ((tokens, 2), jnp.int32, "vmem")
    outs["routes"] = ((tokens, 2), jnp.int32, "vmem")
    scratch = sum_scratch(tokens, 3)
    scratch.update(vmem([name for name in kept if name not in sections], kept))
    scratch.update(vmem(list(weights), weights))
    scratch.update(
        section=pltpu.VMEM((3, tokens, width), single),
        cotangent=pltpu.VMEM(full, low),
        moe_low=pltpu.VMEM(full, low),
        scaled=pltpu.VMEM((2, tokens, width), low),
        routed=pltpu.VMEM((2, SLOTS, width), low),
        total=pltpu.VMEM(full, low),
        moves=pltpu.SemaphoreType.DMA((24,)),
    )
    done = big_call(
        forward_kernel,
        "forward",
        {
            "images": (images, "vmem"),
            "qkv": (qkv, "vmem"),
            "out": (out_weight, "vmem"),
            "qv_bias": (qv_bias, "vmem"),
            "out_bias": (out_bias, "vmem"),
            "gain": (ln_gain, "vmem"),
            "shift": (ln_bias, "vmem"),
            "dense_in_h": (dense_in, "hbm"),
            "dense_out_h": (dense_out, "hbm"),
            "cotangent_h": (cotangent, "hbm"),
            "routes_row": (routes.T, "vmem"),
            "router": (router.T, "vmem"),
        },
        outs,
        scratch,
        1,
    )
    moe = moe_whole(done.sent, done.slots, done.gates, cotangent, expert_in, expert_out, 3)

    outs = {
        "output": (full, low, "vmem"),
        "input_grad": (full, single, "vmem"),
        "qkv_grad": ((6 * part, width), low, "hbm"),
        "out_grad": ((2 * part, width), low, "hbm"),
        "dense_in_grad": (dense_in.shape, low, "hbm"),
        "dense_out_grad": (dense_out.shape, low, "hbm"),
        "small_out": ((SMALL, width), low, "vmem"),
    }
    scratch = sum_scratch(tokens, 3)
    scratch.update(vmem(list(kept), kept))
    scratch.update(vmem(list(weights), weights))
    for tag, rows in (("u", 768), ("d", 1536), ("l", 768)):
        scratch.update(group_scratch(tag, rows, width // 2))
    scratch.update(small_scratch("early", EXPERTS, width))
    scratch.update(small_scratch("late", SMALL - EXPERTS, width))
    scratch.update(
        images=pltpu.VMEM(full, low),
        qkv=pltpu.VMEM(qkv.shape, low),
        out=pltpu.VMEM(out_weight.shape, low),
        total=pltpu.VMEM(full, low),
        grad=pltpu.VMEM(full, single),
        grad_low=pltpu.VMEM(full, low),
        grad_pre=pltpu.VMEM((tokens, hidden), low),
        grad_qkv=pltpu.VMEM((3, tokens, part), low),
        given=pltpu.VMEM((2, BIG, width // 2), low),
        result=pltpu.VMEM((2, BIG, width // 2), low),
        small_wide=pltpu.VMEM((SMALL, width), single),
        m_got=pltpu.VMEM((3, tokens, LANES), low),
        m_sum=pltpu.VMEM((3, tokens, LANES), low),
        m_end=pltpu.VMEM((3, tokens, LANES), low),
        m_sends=pltpu.SemaphoreType.DMA((6,)),
        m_recvs=pltpu.SemaphoreType.DMA((6,)),
        moves=pltpu.SemaphoreType.DMA((32,)),
    )
    ins = {
        "mixed": (moe.mixed, "vmem"),
        "grad_experts": (moe.grad_experts, "vmem"),
        "gate_sums": (moe.gate_sums, "vmem"),
        "gates": (done.gates, "vmem"),
        "routes": (done.routes, "vmem"),
        "router": (router.T, "vmem"),
        "cotangent": (cotangent, "vmem"),
        "gain": (ln_gain, "vmem"),
        "shift": (ln_bias, "vmem"),
        "images_h": (images, "hbm"),
        "qkv_h": (qkv, "hbm"),
        "out_h": (out_weight, "hbm"),
        "dense_in_h": (dense_in, "hbm"),
        "dense_out_h": (dense_out, "hbm"),
    }
    for name in kept:
        ins[name + "_h"] = (getattr(done, name if name in sections else name + "_h"), "hbm")
    last = big_call(backward_kernel, "backward", ins, outs, scratch, 2)
    end = finish(last, moe, part, width)
    qkv_weight_grad = jnp.transpose(end.qkv_f.reshape(2, 3, part, width), (0, 3, 1, 2))
    out_weight_grad = end.out_f.reshape(2, part, width)
    dense_in_grad, dense_out_grad = end.dense_in_f, end.dense_out_f
    router_grad = end.router.T
    ln_gain_grad, ln_bias_grad, out_bias_grad = end.gain, end.shift, end.out_bias
    qv_bias_grad = end.qv_bias
    output, input_grad = end.output_f, end.input_grad_f
    expert_in_grad, expert_out_grad = end.expert_in_f, end.expert_out_f
    return (
        output,
        input_grad,
        qkv_weight_grad,
        out_weight_grad,
        qv_bias_grad,
        out_bias_grad,
        ln_gain_grad,
        ln_bias_grad,
        dense_in_grad,
        dense_out_grad,
        router_grad,
        expert_in_grad,
        expert_out_grad,
    )


def solution(mesh):
    in_specs = (
        P("dp", None),
        P("dp", None),
        P("dp", None),
        P(None, None, None, "tensor"),
        P(None, "tensor", None),
        P(None, None, "tensor"),
        P(),
        P(),
        P(),
        P(None, "tensor"),
        P("tensor", None),
        P(),
        P("dp", None, "tensor"),
        P("dp", "tensor", None),
    )
    out_specs = (
        P("dp", None),
        P("dp", None),
        P(None, None, None, "tensor"),
        P(None, "tensor", None),
        P(None, None, "tensor"),
        P(),
        P(),
        P(),
        P(None, "tensor"),
        P("tensor", None),
        P(),
        P("dp", None, "tensor"),
        P("dp", "tensor", None),
    )
    return jax.shard_map(
        per_device, mesh=mesh, in_specs=in_specs, out_specs=out_specs, check_vma=False
    )
```

```python
import functools

import jax
import jax.numpy as jnp
from jax import lax
from jax.experimental import pallas as pl
from jax.experimental.pallas import tpu as pltpu
from jax.sharding import PartitionSpec as P

HEAD = 64
SEQ = 197


epsilon = 1e-06
bfloat = jnp.bfloat16
single = jnp.float32


MESH = pl.DeviceIdType.MESH


BIG = 3072
SMALL = 48
EXPERTS = 32
STRIDE = 40
SLOTS = EXPERTS * STRIDE


def dot_rows(a, b):
    return lax.dot_general(a, b, (((1,), (0,)), ((), ())), preferred_element_type=single)


def dot_last(a, b):
    return lax.dot_general(a, b, (((1,), (1,)), ((), ())), preferred_element_type=single)


def dot_first(a, b):
    return lax.dot_general(a, b, (((0,), (0,)), ((), ())), preferred_element_type=single)


VMEM_SPEC = pl.BlockSpec(memory_space=pltpu.VMEM)


def dp_peer(k):
    dp = lax.axis_index("dp")
    plane = lax.rem(dp // 16 + k // 16, 2)
    x = lax.rem(lax.rem(dp // 4, 4) + lax.rem(k // 4, 4), 4)
    y = lax.rem(lax.rem(dp, 4) + lax.rem(k, 4), 4)
    return plane * 16 + x * 4 + y


def normal_of(rows):
    average = jnp.mean(rows, axis=-1, keepdims=True)
    centered = rows - average
    variance = jnp.mean(centered * centered, axis=-1, keepdims=True)
    inverse = lax.rsqrt(variance + epsilon)
    return centered * inverse, inverse


def norm_back(grad_normed, rows, gain_row):
    normal, inverse = normal_of(rows)
    scaled = grad_normed * gain_row
    mean_one = jnp.mean(scaled, axis=-1, keepdims=True)
    mean_two = jnp.mean(scaled * normal, axis=-1, keepdims=True)
    grad_in = inverse * (scaled - mean_one - normal * mean_two)
    gain_part = jnp.sum(grad_normed * normal, axis=0, keepdims=True)
    return grad_in, gain_part, jnp.sum(grad_normed, axis=0, keepdims=True)


def same_image(tokens):
    first = lax.broadcasted_iota(jnp.int32, (tokens, tokens), 0) // SEQ
    second = lax.broadcasted_iota(jnp.int32, (tokens, tokens), 1) // SEQ
    return first == second


class Refs:
    def __init__(self, names, refs):
        for name, ref in zip(names, refs):
            setattr(self, name, ref)


def big_call(kernel, name, ins, outs, scratch, collective_id=None, limit=58):
    names = list(ins) + list(outs) + list(scratch)
    hbm = pl.BlockSpec(memory_space=pl.ANY)

    def body(*refs):
        kernel(Refs(names, refs))

    found = pl.pallas_call(
        body,
        out_shape=[jax.ShapeDtypeStruct(shape, kind) for shape, kind, unused in outs.values()],
        in_specs=[hbm if place == "hbm" else VMEM_SPEC for unused, place in ins.values()],
        out_specs=[hbm if place == "hbm" else VMEM_SPEC for _, _, place in outs.values()],
        scratch_shapes=list(scratch.values()),
        compiler_params=pltpu.CompilerParams(
            collective_id=collective_id, has_side_effects=True, vmem_limit_bytes=limit * 2**20
        ),
        name=name,
    )(*[array for array, unused in ins.values()])
    return Refs(list(outs), found)


def tensor_place():
    t = lax.axis_index("tensor")
    core = lax.rem(t, 2)
    return core, {"tensor": t + 1 - 2 * core}, {"tensor": lax.rem(t + 2, 4)}


def remote(source, target, sends, recvs, index, peer):
    return pltpu.make_async_remote_copy(
        src_ref=source,
        dst_ref=target,
        send_sem=sends.at[index],
        recv_sem=recvs.at[index],
        device_id=peer,
        device_id_type=MESH,
    )


LANES = 128
THIRDS = 3


def sum_scratch(tokens, count):
    block = pltpu.VMEM((count, THIRDS, tokens, LANES), bfloat)
    names = ["give", "got_one", "sum_one", "got_two", "sum_two", "got_three"]
    found = {"t_" + name: block for name in names}
    found["t_own"] = pltpu.VMEM((tokens, THIRDS * LANES), single)
    found["t_sends"] = pltpu.SemaphoreType.DMA((count * 9,))
    found["t_recvs"] = pltpu.SemaphoreType.DMA((count * 9,))
    return found


class TensorSum:
    def __init__(self, r, number, total_ref):
        core, sibling, opposite = tensor_place()
        self.core, self.r, self.n, self.total = core, r, number, total_ref

        def copies(source, target, step, peer):
            return [
                remote(source.at[number, j], target.at[number, j], r.t_sends, r.t_recvs, number * 9 + step * 3 + j, peer)
                for j in range(THIRDS)
            ]

        self.first = copies(r.t_give, r.t_got_one, 0, sibling)
        self.second = copies(r.t_sum_one, r.t_got_two, 1, opposite)
        self.third = copies(r.t_sum_two, r.t_got_three, 2, sibling)

    def columns(self, which, j=0, count=1):
        return pl.ds(pl.multiple_of((which * THIRDS + j) * LANES, LANES), count * LANES)

    def start(self, partial):
        r, n = self.r, self.n
        other = partial(self.columns(1 - self.core, 0, THIRDS)).astype(bfloat)
        for j in range(THIRDS):
            r.t_give[n, j] = other[:, j * LANES : (j + 1) * LANES]
            self.first[j].start()
        r.t_own[...] = partial(self.columns(self.core, 0, THIRDS))
        for j in range(THIRDS):
            self.first[j].wait_recv()
            own = r.t_own[:, j * LANES : (j + 1) * LANES]
            r.t_sum_one[n, j] = (own + r.t_got_one[n, j].astype(single)).astype(bfloat)
            self.second[j].start()

    def finish(self):
        r, n = self.r, self.n
        for j in range(THIRDS):
            self.second[j].wait_recv()
            whole = (r.t_sum_one[n, j].astype(single) + r.t_got_two[n, j].astype(single)).astype(bfloat)
            r.t_sum_two[n, j] = whole
            self.third[j].start()
            self.total[:, self.columns(self.core, j)] = whole
        for j in range(THIRDS):
            self.third[j].wait_recv()
            self.total[:, self.columns(1 - self.core, j)] = r.t_got_three[n, j]

    def drain(self):
        for copy in self.first + self.second + self.third:
            copy.wait_send()


class Moves:
    def __init__(self, sems):
        self.sems, self.count = sems, 0

    def start(self, source, target):
        copy = pltpu.make_async_copy(source, target, self.sems.at[self.count])
        self.count += 1
        copy.start()
        return copy


def greet(peers):
    barrier = pltpu.get_barrier_semaphore()
    for peer in peers:
        pl.semaphore_signal(barrier, inc=1, device_id=peer, device_id_type=MESH)


def attend(r, rows, layer):
    width = r.out.shape[1]
    norm = 2 * layer
    normal, unused = normal_of(rows)
    low = (normal * r.gain[norm : norm + 1, :] + r.shift[norm : norm + 1, :]).astype(bfloat)
    r.low[layer] = low
    bias = r.qv_bias[layer]
    q = (dot_last(low, r.qkv[layer, :width, :]) + bias[0:1, :]).astype(bfloat)
    k = dot_last(low, r.qkv[layer, width : 2 * width, :]).astype(bfloat)
    v = (dot_last(low, r.qkv[layer, 2 * width :, :]) + bias[1:2, :]).astype(bfloat)
    r.qkvc[layer, 0], r.qkvc[layer, 1], r.qkvc[layer, 2] = q, k, v
    same = same_image(rows.shape[0])
    contexts = []
    for h in range(width // HEAD):
        at = slice(h * HEAD, (h + 1) * HEAD)
        scores = jnp.where(same, dot_last(q[:, at], k[:, at]) * HEAD ** (-0.5), -1e30)
        largest = jnp.max(scores, axis=-1, keepdims=True)
        exponent = jnp.exp(scores - largest)
        totals = jnp.sum(exponent, axis=-1, keepdims=True)
        r.log[layer, :, h : h + 1] = largest + jnp.log(totals)
        contexts.append(dot_rows((exponent / totals).astype(bfloat), v[:, at]))
    r.qkvc[layer, 3] = jnp.concatenate(contexts, axis=1).astype(bfloat)


def forward_kernel(r):
    core, sibling, opposite = tensor_place()
    greet([sibling, opposite])
    moves = Moves(r.moves)
    loads = [moves.start(r.dense_in_h, r.dense_in), moves.start(r.dense_out_h, r.dense_out)]
    loads += [moves.start(r.cotangent_h, r.cotangent)]
    stores = []
    sums = [TensorSum(r, n, r.total) for n in range(3)]

    def save(source, target):
        stores.append(moves.start(source, target))

    def out_part(layer):
        return lambda at: dot_rows(r.qkvc[layer, 3], r.out[layer, :, at])

    attend(r, r.images[...].astype(single), 0)
    pl.semaphore_wait(pltpu.get_barrier_semaphore(), 2)
    sums[0].start(out_part(0))
    sums[0].finish()

    rows = r.images[...].astype(single) + r.total[...].astype(single) + r.out_bias[0:1, :]
    r.section[0] = rows
    save(r.section.at[0], r.section_one)
    normal, unused = normal_of(rows)
    low = (normal * r.gain[1:2, :] + r.shift[1:2, :]).astype(bfloat)
    r.dense_low[...] = low
    save(r.dense_low, r.dense_low_h)
    for load in loads:
        load.wait()
    pre = dot_rows(low, r.dense_in[...])
    tail = 0.5 * (1.0 + lax.erf(pre * (0.5**0.5)))
    r.slope[...] = tail + pre * (jnp.exp(-0.5 * pre * pre) * 0.3989422804014327)
    save(r.slope, r.slope_h)
    r.act[...] = (pre * tail).astype(bfloat)
    save(r.act, r.act_h)
    sums[1].start(lambda at: dot_rows(r.act[...], r.dense_out[:, at]))
    sums[1].finish()

    rows = r.section[0] + r.total[...].astype(single)
    r.section[1] = rows
    save(r.section.at[1], r.section_two)
    attend(r, rows, 1)
    save(r.low, r.low_h)
    save(r.qkvc, r.qkvc_h)
    save(r.log, r.log_h)
    sums[2].start(out_part(1))
    sums[2].finish()

    rows = r.section[1] + r.total[...].astype(single) + r.out_bias[1:2, :]
    r.section[2] = rows
    save(r.section.at[2], r.section_three)
    moe_route_body(r, rows, save)
    for one in sums:
        one.drain()
    for store in stores:
        store.wait()


def moe_route_body(r, rows, save):
    tokens, width = rows.shape
    half = width // 2
    normal, unused = normal_of(rows)
    r.moe_low[...] = (normal * r.gain[3:4, :] + r.shift[3:4, :]).astype(bfloat)
    logits = dot_last(r.moe_low[...], r.router[...])
    experts = lax.broadcasted_iota(jnp.int32, (tokens, EXPERTS), 1)
    before = lax.broadcasted_iota(jnp.int32, (tokens, tokens), 0)
    after = lax.broadcasted_iota(jnp.int32, (tokens, tokens), 1)
    for k in range(2):
        spread = jnp.where(before == after, r.routes_row[k : k + 1, :].astype(single), 0.0)
        r.routes[:, k : k + 1] = jnp.sum(spread, axis=1, keepdims=True).astype(jnp.int32)
    picks = [r.routes[:, k : k + 1] == experts for k in range(2)]
    chosen = [jnp.sum(jnp.where(pick, logits, 0.0), axis=1, keepdims=True) for pick in picks]
    largest = jnp.maximum(chosen[0], chosen[1])
    powers = [jnp.exp(c - largest) for c in chosen]
    total = powers[0] + powers[1]
    gates = [power / total for power in powers]
    r.table[...] = jnp.zeros_like(r.table)
    for k in range(2):
        r.table[:, k : k + 1] = gates[k]
    cotangent = r.cotangent[...].astype(single)
    for k in range(2):
        r.scaled[k] = (gates[k] * cotangent).astype(bfloat)

    either = [jnp.where(pick, 1.0, 0.0) for pick in picks]
    lower = jnp.where(after < before, 1.0, 0.0).astype(bfloat)
    running = dot_rows(lower, (either[0] + either[1]).astype(bfloat))
    for k in range(2):
        rank = jnp.sum(running * either[k], axis=1, keepdims=True).astype(jnp.int32)
        slots = r.routes[:, k : k + 1] * STRIDE + rank
        r.table[:, 2 + k : 3 + k] = slots.astype(single)
        r.table[:, 4 + k : 5 + k] = r.routes[:, k : k + 1].astype(single)

    experts_row = lax.broadcasted_iota(jnp.int32, (EXPERTS, tokens), 0)
    either_row = [jnp.where(r.routes_row[k : k + 1, :] == experts_row, 1.0, 0.0) for k in range(2)]
    upper = jnp.where(before < after, 1.0, 0.0).astype(bfloat)
    running_row = dot_rows((either_row[0] + either_row[1]).astype(bfloat), upper)
    slots_row = []
    for k in range(2):
        rank = jnp.sum(running_row * either_row[k], axis=0, keepdims=True).astype(jnp.int32)
        slots_row.append(r.routes_row[k : k + 1, :] * STRIDE + rank)

    block = SLOTS // 4
    for i in range(4):
        ids = lax.broadcasted_iota(jnp.int32, (block, tokens), 0) + i * block
        hits = [jnp.where(ids == slots_row[k], 1.0, 0.0) for k in range(2)]
        moved = dot_rows((hits[0] + hits[1]).astype(bfloat), r.moe_low[...]).astype(bfloat)
        moved_grad = (
            dot_rows(hits[0].astype(bfloat), r.scaled[0]) + dot_rows(hits[1].astype(bfloat), r.scaled[1])
        ).astype(bfloat)
        at = slice(i * block, (i + 1) * block)
        for h in range(2):
            r.routed[h, at, :half] = moved[:, h * half : (h + 1) * half]
            r.routed[h, at, half:] = moved_grad[:, h * half : (h + 1) * half]
            save(r.routed.at[h, pl.ds(i * block, block), :], r.sent.at[h, pl.ds(i * block, block), :])


def attend_back(r, layer, grad_out):
    width = r.out.shape[1]
    grad_low = grad_out.astype(bfloat)
    r.grad_low[...] = grad_low
    q, k, v = r.qkvc[layer, 0], r.qkvc[layer, 1], r.qkvc[layer, 2]
    grad_context = dot_last(grad_low, r.out[layer]).astype(bfloat)
    same = same_image(q.shape[0])
    grads = [[], [], []]
    for h in range(width // HEAD):
        at = slice(h * HEAD, (h + 1) * HEAD)
        scores = jnp.where(same, dot_last(q[:, at], k[:, at]) * HEAD ** (-0.5), -1e30)
        probs = jnp.exp(scores - r.log[layer, :, h : h + 1])
        grad_probs = dot_last(grad_context[:, at], v[:, at])
        row_total = jnp.sum(probs * grad_probs, axis=-1, keepdims=True)
        grad_scores = (probs * (grad_probs - row_total)).astype(bfloat)
        grads[0].append(dot_rows(grad_scores, k[:, at]) * HEAD ** (-0.5))
        grads[1].append(dot_first(grad_scores, q[:, at]) * HEAD ** (-0.5))
        grads[2].append(dot_first(probs.astype(bfloat), grad_context[:, at]))
    for part in range(3):
        r.grad_qkv[part] = jnp.concatenate(grads[part], axis=1).astype(bfloat)


def attend_weights(r, layer, base):
    width = r.out.shape[1]
    put_grad(r, base + 3 * width, dot_first(r.qkvc[layer, 3], r.grad_low[...]))
    for part in range(3):
        grad = r.grad_qkv[part]
        put_grad(r, base + part * width, dot_first(grad, r.low[layer]))
        if part != 1:
            row = 42 + 2 * layer + part // 2
            r.small_wide[row : row + 1, :width] = jnp.sum(grad.astype(single), axis=0, keepdims=True)


def attend_back_part(r, layer):
    width = r.out.shape[1]

    def partial(at):
        total = None
        for part in range(3):
            term = dot_rows(r.grad_qkv[part], r.qkv[layer, part * width : (part + 1) * width, at])
            total = term if total is None else total + term
        return total

    return partial


def put_grad(r, row, value):
    low = value.astype(bfloat)
    half = low.shape[1] // 2
    for h in range(2):
        r.given[h, row : row + low.shape[0], :] = low[:, h * half : (h + 1) * half]


def add_blocks(target, row, sources, rows):
    def body(i, carry):
        total = None
        for ref, start in sources:
            value = ref[pl.ds(pl.multiple_of(start + i * 16, 16), 16), :].astype(single)
            total = value if total is None else total + value
        target[pl.ds(pl.multiple_of(row + i * 16, 16), 16), :] = total.astype(bfloat)
        return carry

    lax.fori_loop(0, rows // 16, body, 0)


GROUP_COPIES = 38


def group_scratch(tag, rows, width):
    part, piece = rows // 4, rows // 16
    found = {}
    for name in ("near", "left", "right", "onward", "sum"):
        found[f"{tag}_{name}"] = pltpu.VMEM((2, part, width), bfloat)
    found[f"{tag}_got"] = pltpu.VMEM((2, 3, piece, width), bfloat)
    found[f"{tag}_piece"] = pltpu.VMEM((2, piece, width), bfloat)
    found[f"{tag}_pair"] = pltpu.VMEM((2, piece, width), bfloat)
    found[f"{tag}_sends"] = pltpu.SemaphoreType.DMA((GROUP_COPIES,))
    found[f"{tag}_recvs"] = pltpu.SemaphoreType.DMA((GROUP_COPIES,))
    return found


class Grid:
    def __init__(self):
        dp = lax.axis_index("dp")
        self.plane, self.x, self.y = dp // 16, lax.rem(dp // 4, 4), lax.rem(dp, 4)
        self.across = self.at(1 - self.plane, self.x, self.y)

    def at(self, plane, x, y):
        return {"dp": plane * 16 + x * 4 + y}

    def along_x(self, step):
        return self.at(self.plane, lax.rem(self.x + step, 4), self.y)

    def along_y(self, step):
        return self.at(self.plane, self.x, lax.rem(self.y + step, 4))


class GroupSum:
    def __init__(self, r, tag, base, rows, grid):
        self.r, self.base, self.part, self.piece, self.grid = r, base, rows // 4, rows // 16, grid
        names = ("near", "left", "right", "onward", "sum", "got", "piece", "pair", "sends", "recvs")
        for name in names:
            setattr(self, "b_" + name, getattr(r, f"{tag}_{name}"))
        self.used = []
        self.place = [grid.x, grid.y]
        self.along = [grid.along_x, grid.along_y]

    def send(self, source, target, peer):
        copy = remote(source, target, self.b_sends, self.b_recvs, len(self.used), peer)
        self.used.append(copy)
        copy.start()
        return copy

    def rows(self, ref, row, count):
        return ref.at[pl.ds(pl.multiple_of(row, 16), count), :]

    def row(self, h, step):
        return self.base + lax.rem(self.place[h] + step, 4) * self.part

    def both(self, ref):
        return [ref.at[h] for h in range(2)]

    def step_one(self):
        half = self.part // 2
        self.copies = []
        for h in range(2):
            s, near, left, right = (
                ref.at[h] for ref in (self.r.given, self.b_near, self.b_left, self.b_right)
            )
            fwd, back = self.along[h](1), self.along[h](3)
            self.copies.append([
                self.send(self.rows(s, self.row(h, 2), half), self.rows(near, 0, half), fwd),
                self.send(self.rows(s, self.row(h, 2) + half, half), self.rows(near, half, half), back),
                self.send(self.rows(s, self.row(h, 1) + half, half), self.rows(left, half, half), fwd),
                self.send(self.rows(s, self.row(h, 3), half), self.rows(right, 0, half), back),
            ])

    def step_two(self):
        half = self.part // 2
        for h in range(2):
            s, near, onward, left, right = (
                ref.at[h]
                for ref in (self.r.given, self.b_near, self.b_onward, self.b_left, self.b_right)
            )
            self.copies[h][0].wait_recv()
            add_blocks(onward, 0, [(s, self.row(h, 1)), (near, 0)], half)
            self.copies[h].append(
                self.send(self.rows(onward, 0, half), self.rows(left, 0, half), self.along[h](1))
            )
            self.copies[h][1].wait_recv()
            add_blocks(onward, half, [(s, self.row(h, 3) + half), (near, half)], half)
            self.copies[h].append(
                self.send(self.rows(onward, half, half), self.rows(right, half, half), self.along[h](3))
            )

    def step_three(self):
        self.pieces = []
        for h in range(2):
            for copy in self.copies[h][2:]:
                copy.wait_recv()
            s, left, right, total = (
                ref.at[h] for ref in (self.r.given, self.b_left, self.b_right, self.b_sum)
            )
            add_blocks(total, 0, [(s, self.row(h, 0)), (left, 0), (right, 0)], self.part)
            other = 1 - h
            for k in (2, 1, 3):
                row = lax.rem(self.place[other] + k, 4) * self.piece
                self.pieces.append(
                    self.send(self.rows(total, row, self.piece), self.b_got.at[h, k - 1], self.along[other](k))
                )

    def step_four(self):
        self.pairs = []
        for h in range(2):
            for copy in self.pieces[3 * h : 3 * h + 3]:
                copy.wait_recv()
            row = self.place[1 - h] * self.piece
            sources = [(self.b_sum.at[h], row)] + [(self.b_got.at[h, k], 0) for k in range(3)]
            add_blocks(self.b_piece.at[h], 0, sources, self.piece)
            self.pairs.append(self.send(self.b_piece.at[h], self.b_pair.at[h], self.grid.across))

    def own(self, h):
        return self.row(h, 0) + self.place[1 - h] * self.piece

    def step_five(self):
        self.spread = []
        for h in range(2):
            self.pairs[h].wait_recv()
            result = self.r.result.at[h]
            add_blocks(result, self.own(h), [(self.b_piece.at[h], 0), (self.b_pair.at[h], 0)], self.piece)
            mine = self.rows(result, self.own(h), self.piece)
            for k in (2, 1, 3):
                self.spread.append(self.send(mine, mine, self.along[1 - h](k)))

    def step_six(self):
        half = self.part // 2
        self.copies = []
        for h in range(2):
            for copy in self.spread[3 * h : 3 * h + 3]:
                copy.wait_recv()
            result = self.r.result.at[h]
            first = self.rows(result, self.row(h, 0), half)
            second = self.rows(result, self.row(h, 0) + half, half)
            fwd, back = self.along[h](1), self.along[h](3)
            self.copies.append([
                self.send(first, first, fwd),
                self.send(second, second, back),
                self.send(second, second, fwd),
                self.send(first, first, back),
            ])

    def step_seven(self):
        half = self.part // 2
        for h in range(2):
            result = self.r.result.at[h]
            self.copies[h][0].wait_recv()
            from_left = self.rows(result, self.row(h, 3), half)
            self.copies[h].append(self.send(from_left, from_left, self.along[h](1)))
            self.copies[h][1].wait_recv()
            from_right = self.rows(result, self.row(h, 1) + half, half)
            self.copies[h].append(self.send(from_right, from_right, self.along[h](3)))

    def step_eight(self):
        for h in range(2):
            for copy in self.copies[h][2:]:
                copy.wait_recv()

    def drain(self):
        for copy in self.used:
            copy.wait_send()


class SmallSum:
    def __init__(self, r, tag, first, rows, grid):
        self.r, self.first, self.rows, self.grid, self.used = r, first, rows, grid, []
        for name in ("given", "one", "two", "x", "y", "z", "sends", "recvs"):
            setattr(self, name, getattr(r, f"{tag}_{name}"))

    def send(self, source, target, peer):
        copy = remote(source, target, self.sends, self.recvs, len(self.used), peer)
        self.used.append(copy)
        copy.start()

    def add(self, ref, count):
        total = ref[0].astype(single)
        for k in range(1, count):
            total = total + ref[k].astype(single)
        return total.astype(bfloat)

    def step_one(self):
        grid = self.grid
        self.given[...] = self.r.small_wide[self.first : self.first + self.rows, :].astype(bfloat)
        self.x[grid.x] = self.given[...]
        for k in (2, 1, 3):
            self.send(self.given, self.x.at[grid.x], grid.along_x(k))

    def step_two(self):
        grid = self.grid
        for copy in self.used[:3]:
            copy.wait_recv()
        self.one[...] = self.add(self.x, 4)
        self.y[grid.y] = self.one[...]
        for k in (2, 1, 3):
            self.send(self.one, self.y.at[grid.y], grid.along_y(k))

    def step_three(self):
        grid = self.grid
        for copy in self.used[3:6]:
            copy.wait_recv()
        self.two[...] = self.add(self.y, 4)
        self.z[grid.plane] = self.two[...]
        self.send(self.two, self.z.at[grid.plane], grid.across)

    def step_four(self):
        self.used[6].wait_recv()
        self.r.small_out[self.first : self.first + self.rows, :] = self.add(self.z, 2)

    def drain(self):
        for copy in self.used:
            copy.wait_send()


def small_scratch(tag, rows, width):
    block = pltpu.VMEM((rows, width), bfloat)
    found = {f"{tag}_{name}": block for name in ("given", "one", "two")}
    for name, count in (("x", 4), ("y", 4), ("z", 2)):
        found[f"{tag}_{name}"] = pltpu.VMEM((count, rows, width), bfloat)
    found[f"{tag}_sends"] = pltpu.SemaphoreType.DMA((7,))
    found[f"{tag}_recvs"] = pltpu.SemaphoreType.DMA((7,))
    return found


def backward_kernel(r):
    core, sibling, opposite = tensor_place()
    grid = Grid()
    peers = [sibling, opposite, grid.across]
    peers += [grid.along_x(k) for k in (1, 2, 3)] + [grid.along_y(k) for k in (1, 2, 3)]
    greet(peers)
    moves = Moves(r.moves)

    def fetch(*names):
        return [moves.start(getattr(r, name + "_h"), getattr(r, name)) for name in names]

    def ready(copies):
        for copy in copies:
            copy.wait()

    loads_zero = fetch("section_three")
    loads_one = fetch("out", "qkvc", "log", "qkv", "low")
    loads_two = fetch("section_two", "slope", "act", "dense_low", "dense_in", "dense_out")
    loads_three = fetch("section_one", "images")
    stores = []
    sums = [TensorSum(r, n, r.total) for n in range(3)]
    width = r.out.shape[1]
    upper = GroupSum(r, "u", 0, 768, grid)
    dense = GroupSum(r, "d", 768, 1536, grid)
    lower = GroupSum(r, "l", 2304, 768, grid)
    early = SmallSum(r, "early", 0, EXPERTS, grid)
    late = SmallSum(r, "late", EXPERTS, SMALL - EXPERTS, grid)
    mixed = MixedSum(r)

    def deliver(array, row, rows, target):
        half = array.shape[1] // 2
        for h in range(2):
            source = r.result.at[h, pl.ds(row, rows), :]
            stores.append(
                moves.start(source, array.at[pl.ds(target, rows), pl.ds(h * half, half)])
            )

    r.small_wide[...] = jnp.zeros_like(r.small_wide)
    gates = [r.table[:, k : k + 1] for k in range(2)]
    pulls = [r.gate_sums[:, k : k + 1] for k in range(2)]
    mean = gates[0] * pulls[0] + gates[1] * pulls[1]
    experts = lax.broadcasted_iota(jnp.int32, (r.table.shape[0], EXPERTS), 1).astype(single)
    grad_logits = 0.0
    for k in range(2):
        pick = r.table[:, 4 + k : 5 + k] == experts
        grad_logits = grad_logits + jnp.where(pick, gates[k] * (pulls[k] - mean), 0.0)
    grad_logits = grad_logits.astype(bfloat)
    ready(loads_zero)
    pl.semaphore_wait(pltpu.get_barrier_semaphore(), 9)
    mixed.step_one()
    rows = r.section_three[...]
    normal, unused = normal_of(rows)
    moe_low = (normal * r.gain[3:4, :] + r.shift[3:4, :]).astype(bfloat)
    r.small_wide[0:EXPERTS, :] = dot_first(grad_logits, moe_low)
    grad_normed = r.grad_experts[...].astype(single) + dot_rows(grad_logits, r.router[...])
    grad_in, gain_part, shift_part = norm_back(grad_normed, rows, r.gain[3:4, :])
    grad = r.cotangent[...].astype(single) + grad_in
    r.grad[...] = grad
    r.small_wide[35:36, :] = gain_part
    r.small_wide[39:40, :] = shift_part
    r.small_wide[41:42, :] = jnp.sum(grad, axis=0, keepdims=True)
    ready(loads_one)
    attend_back(r, 1, grad)
    sums[0].start(attend_back_part(r, 1))
    attend_weights(r, 1, 0)
    upper.step_one()
    early.step_one()
    mixed.step_two()
    upper.step_two()
    early.step_two()
    upper.step_three()
    sums[0].finish()

    ready(loads_two)
    grad_in, gain_part, shift_part = norm_back(
        r.total[...].astype(single), r.section_two[...], r.gain[2:3, :]
    )
    r.small_wide[34:35, :] = gain_part
    r.small_wide[38:39, :] = shift_part
    grad = r.grad[...] + grad_in
    r.grad[...] = grad
    upper.step_four()
    early.step_three()
    grad_low = grad.astype(bfloat)
    r.grad_pre[...] = (dot_last(grad_low, r.dense_out[...]) * r.slope[...]).astype(bfloat)
    sums[1].start(lambda at: dot_last(r.grad_pre[...], r.dense_in[at, :]))
    put_grad(r, 768, dot_first(r.dense_low[...], r.grad_pre[...]))
    put_grad(r, 1536, dot_first(r.act[...], grad_low))
    dense.step_one()
    upper.step_five()
    mixed.step_three()
    early.step_four()
    dense.step_two()
    upper.step_six()
    sums[1].finish()

    ready(loads_three)
    grad_in, gain_part, shift_part = norm_back(
        r.total[...].astype(single), r.section_one[...], r.gain[1:2, :]
    )
    r.small_wide[33:34, :] = gain_part
    r.small_wide[37:38, :] = shift_part
    grad = r.grad[...] + grad_in
    r.grad[...] = grad
    r.small_wide[40:41, :] = jnp.sum(grad, axis=0, keepdims=True)
    upper.step_seven()
    attend_back(r, 0, grad)
    dense.step_three()
    sums[2].start(attend_back_part(r, 0))
    attend_weights(r, 0, 2304)
    lower.step_one()
    upper.step_eight()
    deliver(r.qkv_grad, 0, 3 * width, 3 * width)
    deliver(r.out_grad, 3 * width, width, width)
    dense.step_four()
    lower.step_two()
    dense.step_five()
    lower.step_three()
    sums[2].finish()

    grad_in, gain_part, shift_part = norm_back(
        r.total[...].astype(single), r.images[...].astype(single), r.gain[0:1, :]
    )
    r.small_wide[32:33, :] = gain_part
    r.small_wide[36:37, :] = shift_part
    r.input_grad[...] = r.grad[...] + grad_in
    late.step_one()
    dense.step_six()
    lower.step_four()
    late.step_two()
    lower.step_five()
    dense.step_seven()
    late.step_three()
    lower.step_six()
    late.step_four()
    lower.step_seven()
    dense.step_eight()
    deliver(r.dense_in_grad, 768, 768, 0)
    deliver(r.dense_out_grad, 1536, 768, 0)
    lower.step_eight()
    deliver(r.qkv_grad, 2304, 3 * width, 0)
    deliver(r.out_grad, 2304 + 3 * width, width, 0)
    for one in sums + [upper, dense, lower, early, late, mixed]:
        one.drain()
    ready(stores)


def moe_kernel(r):
    core, sibling, opposite = tensor_place()
    dp = lax.axis_index("dp")
    grid = Grid()
    half = r.arrived.shape[3] // 2
    tokens = r.table.shape[0]
    block = 4 * STRIDE
    barrier = pltpu.get_barrier_semaphore()

    def greet_one(k, carry):
        pl.semaphore_signal(barrier, inc=1, device_id={"dp": dp_peer(k)}, device_id_type=MESH)
        return carry

    lax.fori_loop(1, EXPERTS, greet_one, 0)
    greet([sibling, opposite])
    moves = Moves(r.moves)
    load_in = moves.start(r.expert_in_h.at[0], r.expert_in)
    load_out = moves.start(r.expert_out_h.at[0], r.expert_out)
    own_block = moves.start(r.sent.at[core, dp], r.arrived.at[core, dp])
    pl.semaphore_wait(barrier, EXPERTS + 1)

    def dispatch(peer, here):
        return pltpu.make_async_remote_copy(
            src_ref=r.sent.at[core, peer],
            dst_ref=r.arrived.at[core, here],
            send_sem=r.send_sems.at[peer],
            recv_sem=r.recv_sems.at[here],
            device_id={"dp": peer},
            device_id_type=MESH,
        )

    def share(source):
        block_ref = r.arrived.at[core, source]
        return remote(block_ref, block_ref, r.pass_sems, r.land_sems, source, sibling)

    def swap(source):
        return remote(r.give.at[source], r.got.at[source], r.give_sems, r.got_sems, source, sibling)

    def answer(peer, here):
        return pltpu.make_async_remote_copy(
            src_ref=r.answer.at[peer],
            dst_ref=r.returned.at[here],
            send_sem=r.back_sems.at[peer],
            recv_sem=r.home_sems.at[here],
            device_id={"dp": peer},
            device_id_type=MESH,
        )

    def offsets(p):
        return lax.rem(p, 2), lax.rem(p // 2 + lax.rem(p, 2), 4)

    def send_block(p, carry):
        dz, dx = offsets(p)
        base = lax.rem(grid.plane + dz, 2) * 16 + lax.rem(grid.x + dx, 4) * 4
        for dy in range(4):
            peer = base + lax.rem(grid.y + dy, 4)

            @pl.when(peer != dp)
            def start():
                dispatch(peer, dp).start()

        return carry

    def base_of(p):
        dz, dx = offsets(p)
        return lax.rem(grid.plane + dz, 2) * 16 + lax.rem(grid.x + 4 - dx, 4) * 4

    def receive(p):
        base = base_of(p)
        for dy in range(4):
            source = base + lax.rem(grid.y + 4 - dy, 4)

            @pl.when(source != dp)
            def wait():
                dispatch(source, source).wait_recv()

            @pl.when(source == dp)
            def wait_own():
                own_block.wait()

            share(source).start()

    def compute(p):
        base = base_of(p)
        for y in range(4):
            share(base + y).wait_recv()
            at = slice(y * STRIDE, (y + 1) * STRIDE)
            for h in range(2):
                rows = r.arrived[h, base + y].astype(single)
                r.wide_x[at, h * half : (h + 1) * half] = rows[:, :half]
                r.wide_g[at, h * half : (h + 1) * half] = rows[:, half:]
        at = pl.ds(pl.multiple_of(p * block, 16), block)
        rows = r.wide_x[...].astype(bfloat)
        rows_grad = r.wide_g[...].astype(bfloat)
        r.rows[at, :] = rows
        r.rows_grad[at, :] = rows_grad
        pre = dot_rows(rows, r.expert_in[...])
        grad_act = dot_last(rows_grad, r.expert_out[...])
        tail = 0.5 * (1.0 + lax.erf(pre * (0.5**0.5)))
        act = (pre * tail).astype(bfloat)
        slope = tail + pre * (jnp.exp(-0.5 * pre * pre) * 0.3989422804014327)
        grad_pre = (grad_act * slope).astype(bfloat)
        r.act[at, :] = act
        r.grad_pre[at, :] = grad_pre
        r.wide_x[...] = dot_rows(act, r.expert_out[...])
        r.wide_g[...] = dot_last(grad_pre, r.expert_in[...])
        for y in range(4):
            at = slice(y * STRIDE, (y + 1) * STRIDE)
            for which, target in ((1 - core, r.give), (core, r.kept)):
                columns = pl.ds(pl.multiple_of(which * half, LANES), half)
                target[base + y, :, :half] = r.wide_x[at, columns].astype(bfloat)
                target[base + y, :, half:] = r.wide_g[at, columns].astype(bfloat)
            swap(base + y).start()

    def respond(p):
        base = base_of(p)
        for y in range(4):
            source = base + y
            swap(source).wait_recv()
            total = r.kept[source].astype(single) + r.got[source].astype(single)
            r.answer[source] = total.astype(bfloat)

            @pl.when(source != dp)
            def start():
                answer(source, dp).start()

            @pl.when(source == dp)
            def keep():
                r.returned[dp] = total.astype(bfloat)

    def step(i, carry):
        pl.when(i < 8)(lambda: receive(i))
        pl.when((i >= 1) & (i < 9))(lambda: compute(i - 1))
        pl.when(i >= 2)(lambda: respond(i - 2))
        return carry

    lax.fori_loop(0, 8, send_block, 0)
    load_in.wait()
    load_out.wait()
    lax.fori_loop(0, 10, step, 0)
    r.weight_grad[0] = dot_first(r.act[...], r.rows_grad[...])
    store_out = moves.start(r.weight_grad.at[0], r.expert_out_grad.at[0])
    r.weight_grad[1] = dot_first(r.rows[...], r.grad_pre[...])
    store_in = moves.start(r.weight_grad.at[1], r.expert_in_grad.at[0])

    ids = lax.broadcasted_iota(jnp.int32, (tokens, SLOTS), 1).astype(single)
    for k in range(2):
        r.hits[k] = jnp.where(ids == r.table[:, 2 + k : 3 + k], 1.0, 0.0).astype(bfloat)

    def come_home(i, carry):
        p, dy = i // 4, lax.rem(i, 4)
        dz, dx = offsets(p)
        source = lax.rem(grid.plane + dz, 2) * 16 + lax.rem(grid.x + dx, 4) * 4 + lax.rem(grid.y + dy, 4)

        @pl.when(source != dp)
        def wait():
            answer(source, source).wait_recv()

        at = pl.ds(pl.multiple_of(source * STRIDE, 8), STRIDE)
        r.wide_home[at, :] = r.returned[source].astype(single)
        return carry

    lax.fori_loop(0, EXPERTS, come_home, 0)
    back = r.wide_home[:, half:].astype(bfloat)
    r.home[...] = r.wide_home[:, :half].astype(bfloat)
    own = r.cotangent[:, pl.ds(pl.multiple_of(core * half, LANES), half)].astype(single)

    second = [remote(r.part.at[j], r.part_got.at[j], r.z_sends, r.z_recvs, j, opposite) for j in range(3)]
    third = [remote(r.part_sum.at[j], r.part_end.at[j], r.z_sends, r.z_recvs, 4 + j, sibling) for j in range(3)]
    second.append(remote(r.gate_rows, r.gate_got, r.z_sends, r.z_recvs, 3, opposite))
    third.append(remote(r.gate_mid, r.gate_end, r.z_sends, r.z_recvs, 7, sibling))
    normed = dot_rows(r.hits[0], back) + dot_rows(r.hits[1], back)
    for j in range(3):
        r.part[j] = normed[:, j * LANES : (j + 1) * LANES].astype(bfloat)
        second[j].start()
    picked = [dot_rows(r.hits[k], r.home[...]) for k in range(2)]
    gate = [jnp.sum(p * own, axis=1, keepdims=True) for p in picked]
    level = lax.broadcasted_iota(jnp.int32, (tokens, tokens), 0)
    across = lax.broadcasted_iota(jnp.int32, (tokens, tokens), 1)
    r.gate_rows[...] = jnp.zeros_like(r.gate_rows)
    for k in range(2):
        spread = jnp.where(level == across, gate[k], 0.0)
        r.gate_rows[k : k + 1, :] = jnp.sum(spread, axis=0, keepdims=True)
    second[3].start()
    mixed = r.table[:, 0:1] * picked[0] + r.table[:, 1:2] * picked[1]
    for j in range(3):
        r.mixed[j] = mixed[:, j * LANES : (j + 1) * LANES].astype(bfloat)

    def columns(which, j):
        return pl.ds(pl.multiple_of((which * THIRDS + j) * LANES, LANES), LANES)

    for j in range(3):
        second[j].wait_recv()
        whole = (r.part[j].astype(single) + r.part_got[j].astype(single)).astype(bfloat)
        r.part_sum[j] = whole
        third[j].start()
        r.grad_experts[:, columns(core, j)] = whole
    second[3].wait_recv()
    r.gate_mid[...] = r.gate_rows[...] + r.gate_got[...]
    third[3].start()
    for j in range(3):
        third[j].wait_recv()
        r.grad_experts[:, columns(1 - core, j)] = r.part_end[j]
    third[3].wait_recv()
    r.gate_sums[...] = jnp.zeros_like(r.gate_sums)
    for k in range(2):
        sums = r.gate_mid[k : k + 1, :] + r.gate_end[k : k + 1, :]
        spread = jnp.where(level == across, sums, 0.0)
        r.gate_sums[:, k : k + 1] = jnp.sum(spread, axis=1, keepdims=True)
    for copy in second + third:
        copy.wait_send()

    def drain(k, carry):
        share(k).wait_send()
        swap(k).wait_send()

        @pl.when(k != dp)
        def wait():
            dispatch(k, dp).wait_send()
            answer(k, dp).wait_send()

        return carry

    lax.fori_loop(0, EXPERTS, drain, 0)
    store_out.wait()
    store_in.wait()


def moe_whole(sent, table, cotangent, expert_in, expert_out, collective_id):
    tokens, width = cotangent.shape
    half = width // 2
    slab = pltpu.VMEM((EXPERTS, STRIDE, width), bfloat)
    rows = pltpu.VMEM((SLOTS, width), bfloat)
    parts = pltpu.VMEM((3, tokens, LANES), bfloat)
    gate = pltpu.VMEM((8, tokens), single)
    block = pltpu.VMEM((4 * STRIDE, width), single)
    every = pltpu.SemaphoreType.DMA((EXPERTS,))
    scratch = {name: slab for name in ("give", "kept", "got", "answer", "returned")}
    scratch.update({name: rows for name in ("rows", "rows_grad", "act", "grad_pre")})
    scratch.update({name: parts for name in ("part", "part_got", "part_sum", "part_end")})
    scratch.update({"gate_" + name: gate for name in ("rows", "got", "mid", "end")})
    names = ("send", "recv", "pass", "land", "give", "got", "back", "home")
    scratch.update({name + "_sems": every for name in names})
    scratch.update(
        arrived=pltpu.VMEM((2, EXPERTS, STRIDE, width), bfloat),
        expert_in=pltpu.VMEM(expert_in.shape[1:], bfloat),
        expert_out=pltpu.VMEM(expert_out.shape[1:], bfloat),
        weight_grad=pltpu.VMEM((2,) + expert_in.shape[1:], single),
        wide_x=block,
        wide_g=block,
        wide_home=pltpu.VMEM((SLOTS, width), single),
        home=pltpu.VMEM((SLOTS, half), bfloat),
        hits=pltpu.VMEM((2, tokens, SLOTS), bfloat),
        z_sends=pltpu.SemaphoreType.DMA((8,)),
        z_recvs=pltpu.SemaphoreType.DMA((8,)),
        moves=pltpu.SemaphoreType.DMA((8,)),
    )
    return big_call(
        moe_kernel,
        "moe",
        {
            "sent": (sent.reshape(2, EXPERTS, STRIDE, width), "hbm"),
            "table": (table, "vmem"),
            "cotangent": (cotangent, "vmem"),
            "expert_in_h": (expert_in, "hbm"),
            "expert_out_h": (expert_out, "hbm"),
        },
        {
            "expert_in_grad": (expert_in.shape, single, "hbm"),
            "expert_out_grad": (expert_out.shape, single, "hbm"),
            "mixed": ((3, tokens, LANES), bfloat, "vmem"),
            "grad_experts": ((tokens, width), bfloat, "vmem"),
            "gate_sums": ((tokens, LANES), single, "vmem"),
        },
        scratch,
        collective_id,
    )


class MixedSum:
    def __init__(self, r):
        core, sibling, opposite = tensor_place()
        self.r, self.core = r, core
        self.second = [
            remote(r.mixed.at[j], r.m_got.at[j], r.m_sends, r.m_recvs, j, opposite) for j in range(3)
        ]
        self.third = [
            remote(r.m_sum.at[j], r.m_end.at[j], r.m_sends, r.m_recvs, 3 + j, sibling) for j in range(3)
        ]

    def step_one(self):
        for copy in self.second:
            copy.start()

    def step_two(self):
        r = self.r
        for j in range(3):
            self.second[j].wait_recv()
            whole = r.mixed[j].astype(single) + r.m_got[j].astype(single)
            r.m_sum[j] = whole.astype(bfloat)
            self.third[j].start()
            self.put(self.core, j, r.m_sum[j])

    def put(self, which, j, value):
        at = pl.ds(pl.multiple_of((which * THIRDS + j) * LANES, LANES), LANES)
        rows = self.r.section_three[:, at] + value.astype(single)
        self.r.output[:, at] = rows.astype(bfloat)

    def step_three(self):
        for j in range(3):
            self.third[j].wait_recv()
            self.put(1 - self.core, j, self.r.m_end[j])

    def drain(self):
        for copy in self.second + self.third:
            copy.wait_send()


def finish_kernel(r):
    moves = Moves(r.moves)
    names = ("qkv", "out", "dense_in", "dense_out")
    whole = ("expert_in", "expert_out", "input_grad", "output")
    passing = [moves.start(getattr(r, name + "_h"), getattr(r, name + "_pass")) for name in whole]
    loads = [moves.start(getattr(r, name + "_h"), getattr(r, name + "_low")) for name in names]
    stores = []
    for name, load in zip(whole, passing):
        load.wait()
        stores.append(moves.start(getattr(r, name + "_pass"), getattr(r, name + "_f")))
    small = r.small[...].astype(single)
    part = r.qv_bias.shape[2]
    r.router[...] = small[:EXPERTS]
    r.gain[...] = small[32:36]
    r.shift[...] = small[36:40]
    r.out_bias[...] = small[40:42]
    r.qv_bias[0] = small[42:44, :part]
    r.qv_bias[1] = small[44:46, :part]
    for name, load in zip(names, loads):
        load.wait()
        low, wide = getattr(r, name + "_low"), getattr(r, name + "_wide")
        rows = low.shape[0]
        piece = 192

        def cast(i, carry):
            at = pl.ds(pl.multiple_of(i * piece, 16), piece)
            wide[at, :] = low[at, :].astype(single)
            return carry

        lax.fori_loop(0, rows // piece, cast, 0)
        stores.append(moves.start(wide, getattr(r, name + "_f")))
    for store in stores:
        store.wait()


def finish(last, moe, part, width):
    arrays = {"qkv": last.qkv_grad, "out": last.out_grad}
    arrays.update({"dense_in": last.dense_in_grad, "dense_out": last.dense_out_grad})
    ins = {name + "_h": (array, "hbm") for name, array in arrays.items()}
    ins["small"] = (last.small_out, "vmem")
    outs = {name + "_f": (array.shape, single, "hbm") for name, array in arrays.items()}
    whole = {"expert_in": moe.expert_in_grad, "expert_out": moe.expert_out_grad}
    whole.update(input_grad=last.input_grad, output=last.output)
    for name, array in whole.items():
        ins[name + "_h"] = (array, "hbm")
        outs[name + "_f"] = (array.shape, array.dtype, "hbm")
    outs.update(
        router=((EXPERTS, width), single, "vmem"),
        gain=((4, width), single, "vmem"),
        shift=((4, width), single, "vmem"),
        out_bias=((2, width), single, "vmem"),
        qv_bias=((2, 2, part), single, "vmem"),
    )
    scratch = {name + "_low": pltpu.VMEM(array.shape, bfloat) for name, array in arrays.items()}
    scratch.update({name + "_wide": pltpu.VMEM(a.shape, single) for name, a in arrays.items()})
    scratch.update({name + "_pass": pltpu.VMEM(a.shape, a.dtype) for name, a in whole.items()})
    scratch["moves"] = pltpu.SemaphoreType.DMA((16,))
    return big_call(finish_kernel, "finish", ins, outs, scratch)


def per_device(
    images,
    routes,
    cotangent,
    qkv_weight,
    out_weight,
    qv_bias,
    out_bias,
    ln_gain,
    ln_bias,
    dense_in,
    dense_out,
    router,
    expert_in,
    expert_out,
):
    tokens, width = images.shape
    part = out_weight.shape[1]
    hidden = dense_in.shape[1]
    qkv = jnp.transpose(qkv_weight, (0, 2, 3, 1)).reshape(2, 3 * part, width)
    full, low = (tokens, width), bfloat
    kept = {
        "section_one": (full, single),
        "section_two": (full, single),
        "section_three": (full, single),
        "dense_low": (full, low),
        "slope": ((tokens, hidden), single),
        "act": ((tokens, hidden), low),
        "low": ((2, tokens, width), low),
        "qkvc": ((2, 4, tokens, part), low),
        "log": ((2, tokens, LANES), single),
    }
    weights = {
        "dense_in": (dense_in.shape, low),
        "dense_out": (dense_out.shape, low),
    }

    def vmem(names, table):
        return {name: pltpu.VMEM(*table[name]) for name in names}

    sections = ("section_one", "section_two", "section_three")
    outs = {name + ("" if name in sections else "_h"): kept[name] + ("hbm",) for name in kept}
    outs["sent"] = ((2, SLOTS, width), low, "hbm")
    outs["table"] = ((tokens, LANES), single, "vmem")
    scratch = sum_scratch(tokens, 3)
    scratch.update(vmem([name for name in kept if name not in sections], kept))
    scratch.update(vmem(list(weights), weights))
    scratch.update(
        section=pltpu.VMEM((3, tokens, width), single),
        cotangent=pltpu.VMEM(full, low),
        moe_low=pltpu.VMEM(full, low),
        routes=pltpu.VMEM((tokens, 2), jnp.int32),
        scaled=pltpu.VMEM((2, tokens, width), low),
        routed=pltpu.VMEM((2, SLOTS, width), low),
        total=pltpu.VMEM(full, low),
        moves=pltpu.SemaphoreType.DMA((24,)),
    )
    done = big_call(
        forward_kernel,
        "forward",
        {
            "images": (images, "vmem"),
            "qkv": (qkv, "vmem"),
            "out": (out_weight, "vmem"),
            "qv_bias": (qv_bias, "vmem"),
            "out_bias": (out_bias, "vmem"),
            "gain": (ln_gain, "vmem"),
            "shift": (ln_bias, "vmem"),
            "dense_in_h": (dense_in, "hbm"),
            "dense_out_h": (dense_out, "hbm"),
            "cotangent_h": (cotangent, "hbm"),
            "routes_row": (routes.T, "vmem"),
            "router": (router.T, "vmem"),
        },
        outs,
        scratch,
        1,
    )
    moe = moe_whole(done.sent, done.table, cotangent, expert_in, expert_out, 3)

    outs = {
        "output": (full, low, "vmem"),
        "input_grad": (full, single, "vmem"),
        "qkv_grad": ((6 * part, width), low, "hbm"),
        "out_grad": ((2 * part, width), low, "hbm"),
        "dense_in_grad": (dense_in.shape, low, "hbm"),
        "dense_out_grad": (dense_out.shape, low, "hbm"),
        "small_out": ((SMALL, width), low, "vmem"),
    }
    scratch = sum_scratch(tokens, 3)
    scratch.update(vmem(list(kept), kept))
    scratch.update(vmem(list(weights), weights))
    for tag, rows in (("u", 768), ("d", 1536), ("l", 768)):
        scratch.update(group_scratch(tag, rows, width // 2))
    scratch.update(small_scratch("early", EXPERTS, width))
    scratch.update(small_scratch("late", SMALL - EXPERTS, width))
    scratch.update(
        images=pltpu.VMEM(full, low),
        qkv=pltpu.VMEM(qkv.shape, low),
        out=pltpu.VMEM(out_weight.shape, low),
        total=pltpu.VMEM(full, low),
        grad=pltpu.VMEM(full, single),
        grad_low=pltpu.VMEM(full, low),
        grad_pre=pltpu.VMEM((tokens, hidden), low),
        grad_qkv=pltpu.VMEM((3, tokens, part), low),
        given=pltpu.VMEM((2, BIG, width // 2), low),
        result=pltpu.VMEM((2, BIG, width // 2), low),
        small_wide=pltpu.VMEM((SMALL, width), single),
        m_got=pltpu.VMEM((3, tokens, LANES), low),
        m_sum=pltpu.VMEM((3, tokens, LANES), low),
        m_end=pltpu.VMEM((3, tokens, LANES), low),
        m_sends=pltpu.SemaphoreType.DMA((6,)),
        m_recvs=pltpu.SemaphoreType.DMA((6,)),
        moves=pltpu.SemaphoreType.DMA((32,)),
    )
    ins = {
        "mixed": (moe.mixed, "vmem"),
        "grad_experts": (moe.grad_experts, "vmem"),
        "gate_sums": (moe.gate_sums, "vmem"),
        "table": (done.table, "vmem"),
        "router": (router.T, "vmem"),
        "cotangent": (cotangent, "vmem"),
        "gain": (ln_gain, "vmem"),
        "shift": (ln_bias, "vmem"),
        "images_h": (images, "hbm"),
        "qkv_h": (qkv, "hbm"),
        "out_h": (out_weight, "hbm"),
        "dense_in_h": (dense_in, "hbm"),
        "dense_out_h": (dense_out, "hbm"),
    }
    for name in kept:
        ins[name + "_h"] = (getattr(done, name if name in sections else name + "_h"), "hbm")
    last = big_call(backward_kernel, "backward", ins, outs, scratch, 2)
    end = finish(last, moe, part, width)
    qkv_weight_grad = jnp.transpose(end.qkv_f.reshape(2, 3, part, width), (0, 3, 1, 2))
    out_weight_grad = end.out_f.reshape(2, part, width)
    dense_in_grad, dense_out_grad = end.dense_in_f, end.dense_out_f
    router_grad = end.router.T
    ln_gain_grad, ln_bias_grad, out_bias_grad = end.gain, end.shift, end.out_bias
    qv_bias_grad = end.qv_bias
    output, input_grad = end.output_f, end.input_grad_f
    expert_in_grad, expert_out_grad = end.expert_in_f, end.expert_out_f
    return (
        output,
        input_grad,
        qkv_weight_grad,
        out_weight_grad,
        qv_bias_grad,
        out_bias_grad,
        ln_gain_grad,
        ln_bias_grad,
        dense_in_grad,
        dense_out_grad,
        router_grad,
        expert_in_grad,
        expert_out_grad,
    )


def solution(mesh):
    in_specs = (
        P("dp", None),
        P("dp", None),
        P("dp", None),
        P(None, None, None, "tensor"),
        P(None, "tensor", None),
        P(None, None, "tensor"),
        P(),
        P(),
        P(),
        P(None, "tensor"),
        P("tensor", None),
        P(),
        P("dp", None, "tensor"),
        P("dp", "tensor", None),
    )
    out_specs = (
        P("dp", None),
        P("dp", None),
        P(None, None, None, "tensor"),
        P(None, "tensor", None),
        P(None, None, "tensor"),
        P(),
        P(),
        P(),
        P(None, "tensor"),
        P("tensor", None),
        P(),
        P("dp", None, "tensor"),
        P("dp", "tensor", None),
    )
    return jax.shard_map(
        per_device, mesh=mesh, in_specs=in_specs, out_specs=out_specs, check_vma=False
    )
```

```python
import functools

import jax
import jax.numpy as jnp
from jax import lax
from jax.experimental import pallas as pl
from jax.experimental.pallas import tpu as pltpu
from jax.sharding import PartitionSpec as P

HEAD = 64
SEQ = 197


epsilon = 1e-06
bfloat = jnp.bfloat16
single = jnp.float32


MESH = pl.DeviceIdType.MESH


BIG = 3072
SMALL = 48
EXPERTS = 32
STRIDE = 40
SLOTS = EXPERTS * STRIDE


def dot_rows(a, b):
    return lax.dot_general(a, b, (((1,), (0,)), ((), ())), preferred_element_type=single)


def dot_last(a, b):
    return lax.dot_general(a, b, (((1,), (1,)), ((), ())), preferred_element_type=single)


def dot_first(a, b):
    return lax.dot_general(a, b, (((0,), (0,)), ((), ())), preferred_element_type=single)


VMEM_SPEC = pl.BlockSpec(memory_space=pltpu.VMEM)


def dp_peer(k):
    dp = lax.axis_index("dp")
    plane = lax.rem(dp // 16 + k // 16, 2)
    x = lax.rem(lax.rem(dp // 4, 4) + lax.rem(k // 4, 4), 4)
    y = lax.rem(lax.rem(dp, 4) + lax.rem(k, 4), 4)
    return plane * 16 + x * 4 + y


def normal_of(rows):
    average = jnp.mean(rows, axis=-1, keepdims=True)
    centered = rows - average
    variance = jnp.mean(centered * centered, axis=-1, keepdims=True)
    inverse = lax.rsqrt(variance + epsilon)
    return centered * inverse, inverse


def norm_back(grad_normed, rows, gain_row):
    normal, inverse = normal_of(rows)
    scaled = grad_normed * gain_row
    mean_one = jnp.mean(scaled, axis=-1, keepdims=True)
    mean_two = jnp.mean(scaled * normal, axis=-1, keepdims=True)
    grad_in = inverse * (scaled - mean_one - normal * mean_two)
    gain_part = jnp.sum(grad_normed * normal, axis=0, keepdims=True)
    return grad_in, gain_part, jnp.sum(grad_normed, axis=0, keepdims=True)


def same_image(tokens):
    first = lax.broadcasted_iota(jnp.int32, (tokens, tokens), 0) // SEQ
    second = lax.broadcasted_iota(jnp.int32, (tokens, tokens), 1) // SEQ
    return first == second


class Refs:
    def __init__(self, names, refs):
        for name, ref in zip(names, refs):
            setattr(self, name, ref)


def big_call(kernel, name, ins, outs, scratch, collective_id=None, limit=58):
    names = list(ins) + list(outs) + list(scratch)
    hbm = pl.BlockSpec(memory_space=pl.ANY)

    def body(*refs):
        kernel(Refs(names, refs))

    found = pl.pallas_call(
        body,
        out_shape=[jax.ShapeDtypeStruct(shape, kind) for shape, kind, unused in outs.values()],
        in_specs=[hbm if place == "hbm" else VMEM_SPEC for unused, place in ins.values()],
        out_specs=[hbm if place == "hbm" else VMEM_SPEC for _, _, place in outs.values()],
        scratch_shapes=list(scratch.values()),
        compiler_params=pltpu.CompilerParams(
            collective_id=collective_id, has_side_effects=True, vmem_limit_bytes=limit * 2**20
        ),
        name=name,
    )(*[array for array, unused in ins.values()])
    return Refs(list(outs), found)


def tensor_place():
    t = lax.axis_index("tensor")
    core = lax.rem(t, 2)
    return core, {"tensor": t + 1 - 2 * core}, {"tensor": lax.rem(t + 2, 4)}


def remote(source, target, sends, recvs, index, peer):
    return pltpu.make_async_remote_copy(
        src_ref=source,
        dst_ref=target,
        send_sem=sends.at[index],
        recv_sem=recvs.at[index],
        device_id=peer,
        device_id_type=MESH,
    )


LANES = 128
THIRDS = 3


def sum_scratch(tokens, count):
    block = pltpu.VMEM((count, THIRDS, tokens, LANES), bfloat)
    names = ["give", "got_one", "sum_one", "got_two", "sum_two", "got_three"]
    found = {"t_" + name: block for name in names}
    found["t_own"] = pltpu.VMEM((tokens, THIRDS * LANES), single)
    found["t_sends"] = pltpu.SemaphoreType.DMA((count * 9,))
    found["t_recvs"] = pltpu.SemaphoreType.DMA((count * 9,))
    return found


class TensorSum:
    def __init__(self, r, number, total_ref):
        core, sibling, opposite = tensor_place()
        self.core, self.r, self.n, self.total = core, r, number, total_ref

        def copies(source, target, step, peer):
            return [
                remote(source.at[number, j], target.at[number, j], r.t_sends, r.t_recvs, number * 9 + step * 3 + j, peer)
                for j in range(THIRDS)
            ]

        self.first = copies(r.t_give, r.t_got_one, 0, sibling)
        self.second = copies(r.t_sum_one, r.t_got_two, 1, opposite)
        self.third = copies(r.t_sum_two, r.t_got_three, 2, sibling)

    def columns(self, which, j=0, count=1):
        return pl.ds(pl.multiple_of((which * THIRDS + j) * LANES, LANES), count * LANES)

    def start(self, partial):
        r, n = self.r, self.n
        other = partial(self.columns(1 - self.core, 0, THIRDS)).astype(bfloat)
        for j in range(THIRDS):
            r.t_give[n, j] = other[:, j * LANES : (j + 1) * LANES]
            self.first[j].start()
        r.t_own[...] = partial(self.columns(self.core, 0, THIRDS))
        for j in range(THIRDS):
            self.first[j].wait_recv()
            own = r.t_own[:, j * LANES : (j + 1) * LANES]
            r.t_sum_one[n, j] = (own + r.t_got_one[n, j].astype(single)).astype(bfloat)
            self.second[j].start()

    def finish(self):
        r, n = self.r, self.n
        for j in range(THIRDS):
            self.second[j].wait_recv()
            whole = (r.t_sum_one[n, j].astype(single) + r.t_got_two[n, j].astype(single)).astype(bfloat)
            r.t_sum_two[n, j] = whole
            self.third[j].start()
            self.total[:, self.columns(self.core, j)] = whole
        for j in range(THIRDS):
            self.third[j].wait_recv()
            self.total[:, self.columns(1 - self.core, j)] = r.t_got_three[n, j]

    def drain(self):
        for copy in self.first + self.second + self.third:
            copy.wait_send()


class Moves:
    def __init__(self, sems):
        self.sems, self.count = sems, 0

    def start(self, source, target):
        copy = pltpu.make_async_copy(source, target, self.sems.at[self.count])
        self.count += 1
        copy.start()
        return copy


def greet(peers):
    barrier = pltpu.get_barrier_semaphore()
    for peer in peers:
        pl.semaphore_signal(barrier, inc=1, device_id=peer, device_id_type=MESH)


def attend(r, rows, layer):
    width = r.out.shape[1]
    norm = 2 * layer
    normal, unused = normal_of(rows)
    low = (normal * r.gain[norm : norm + 1, :] + r.shift[norm : norm + 1, :]).astype(bfloat)
    r.low[layer] = low
    bias = r.qv_bias[layer]
    q = (dot_last(low, r.qkv[layer, :width, :]) + bias[0:1, :]).astype(bfloat)
    k = dot_last(low, r.qkv[layer, width : 2 * width, :]).astype(bfloat)
    v = (dot_last(low, r.qkv[layer, 2 * width :, :]) + bias[1:2, :]).astype(bfloat)
    r.qkvc[layer, 0], r.qkvc[layer, 1], r.qkvc[layer, 2] = q, k, v
    same = same_image(rows.shape[0])
    contexts = []
    for h in range(width // HEAD):
        at = slice(h * HEAD, (h + 1) * HEAD)
        scores = jnp.where(same, dot_last(q[:, at], k[:, at]) * HEAD ** (-0.5), -1e30)
        largest = jnp.max(scores, axis=-1, keepdims=True)
        exponent = jnp.exp(scores - largest)
        totals = jnp.sum(exponent, axis=-1, keepdims=True)
        r.log[layer, :, h : h + 1] = largest + jnp.log(totals)
        contexts.append(dot_rows((exponent / totals).astype(bfloat), v[:, at]))
    r.qkvc[layer, 3] = jnp.concatenate(contexts, axis=1).astype(bfloat)


def forward_kernel(r):
    core, sibling, opposite = tensor_place()
    greet([sibling, opposite])
    moves = Moves(r.moves)
    loads = [moves.start(r.dense_in_h, r.dense_in), moves.start(r.dense_out_h, r.dense_out)]
    loads += [moves.start(r.cotangent_h, r.cotangent)]
    stores = []
    sums = [TensorSum(r, n, r.total) for n in range(3)]

    def save(source, target):
        stores.append(moves.start(source, target))

    def out_part(layer):
        return lambda at: dot_rows(r.qkvc[layer, 3], r.out[layer, :, at])

    attend(r, r.images[...].astype(single), 0)
    pl.semaphore_wait(pltpu.get_barrier_semaphore(), 2)
    sums[0].start(out_part(0))
    sums[0].finish()

    rows = r.images[...].astype(single) + r.total[...].astype(single) + r.out_bias[0:1, :]
    r.section[0] = rows
    save(r.section.at[0], r.section_one)
    normal, unused = normal_of(rows)
    low = (normal * r.gain[1:2, :] + r.shift[1:2, :]).astype(bfloat)
    r.dense_low[...] = low
    save(r.dense_low, r.dense_low_h)
    for load in loads:
        load.wait()
    pre = dot_rows(low, r.dense_in[...])
    tail = 0.5 * (1.0 + lax.erf(pre * (0.5**0.5)))
    r.slope[...] = tail + pre * (jnp.exp(-0.5 * pre * pre) * 0.3989422804014327)
    save(r.slope, r.slope_h)
    r.act[...] = (pre * tail).astype(bfloat)
    save(r.act, r.act_h)
    sums[1].start(lambda at: dot_rows(r.act[...], r.dense_out[:, at]))
    sums[1].finish()

    rows = r.section[0] + r.total[...].astype(single)
    r.section[1] = rows
    save(r.section.at[1], r.section_two)
    attend(r, rows, 1)
    save(r.low, r.low_h)
    save(r.qkvc, r.qkvc_h)
    save(r.log, r.log_h)
    sums[2].start(out_part(1))
    sums[2].finish()

    rows = r.section[1] + r.total[...].astype(single) + r.out_bias[1:2, :]
    r.section[2] = rows
    save(r.section.at[2], r.section_three)
    moe_route_body(r, rows, save)
    for one in sums:
        one.drain()
    for store in stores:
        store.wait()


def moe_route_body(r, rows, save):
    tokens, width = rows.shape
    half = width // 2
    normal, unused = normal_of(rows)
    r.moe_low[...] = (normal * r.gain[3:4, :] + r.shift[3:4, :]).astype(bfloat)
    logits = dot_last(r.moe_low[...], r.router[...])
    experts = lax.broadcasted_iota(jnp.int32, (tokens, EXPERTS), 1)
    before = lax.broadcasted_iota(jnp.int32, (tokens, tokens), 0)
    after = lax.broadcasted_iota(jnp.int32, (tokens, tokens), 1)
    for k in range(2):
        spread = jnp.where(before == after, r.routes_row[k : k + 1, :].astype(single), 0.0)
        r.routes[:, k : k + 1] = jnp.sum(spread, axis=1, keepdims=True).astype(jnp.int32)
    picks = [r.routes[:, k : k + 1] == experts for k in range(2)]
    chosen = [jnp.sum(jnp.where(pick, logits, 0.0), axis=1, keepdims=True) for pick in picks]
    largest = jnp.maximum(chosen[0], chosen[1])
    powers = [jnp.exp(c - largest) for c in chosen]
    total = powers[0] + powers[1]
    gates = [power / total for power in powers]
    r.table[...] = jnp.zeros_like(r.table)
    for k in range(2):
        r.table[:, k : k + 1] = gates[k]
    cotangent = r.cotangent[...].astype(single)
    for k in range(2):
        r.scaled[k] = (gates[k] * cotangent).astype(bfloat)

    either = [jnp.where(pick, 1.0, 0.0) for pick in picks]
    lower = jnp.where(after < before, 1.0, 0.0).astype(bfloat)
    running = dot_rows(lower, (either[0] + either[1]).astype(bfloat))
    for k in range(2):
        rank = jnp.sum(running * either[k], axis=1, keepdims=True).astype(jnp.int32)
        slots = r.routes[:, k : k + 1] * STRIDE + rank
        r.table[:, 2 + k : 3 + k] = slots.astype(single)
        r.table[:, 4 + k : 5 + k] = r.routes[:, k : k + 1].astype(single)

    experts_row = lax.broadcasted_iota(jnp.int32, (EXPERTS, tokens), 0)
    either_row = [jnp.where(r.routes_row[k : k + 1, :] == experts_row, 1.0, 0.0) for k in range(2)]
    upper = jnp.where(before < after, 1.0, 0.0).astype(bfloat)
    running_row = dot_rows((either_row[0] + either_row[1]).astype(bfloat), upper)
    slots_row = []
    for k in range(2):
        rank = jnp.sum(running_row * either_row[k], axis=0, keepdims=True).astype(jnp.int32)
        slots_row.append(r.routes_row[k : k + 1, :] * STRIDE + rank)

    block = SLOTS // 4
    for i in range(4):
        ids = lax.broadcasted_iota(jnp.int32, (block, tokens), 0) + i * block
        hits = [jnp.where(ids == slots_row[k], 1.0, 0.0) for k in range(2)]
        moved = dot_rows((hits[0] + hits[1]).astype(bfloat), r.moe_low[...]).astype(bfloat)
        moved_grad = (
            dot_rows(hits[0].astype(bfloat), r.scaled[0]) + dot_rows(hits[1].astype(bfloat), r.scaled[1])
        ).astype(bfloat)
        at = slice(i * block, (i + 1) * block)
        for h in range(2):
            r.routed[h, at, :half] = moved[:, h * half : (h + 1) * half]
            r.routed[h, at, half:] = moved_grad[:, h * half : (h + 1) * half]
            save(r.routed.at[h, pl.ds(i * block, block), :], r.sent.at[h, pl.ds(i * block, block), :])


def attend_back(r, layer, grad_out):
    width = r.out.shape[1]
    grad_low = grad_out.astype(bfloat)
    r.grad_low[...] = grad_low
    q, k, v = r.qkvc[layer, 0], r.qkvc[layer, 1], r.qkvc[layer, 2]
    grad_context = dot_last(grad_low, r.out[layer]).astype(bfloat)
    same = same_image(q.shape[0])
    grads = [[], [], []]
    for h in range(width // HEAD):
        at = slice(h * HEAD, (h + 1) * HEAD)
        scores = jnp.where(same, dot_last(q[:, at], k[:, at]) * HEAD ** (-0.5), -1e30)
        probs = jnp.exp(scores - r.log[layer, :, h : h + 1])
        grad_probs = dot_last(grad_context[:, at], v[:, at])
        row_total = jnp.sum(probs * grad_probs, axis=-1, keepdims=True)
        grad_scores = (probs * (grad_probs - row_total)).astype(bfloat)
        grads[0].append(dot_rows(grad_scores, k[:, at]) * HEAD ** (-0.5))
        grads[1].append(dot_first(grad_scores, q[:, at]) * HEAD ** (-0.5))
        grads[2].append(dot_first(probs.astype(bfloat), grad_context[:, at]))
    for part in range(3):
        r.grad_qkv[part] = jnp.concatenate(grads[part], axis=1).astype(bfloat)


def attend_weights(r, layer, base):
    width = r.out.shape[1]
    put_grad(r, base + 3 * width, dot_first(r.qkvc[layer, 3], r.grad_low[...]))
    for part in range(3):
        grad = r.grad_qkv[part]
        put_grad(r, base + part * width, dot_first(grad, r.low[layer]))
        if part != 1:
            row = 42 + 2 * layer + part // 2
            r.small_wide[row : row + 1, :width] = jnp.sum(grad.astype(single), axis=0, keepdims=True)


def attend_back_part(r, layer):
    width = r.out.shape[1]

    def partial(at):
        total = None
        for part in range(3):
            term = dot_rows(r.grad_qkv[part], r.qkv[layer, part * width : (part + 1) * width, at])
            total = term if total is None else total + term
        return total

    return partial


def put_grad(r, row, value):
    low = value.astype(bfloat)
    half = low.shape[1] // 2
    for h in range(2):
        r.given[h, row : row + low.shape[0], :] = low[:, h * half : (h + 1) * half]


def add_blocks(target, row, sources, rows):
    def body(i, carry):
        total = None
        for ref, start in sources:
            value = ref[pl.ds(pl.multiple_of(start + i * 16, 16), 16), :].astype(single)
            total = value if total is None else total + value
        target[pl.ds(pl.multiple_of(row + i * 16, 16), 16), :] = total.astype(bfloat)
        return carry

    lax.fori_loop(0, rows // 16, body, 0)


GROUP_COPIES = 38


def group_scratch(tag, rows, width):
    part, piece = rows // 4, rows // 16
    found = {}
    for name in ("near", "left", "right", "onward", "sum"):
        found[f"{tag}_{name}"] = pltpu.VMEM((2, part, width), bfloat)
    found[f"{tag}_got"] = pltpu.VMEM((2, 3, piece, width), bfloat)
    found[f"{tag}_piece"] = pltpu.VMEM((2, piece, width), bfloat)
    found[f"{tag}_pair"] = pltpu.VMEM((2, piece, width), bfloat)
    found[f"{tag}_sends"] = pltpu.SemaphoreType.DMA((GROUP_COPIES,))
    found[f"{tag}_recvs"] = pltpu.SemaphoreType.DMA((GROUP_COPIES,))
    return found


class Grid:
    def __init__(self):
        dp = lax.axis_index("dp")
        self.plane, self.x, self.y = dp // 16, lax.rem(dp // 4, 4), lax.rem(dp, 4)
        self.across = self.at(1 - self.plane, self.x, self.y)

    def at(self, plane, x, y):
        return {"dp": plane * 16 + x * 4 + y}

    def along_x(self, step):
        return self.at(self.plane, lax.rem(self.x + step, 4), self.y)

    def along_y(self, step):
        return self.at(self.plane, self.x, lax.rem(self.y + step, 4))


class GroupSum:
    def __init__(self, r, tag, base, rows, grid):
        self.r, self.base, self.part, self.piece, self.grid = r, base, rows // 4, rows // 16, grid
        names = ("near", "left", "right", "onward", "sum", "got", "piece", "pair", "sends", "recvs")
        for name in names:
            setattr(self, "b_" + name, getattr(r, f"{tag}_{name}"))
        self.used = []
        self.place = [grid.x, grid.y]
        self.along = [grid.along_x, grid.along_y]

    def send(self, source, target, peer):
        copy = remote(source, target, self.b_sends, self.b_recvs, len(self.used), peer)
        self.used.append(copy)
        copy.start()
        return copy

    def rows(self, ref, row, count):
        return ref.at[pl.ds(pl.multiple_of(row, 16), count), :]

    def row(self, h, step):
        return self.base + lax.rem(self.place[h] + step, 4) * self.part

    def both(self, ref):
        return [ref.at[h] for h in range(2)]

    def step_one(self):
        half = self.part // 2
        self.copies = []
        for h in range(2):
            s, near, left, right = (
                ref.at[h] for ref in (self.r.given, self.b_near, self.b_left, self.b_right)
            )
            fwd, back = self.along[h](1), self.along[h](3)
            self.copies.append([
                self.send(self.rows(s, self.row(h, 2), half), self.rows(near, 0, half), fwd),
                self.send(self.rows(s, self.row(h, 2) + half, half), self.rows(near, half, half), back),
                self.send(self.rows(s, self.row(h, 1) + half, half), self.rows(left, half, half), fwd),
                self.send(self.rows(s, self.row(h, 3), half), self.rows(right, 0, half), back),
            ])

    def step_two(self):
        half = self.part // 2
        for h in range(2):
            s, near, onward, left, right = (
                ref.at[h]
                for ref in (self.r.given, self.b_near, self.b_onward, self.b_left, self.b_right)
            )
            self.copies[h][0].wait_recv()
            add_blocks(onward, 0, [(s, self.row(h, 1)), (near, 0)], half)
            self.copies[h].append(
                self.send(self.rows(onward, 0, half), self.rows(left, 0, half), self.along[h](1))
            )
            self.copies[h][1].wait_recv()
            add_blocks(onward, half, [(s, self.row(h, 3) + half), (near, half)], half)
            self.copies[h].append(
                self.send(self.rows(onward, half, half), self.rows(right, half, half), self.along[h](3))
            )

    def step_three(self):
        self.pieces = []
        for h in range(2):
            for copy in self.copies[h][2:]:
                copy.wait_recv()
            s, left, right, total = (
                ref.at[h] for ref in (self.r.given, self.b_left, self.b_right, self.b_sum)
            )
            add_blocks(total, 0, [(s, self.row(h, 0)), (left, 0), (right, 0)], self.part)
            other = 1 - h
            for k in (2, 1, 3):
                row = lax.rem(self.place[other] + k, 4) * self.piece
                self.pieces.append(
                    self.send(self.rows(total, row, self.piece), self.b_got.at[h, k - 1], self.along[other](k))
                )

    def step_four(self):
        self.pairs = []
        for h in range(2):
            for copy in self.pieces[3 * h : 3 * h + 3]:
                copy.wait_recv()
            row = self.place[1 - h] * self.piece
            sources = [(self.b_sum.at[h], row)] + [(self.b_got.at[h, k], 0) for k in range(3)]
            add_blocks(self.b_piece.at[h], 0, sources, self.piece)
            self.pairs.append(self.send(self.b_piece.at[h], self.b_pair.at[h], self.grid.across))

    def own(self, h):
        return self.row(h, 0) + self.place[1 - h] * self.piece

    def step_five(self):
        self.spread = []
        for h in range(2):
            self.pairs[h].wait_recv()
            result = self.r.result.at[h]
            add_blocks(result, self.own(h), [(self.b_piece.at[h], 0), (self.b_pair.at[h], 0)], self.piece)
            mine = self.rows(result, self.own(h), self.piece)
            for k in (2, 1, 3):
                self.spread.append(self.send(mine, mine, self.along[1 - h](k)))

    def step_six(self):
        half = self.part // 2
        self.copies = []
        for h in range(2):
            for copy in self.spread[3 * h : 3 * h + 3]:
                copy.wait_recv()
            result = self.r.result.at[h]
            first = self.rows(result, self.row(h, 0), half)
            second = self.rows(result, self.row(h, 0) + half, half)
            fwd, back = self.along[h](1), self.along[h](3)
            self.copies.append([
                self.send(first, first, fwd),
                self.send(second, second, back),
                self.send(second, second, fwd),
                self.send(first, first, back),
            ])

    def step_seven(self):
        half = self.part // 2
        for h in range(2):
            result = self.r.result.at[h]
            self.copies[h][0].wait_recv()
            from_left = self.rows(result, self.row(h, 3), half)
            self.copies[h].append(self.send(from_left, from_left, self.along[h](1)))
            self.copies[h][1].wait_recv()
            from_right = self.rows(result, self.row(h, 1) + half, half)
            self.copies[h].append(self.send(from_right, from_right, self.along[h](3)))

    def step_eight(self):
        for h in range(2):
            for copy in self.copies[h][2:]:
                copy.wait_recv()

    def drain(self):
        for copy in self.used:
            copy.wait_send()


class SmallSum:
    def __init__(self, r, tag, first, rows, grid):
        self.r, self.first, self.rows, self.grid, self.used = r, first, rows, grid, []
        for name in ("given", "one", "two", "x", "y", "z", "sends", "recvs"):
            setattr(self, name, getattr(r, f"{tag}_{name}"))

    def send(self, source, target, peer):
        copy = remote(source, target, self.sends, self.recvs, len(self.used), peer)
        self.used.append(copy)
        copy.start()

    def add(self, ref, count):
        total = ref[0].astype(single)
        for k in range(1, count):
            total = total + ref[k].astype(single)
        return total.astype(bfloat)

    def step_one(self):
        grid = self.grid
        self.given[...] = self.r.small_wide[self.first : self.first + self.rows, :].astype(bfloat)
        self.x[grid.x] = self.given[...]
        for k in (2, 1, 3):
            self.send(self.given, self.x.at[grid.x], grid.along_x(k))

    def step_two(self):
        grid = self.grid
        for copy in self.used[:3]:
            copy.wait_recv()
        self.one[...] = self.add(self.x, 4)
        self.y[grid.y] = self.one[...]
        for k in (2, 1, 3):
            self.send(self.one, self.y.at[grid.y], grid.along_y(k))

    def step_three(self):
        grid = self.grid
        for copy in self.used[3:6]:
            copy.wait_recv()
        self.two[...] = self.add(self.y, 4)
        self.z[grid.plane] = self.two[...]
        self.send(self.two, self.z.at[grid.plane], grid.across)

    def step_four(self):
        self.used[6].wait_recv()
        self.r.small_out[self.first : self.first + self.rows, :] = self.add(self.z, 2)

    def drain(self):
        for copy in self.used:
            copy.wait_send()


def small_scratch(tag, rows, width):
    block = pltpu.VMEM((rows, width), bfloat)
    found = {f"{tag}_{name}": block for name in ("given", "one", "two")}
    for name, count in (("x", 4), ("y", 4), ("z", 2)):
        found[f"{tag}_{name}"] = pltpu.VMEM((count, rows, width), bfloat)
    found[f"{tag}_sends"] = pltpu.SemaphoreType.DMA((7,))
    found[f"{tag}_recvs"] = pltpu.SemaphoreType.DMA((7,))
    return found


def backward_kernel(r):
    core, sibling, opposite = tensor_place()
    grid = Grid()
    peers = [sibling, opposite, grid.across]
    peers += [grid.along_x(k) for k in (1, 2, 3)] + [grid.along_y(k) for k in (1, 2, 3)]
    greet(peers)
    moves = Moves(r.moves)

    def fetch(*names):
        return [moves.start(getattr(r, name + "_h"), getattr(r, name)) for name in names]

    def ready(copies):
        for copy in copies:
            copy.wait()

    loads_zero = fetch("section_three")
    loads_one = fetch("out", "qkvc", "log", "qkv", "low")
    loads_two = fetch("section_two", "slope", "act", "dense_low", "dense_in", "dense_out")
    loads_three = fetch("section_one", "images")
    stores = []
    sums = [TensorSum(r, n, r.total) for n in range(3)]
    width = r.out.shape[1]
    upper = GroupSum(r, "u", 0, 768, grid)
    dense = GroupSum(r, "d", 768, 1536, grid)
    lower = GroupSum(r, "l", 2304, 768, grid)
    early = SmallSum(r, "early", 0, EXPERTS, grid)
    late = SmallSum(r, "late", EXPERTS, SMALL - EXPERTS, grid)
    mixed = MixedSum(r)

    def deliver(array, row, rows, target):
        half = array.shape[1] // 2
        for h in range(2):
            source = r.result.at[h, pl.ds(row, rows), :]
            stores.append(
                moves.start(source, array.at[pl.ds(target, rows), pl.ds(h * half, half)])
            )

    r.small_wide[...] = jnp.zeros_like(r.small_wide)
    gates = [r.table[:, k : k + 1] for k in range(2)]
    pulls = [r.gate_sums[:, k : k + 1] for k in range(2)]
    mean = gates[0] * pulls[0] + gates[1] * pulls[1]
    experts = lax.broadcasted_iota(jnp.int32, (r.table.shape[0], EXPERTS), 1).astype(single)
    grad_logits = 0.0
    for k in range(2):
        pick = r.table[:, 4 + k : 5 + k] == experts
        grad_logits = grad_logits + jnp.where(pick, gates[k] * (pulls[k] - mean), 0.0)
    grad_logits = grad_logits.astype(bfloat)
    ready(loads_zero)
    pl.semaphore_wait(pltpu.get_barrier_semaphore(), 9)
    mixed.step_one()
    rows = r.section_three[...]
    normal, unused = normal_of(rows)
    moe_low = (normal * r.gain[3:4, :] + r.shift[3:4, :]).astype(bfloat)
    r.small_wide[0:EXPERTS, :] = dot_first(grad_logits, moe_low)
    grad_normed = r.grad_experts[...].astype(single) + dot_rows(grad_logits, r.router[...])
    grad_in, gain_part, shift_part = norm_back(grad_normed, rows, r.gain[3:4, :])
    grad = r.cotangent[...].astype(single) + grad_in
    r.grad[...] = grad
    r.small_wide[35:36, :] = gain_part
    r.small_wide[39:40, :] = shift_part
    r.small_wide[41:42, :] = jnp.sum(grad, axis=0, keepdims=True)
    ready(loads_one)
    attend_back(r, 1, grad)
    sums[0].start(attend_back_part(r, 1))
    attend_weights(r, 1, 0)
    upper.step_one()
    early.step_one()
    mixed.step_two()
    upper.step_two()
    early.step_two()
    upper.step_three()
    sums[0].finish()

    ready(loads_two)
    grad_in, gain_part, shift_part = norm_back(
        r.total[...].astype(single), r.section_two[...], r.gain[2:3, :]
    )
    r.small_wide[34:35, :] = gain_part
    r.small_wide[38:39, :] = shift_part
    grad = r.grad[...] + grad_in
    r.grad[...] = grad
    upper.step_four()
    early.step_three()
    grad_low = grad.astype(bfloat)
    r.grad_pre[...] = (dot_last(grad_low, r.dense_out[...]) * r.slope[...]).astype(bfloat)
    sums[1].start(lambda at: dot_last(r.grad_pre[...], r.dense_in[at, :]))
    put_grad(r, 768, dot_first(r.dense_low[...], r.grad_pre[...]))
    put_grad(r, 1536, dot_first(r.act[...], grad_low))
    dense.step_one()
    upper.step_five()
    mixed.step_three()
    early.step_four()
    dense.step_two()
    upper.step_six()
    sums[1].finish()

    ready(loads_three)
    grad_in, gain_part, shift_part = norm_back(
        r.total[...].astype(single), r.section_one[...], r.gain[1:2, :]
    )
    r.small_wide[33:34, :] = gain_part
    r.small_wide[37:38, :] = shift_part
    grad = r.grad[...] + grad_in
    r.grad[...] = grad
    r.small_wide[40:41, :] = jnp.sum(grad, axis=0, keepdims=True)
    upper.step_seven()
    attend_back(r, 0, grad)
    dense.step_three()
    sums[2].start(attend_back_part(r, 0))
    attend_weights(r, 0, 2304)
    lower.step_one()
    upper.step_eight()
    deliver(r.qkv_grad, 0, 3 * width, 3 * width)
    deliver(r.out_grad, 3 * width, width, width)
    dense.step_four()
    lower.step_two()
    dense.step_five()
    lower.step_three()
    sums[2].finish()

    grad_in, gain_part, shift_part = norm_back(
        r.total[...].astype(single), r.images[...].astype(single), r.gain[0:1, :]
    )
    r.small_wide[32:33, :] = gain_part
    r.small_wide[36:37, :] = shift_part
    r.input_grad[...] = r.grad[...] + grad_in
    late.step_one()
    dense.step_six()
    lower.step_four()
    late.step_two()
    lower.step_five()
    dense.step_seven()
    late.step_three()
    lower.step_six()
    late.step_four()
    lower.step_seven()
    dense.step_eight()
    deliver(r.dense_in_grad, 768, 768, 0)
    deliver(r.dense_out_grad, 1536, 768, 0)
    lower.step_eight()
    deliver(r.qkv_grad, 2304, 3 * width, 0)
    deliver(r.out_grad, 2304 + 3 * width, width, 0)
    for one in sums + [upper, dense, lower, early, late, mixed]:
        one.drain()
    ready(stores)


def moe_kernel(r):
    core, sibling, opposite = tensor_place()
    dp = lax.axis_index("dp")
    grid = Grid()
    half = r.arrived.shape[3] // 2
    tokens = r.table.shape[0]
    block = 4 * STRIDE
    barrier = pltpu.get_barrier_semaphore()

    def greet_one(k, carry):
        pl.semaphore_signal(barrier, inc=1, device_id={"dp": dp_peer(k)}, device_id_type=MESH)
        return carry

    lax.fori_loop(1, EXPERTS, greet_one, 0)
    greet([sibling, opposite])
    moves = Moves(r.moves)
    load_in = moves.start(r.expert_in_h.at[0], r.expert_in)
    load_out = moves.start(r.expert_out_h.at[0], r.expert_out)
    own_block = moves.start(r.sent.at[core, dp], r.arrived.at[core, dp])
    pl.semaphore_wait(barrier, EXPERTS + 1)

    def dispatch(peer, here):
        return pltpu.make_async_remote_copy(
            src_ref=r.sent.at[core, peer],
            dst_ref=r.arrived.at[core, here],
            send_sem=r.send_sems.at[peer],
            recv_sem=r.recv_sems.at[here],
            device_id={"dp": peer},
            device_id_type=MESH,
        )

    def share(source):
        block_ref = r.arrived.at[core, source]
        return remote(block_ref, block_ref, r.pass_sems, r.land_sems, source, sibling)

    def swap(source):
        return remote(r.give.at[source], r.got.at[source], r.give_sems, r.got_sems, source, sibling)

    def answer(peer, here):
        return pltpu.make_async_remote_copy(
            src_ref=r.answer.at[peer],
            dst_ref=r.returned.at[here],
            send_sem=r.back_sems.at[peer],
            recv_sem=r.home_sems.at[here],
            device_id={"dp": peer},
            device_id_type=MESH,
        )

    def offsets(p):
        return lax.rem(p + 1, 2), lax.rem(2 + p // 2 + lax.rem(p, 2), 4)

    def send_block(p, carry):
        dz, dx = offsets(p)
        base = lax.rem(grid.plane + dz, 2) * 16 + lax.rem(grid.x + dx, 4) * 4
        for dy in range(4):
            peer = base + lax.rem(grid.y + dy, 4)

            @pl.when(peer != dp)
            def start():
                dispatch(peer, dp).start()

        return carry

    def base_of(p):
        dz, dx = offsets(p)
        return lax.rem(grid.plane + dz, 2) * 16 + lax.rem(grid.x + 4 - dx, 4) * 4

    def receive(p):
        base = base_of(p)
        for dy in range(4):
            source = base + lax.rem(grid.y + 4 - dy, 4)

            @pl.when(source != dp)
            def wait():
                dispatch(source, source).wait_recv()

            @pl.when(source == dp)
            def wait_own():
                own_block.wait()

            share(source).start()

    def compute(p):
        base = base_of(p)
        for y in range(4):
            share(base + y).wait_recv()
            at = slice(y * STRIDE, (y + 1) * STRIDE)
            for h in range(2):
                rows = r.arrived[h, base + y].astype(single)
                r.wide_x[at, h * half : (h + 1) * half] = rows[:, :half]
                r.wide_g[at, h * half : (h + 1) * half] = rows[:, half:]
        at = pl.ds(pl.multiple_of(p * block, 16), block)
        rows = r.wide_x[...].astype(bfloat)
        rows_grad = r.wide_g[...].astype(bfloat)
        r.rows[at, :] = rows
        r.rows_grad[at, :] = rows_grad
        pre = dot_rows(rows, r.expert_in[...])
        grad_act = dot_last(rows_grad, r.expert_out[...])
        tail = 0.5 * (1.0 + lax.erf(pre * (0.5**0.5)))
        act = (pre * tail).astype(bfloat)
        slope = tail + pre * (jnp.exp(-0.5 * pre * pre) * 0.3989422804014327)
        grad_pre = (grad_act * slope).astype(bfloat)
        r.act[at, :] = act
        r.grad_pre[at, :] = grad_pre
        r.wide_x[...] = dot_rows(act, r.expert_out[...])
        r.wide_g[...] = dot_last(grad_pre, r.expert_in[...])
        for y in range(4):
            at = slice(y * STRIDE, (y + 1) * STRIDE)
            for which, target in ((1 - core, r.give), (core, r.kept)):
                columns = pl.ds(pl.multiple_of(which * half, LANES), half)
                target[base + y, :, :half] = r.wide_x[at, columns].astype(bfloat)
                target[base + y, :, half:] = r.wide_g[at, columns].astype(bfloat)
            swap(base + y).start()

    def respond(p):
        base = base_of(p)
        for y in range(4):
            source = base + y
            swap(source).wait_recv()
            total = r.kept[source].astype(single) + r.got[source].astype(single)
            r.answer[source] = total.astype(bfloat)

            @pl.when(source != dp)
            def start():
                answer(source, dp).start()

            @pl.when(source == dp)
            def keep():
                r.returned[dp] = total.astype(bfloat)

    def step(i, carry):
        pl.when(i < 8)(lambda: receive(i))
        pl.when((i >= 1) & (i < 9))(lambda: compute(i - 1))
        pl.when(i >= 2)(lambda: respond(i - 2))
        return carry

    lax.fori_loop(0, 8, send_block, 0)
    load_in.wait()
    load_out.wait()
    lax.fori_loop(0, 10, step, 0)
    r.weight_grad[0] = dot_first(r.act[...], r.rows_grad[...]).astype(bfloat)
    store_out = moves.start(r.weight_grad.at[0], r.expert_out_grad)
    r.weight_grad[1] = dot_first(r.rows[...], r.grad_pre[...]).astype(bfloat)
    store_in = moves.start(r.weight_grad.at[1], r.expert_in_grad)

    ids = lax.broadcasted_iota(jnp.int32, (tokens, SLOTS), 1).astype(single)
    for k in range(2):
        r.hits[k] = jnp.where(ids == r.table[:, 2 + k : 3 + k], 1.0, 0.0).astype(bfloat)

    def come_home(i, carry):
        p, dy = i // 4, lax.rem(i, 4)
        dz, dx = offsets(p)
        source = lax.rem(grid.plane + dz, 2) * 16 + lax.rem(grid.x + dx, 4) * 4 + lax.rem(grid.y + dy, 4)

        @pl.when(source != dp)
        def wait():
            answer(source, source).wait_recv()

        at = pl.ds(pl.multiple_of(source * STRIDE, 8), STRIDE)
        r.wide_home[at, :] = r.returned[source].astype(single)
        return carry

    lax.fori_loop(0, EXPERTS, come_home, 0)
    back = r.wide_home[:, half:].astype(bfloat)
    r.home[...] = r.wide_home[:, :half].astype(bfloat)
    own = r.cotangent[:, pl.ds(pl.multiple_of(core * half, LANES), half)].astype(single)

    second = [remote(r.part.at[j], r.part_got.at[j], r.z_sends, r.z_recvs, j, opposite) for j in range(3)]
    third = [remote(r.part_sum.at[j], r.part_end.at[j], r.z_sends, r.z_recvs, 4 + j, sibling) for j in range(3)]
    second.append(remote(r.gate_rows, r.gate_got, r.z_sends, r.z_recvs, 3, opposite))
    third.append(remote(r.gate_mid, r.gate_end, r.z_sends, r.z_recvs, 7, sibling))
    normed = dot_rows(r.hits[0], back) + dot_rows(r.hits[1], back)
    for j in range(3):
        r.part[j] = normed[:, j * LANES : (j + 1) * LANES].astype(bfloat)
        second[j].start()
    picked = [dot_rows(r.hits[k], r.home[...]) for k in range(2)]
    gate = [jnp.sum(p * own, axis=1, keepdims=True) for p in picked]
    level = lax.broadcasted_iota(jnp.int32, (tokens, tokens), 0)
    across = lax.broadcasted_iota(jnp.int32, (tokens, tokens), 1)
    r.gate_rows[...] = jnp.zeros_like(r.gate_rows)
    for k in range(2):
        spread = jnp.where(level == across, gate[k], 0.0)
        r.gate_rows[k : k + 1, :] = jnp.sum(spread, axis=0, keepdims=True)
    second[3].start()
    mixed = r.table[:, 0:1] * picked[0] + r.table[:, 1:2] * picked[1]
    for j in range(3):
        r.mixed[j] = mixed[:, j * LANES : (j + 1) * LANES].astype(bfloat)

    def columns(which, j):
        return pl.ds(pl.multiple_of((which * THIRDS + j) * LANES, LANES), LANES)

    for j in range(3):
        second[j].wait_recv()
        whole = (r.part[j].astype(single) + r.part_got[j].astype(single)).astype(bfloat)
        r.part_sum[j] = whole
        third[j].start()
        r.grad_experts[:, columns(core, j)] = whole
    second[3].wait_recv()
    r.gate_mid[...] = r.gate_rows[...] + r.gate_got[...]
    third[3].start()
    for j in range(3):
        third[j].wait_recv()
        r.grad_experts[:, columns(1 - core, j)] = r.part_end[j]
    third[3].wait_recv()
    r.gate_sums[...] = jnp.zeros_like(r.gate_sums)
    for k in range(2):
        sums = r.gate_mid[k : k + 1, :] + r.gate_end[k : k + 1, :]
        spread = jnp.where(level == across, sums, 0.0)
        r.gate_sums[:, k : k + 1] = jnp.sum(spread, axis=1, keepdims=True)
    for copy in second + third:
        copy.wait_send()

    def drain(k, carry):
        share(k).wait_send()
        swap(k).wait_send()

        @pl.when(k != dp)
        def wait():
            dispatch(k, dp).wait_send()
            answer(k, dp).wait_send()

        return carry

    lax.fori_loop(0, EXPERTS, drain, 0)
    store_out.wait()
    store_in.wait()


def moe_whole(sent, table, cotangent, expert_in, expert_out, collective_id):
    tokens, width = cotangent.shape
    half = width // 2
    slab = pltpu.VMEM((EXPERTS, STRIDE, width), bfloat)
    rows = pltpu.VMEM((SLOTS, width), bfloat)
    parts = pltpu.VMEM((3, tokens, LANES), bfloat)
    gate = pltpu.VMEM((8, tokens), single)
    block = pltpu.VMEM((4 * STRIDE, width), single)
    every = pltpu.SemaphoreType.DMA((EXPERTS,))
    scratch = {name: slab for name in ("give", "kept", "got", "answer", "returned")}
    scratch.update({name: rows for name in ("rows", "rows_grad", "act", "grad_pre")})
    scratch.update({name: parts for name in ("part", "part_got", "part_sum", "part_end")})
    scratch.update({"gate_" + name: gate for name in ("rows", "got", "mid", "end")})
    names = ("send", "recv", "pass", "land", "give", "got", "back", "home")
    scratch.update({name + "_sems": every for name in names})
    scratch.update(
        arrived=pltpu.VMEM((2, EXPERTS, STRIDE, width), bfloat),
        expert_in=pltpu.VMEM(expert_in.shape[1:], bfloat),
        expert_out=pltpu.VMEM(expert_out.shape[1:], bfloat),
        weight_grad=pltpu.VMEM((2,) + expert_in.shape[1:], bfloat),
        wide_x=block,
        wide_g=block,
        wide_home=pltpu.VMEM((SLOTS, width), single),
        home=pltpu.VMEM((SLOTS, half), bfloat),
        hits=pltpu.VMEM((2, tokens, SLOTS), bfloat),
        z_sends=pltpu.SemaphoreType.DMA((8,)),
        z_recvs=pltpu.SemaphoreType.DMA((8,)),
        moves=pltpu.SemaphoreType.DMA((8,)),
    )
    return big_call(
        moe_kernel,
        "moe",
        {
            "sent": (sent.reshape(2, EXPERTS, STRIDE, width), "hbm"),
            "table": (table, "vmem"),
            "cotangent": (cotangent, "vmem"),
            "expert_in_h": (expert_in, "hbm"),
            "expert_out_h": (expert_out, "hbm"),
        },
        {
            "expert_in_grad": (expert_in.shape[1:], bfloat, "hbm"),
            "expert_out_grad": (expert_out.shape[1:], bfloat, "hbm"),
            "mixed": ((3, tokens, LANES), bfloat, "vmem"),
            "grad_experts": ((tokens, width), bfloat, "vmem"),
            "gate_sums": ((tokens, LANES), single, "vmem"),
        },
        scratch,
        collective_id,
    )


class MixedSum:
    def __init__(self, r):
        core, sibling, opposite = tensor_place()
        self.r, self.core = r, core
        self.second = [
            remote(r.mixed.at[j], r.m_got.at[j], r.m_sends, r.m_recvs, j, opposite) for j in range(3)
        ]
        self.third = [
            remote(r.m_sum.at[j], r.m_end.at[j], r.m_sends, r.m_recvs, 3 + j, sibling) for j in range(3)
        ]

    def step_one(self):
        for copy in self.second:
            copy.start()

    def step_two(self):
        r = self.r
        for j in range(3):
            self.second[j].wait_recv()
            whole = r.mixed[j].astype(single) + r.m_got[j].astype(single)
            r.m_sum[j] = whole.astype(bfloat)
            self.third[j].start()
            self.put(self.core, j, r.m_sum[j])

    def put(self, which, j, value):
        at = pl.ds(pl.multiple_of((which * THIRDS + j) * LANES, LANES), LANES)
        rows = self.r.section_three[:, at] + value.astype(single)
        self.r.output[:, at] = rows.astype(bfloat)

    def step_three(self):
        for j in range(3):
            self.third[j].wait_recv()
            self.put(1 - self.core, j, self.r.m_end[j])

    def drain(self):
        for copy in self.second + self.third:
            copy.wait_send()


def finish_kernel(r):
    moves = Moves(r.moves)
    names = ("expert_in", "expert_out", "qkv", "out", "dense_in", "dense_out")
    whole = ("input_grad", "output")
    passing = [moves.start(getattr(r, name + "_h"), getattr(r, name + "_pass")) for name in whole]
    loads = [moves.start(getattr(r, name + "_h"), getattr(r, name + "_low")) for name in names]
    stores = []
    for name, load in zip(whole, passing):
        load.wait()
        stores.append(moves.start(getattr(r, name + "_pass"), getattr(r, name + "_f")))
    small = r.small[...].astype(single)
    part = r.qv_bias.shape[2]
    r.router[...] = small[:EXPERTS]
    r.gain[...] = small[32:36]
    r.shift[...] = small[36:40]
    r.out_bias[...] = small[40:42]
    r.qv_bias[0] = small[42:44, :part]
    r.qv_bias[1] = small[44:46, :part]
    for name, load in zip(names, loads):
        load.wait()
        low, wide = getattr(r, name + "_low"), getattr(r, name + "_wide")
        rows = low.shape[0]
        piece = 192

        def cast(i, carry):
            at = pl.ds(pl.multiple_of(i * piece, 16), piece)
            wide[at, :] = low[at, :].astype(single)
            return carry

        lax.fori_loop(0, rows // piece, cast, 0)
        stores.append(moves.start(wide, getattr(r, name + "_f")))
    for store in stores:
        store.wait()


def finish(last, moe, part, width):
    arrays = {"expert_in": moe.expert_in_grad, "expert_out": moe.expert_out_grad}
    arrays.update({"qkv": last.qkv_grad, "out": last.out_grad})
    arrays.update({"dense_in": last.dense_in_grad, "dense_out": last.dense_out_grad})
    ins = {name + "_h": (array, "hbm") for name, array in arrays.items()}
    ins["small"] = (last.small_out, "vmem")
    outs = {name + "_f": (array.shape, single, "hbm") for name, array in arrays.items()}
    whole = {"input_grad": last.input_grad, "output": last.output}
    for name, array in whole.items():
        ins[name + "_h"] = (array, "hbm")
        outs[name + "_f"] = (array.shape, array.dtype, "hbm")
    outs.update(
        router=((EXPERTS, width), single, "vmem"),
        gain=((4, width), single, "vmem"),
        shift=((4, width), single, "vmem"),
        out_bias=((2, width), single, "vmem"),
        qv_bias=((2, 2, part), single, "vmem"),
    )
    scratch = {name + "_low": pltpu.VMEM(array.shape, bfloat) for name, array in arrays.items()}
    scratch.update({name + "_wide": pltpu.VMEM(a.shape, single) for name, a in arrays.items()})
    scratch.update({name + "_pass": pltpu.VMEM(a.shape, a.dtype) for name, a in whole.items()})
    scratch["moves"] = pltpu.SemaphoreType.DMA((16,))
    return big_call(finish_kernel, "finish", ins, outs, scratch)


def per_device(
    images,
    routes,
    cotangent,
    qkv_weight,
    out_weight,
    qv_bias,
    out_bias,
    ln_gain,
    ln_bias,
    dense_in,
    dense_out,
    router,
    expert_in,
    expert_out,
):
    tokens, width = images.shape
    part = out_weight.shape[1]
    hidden = dense_in.shape[1]
    qkv = jnp.transpose(qkv_weight, (0, 2, 3, 1)).reshape(2, 3 * part, width)
    full, low = (tokens, width), bfloat
    kept = {
        "section_one": (full, single),
        "section_two": (full, single),
        "section_three": (full, single),
        "dense_low": (full, low),
        "slope": ((tokens, hidden), single),
        "act": ((tokens, hidden), low),
        "low": ((2, tokens, width), low),
        "qkvc": ((2, 4, tokens, part), low),
        "log": ((2, tokens, LANES), single),
    }
    weights = {
        "dense_in": (dense_in.shape, low),
        "dense_out": (dense_out.shape, low),
    }

    def vmem(names, table):
        return {name: pltpu.VMEM(*table[name]) for name in names}

    sections = ("section_one", "section_two", "section_three")
    outs = {name + ("" if name in sections else "_h"): kept[name] + ("hbm",) for name in kept}
    outs["sent"] = ((2, SLOTS, width), low, "hbm")
    outs["table"] = ((tokens, LANES), single, "vmem")
    scratch = sum_scratch(tokens, 3)
    scratch.update(vmem([name for name in kept if name not in sections], kept))
    scratch.update(vmem(list(weights), weights))
    scratch.update(
        section=pltpu.VMEM((3, tokens, width), single),
        cotangent=pltpu.VMEM(full, low),
        moe_low=pltpu.VMEM(full, low),
        routes=pltpu.VMEM((tokens, 2), jnp.int32),
        scaled=pltpu.VMEM((2, tokens, width), low),
        routed=pltpu.VMEM((2, SLOTS, width), low),
        total=pltpu.VMEM(full, low),
        moves=pltpu.SemaphoreType.DMA((24,)),
    )
    done = big_call(
        forward_kernel,
        "forward",
        {
            "images": (images, "vmem"),
            "qkv": (qkv, "vmem"),
            "out": (out_weight, "vmem"),
            "qv_bias": (qv_bias, "vmem"),
            "out_bias": (out_bias, "vmem"),
            "gain": (ln_gain, "vmem"),
            "shift": (ln_bias, "vmem"),
            "dense_in_h": (dense_in, "hbm"),
            "dense_out_h": (dense_out, "hbm"),
            "cotangent_h": (cotangent, "hbm"),
            "routes_row": (routes.T, "vmem"),
            "router": (router.T, "vmem"),
        },
        outs,
        scratch,
        1,
    )
    moe = moe_whole(done.sent, done.table, cotangent, expert_in, expert_out, 3)

    outs = {
        "output": (full, low, "vmem"),
        "input_grad": (full, single, "vmem"),
        "qkv_grad": ((6 * part, width), low, "hbm"),
        "out_grad": ((2 * part, width), low, "hbm"),
        "dense_in_grad": (dense_in.shape, low, "hbm"),
        "dense_out_grad": (dense_out.shape, low, "hbm"),
        "small_out": ((SMALL, width), low, "vmem"),
    }
    scratch = sum_scratch(tokens, 3)
    scratch.update(vmem(list(kept), kept))
    scratch.update(vmem(list(weights), weights))
    for tag, rows in (("u", 768), ("d", 1536), ("l", 768)):
        scratch.update(group_scratch(tag, rows, width // 2))
    scratch.update(small_scratch("early", EXPERTS, width))
    scratch.update(small_scratch("late", SMALL - EXPERTS, width))
    scratch.update(
        images=pltpu.VMEM(full, low),
        qkv=pltpu.VMEM(qkv.shape, low),
        out=pltpu.VMEM(out_weight.shape, low),
        total=pltpu.VMEM(full, low),
        grad=pltpu.VMEM(full, single),
        grad_low=pltpu.VMEM(full, low),
        grad_pre=pltpu.VMEM((tokens, hidden), low),
        grad_qkv=pltpu.VMEM((3, tokens, part), low),
        given=pltpu.VMEM((2, BIG, width // 2), low),
        result=pltpu.VMEM((2, BIG, width // 2), low),
        small_wide=pltpu.VMEM((SMALL, width), single),
        m_got=pltpu.VMEM((3, tokens, LANES), low),
        m_sum=pltpu.VMEM((3, tokens, LANES), low),
        m_end=pltpu.VMEM((3, tokens, LANES), low),
        m_sends=pltpu.SemaphoreType.DMA((6,)),
        m_recvs=pltpu.SemaphoreType.DMA((6,)),
        moves=pltpu.SemaphoreType.DMA((32,)),
    )
    ins = {
        "mixed": (moe.mixed, "vmem"),
        "grad_experts": (moe.grad_experts, "vmem"),
        "gate_sums": (moe.gate_sums, "vmem"),
        "table": (done.table, "vmem"),
        "router": (router.T, "vmem"),
        "cotangent": (cotangent, "vmem"),
        "gain": (ln_gain, "vmem"),
        "shift": (ln_bias, "vmem"),
        "images_h": (images, "hbm"),
        "qkv_h": (qkv, "hbm"),
        "out_h": (out_weight, "hbm"),
        "dense_in_h": (dense_in, "hbm"),
        "dense_out_h": (dense_out, "hbm"),
    }
    for name in kept:
        ins[name + "_h"] = (getattr(done, name if name in sections else name + "_h"), "hbm")
    last = big_call(backward_kernel, "backward", ins, outs, scratch, 2)
    end = finish(last, moe, part, width)
    qkv_weight_grad = jnp.transpose(end.qkv_f.reshape(2, 3, part, width), (0, 3, 1, 2))
    out_weight_grad = end.out_f.reshape(2, part, width)
    dense_in_grad, dense_out_grad = end.dense_in_f, end.dense_out_f
    router_grad = end.router.T
    ln_gain_grad, ln_bias_grad, out_bias_grad = end.gain, end.shift, end.out_bias
    qv_bias_grad = end.qv_bias
    output, input_grad = end.output_f, end.input_grad_f
    expert_in_grad, expert_out_grad = end.expert_in_f[None], end.expert_out_f[None]
    return (
        output,
        input_grad,
        qkv_weight_grad,
        out_weight_grad,
        qv_bias_grad,
        out_bias_grad,
        ln_gain_grad,
        ln_bias_grad,
        dense_in_grad,
        dense_out_grad,
        router_grad,
        expert_in_grad,
        expert_out_grad,
    )


def solution(mesh):
    in_specs = (
        P("dp", None),
        P("dp", None),
        P("dp", None),
        P(None, None, None, "tensor"),
        P(None, "tensor", None),
        P(None, None, "tensor"),
        P(),
        P(),
        P(),
        P(None, "tensor"),
        P("tensor", None),
        P(),
        P("dp", None, "tensor"),
        P("dp", "tensor", None),
    )
    out_specs = (
        P("dp", None),
        P("dp", None),
        P(None, None, None, "tensor"),
        P(None, "tensor", None),
        P(None, None, "tensor"),
        P(),
        P(),
        P(),
        P(None, "tensor"),
        P("tensor", None),
        P(),
        P("dp", None, "tensor"),
        P("dp", "tensor", None),
    )
    return jax.shard_map(
        per_device, mesh=mesh, in_specs=in_specs, out_specs=out_specs, check_vma=False
    )
```
